32 devices in a mesh: grp: 2 (over y), feat: 8 (over z, x), tok: 2 (over core).
Axes of the slice: x: 2, y: 2, z: 4, core: 2. Of those that a mesh axis runs over, the one named last changes fastest.
Arguments:
- tokens: bfloat16 [32, 8192], P(('grp', 'feat'), 'tok'), parts along dimension 0, may hold values from -6 to 6
- b_pre: bfloat16 [16384], P(('grp', 'tok')), parts along dimension 0, may hold values from -3 to 3
- pre_codes: float32 [32, 64], P('grp'), parts along dimension 0, may hold values from -6 to 6
- top_idx: int32 [32, 64], P('grp'), parts along dimension 0, may hold values from 0 to 16777215, as said below
- blocks: int32 [16], P(('grp', 'feat')), parts along dimension 0, may hold values from 0 to 131071, as said below
- counts: int32 [16], P(('grp', 'feat')), parts along dimension 0, may hold values from 43 to 128, as said below
- dict_rows: bfloat16 [2048, 8192], P(('grp', 'feat'), 'tok'), parts along dimension 0, may hold values from -0.5 to 0.5
Outputs:
- grad_rows: bfloat16 [2048, 8192], P(('grp', 'feat'), 'tok'), parts along dimension 0
- grad_enc: bfloat16 [16384, 1024], P(('grp', 'tok'), 'feat'), parts along dimension 0
- grad_benc: float32 [2048], P(('grp', 'feat')), parts along dimension 0
The draws below stay inside these ranges and needn't reach their ends.
There are 2 independent parts, one for each index of `grp`. The reference program is written for one: setup_inputs(seed, part) draws one part's arguments, and reference() takes and returns one part's arrays. A program takes and returns all parts, laid end to end along the dimension named above; each array names one. Nothing has to cross between parts.
Inputs may be any that keep to these rules, and one draw needn't show every extreme that they name: `blocks`: each index of feat holds a different block, block f lying in [f * 131072 / 8, (f + 1) * 131072 / 8). `counts`: some block has exactly 128 live slots and some exactly 43. `top_idx`: each row names 64 different latents, each of them a live slot's latent: blocks[f] * 128 + j with j < counts[f].
All inputs are finite; a program needn't handle non-finite values.
Results may differ from the reference program's by a relative error of at most 0.0064.
Values may be sent and summed in bfloat16 or wider, within the bound.
No kernel may reach another device: no remote copies, remote signals or barrier semaphores. Data moves between devices by JAX's collectives and lax.ppermute only.
A program may use at most 64 MiB of HBM per device.

```python
import jax
import jax.numpy as jnp
from jax import lax

D = 8192
K = 64
BLOCK = 128
TOKENS = 16
SLOTS = 1024
BLOCKS = 131072
N_FEAT = 8


def layout(key):
    per_shard = BLOCKS // N_FEAT
    offsets_drawn = jax.random.randint(jax.random.fold_in(key, 101), (N_FEAT,), 0, per_shard)
    blocks_drawn = jnp.arange(N_FEAT, dtype=jnp.int32) * per_shard + offsets_drawn
    lowest = BLOCK // 3 + 1
    uniform_int = jax.random.randint(jax.random.fold_in(key, 102), (N_FEAT,), 0, 1000)
    spread_part = (BLOCK - lowest) * uniform_int * uniform_int // 1000
    counts_drawn = lowest + spread_part * uniform_int // 1000000
    order = jax.random.permutation(jax.random.fold_in(key, 103), N_FEAT)
    counts_drawn = counts_drawn.at[order[0]].set(BLOCK).at[order[1]].set(lowest)
    return (blocks_drawn.astype(jnp.int32), counts_drawn.astype(jnp.int32))


def draw_blocks(key, part):
    shared = layout(key)
    return shared[0]


def draw_counts(key, part):
    shared = layout(key)
    return shared[1]


def draw_top_idx(key, part):
    blocks_drawn, counts_drawn = layout(key)
    key = jax.random.fold_in(key, 7)
    positions = jnp.arange(SLOTS, dtype=jnp.int32)
    live_slots = positions % BLOCK < counts_drawn[positions // BLOCK]
    scores = jax.random.randint(key, (TOKENS, SLOTS), 0, 65536) * SLOTS + positions[None, :]
    scores = jnp.where(live_slots[None, :], scores, -1 - positions[None, :])
    best_scores, chosen = lax.top_k(scores, K)
    return (blocks_drawn[chosen // BLOCK] * BLOCK + chosen % BLOCK).astype(jnp.int32)


def shard_levels(rng, shape, pieces, low, high):
    loudness, own = 1.0, jax.random.fold_in(rng, 6)
    for axis_at, parts in pieces:
        draws = jnp.exp(jax.random.uniform(jax.random.fold_in(own, axis_at), (parts,), jnp.float32, low / len(pieces), high / len(pieces)))
        loudness = loudness * jnp.repeat(draws, shape[axis_at] // parts).reshape([-1 if axis == axis_at else 1 for axis in range(len(shape))])
    return loudness


def scatter_about(rng, shape, deviation, limit, pieces=(), kind=jnp.bfloat16):
    array = jax.random.normal(rng, shape, jnp.float32) * deviation
    if len(pieces) > 0:
        array = shard_levels(rng, shape, pieces, -0.22, 0.18) * array
    return jnp.clip(array, min=-limit, max=limit).astype(kind)


def setup_inputs(seed: int = 0, part: int = 0) -> dict:
    seeds = jax.random.split(jax.random.key(seed), 8)
    part_splits = jax.random.split(jax.random.fold_in(seeds[7], part), 8)
    tokens = scatter_about(part_splits[0], (TOKENS, D), 1.0, 6.0, ((0, 8), (1, 2)))
    b_pre = scatter_about(part_splits[1], (D,), 0.5, 3.0, ((0, 2),))
    pre_codes = scatter_about(part_splits[2], (TOKENS, K), 1.5, 6.0, (), jnp.float32)
    top_idx = draw_top_idx(jax.random.fold_in(jax.random.fold_in(seeds[7], part), 71), part)
    blocks = draw_blocks(jax.random.fold_in(jax.random.fold_in(seeds[7], part), 71), part)
    counts = draw_counts(jax.random.fold_in(jax.random.fold_in(seeds[7], part), 71), part)
    dict_rows = scatter_about(part_splits[6], (SLOTS, D), 128 ** -0.5, 0.5, ((0, 8), (1, 2)))
    return dict(tokens=tokens, b_pre=b_pre, pre_codes=pre_codes, top_idx=top_idx, blocks=blocks, counts=counts, dict_rows=dict_rows)


def slot_codes(slot_ids, live_slots, top_idx, pre_codes):
    matches = (top_idx[:, :, None] == slot_ids[None, None, :]) & live_slots[None, None, :]
    positive = jnp.maximum(pre_codes, 0.0)
    code_block = jnp.sum(jnp.where(matches, positive[:, :, None], jnp.zeros_like(positive)[:, :, None]), axis=1)
    keep_mask = jnp.any(matches & (pre_codes > 0.0)[:, :, None], axis=1)
    return code_block, keep_mask


def reference(tokens, b_pre, pre_codes, top_idx, blocks, counts, dict_rows):
    offsets = jnp.arange(BLOCK, dtype=jnp.int32)
    slot_ids = blocks.astype(jnp.int32)[:, None] * BLOCK + offsets[None, :]
    live_slots = offsets[None, :] < counts.astype(jnp.int32)[:, None]

    def per_shard(pair):
        return slot_codes(pair[0], pair[1], top_idx.astype(jnp.int32), pre_codes)

    code_all, keep_all = lax.map(per_shard, (slot_ids, live_slots))
    code_dense = jnp.transpose(code_all, (1, 0, 2)).reshape(TOKENS, SLOTS).astype(jnp.bfloat16)
    keep_dense = jnp.transpose(keep_all, (1, 0, 2)).reshape(TOKENS, SLOTS)
    centered = lax.optimization_barrier((tokens.astype(jnp.float32) - b_pre.astype(jnp.float32)).astype(jnp.bfloat16))
    rebuilt = jnp.dot(code_dense, dict_rows, preferred_element_type=jnp.float32)
    scaled = (0.25 * (rebuilt - centered.astype(jnp.float32))).astype(jnp.bfloat16)
    code_grad = jnp.dot(scaled, dict_rows.T, preferred_element_type=jnp.float32)
    pre_grad = jnp.where(keep_dense, code_grad, jnp.zeros_like(code_grad)).astype(jnp.bfloat16)
    grad_rows = jnp.dot(code_dense.T, scaled, preferred_element_type=jnp.float32).astype(jnp.bfloat16)
    grad_enc = jnp.dot(centered.T, pre_grad, preferred_element_type=jnp.float32).astype(jnp.bfloat16)
    grad_benc = jnp.sum(pre_grad.astype(jnp.float32), axis=0)
    return grad_rows, grad_enc, grad_benc
```

```python
import jax
import jax.numpy as jnp
from jax import lax
from jax.sharding import PartitionSpec as P

DIRECT = 8


def swapped(shard, axis, distance):
    return lax.ppermute(shard, axis, [(i, i ^ distance) for i in range(lax.axis_size(axis))])


def is_direct(axis):
    size = lax.axis_size(axis)
    return size <= DIRECT and size & (size - 1) == 0


def by_distance(array, axis):
    size = lax.axis_size(axis)
    if not is_direct(axis):
        return array
    blocks = array.reshape((size, array.shape[0] // size) + array.shape[1:])
    order = lax.axis_index(axis) ^ jnp.arange(size, dtype=jnp.int32)
    return blocks[order].reshape(array.shape)


def gathered(own, axis):
    if not is_direct(axis):
        return lax.all_gather(own, axis, axis=0, tiled=True)
    parts = [own] + [swapped(own, axis, k) for k in range(1, lax.axis_size(axis))]
    return jnp.concatenate(parts, axis=0)


def scattered_sum(whole, axis):
    size = lax.axis_size(axis)
    if not is_direct(axis):
        return lax.psum_scatter(whole, axis, scatter_dimension=0, tiled=True)
    rows = whole.shape[0] // size
    total = whole[:rows]
    for k in range(1, size):
        part = whole[k * rows : (k + 1) * rows].astype(jnp.bfloat16)
        total = total + swapped(part, axis, k).astype(jnp.float32)
    return total


def slot_codes(slot_ids, live_slots, top_idx, pre_codes):
    matches = (top_idx[:, :, None] == slot_ids[None, None, :]) & live_slots[None, None, :]
    positive = jnp.maximum(pre_codes, 0.0)
    code_block = jnp.sum(
        jnp.where(matches, positive[:, :, None], jnp.zeros_like(positive)[:, :, None]), axis=1
    )
    keep_mask = jnp.any(matches & (pre_codes > 0.0)[:, :, None], axis=1)
    return (code_block, keep_mask)


def local(tokens, b_pre, pre_codes, top_idx, blocks, counts, dict_rows):
    block_rows = dict_rows.shape[0]
    centered_own = lax.optimization_barrier(
        (tokens.astype(jnp.float32) - b_pre.astype(jnp.float32)).astype(jnp.bfloat16)
    )
    centered = gathered(centered_own, "feat")
    offsets = jnp.arange(block_rows, dtype=jnp.int32)
    slot_ids = blocks[0] * block_rows + offsets
    live_slots = offsets < counts[0]
    code_block, keep_mask = slot_codes(
        slot_ids, live_slots, by_distance(top_idx, "feat"), by_distance(pre_codes, "feat")
    )
    code_block = code_block.astype(jnp.bfloat16)
    rebuilt_own = scattered_sum(
        jnp.dot(code_block, dict_rows, preferred_element_type=jnp.float32), "feat"
    )
    scaled_own = (0.25 * (rebuilt_own - centered_own.astype(jnp.float32))).astype(jnp.bfloat16)
    scaled = gathered(scaled_own, "feat")
    code_half = lax.dot_general(
        scaled, dict_rows, (((1,), (1,)), ((), ())), preferred_element_type=jnp.float32
    )
    code_grad = code_half + swapped(code_half, "tok", 1)
    pre_grad = jnp.where(keep_mask, code_grad, jnp.zeros_like(code_grad)).astype(jnp.bfloat16)
    grad_rows = lax.dot_general(
        code_block, scaled, (((0,), (0,)), ((), ())), preferred_element_type=jnp.float32
    ).astype(jnp.bfloat16)
    grad_enc = lax.dot_general(
        centered, pre_grad, (((0,), (0,)), ((), ())), preferred_element_type=jnp.float32
    ).astype(jnp.bfloat16)
    grad_benc = jnp.sum(pre_grad.astype(jnp.float32), axis=0)
    return (grad_rows, grad_enc, grad_benc)


def solution(mesh):
    return jax.shard_map(
        local,
        mesh=mesh,
        in_specs=(
            P(("grp", "feat"), "tok"),
            P(("grp", "tok")),
            P("grp", None),
            P("grp", None),
            P(("grp", "feat")),
            P(("grp", "feat")),
            P(("grp", "feat"), "tok"),
        ),
        out_specs=(P(("grp", "feat"), "tok"), P(("grp", "tok"), "feat"), P(("grp", "feat"))),
        check_vma=False,
    )
```

```python
import jax
import jax.numpy as jnp
from jax import lax
from jax.sharding import PartitionSpec as P


def swapped(shard, axis, distance):
    return lax.ppermute(shard, axis, [(i, i ^ 1 << distance) for i in range(lax.axis_size(axis))])


def exchanged(blocks, axis):
    return lax.all_to_all(blocks, axis, split_axis=0, concat_axis=0, tiled=True)


def gathered(own, axis):
    size = lax.axis_size(axis)
    copies = jnp.broadcast_to(own[None], (size,) + own.shape)
    return exchanged(copies, axis).reshape((size * own.shape[0],) + own.shape[1:])


def scattered_sum(whole, axis):
    size = lax.axis_size(axis)
    parts = whole.astype(jnp.bfloat16).reshape((size, whole.shape[0] // size) + whole.shape[1:])
    return jnp.sum(exchanged(parts, axis).astype(jnp.float32), axis=0)


def slot_codes(slot_ids, live_slots, top_idx, pre_codes):
    matches = (top_idx[:, :, None] == slot_ids[None, None, :]) & live_slots[None, None, :]
    positive = jnp.maximum(pre_codes, 0.0)
    code_block = jnp.sum(
        jnp.where(matches, positive[:, :, None], jnp.zeros_like(positive)[:, :, None]), axis=1
    )
    keep_mask = jnp.any(matches & (pre_codes > 0.0)[:, :, None], axis=1)
    return (code_block, keep_mask)


def local(tokens, b_pre, pre_codes, top_idx, blocks, counts, dict_rows):
    block_rows = dict_rows.shape[0]
    offsets = jnp.arange(block_rows, dtype=jnp.int32)
    slot_ids = blocks[0] * block_rows + offsets
    live_slots = offsets < counts[0]
    code_block, keep_mask = slot_codes(slot_ids, live_slots, top_idx, pre_codes)
    code_block = code_block.astype(jnp.bfloat16)
    centered_own = lax.optimization_barrier(
        (tokens.astype(jnp.float32) - b_pre.astype(jnp.float32)).astype(jnp.bfloat16)
    )
    centered = gathered(centered_own, "feat")
    rebuilt_own = scattered_sum(
        jnp.dot(code_block, dict_rows, preferred_element_type=jnp.float32), "feat"
    )
    scaled_own = (0.25 * (rebuilt_own - centered_own.astype(jnp.float32))).astype(jnp.bfloat16)
    scaled = gathered(scaled_own, "feat")
    code_half = lax.dot_general(
        scaled, dict_rows, (((1,), (1,)), ((), ())), preferred_element_type=jnp.float32
    )
    code_grad = code_half + swapped(code_half, "tok", 0)
    pre_grad = jnp.where(keep_mask, code_grad, jnp.zeros_like(code_grad)).astype(jnp.bfloat16)
    grad_rows = lax.dot_general(
        code_block, scaled, (((0,), (0,)), ((), ())), preferred_element_type=jnp.float32
    ).astype(jnp.bfloat16)
    grad_enc = lax.dot_general(
        centered, pre_grad, (((0,), (0,)), ((), ())), preferred_element_type=jnp.float32
    ).astype(jnp.bfloat16)
    grad_benc = jnp.sum(pre_grad.astype(jnp.float32), axis=0)
    return (grad_rows, grad_enc, grad_benc)


def solution(mesh):
    return jax.shard_map(
        local,
        mesh=mesh,
        in_specs=(
            P(("grp", "feat"), "tok"),
            P(("grp", "tok")),
            P("grp", None),
            P("grp", None),
            P(("grp", "feat")),
            P(("grp", "feat")),
            P(("grp", "feat"), "tok"),
        ),
        out_specs=(P(("grp", "feat"), "tok"), P(("grp", "tok"), "feat"), P(("grp", "feat"))),
        check_vma=False,
    )
```

```python
import functools

import jax
import jax.numpy as jnp
from jax import lax
from jax.experimental import pallas as pl
from jax.experimental.pallas import tpu as pltpu
from jax.sharding import PartitionSpec as P

VMEM = pl.BlockSpec(memory_space=pltpu.VMEM)


def swapped(shard, axis, distance):
    return lax.ppermute(shard, axis, [(i, i ^ distance) for i in range(lax.axis_size(axis))])


def halves(width):
    half = width // 2
    bit = lax.axis_index("feat") & 1
    return (
        pl.multiple_of(bit * half, half),
        pl.multiple_of((1 - bit) * half, half),
        half,
    )


def share(code, rows_ref, centered_ref, at, half):
    total = jnp.dot(code, rows_ref[:, pl.ds(at, half)], preferred_element_type=jnp.float32)
    rows = centered_ref.shape[0]
    centered = centered_ref[:, pl.ds(at, half)].astype(jnp.float32)
    token = lax.broadcasted_iota(jnp.int32, (total.shape[0], 1), 0)
    first = lax.axis_index("feat") * rows
    for i in range(rows):
        total -= jnp.where(token == first + i, centered[i : i + 1, :], 0.0)
    return total


def codes_kernel(
    top_ref, pre_ref, block_ref, count_ref, rows_ref, centered_ref, code_ref, raw_ref, send_ref
):
    tokens, latents = top_ref.shape
    slots, width = rows_ref.shape
    offsets = lax.broadcasted_iota(jnp.int32, (1, slots), 1)
    slot_ids = jnp.where(offsets < count_ref[...], block_ref[...] * slots + offsets, -1)
    top, pre = top_ref[...], pre_ref[...]
    raw = jnp.zeros((tokens, slots), jnp.float32)
    for k in range(latents):
        raw = jnp.where(top[:, k : k + 1] == slot_ids, pre[:, k : k + 1], raw)
    raw_ref[...] = raw
    code = jnp.maximum(raw, 0.0).astype(jnp.bfloat16)
    code_ref[...] = code
    _, other, half = halves(width)
    send_ref[...] = share(code, rows_ref, centered_ref, other, half).astype(jnp.bfloat16)


def codes(top_idx, pre_codes, blocks, counts, dict_rows, centered_own):
    tokens = top_idx.shape[0]
    slots, width = dict_rows.shape
    return pl.pallas_call(
        codes_kernel,
        out_shape=(
            jax.ShapeDtypeStruct((tokens, slots), jnp.bfloat16),
            jax.ShapeDtypeStruct((tokens, slots), jnp.float32),
            jax.ShapeDtypeStruct((tokens, width // 2), jnp.bfloat16),
        ),
        in_specs=[VMEM] * 6,
        out_specs=(VMEM,) * 3,
        cost_estimate=pl.CostEstimate(flops=10**6, bytes_accessed=2**20, transcendentals=0),
        name="codes",
    )(top_idx, pre_codes, blocks.reshape(1, 1), counts.reshape(1, 1), dict_rows, centered_own)


def own_kernel(code_ref, rows_ref, centered_ref, total_ref):
    own, _, half = halves(rows_ref.shape[1])
    total_ref[...] = share(code_ref[...], rows_ref, centered_ref, own, half)


def own_part(code, dict_rows, centered_own):
    half = dict_rows.shape[1] // 2
    return pl.pallas_call(
        own_kernel,
        out_shape=jax.ShapeDtypeStruct((code.shape[0], half), jnp.float32),
        in_specs=[VMEM] * 3,
        out_specs=VMEM,
        cost_estimate=pl.CostEstimate(flops=10**6, bytes_accessed=2**19, transcendentals=0),
        name="own_part",
    )(code, dict_rows, centered_own)


def code_half_kernel(own_ref, other_ref, rows_ref, half_ref, scaled_ref):
    own_at, other_at, half = halves(rows_ref.shape[1])
    total = jnp.zeros(half_ref.shape, jnp.float32)
    for ref, at in ((own_ref, own_at), (other_ref, other_at)):
        part = ref[...]
        scaled_ref[:, pl.ds(at, half)] = part
        total += lax.dot_general(
            part,
            rows_ref[:, pl.ds(at, half)],
            (((1,), (1,)), ((), ())),
            preferred_element_type=jnp.float32,
        )
    half_ref[...] = total


def code_half_of(scaled_own, scaled_other, dict_rows):
    tokens = scaled_own.shape[0]
    slots, width = dict_rows.shape
    return pl.pallas_call(
        code_half_kernel,
        out_shape=(
            jax.ShapeDtypeStruct((tokens, slots), jnp.float32),
            jax.ShapeDtypeStruct((tokens, width), jnp.bfloat16),
        ),
        in_specs=[VMEM] * 3,
        out_specs=(VMEM, VMEM),
        cost_estimate=pl.CostEstimate(flops=10**6, bytes_accessed=2**20, transcendentals=0),
        name="code_half",
    )(scaled_own, scaled_other, dict_rows)


def masked_kernel(rows, raw_ref, mine_ref, theirs_ref, grad_ref, benc_ref):
    tokens = raw_ref.shape[0]
    code_grad = mine_ref[...] + theirs_ref[...]
    pre_grad = jnp.where(raw_ref[...] > 0.0, code_grad, 0.0).astype(jnp.bfloat16)
    benc_ref[...] = jnp.sum(pre_grad.astype(jnp.float32), axis=0, keepdims=True)
    place = lax.broadcasted_iota(jnp.int32, (tokens, tokens), 0)
    token = lax.broadcasted_iota(jnp.int32, (tokens, tokens), 1)
    first = lax.axis_index("feat") * rows
    order = jnp.where(token == (place ^ first), 1.0, 0.0).astype(jnp.bfloat16)
    grad_ref[...] = jnp.dot(order, pre_grad, preferred_element_type=jnp.float32).astype(
        jnp.bfloat16
    )


def masked(raw, mine, theirs, rows):
    tokens, slots = raw.shape
    return pl.pallas_call(
        functools.partial(masked_kernel, rows),
        out_shape=(
            jax.ShapeDtypeStruct((tokens, slots), jnp.bfloat16),
            jax.ShapeDtypeStruct((1, slots), jnp.float32),
        ),
        in_specs=[VMEM] * 3,
        out_specs=(VMEM, VMEM),
        cost_estimate=pl.CostEstimate(flops=10**5, bytes_accessed=2**15, transcendentals=0),
        name="masked",
    )(raw, mine, theirs)


def local(tokens, b_pre, pre_codes, top_idx, blocks, counts, dict_rows):
    size = lax.axis_size("feat")
    rows, width = tokens.shape
    centered_own = lax.optimization_barrier(
        (tokens.astype(jnp.float32) - b_pre.astype(jnp.float32)).astype(jnp.bfloat16)
    )
    code, raw, send = codes(top_idx, pre_codes, blocks, counts, dict_rows, centered_own)

    arrived = swapped(send, "feat", 1)
    total = own_part(code, dict_rows, centered_own) + arrived.astype(jnp.float32)
    distance = 2
    while distance < size:
        total = total + swapped(total.astype(jnp.bfloat16), "feat", distance).astype(jnp.float32)
        distance *= 2
    scaled_own = (0.25 * total).astype(jnp.bfloat16)
    scaled_other = swapped(scaled_own, "feat", 1)

    centered = centered_own[None]
    distance = 1
    while distance < size:
        centered = jnp.concatenate([centered, swapped(centered, "feat", distance)], axis=0)
        distance *= 2
    centered = centered.reshape(size * rows, width)

    code_half, scaled = code_half_of(scaled_own, scaled_other, dict_rows)
    theirs = swapped(code_half, "tok", 1)
    grad_rows = lax.dot_general(
        code, scaled, (((0,), (0,)), ((), ())), preferred_element_type=jnp.float32
    ).astype(jnp.bfloat16)
    pre_grad, grad_benc = masked(raw, code_half, theirs, rows)
    grad_enc = lax.dot_general(
        centered, pre_grad, (((0,), (0,)), ((), ())), preferred_element_type=jnp.float32
    ).astype(jnp.bfloat16)
    return (grad_rows, grad_enc, grad_benc.reshape(-1))


def solution(mesh):
    return jax.shard_map(
        local,
        mesh=mesh,
        in_specs=(
            P(("grp", "feat"), "tok"),
            P(("grp", "tok")),
            P("grp", None),
            P("grp", None),
            P(("grp", "feat")),
            P(("grp", "feat")),
            P(("grp", "feat"), "tok"),
        ),
        out_specs=(P(("grp", "feat"), "tok"), P(("grp", "tok"), "feat"), P(("grp", "feat"))),
        check_vma=False,
    )
```

```python
import functools

import jax
import jax.numpy as jnp
from jax import lax
from jax.experimental import pallas as pl
from jax.experimental.pallas import tpu as pltpu
from jax.sharding import PartitionSpec as P

VMEM = pl.BlockSpec(memory_space=pltpu.VMEM)
PARAMS = pltpu.CompilerParams(vmem_limit_bytes=16 * 2**20)


def swapped(shard, axis, distance):
    return lax.ppermute(shard, axis, [(i, i ^ distance) for i in range(lax.axis_size(axis))])


def halves(width):
    half = width // 2
    bit = lax.axis_index("feat") & 1
    return (
        pl.multiple_of(bit * half, half),
        pl.multiple_of((1 - bit) * half, half),
        half,
    )


def share(code, rows_ref, centered_ref, at, half):
    total = jnp.dot(code, rows_ref[:, pl.ds(at, half)], preferred_element_type=jnp.float32)
    rows = centered_ref.shape[0]
    centered = centered_ref[:, pl.ds(at, half)].astype(jnp.float32)
    token = lax.broadcasted_iota(jnp.int32, (total.shape[0], 1), 0)
    first = lax.axis_index("feat") * rows
    for i in range(rows):
        total -= jnp.where(token == first + i, centered[i : i + 1, :], 0.0)
    return total


def codes_kernel(
    top_ref, pre_ref, block_ref, count_ref, rows_ref, centered_ref, code_ref, raw_ref, send_ref
):
    tokens, latents = top_ref.shape
    slots, width = rows_ref.shape
    offsets = lax.broadcasted_iota(jnp.int32, (1, slots), 1)
    slot_ids = jnp.where(offsets < count_ref[...], block_ref[...] * slots + offsets, -1)
    top, pre = top_ref[...], pre_ref[...]
    raw = jnp.zeros((tokens, slots), jnp.float32)
    for k in range(latents):
        raw = jnp.where(top[:, k : k + 1] == slot_ids, pre[:, k : k + 1], raw)
    raw_ref[...] = raw
    code = jnp.maximum(raw, 0.0).astype(jnp.bfloat16)
    code_ref[...] = code
    _, other, half = halves(width)
    send_ref[...] = share(code, rows_ref, centered_ref, other, half).astype(jnp.bfloat16)


def codes(top_idx, pre_codes, blocks, counts, dict_rows, centered_own):
    tokens = top_idx.shape[0]
    slots, width = dict_rows.shape
    return pl.pallas_call(
        codes_kernel,
        out_shape=(
            jax.ShapeDtypeStruct((tokens, slots), jnp.bfloat16),
            jax.ShapeDtypeStruct((tokens, slots), jnp.float32),
            jax.ShapeDtypeStruct((tokens, width // 2), jnp.bfloat16),
        ),
        in_specs=[VMEM] * 6,
        out_specs=(VMEM,) * 3,
        compiler_params=PARAMS,
        cost_estimate=pl.CostEstimate(flops=10**6, bytes_accessed=2**20, transcendentals=0),
        name="codes",
    )(top_idx, pre_codes, blocks.reshape(1, 1), counts.reshape(1, 1), dict_rows, centered_own)


def own_kernel(code_ref, rows_ref, centered_ref, total_ref):
    own, _, half = halves(rows_ref.shape[1])
    total_ref[...] = share(code_ref[...], rows_ref, centered_ref, own, half)


def own_part(code, dict_rows, centered_own):
    half = dict_rows.shape[1] // 2
    return pl.pallas_call(
        own_kernel,
        out_shape=jax.ShapeDtypeStruct((code.shape[0], half), jnp.float32),
        in_specs=[VMEM] * 3,
        out_specs=VMEM,
        compiler_params=PARAMS,
        cost_estimate=pl.CostEstimate(flops=10**6, bytes_accessed=2**19, transcendentals=0),
        name="own_part",
    )(code, dict_rows, centered_own)


def code_half_kernel(own_ref, other_ref, rows_ref, half_ref, scaled_ref):
    own_at, other_at, half = halves(rows_ref.shape[1])
    total = jnp.zeros(half_ref.shape, jnp.float32)
    for ref, at in ((own_ref, own_at), (other_ref, other_at)):
        part = ref[...]
        scaled_ref[:, pl.ds(at, half)] = part
        total += lax.dot_general(
            part,
            rows_ref[:, pl.ds(at, half)],
            (((1,), (1,)), ((), ())),
            preferred_element_type=jnp.float32,
        )
    half_ref[...] = total


def code_half_of(scaled_own, scaled_other, dict_rows):
    tokens = scaled_own.shape[0]
    slots, width = dict_rows.shape
    return pl.pallas_call(
        code_half_kernel,
        out_shape=(
            jax.ShapeDtypeStruct((tokens, slots), jnp.float32),
            jax.ShapeDtypeStruct((tokens, width), jnp.bfloat16),
        ),
        in_specs=[VMEM] * 3,
        out_specs=(VMEM, VMEM),
        compiler_params=PARAMS,
        cost_estimate=pl.CostEstimate(flops=10**6, bytes_accessed=2**20, transcendentals=0),
        name="code_half",
    )(scaled_own, scaled_other, dict_rows)


def masked_kernel(rows, raw_ref, mine_ref, theirs_ref, grad_ref, benc_ref):
    tokens = raw_ref.shape[0]
    code_grad = mine_ref[...] + theirs_ref[...]
    pre_grad = jnp.where(raw_ref[...] > 0.0, code_grad, 0.0).astype(jnp.bfloat16)
    benc_ref[...] = jnp.sum(pre_grad.astype(jnp.float32), axis=0, keepdims=True)
    place = lax.broadcasted_iota(jnp.int32, (tokens, tokens), 0)
    token = lax.broadcasted_iota(jnp.int32, (tokens, tokens), 1)
    first = lax.axis_index("feat") * rows
    order = jnp.where(token == (place ^ first), 1.0, 0.0).astype(jnp.bfloat16)
    grad_ref[...] = jnp.dot(order, pre_grad, preferred_element_type=jnp.float32).astype(
        jnp.bfloat16
    )


def masked(raw, mine, theirs, rows):
    tokens, slots = raw.shape
    return pl.pallas_call(
        functools.partial(masked_kernel, rows),
        out_shape=(
            jax.ShapeDtypeStruct((tokens, slots), jnp.bfloat16),
            jax.ShapeDtypeStruct((1, slots), jnp.float32),
        ),
        in_specs=[VMEM] * 3,
        out_specs=(VMEM, VMEM),
        compiler_params=PARAMS,
        cost_estimate=pl.CostEstimate(flops=10**5, bytes_accessed=2**15, transcendentals=0),
        name="masked",
    )(raw, mine, theirs)


def local(tokens, b_pre, pre_codes, top_idx, blocks, counts, dict_rows):
    size = lax.axis_size("feat")
    rows, width = tokens.shape
    centered_own = lax.optimization_barrier(
        (tokens.astype(jnp.float32) - b_pre.astype(jnp.float32)).astype(jnp.bfloat16)
    )
    code, raw, send = codes(top_idx, pre_codes, blocks, counts, dict_rows, centered_own)

    arrived = swapped(send, "feat", 1)
    total = own_part(code, dict_rows, centered_own) + arrived.astype(jnp.float32)
    distance = 2
    while distance < size:
        total = total + swapped(total.astype(jnp.bfloat16), "feat", distance).astype(jnp.float32)
        distance *= 2
    scaled_own = (0.25 * total).astype(jnp.bfloat16)
    scaled_other = swapped(scaled_own, "feat", 1)

    centered = centered_own[None]
    distance = 1
    while distance < size:
        centered = jnp.concatenate([centered, swapped(centered, "feat", distance)], axis=0)
        distance *= 2
    centered = centered.reshape(size * rows, width)

    code_half, scaled = code_half_of(scaled_own, scaled_other, dict_rows)
    theirs = swapped(code_half, "tok", 1)
    grad_rows = lax.dot_general(
        code, scaled, (((0,), (0,)), ((), ())), preferred_element_type=jnp.float32
    ).astype(jnp.bfloat16)
    pre_grad, grad_benc = masked(raw, code_half, theirs, rows)
    grad_enc = lax.dot_general(
        centered, pre_grad, (((0,), (0,)), ((), ())), preferred_element_type=jnp.float32
    ).astype(jnp.bfloat16)
    return (grad_rows, grad_enc, grad_benc.reshape(-1))


def solution(mesh):
    return jax.shard_map(
        local,
        mesh=mesh,
        in_specs=(
            P(("grp", "feat"), "tok"),
            P(("grp", "tok")),
            P("grp", None),
            P("grp", None),
            P(("grp", "feat")),
            P(("grp", "feat")),
            P(("grp", "feat"), "tok"),
        ),
        out_specs=(P(("grp", "feat"), "tok"), P(("grp", "tok"), "feat"), P(("grp", "feat"))),
        check_vma=False,
    )
```

```python
import functools

import jax
import jax.numpy as jnp
from jax import lax
from jax.experimental import pallas as pl
from jax.experimental.pallas import tpu as pltpu
from jax.sharding import PartitionSpec as P

VMEM = pl.BlockSpec(memory_space=pltpu.VMEM)
SMEM = pl.BlockSpec(memory_space=pltpu.SMEM)
HBM = pl.BlockSpec(memory_space=pltpu.HBM)
PARAMS = pltpu.CompilerParams(vmem_limit_bytes=16 * 2**20)


def feat_bits():
    return (lax.axis_size("feat") - 1).bit_length()


def sum_bit(step, core):
    return (step + core) % feat_bits()


def token_bit(step, core):
    return (feat_bits() - 1 - step + core) % feat_bits()


def swapped(shard, bit_of):
    cores = lax.axis_size("tok")
    pairs = [
        (f * cores + c, (f ^ 1 << bit_of(c)) * cores + c)
        for f in range(lax.axis_size("feat"))
        for c in range(cores)
    ]
    return lax.ppermute(shard, ("feat", "tok"), pairs)


def halves(width):
    half = width // 2
    bit = lax.axis_index("feat") >> (lax.axis_index("tok") % feat_bits()) & 1
    return (
        pl.multiple_of(bit * half, half),
        pl.multiple_of((1 - bit) * half, half),
        half,
    )


def share(code, rows_ref, tokens_ref, bias_ref, at, half):
    total = jnp.dot(code, rows_ref[:, pl.ds(at, half)], preferred_element_type=jnp.float32)
    rows = tokens_ref.shape[0]
    centered = tokens_ref[:, pl.ds(at, half)].astype(jnp.float32) - bias_ref[:, pl.ds(at, half)]
    centered = centered.astype(jnp.bfloat16).astype(jnp.float32)
    token = lax.broadcasted_iota(jnp.int32, (total.shape[0], 1), 0)
    first = lax.axis_index("feat") * rows
    for i in range(rows):
        total -= jnp.where(token == first + i, centered[i : i + 1, :], 0.0)
    return total


def front_kernel(
    tokens_hbm,
    bias_hbm,
    pre_hbm,
    top_hbm,
    rows_hbm,
    block_ref,
    count_ref,
    code_ref,
    raw_ref,
    send_ref,
    rows_ref,
    bias_ref,
    tokens_ref,
    bias_flat,
    pre_ref,
    top_ref,
    sems,
):
    copies = [
        pltpu.make_async_copy(source, target, sems.at[i])
        for i, (source, target) in enumerate(
            (
                (top_hbm, top_ref),
                (pre_hbm, pre_ref),
                (rows_hbm, rows_ref),
                (tokens_hbm, tokens_ref),
                (bias_hbm, bias_flat),
            )
        )
    ]
    for copy in copies:
        copy.start()
    for copy in copies[:2]:
        copy.wait()
    tokens, latents = top_ref.shape
    slots, width = rows_ref.shape
    offsets = lax.broadcasted_iota(jnp.int32, (1, slots), 1)
    slot_ids = jnp.where(offsets < count_ref[0], block_ref[0] * slots + offsets, -1)
    top, pre = top_ref[...], pre_ref[...]
    raw = jnp.zeros((tokens, slots), jnp.float32)
    for k in range(latents):
        raw = jnp.where(top[:, k : k + 1] == slot_ids, pre[:, k : k + 1], raw)
    raw_ref[...] = raw
    code = jnp.maximum(raw, 0.0).astype(jnp.bfloat16)
    code_ref[...] = code
    for copy in copies[2:]:
        copy.wait()
    bias_ref[...] = bias_flat[...].astype(jnp.float32).reshape(1, width)
    _, other, half = halves(width)
    send_ref[...] = share(code, rows_ref, tokens_ref, bias_ref, other, half).astype(jnp.bfloat16)


def front(tokens, b_pre, pre_codes, top_idx, blocks, counts, dict_rows):
    count = top_idx.shape[0]
    slots, width = dict_rows.shape
    return pl.pallas_call(
        front_kernel,
        out_shape=(
            jax.ShapeDtypeStruct((count, slots), jnp.bfloat16),
            jax.ShapeDtypeStruct((count, slots), jnp.float32),
            jax.ShapeDtypeStruct((count, width // 2), jnp.bfloat16),
            jax.ShapeDtypeStruct(dict_rows.shape, jnp.bfloat16),
            jax.ShapeDtypeStruct((1, width), jnp.float32),
        ),
        in_specs=[HBM] * 5 + [SMEM] * 2,
        out_specs=(VMEM,) * 5,
        scratch_shapes=[
            pltpu.VMEM(tokens.shape, tokens.dtype),
            pltpu.VMEM(b_pre.shape, b_pre.dtype),
            pltpu.VMEM(pre_codes.shape, pre_codes.dtype),
            pltpu.VMEM(top_idx.shape, top_idx.dtype),
            pltpu.SemaphoreType.DMA((5,)),
        ],
        compiler_params=PARAMS,
        cost_estimate=pl.CostEstimate(flops=10**6, bytes_accessed=2**20, transcendentals=0),
        name="front",
    )(
        *(
            pltpu.with_memory_space_constraint(array, pltpu.HBM)
            for array in (tokens, b_pre, pre_codes, top_idx, dict_rows)
        ),
        blocks,
        counts,
    )


def own_kernel(code_ref, rows_ref, tokens_ref, bias_ref, total_ref):
    own, _, half = halves(rows_ref.shape[1])
    total_ref[...] = share(code_ref[...], rows_ref, tokens_ref, bias_ref, own, half)


def own_part(code, dict_rows, tokens, bias):
    half = dict_rows.shape[1] // 2
    return pl.pallas_call(
        own_kernel,
        out_shape=jax.ShapeDtypeStruct((code.shape[0], half), jnp.float32),
        in_specs=[VMEM] * 4,
        out_specs=VMEM,
        compiler_params=PARAMS,
        cost_estimate=pl.CostEstimate(flops=10**6, bytes_accessed=2**19, transcendentals=0),
        name="own_part",
    )(code, dict_rows, tokens, bias)


def code_half_kernel(own_ref, other_ref, rows_ref, half_ref, scaled_ref):
    own_at, other_at, half = halves(rows_ref.shape[1])
    total = jnp.zeros(half_ref.shape, jnp.float32)
    for ref, at in ((own_ref, own_at), (other_ref, other_at)):
        part = ref[...]
        scaled_ref[:, pl.ds(at, half)] = part
        total += lax.dot_general(
            part,
            rows_ref[:, pl.ds(at, half)],
            (((1,), (1,)), ((), ())),
            preferred_element_type=jnp.float32,
        )
    half_ref[...] = total


def code_half_of(scaled_own, scaled_other, dict_rows):
    tokens = scaled_own.shape[0]
    slots, width = dict_rows.shape
    return pl.pallas_call(
        code_half_kernel,
        out_shape=(
            jax.ShapeDtypeStruct((tokens, slots), jnp.float32),
            jax.ShapeDtypeStruct((tokens, width), jnp.bfloat16),
        ),
        in_specs=[VMEM] * 3,
        out_specs=(VMEM, VMEM),
        compiler_params=PARAMS,
        cost_estimate=pl.CostEstimate(flops=10**6, bytes_accessed=2**20, transcendentals=0),
        name="code_half",
    )(scaled_own, scaled_other, dict_rows)


def masked_kernel(rows, raw_ref, mine_ref, theirs_ref, grad_ref, benc_ref):
    tokens = raw_ref.shape[0]
    code_grad = mine_ref[...] + theirs_ref[...]
    pre_grad = jnp.where(raw_ref[...] > 0.0, code_grad, 0.0).astype(jnp.bfloat16)
    benc_ref[...] = jnp.sum(pre_grad.astype(jnp.float32), axis=0, keepdims=True)
    place = lax.broadcasted_iota(jnp.int32, (tokens, tokens), 0)
    token = lax.broadcasted_iota(jnp.int32, (tokens, tokens), 1)
    core = lax.axis_index("tok")
    block = place // rows
    distance = jnp.zeros_like(place)
    for step in range(feat_bits()):
        distance |= (block >> step & 1) << token_bit(step, core)
    source = (lax.axis_index("feat") ^ distance) * rows + place % rows
    order = jnp.where(token == source, 1.0, 0.0).astype(jnp.bfloat16)
    grad_ref[...] = jnp.dot(order, pre_grad, preferred_element_type=jnp.float32).astype(
        jnp.bfloat16
    )


def masked(raw, mine, theirs, rows):
    tokens, slots = raw.shape
    return pl.pallas_call(
        functools.partial(masked_kernel, rows),
        out_shape=(
            jax.ShapeDtypeStruct((tokens, slots), jnp.bfloat16),
            jax.ShapeDtypeStruct((1, slots), jnp.float32),
        ),
        in_specs=[VMEM] * 3,
        out_specs=(VMEM, VMEM),
        compiler_params=PARAMS,
        cost_estimate=pl.CostEstimate(flops=10**5, bytes_accessed=2**15, transcendentals=0),
        name="masked",
    )(raw, mine, theirs)


def local(tokens, b_pre, pre_codes, top_idx, blocks, counts, dict_rows):
    rows, width = tokens.shape
    gathered = tokens[None]
    for step in range(feat_bits()):
        arrived = swapped(gathered, functools.partial(token_bit, step))
        gathered = jnp.concatenate([gathered, arrived], axis=0)

    code, raw, send, dict_rows, bias = front(
        tokens, b_pre, pre_codes, top_idx, blocks, counts, dict_rows
    )
    arrived = swapped(send, functools.partial(sum_bit, 0))
    total = own_part(code, dict_rows, tokens, bias) + arrived.astype(jnp.float32)
    for step in range(1, feat_bits()):
        arrived = swapped(total.astype(jnp.bfloat16), functools.partial(sum_bit, step))
        total = total + arrived.astype(jnp.float32)
    scaled_own = (0.25 * total).astype(jnp.bfloat16)
    scaled_other = swapped(scaled_own, functools.partial(sum_bit, 0))

    centered = gathered.reshape(-1, width).astype(jnp.float32) - bias
    centered = lax.optimization_barrier(centered.astype(jnp.bfloat16))

    code_half, scaled = code_half_of(scaled_own, scaled_other, dict_rows)
    theirs = lax.ppermute(code_half, "tok", [(i, 1 - i) for i in range(2)])
    grad_rows = lax.dot_general(
        code, scaled, (((0,), (0,)), ((), ())), preferred_element_type=jnp.float32
    ).astype(jnp.bfloat16)
    pre_grad, grad_benc = masked(raw, code_half, theirs, rows)
    grad_enc = lax.dot_general(
        centered, pre_grad, (((0,), (0,)), ((), ())), preferred_element_type=jnp.float32
    ).astype(jnp.bfloat16)
    return (grad_rows, grad_enc, grad_benc.reshape(-1))


def solution(mesh):
    return jax.shard_map(
        local,
        mesh=mesh,
        in_specs=(
            P(("grp", "feat"), "tok"),
            P(("grp", "tok")),
            P("grp", None),
            P("grp", None),
            P(("grp", "feat")),
            P(("grp", "feat")),
            P(("grp", "feat"), "tok"),
        ),
        out_specs=(P(("grp", "feat"), "tok"), P(("grp", "tok"), "feat"), P(("grp", "feat"))),
        check_vma=False,
    )
```

```python
import functools

import jax
import jax.numpy as jnp
from jax import lax
from jax.experimental import pallas as pl
from jax.experimental.pallas import tpu as pltpu
from jax.sharding import PartitionSpec as P

VMEM = pl.BlockSpec(memory_space=pltpu.VMEM)
SMEM = pl.BlockSpec(memory_space=pltpu.SMEM)
HBM = pl.BlockSpec(memory_space=pltpu.HBM)
PARAMS = pltpu.CompilerParams(vmem_limit_bytes=16 * 2**20)


def feat_bits():
    return (lax.axis_size("feat") - 1).bit_length()


def sum_bit(step, core):
    return (step + core) % feat_bits()


def swapped(shard, bit_of):
    cores = lax.axis_size("tok")
    pairs = [
        (f * cores + c, (f ^ 1 << bit_of(c)) * cores + c)
        for f in range(lax.axis_size("feat"))
        for c in range(cores)
    ]
    return lax.ppermute(shard, ("feat", "tok"), pairs)


def share(code, rows_ref, tokens_ref, bias_ref):
    total = jnp.dot(code, rows_ref[...], preferred_element_type=jnp.float32)
    rows = tokens_ref.shape[0]
    centered = tokens_ref[...].astype(jnp.float32) - bias_ref[...]
    centered = centered.astype(jnp.bfloat16).astype(jnp.float32)
    token = lax.broadcasted_iota(jnp.int32, (total.shape[0], 1), 0)
    first = lax.axis_index("feat") * rows
    for i in range(rows):
        total -= jnp.where(token == first + i, centered[i : i + 1, :], 0.0)
    return total


def front_kernel(
    tokens_hbm,
    bias_hbm,
    pre_hbm,
    top_hbm,
    rows_hbm,
    block_ref,
    count_ref,
    code_ref,
    raw_ref,
    total_ref,
    rows_ref,
    bias_ref,
    tokens_ref,
    bias_flat,
    pre_ref,
    top_ref,
    sems,
):
    copies = [
        pltpu.make_async_copy(source, target, sems.at[i])
        for i, (source, target) in enumerate(
            (
                (top_hbm, top_ref),
                (pre_hbm, pre_ref),
                (rows_hbm, rows_ref),
                (tokens_hbm, tokens_ref),
                (bias_hbm, bias_flat),
            )
        )
    ]
    for copy in copies:
        copy.start()
    for copy in copies[:2]:
        copy.wait()
    tokens, latents = top_ref.shape
    slots, width = rows_ref.shape
    offsets = lax.broadcasted_iota(jnp.int32, (1, slots), 1)
    slot_ids = jnp.where(offsets < count_ref[0], block_ref[0] * slots + offsets, -1)
    top, pre = top_ref[...], pre_ref[...]
    raw = jnp.zeros((tokens, slots), jnp.float32)
    for k in range(latents):
        raw = jnp.where(top[:, k : k + 1] == slot_ids, pre[:, k : k + 1], raw)
    raw_ref[...] = raw
    code = jnp.maximum(raw, 0.0).astype(jnp.bfloat16)
    code_ref[...] = code
    for copy in copies[2:]:
        copy.wait()
    bias_ref[...] = bias_flat[...].astype(jnp.float32).reshape(1, width)
    total_ref[...] = share(code, rows_ref, tokens_ref, bias_ref)


def front(tokens, b_pre, pre_codes, top_idx, blocks, counts, dict_rows):
    count = top_idx.shape[0]
    slots, width = dict_rows.shape
    return pl.pallas_call(
        front_kernel,
        out_shape=(
            jax.ShapeDtypeStruct((count, slots), jnp.bfloat16),
            jax.ShapeDtypeStruct((count, slots), jnp.float32),
            jax.ShapeDtypeStruct((count, width), jnp.float32),
            jax.ShapeDtypeStruct(dict_rows.shape, jnp.bfloat16),
            jax.ShapeDtypeStruct((1, width), jnp.float32),
        ),
        in_specs=[HBM] * 5 + [SMEM] * 2,
        out_specs=(VMEM,) * 5,
        scratch_shapes=[
            pltpu.VMEM(tokens.shape, tokens.dtype),
            pltpu.VMEM(b_pre.shape, b_pre.dtype),
            pltpu.VMEM(pre_codes.shape, pre_codes.dtype),
            pltpu.VMEM(top_idx.shape, top_idx.dtype),
            pltpu.SemaphoreType.DMA((5,)),
        ],
        compiler_params=PARAMS,
        cost_estimate=pl.CostEstimate(flops=10**6, bytes_accessed=2**20, transcendentals=0),
        name="front",
    )(
        *(
            pltpu.with_memory_space_constraint(array, pltpu.HBM)
            for array in (tokens, b_pre, pre_codes, top_idx, dict_rows)
        ),
        blocks,
        counts,
    )


def joined_kernel(first_ref, second_ref, after_ref, out_ref):
    count = first_ref.shape[0]
    out_ref[:count] = first_ref[...]
    out_ref[count:] = second_ref[...]


def joined(first, second, after):
    return pl.pallas_call(
        joined_kernel,
        out_shape=jax.ShapeDtypeStruct((2 * first.shape[0],) + first.shape[1:], first.dtype),
        in_specs=[VMEM, VMEM, pl.BlockSpec(memory_space=pl.ANY)],
        out_specs=VMEM,
        compiler_params=PARAMS,
        cost_estimate=pl.CostEstimate(flops=10**6, bytes_accessed=2**20, transcendentals=0),
        name="joined",
    )(first, second, after)


def code_half_kernel(scaled_ref, rows_ref, half_ref):
    half_ref[...] = lax.dot_general(
        scaled_ref[...],
        rows_ref[...],
        (((1,), (1,)), ((), ())),
        preferred_element_type=jnp.float32,
    )


def code_half_of(scaled, dict_rows):
    return pl.pallas_call(
        code_half_kernel,
        out_shape=jax.ShapeDtypeStruct((scaled.shape[0], dict_rows.shape[0]), jnp.float32),
        in_specs=[VMEM] * 2,
        out_specs=VMEM,
        compiler_params=PARAMS,
        cost_estimate=pl.CostEstimate(flops=10**6, bytes_accessed=2**20, transcendentals=0),
        name="code_half",
    )(scaled, dict_rows)


def masked_kernel(rows, raw_ref, mine_ref, theirs_ref, grad_ref, benc_ref):
    tokens = raw_ref.shape[0]
    code_grad = mine_ref[...] + theirs_ref[...]
    pre_grad = jnp.where(raw_ref[...] > 0.0, code_grad, 0.0).astype(jnp.bfloat16)
    benc_ref[...] = jnp.sum(pre_grad.astype(jnp.float32), axis=0, keepdims=True)
    place = lax.broadcasted_iota(jnp.int32, (tokens, tokens), 0)
    token = lax.broadcasted_iota(jnp.int32, (tokens, tokens), 1)
    core = lax.axis_index("tok")
    block = place // rows
    distance = jnp.zeros_like(place)
    for step in range(feat_bits()):
        distance |= (block >> step & 1) << sum_bit(step, core)
    source = (lax.axis_index("feat") ^ distance) * rows + place % rows
    order = jnp.where(token == source, 1.0, 0.0).astype(jnp.bfloat16)
    grad_ref[...] = jnp.dot(order, pre_grad, preferred_element_type=jnp.float32).astype(
        jnp.bfloat16
    )


def masked(raw, mine, theirs, rows):
    tokens, slots = raw.shape
    return pl.pallas_call(
        functools.partial(masked_kernel, rows),
        out_shape=(
            jax.ShapeDtypeStruct((tokens, slots), jnp.bfloat16),
            jax.ShapeDtypeStruct((1, slots), jnp.float32),
        ),
        in_specs=[VMEM] * 3,
        out_specs=(VMEM, VMEM),
        compiler_params=PARAMS,
        cost_estimate=pl.CostEstimate(flops=10**5, bytes_accessed=2**15, transcendentals=0),
        name="masked",
    )(raw, mine, theirs)


def local(tokens, b_pre, pre_codes, top_idx, blocks, counts, dict_rows):
    rows, width = tokens.shape
    gathered = [tokens[None], swapped(tokens[None], functools.partial(sum_bit, 0))]
    code, raw, total, dict_rows, bias = front(
        tokens, b_pre, pre_codes, top_idx, blocks, counts, dict_rows
    )
    for step in range(feat_bits()):
        bit_of = functools.partial(sum_bit, step)
        total, gathered = lax.optimization_barrier((total, gathered))
        sent = total.astype(jnp.bfloat16)
        arrived = swapped(sent, bit_of)
        if step > 0:
            block = joined(*gathered, sent)
            gathered = [block, swapped(block, bit_of)]
        total = total + arrived.astype(jnp.float32)
    scaled = (0.25 * total).astype(jnp.bfloat16)
    code_half = code_half_of(scaled, dict_rows)

    gathered = joined(*gathered, code_half).reshape(-1, width)
    centered = gathered.astype(jnp.float32) - bias
    centered = lax.optimization_barrier(centered.astype(jnp.bfloat16))

    theirs = lax.ppermute(code_half, "tok", [(i, 1 - i) for i in range(2)])
    grad_rows = lax.dot_general(
        code, scaled, (((0,), (0,)), ((), ())), preferred_element_type=jnp.float32
    ).astype(jnp.bfloat16)
    pre_grad, grad_benc = masked(raw, code_half, theirs, rows)
    grad_enc = lax.dot_general(
        centered, pre_grad, (((0,), (0,)), ((), ())), preferred_element_type=jnp.float32
    ).astype(jnp.bfloat16)
    return (grad_rows, grad_enc, grad_benc.reshape(-1))


def solution(mesh):
    return jax.shard_map(
        local,
        mesh=mesh,
        in_specs=(
            P(("grp", "feat"), "tok"),
            P(("grp", "tok")),
            P("grp", None),
            P("grp", None),
            P(("grp", "feat")),
            P(("grp", "feat")),
            P(("grp", "feat"), "tok"),
        ),
        out_specs=(P(("grp", "feat"), "tok"), P(("grp", "tok"), "feat"), P(("grp", "feat"))),
        check_vma=False,
    )
```

```python
import functools

import jax
import jax.numpy as jnp
from jax import lax
from jax.experimental import pallas as pl
from jax.experimental.pallas import tpu as pltpu
from jax.sharding import PartitionSpec as P

VMEM = pl.BlockSpec(memory_space=pltpu.VMEM)
SMEM = pl.BlockSpec(memory_space=pltpu.SMEM)
HBM = pl.BlockSpec(memory_space=pltpu.HBM)
PARAMS = pltpu.CompilerParams(vmem_limit_bytes=16 * 2**20)


def feat_bits():
    return (lax.axis_size("feat") - 1).bit_length()


def sum_bit(step, core):
    return (step + core) % feat_bits()


def swapped(shard, bit_of):
    cores = lax.axis_size("tok")
    pairs = [
        (f * cores + c, (f ^ 1 << bit_of(c)) * cores + c)
        for f in range(lax.axis_size("feat"))
        for c in range(cores)
    ]
    return lax.ppermute(shard, ("feat", "tok"), pairs)


def halves(width):
    half = width // 2
    bit = lax.axis_index("feat") >> (lax.axis_index("tok") % feat_bits()) & 1
    return (
        pl.multiple_of(bit * half, half),
        pl.multiple_of((1 - bit) * half, half),
        half,
    )


def share(code, rows_ref, tokens_ref, bias_ref, at, half):
    total = jnp.dot(code, rows_ref[:, pl.ds(at, half)], preferred_element_type=jnp.float32)
    rows = tokens_ref.shape[0]
    centered = tokens_ref[:, pl.ds(at, half)].astype(jnp.float32) - bias_ref[:, pl.ds(at, half)]
    centered = centered.astype(jnp.bfloat16).astype(jnp.float32)
    token = lax.broadcasted_iota(jnp.int32, (total.shape[0], 1), 0)
    first = lax.axis_index("feat") * rows
    for i in range(rows):
        total -= jnp.where(token == first + i, centered[i : i + 1, :], 0.0)
    return total


def front_kernel(
    tokens_hbm,
    bias_hbm,
    pre_hbm,
    top_hbm,
    rows_hbm,
    block_ref,
    count_ref,
    code_ref,
    raw_ref,
    send_ref,
    rows_ref,
    tokens_ref,
    bias_ref,
    bias_flat,
    pre_ref,
    top_ref,
    sems,
):
    copies = [
        pltpu.make_async_copy(source, target, sems.at[i])
        for i, (source, target) in enumerate(
            (
                (top_hbm, top_ref),
                (pre_hbm, pre_ref),
                (rows_hbm, rows_ref),
                (tokens_hbm, tokens_ref),
                (bias_hbm, bias_flat),
            )
        )
    ]
    for copy in copies:
        copy.start()
    for copy in copies[:2]:
        copy.wait()
    tokens, latents = top_ref.shape
    slots, width = rows_ref.shape
    offsets = lax.broadcasted_iota(jnp.int32, (1, slots), 1)
    slot_ids = jnp.where(offsets < count_ref[0], block_ref[0] * slots + offsets, -1)
    top, pre = top_ref[...], pre_ref[...]
    raw = jnp.zeros((tokens, slots), jnp.float32)
    for k in range(latents):
        raw = jnp.where(top[:, k : k + 1] == slot_ids, pre[:, k : k + 1], raw)
    raw_ref[...] = raw
    code = jnp.maximum(raw, 0.0).astype(jnp.bfloat16)
    code_ref[...] = code
    for copy in copies[2:]:
        copy.wait()
    bias_ref[...] = bias_flat[...].astype(jnp.float32).reshape(1, width)
    _, other, half = halves(width)
    send_ref[...] = share(code, rows_ref, tokens_ref, bias_ref, other, half).astype(jnp.bfloat16)


def front(tokens, b_pre, pre_codes, top_idx, blocks, counts, dict_rows):
    count = top_idx.shape[0]
    slots, width = dict_rows.shape
    return pl.pallas_call(
        front_kernel,
        out_shape=(
            jax.ShapeDtypeStruct((count, slots), jnp.bfloat16),
            jax.ShapeDtypeStruct((count, slots), jnp.float32),
            jax.ShapeDtypeStruct((count, width // 2), jnp.bfloat16),
            jax.ShapeDtypeStruct(dict_rows.shape, jnp.bfloat16),
            jax.ShapeDtypeStruct(tokens.shape, tokens.dtype),
            jax.ShapeDtypeStruct((1, width), jnp.float32),
        ),
        in_specs=[HBM] * 5 + [SMEM] * 2,
        out_specs=(VMEM,) * 6,
        scratch_shapes=[
            pltpu.VMEM(b_pre.shape, b_pre.dtype),
            pltpu.VMEM(pre_codes.shape, pre_codes.dtype),
            pltpu.VMEM(top_idx.shape, top_idx.dtype),
            pltpu.SemaphoreType.DMA((5,)),
        ],
        compiler_params=PARAMS,
        cost_estimate=pl.CostEstimate(flops=10**6, bytes_accessed=2**20, transcendentals=0),
        name="front",
    )(
        *(
            pltpu.with_memory_space_constraint(array, pltpu.HBM)
            for array in (tokens, b_pre, pre_codes, top_idx, dict_rows)
        ),
        blocks,
        counts,
    )


def own_kernel(code_ref, rows_ref, tokens_ref, bias_ref, total_ref):
    own, _, half = halves(rows_ref.shape[1])
    total_ref[...] = share(code_ref[...], rows_ref, tokens_ref, bias_ref, own, half)


def own_part(code, dict_rows, tokens, bias):
    half = dict_rows.shape[1] // 2
    return pl.pallas_call(
        own_kernel,
        out_shape=jax.ShapeDtypeStruct((code.shape[0], half), jnp.float32),
        in_specs=[VMEM] * 4,
        out_specs=VMEM,
        compiler_params=PARAMS,
        cost_estimate=pl.CostEstimate(flops=10**6, bytes_accessed=2**19, transcendentals=0),
        name="own_part",
    )(code, dict_rows, tokens, bias)


def joined_kernel(first_ref, second_ref, after_ref, out_ref):
    count = first_ref.shape[0]
    out_ref[:count] = first_ref[...]
    out_ref[count:] = second_ref[...]


def copied_kernel(block_ref, after_ref, out_ref):
    out_ref[...] = block_ref[...]


def copied(block, after):
    return pl.pallas_call(
        copied_kernel,
        out_shape=jax.ShapeDtypeStruct(block.shape, block.dtype),
        in_specs=[VMEM, pl.BlockSpec(memory_space=pl.ANY)],
        out_specs=VMEM,
        compiler_params=PARAMS,
        cost_estimate=pl.CostEstimate(flops=10**6, bytes_accessed=2**20, transcendentals=0),
        name="copied",
    )(block, after)


def joined(first, second, after):
    return pl.pallas_call(
        joined_kernel,
        out_shape=jax.ShapeDtypeStruct((2 * first.shape[0],) + first.shape[1:], first.dtype),
        in_specs=[VMEM, VMEM, pl.BlockSpec(memory_space=pl.ANY)],
        out_specs=VMEM,
        compiler_params=PARAMS,
        cost_estimate=pl.CostEstimate(flops=10**6, bytes_accessed=2**20, transcendentals=0),
        name="joined",
    )(first, second, after)


def product(part_ref, rows_ref, at, half):
    return lax.dot_general(
        part_ref[...],
        rows_ref[:, pl.ds(at, half)],
        (((1,), (1,)), ((), ())),
        preferred_element_type=jnp.float32,
    )


def first_product_kernel(own_ref, rows_ref, half_ref):
    own, _, half = halves(rows_ref.shape[1])
    half_ref[...] = product(own_ref, rows_ref, own, half)


def code_half_kernel(own_ref, other_ref, first_ref, rows_ref, half_ref, scaled_ref):
    own, other, half = halves(rows_ref.shape[1])
    half_ref[...] = first_ref[...] + product(other_ref, rows_ref, other, half)
    scaled_ref[:, pl.ds(own, half)] = own_ref[...]
    scaled_ref[:, pl.ds(other, half)] = other_ref[...]


def first_product(scaled_own, dict_rows):
    tokens = scaled_own.shape[0]
    return pl.pallas_call(
        first_product_kernel,
        out_shape=jax.ShapeDtypeStruct((tokens, dict_rows.shape[0]), jnp.float32),
        in_specs=[VMEM] * 2,
        out_specs=VMEM,
        compiler_params=PARAMS,
        cost_estimate=pl.CostEstimate(flops=10**6, bytes_accessed=2**20, transcendentals=0),
        name="first_product",
    )(scaled_own, dict_rows)


def code_half_of(scaled_own, scaled_other, first, dict_rows):
    tokens = scaled_own.shape[0]
    slots, width = dict_rows.shape
    return pl.pallas_call(
        code_half_kernel,
        out_shape=(
            jax.ShapeDtypeStruct((tokens, slots), jnp.float32),
            jax.ShapeDtypeStruct((tokens, width), jnp.bfloat16),
        ),
        in_specs=[VMEM] * 4,
        out_specs=(VMEM, VMEM),
        compiler_params=PARAMS,
        cost_estimate=pl.CostEstimate(flops=10**6, bytes_accessed=2**20, transcendentals=0),
        name="code_half",
    )(scaled_own, scaled_other, first, dict_rows)


def masked_kernel(rows, raw_ref, mine_ref, theirs_ref, grad_ref, benc_ref):
    tokens = raw_ref.shape[0]
    code_grad = mine_ref[...] + theirs_ref[...]
    pre_grad = jnp.where(raw_ref[...] > 0.0, code_grad, 0.0).astype(jnp.bfloat16)
    benc_ref[...] = jnp.sum(pre_grad.astype(jnp.float32), axis=0, keepdims=True)
    place = lax.broadcasted_iota(jnp.int32, (tokens, tokens), 0)
    token = lax.broadcasted_iota(jnp.int32, (tokens, tokens), 1)
    core = lax.axis_index("tok")
    block = place // rows
    distance = jnp.zeros_like(place)
    for step in range(feat_bits()):
        distance |= (block >> step & 1) << sum_bit(step, core)
    source = (lax.axis_index("feat") ^ distance) * rows + place % rows
    order = jnp.where(token == source, 1.0, 0.0).astype(jnp.bfloat16)
    grad_ref[...] = jnp.dot(order, pre_grad, preferred_element_type=jnp.float32).astype(
        jnp.bfloat16
    )


def masked(raw, mine, theirs, rows):
    tokens, slots = raw.shape
    return pl.pallas_call(
        functools.partial(masked_kernel, rows),
        out_shape=(
            jax.ShapeDtypeStruct((tokens, slots), jnp.bfloat16),
            jax.ShapeDtypeStruct((1, slots), jnp.float32),
        ),
        in_specs=[VMEM] * 3,
        out_specs=(VMEM, VMEM),
        compiler_params=PARAMS,
        cost_estimate=pl.CostEstimate(flops=10**5, bytes_accessed=2**15, transcendentals=0),
        name="masked",
    )(raw, mine, theirs)


def local(tokens, b_pre, pre_codes, top_idx, blocks, counts, dict_rows):
    rows, width = tokens.shape
    code, raw, sent, dict_rows, tokens, bias = front(
        tokens, b_pre, pre_codes, top_idx, blocks, counts, dict_rows
    )
    gathered = tokens[None]
    for step in range(feat_bits()):
        bit_of = functools.partial(sum_bit, step)
        arrived = swapped(sent, bit_of)
        if step == 0:
            total = own_part(code, dict_rows, tokens, bias)
            block = copied(gathered, sent)
        else:
            block = joined(*gathered, sent)
        gathered = [block, swapped(block, bit_of)]
        total = total + arrived.astype(jnp.float32)
        if step < feat_bits() - 1:
            total, gathered = lax.optimization_barrier((total, gathered))
            sent = total.astype(jnp.bfloat16)
    scaled_own = (0.25 * total).astype(jnp.bfloat16)
    scaled_other = swapped(scaled_own, functools.partial(sum_bit, 0))

    first = first_product(scaled_own, dict_rows)
    gathered = joined(*gathered, scaled_own).reshape(-1, width)
    centered = gathered.astype(jnp.float32) - bias
    centered = lax.optimization_barrier(centered.astype(jnp.bfloat16))

    code_half, scaled = code_half_of(scaled_own, scaled_other, first, dict_rows)
    theirs = lax.ppermute(code_half, "tok", [(i, 1 - i) for i in range(2)])
    grad_rows = lax.dot_general(
        code, scaled, (((0,), (0,)), ((), ())), preferred_element_type=jnp.float32
    ).astype(jnp.bfloat16)
    pre_grad, grad_benc = masked(raw, code_half, theirs, rows)
    grad_enc = lax.dot_general(
        centered, pre_grad, (((0,), (0,)), ((), ())), preferred_element_type=jnp.float32
    ).astype(jnp.bfloat16)
    return (grad_rows, grad_enc, grad_benc.reshape(-1))


def solution(mesh):
    return jax.shard_map(
        local,
        mesh=mesh,
        in_specs=(
            P(("grp", "feat"), "tok"),
            P(("grp", "tok")),
            P("grp", None),
            P("grp", None),
            P(("grp", "feat")),
            P(("grp", "feat")),
            P(("grp", "feat"), "tok"),
        ),
        out_specs=(P(("grp", "feat"), "tok"), P(("grp", "tok"), "feat"), P(("grp", "feat"))),
        check_vma=False,
    )
```

```python
import functools

import jax
import jax.numpy as jnp
from jax import lax
from jax.experimental import pallas as pl
from jax.experimental.pallas import tpu as pltpu
from jax.sharding import PartitionSpec as P

VMEM = pl.BlockSpec(memory_space=pltpu.VMEM)
SMEM = pl.BlockSpec(memory_space=pltpu.SMEM)
HBM = pl.BlockSpec(memory_space=pltpu.HBM)
ANY = pl.BlockSpec(memory_space=pl.ANY)
ROWS = 16
MERGED = 2


def kernel_call(kernel, out_shape, in_specs, out_specs, tokens, scratch_shapes=()):
    limit = (16 if tokens <= ROWS else 40) * 2**20
    return pl.pallas_call(
        kernel,
        out_shape=out_shape,
        in_specs=in_specs,
        out_specs=out_specs,
        scratch_shapes=scratch_shapes,
        compiler_params=pltpu.CompilerParams(vmem_limit_bytes=limit),
        cost_estimate=pl.CostEstimate(flops=10**6, bytes_accessed=2**20, transcendentals=0),
    )


def shape(*sizes, dtype=jnp.bfloat16):
    return jax.ShapeDtypeStruct(sizes, dtype)


def feat_bits():
    return (lax.axis_size("feat") - 1).bit_length()


def sum_bit(step, core):
    return (step + core) % feat_bits()


def swapped(shard, step):
    cores = lax.axis_size("tok")
    pairs = [
        (f * cores + c, (f ^ 1 << sum_bit(step, c)) * cores + c)
        for f in range(lax.axis_size("feat"))
        for c in range(cores)
    ]
    return lax.ppermute(shard, ("feat", "tok"), pairs)


def halves(width):
    half = width // 2
    bit = lax.axis_index("feat") >> (lax.axis_index("tok") % feat_bits()) & 1
    return (
        pl.multiple_of(bit * half, half),
        pl.multiple_of((1 - bit) * half, half),
        half,
    )


def stacked(rows, pieces):
    width = rows.shape[1] // pieces
    return jnp.concatenate(
        [
            rows[i : i + 1, c * width : (c + 1) * width]
            for i in range(rows.shape[0])
            for c in range(pieces)
        ],
        axis=0,
    )


def share(code, rows_ref, centered_ref, at, half):
    total = jnp.dot(code, rows_ref[:, pl.ds(at, half)], preferred_element_type=jnp.float32)
    rows = centered_ref.shape[0]
    centered = centered_ref[:, pl.ds(at, half)]
    token = lax.broadcasted_iota(jnp.int32, (total.shape[0], 1), 0)
    first = lax.axis_index("feat") * rows
    for i in range(rows):
        total -= jnp.where(token == first + i, centered[i : i + 1, :], 0.0)
    return total


def front_kernel(
    tokens_hbm,
    bias_hbm,
    pre_hbm,
    top_hbm,
    rows_hbm,
    block_ref,
    count_ref,
    code_ref,
    raw_ref,
    sent_ref,
    tokens_block_ref,
    rows_ref,
    centered_ref,
    bias_ref,
    tokens_ref,
    bias_flat,
    pre_ref,
    top_ref,
    sems,
):
    copies = [
        pltpu.make_async_copy(source, target, sems.at[i])
        for i, (source, target) in enumerate(
            (
                (top_hbm, top_ref),
                (pre_hbm, pre_ref),
                (tokens_hbm, tokens_ref),
                (bias_hbm, bias_flat),
                (rows_hbm, rows_ref),
            )
        )
    ]
    for copy in copies:
        copy.start()
    for copy in copies[:2]:
        copy.wait()
    count, latents = top_ref.shape
    slots, width = rows_ref.shape
    offsets = lax.broadcasted_iota(jnp.int32, (1, slots), 1)
    slot_ids = jnp.where(offsets < count_ref[0], block_ref[0] * slots + offsets, -1)
    top, pre = top_ref[...], pre_ref[...]
    raw = jnp.zeros((count, slots), jnp.float32)
    for k in range(latents):
        raw = jnp.where(top[:, k : k + 1] == slot_ids, pre[:, k : k + 1], raw)
    raw_ref[...] = raw
    code = jnp.maximum(raw, 0.0).astype(jnp.bfloat16)
    code_ref[...] = code

    for copy in copies[2:4]:
        copy.wait()
    tokens = tokens_ref[...].astype(jnp.float32)
    pieces = ROWS // tokens.shape[0]
    bias = bias_flat[...].astype(jnp.float32).reshape(1, width)
    bias_ref[...] = stacked(bias, pieces)
    centered_ref[...] = (tokens - bias).astype(jnp.bfloat16).astype(jnp.float32)
    tokens_block = stacked(tokens, pieces).astype(jnp.bfloat16)
    tokens_block_ref[...] = tokens_block

    copies[4].wait()
    _, other, half = halves(width)
    sent_ref[:, :half] = share(code, rows_ref, centered_ref, other, half).astype(jnp.bfloat16)
    if sent_ref.shape[1] > half:
        sent_ref[:, half:] = tokens_block


def front(tokens, b_pre, pre_codes, top_idx, blocks, counts, dict_rows, merged):
    count = top_idx.shape[0]
    slots, width = dict_rows.shape
    pieces = ROWS // tokens.shape[0]
    block = width // pieces
    return kernel_call(
        front_kernel,
        (
            shape(count, slots),
            shape(count, slots, dtype=jnp.float32),
            shape(count, width // 2 + merged * block),
            shape(ROWS, block),
            shape(slots, width),
            shape(*tokens.shape, dtype=jnp.float32),
            shape(pieces, block, dtype=jnp.float32),
        ),
        [HBM] * 5 + [SMEM] * 2,
        (VMEM,) * 7,
        count,
        [
            pltpu.VMEM(tokens.shape, tokens.dtype),
            pltpu.VMEM(b_pre.shape, b_pre.dtype),
            pltpu.VMEM(pre_codes.shape, pre_codes.dtype),
            pltpu.VMEM(top_idx.shape, top_idx.dtype),
            pltpu.SemaphoreType.DMA((5,)),
        ],
    )(
        *(
            pltpu.with_memory_space_constraint(array, pltpu.HBM)
            for array in (tokens, b_pre, pre_codes, top_idx, dict_rows)
        ),
        blocks,
        counts,
    )


def own_kernel(code_ref, rows_ref, centered_ref, total_ref):
    own, _, half = halves(rows_ref.shape[1])
    total_ref[...] = share(code_ref[...], rows_ref, centered_ref, own, half)


def own_part(code, dict_rows, centered):
    count, half = code.shape[0], dict_rows.shape[1] // 2
    return kernel_call(
        own_kernel, shape(count, half, dtype=jnp.float32), [VMEM] * 3, VMEM, count
    )(code, dict_rows, centered)


def added_kernel(total_ref, own_ref, arrived_ref, sum_ref, sent_ref):
    half = total_ref.shape[1]
    total = total_ref[...] + arrived_ref[:, :half].astype(jnp.float32)
    sum_ref[...] = total
    sent_ref[:, :half] = total.astype(jnp.bfloat16)
    if sent_ref.shape[1] > half:
        block = own_ref.shape[1] - half
        sent_ref[:, half : half + block] = own_ref[:, half:]
        sent_ref[:, half + block :] = arrived_ref[:, half:]


def added(total, own, arrived, merged):
    count, half = total.shape
    block = own.shape[1] - half
    return kernel_call(
        added_kernel,
        (
            shape(count, half, dtype=jnp.float32),
            shape(count, half + (2 * block if merged else 0)),
        ),
        [VMEM] * 3,
        (VMEM, VMEM),
        count,
    )(total, own, arrived)


def joined_kernel(skip, first_ref, second_ref, after_ref, out_ref):
    width = first_ref.shape[1] - skip
    out_ref[:, :width] = first_ref[:, skip:]
    out_ref[:, width:] = second_ref[:, skip:]


def joined(first, second, skip, after):
    return kernel_call(
        functools.partial(joined_kernel, skip),
        shape(first.shape[0], 2 * (first.shape[1] - skip)),
        [VMEM, VMEM, ANY],
        VMEM,
        first.shape[0],
    )(first, second, after)


def turned_kernel(own_ref, arrived_ref, bias_ref, after_ref, out_ref):
    pieces, width = bias_ref.shape
    bias = jnp.concatenate([bias_ref[...]] * (ROWS // pieces), axis=0)
    blocks = [
        (ref[:, at : at + width].astype(jnp.float32) - bias).astype(jnp.bfloat16)
        for ref in (own_ref, arrived_ref)
        for at in range(0, ref.shape[1], width)
    ]
    out_ref[...] = jnp.concatenate(blocks, axis=0).astype(jnp.float32).T.astype(jnp.bfloat16)


def turned(own, arrived, bias, after, count):
    blocks = 2 * own.shape[1] // bias.shape[1]
    return kernel_call(
        turned_kernel,
        shape(bias.shape[1], blocks * ROWS),
        [VMEM, VMEM, VMEM, ANY],
        VMEM,
        count,
    )(own, arrived, bias, after)


def product(part_ref, rows_ref, at, half):
    return lax.dot_general(
        part_ref[...],
        rows_ref[:, pl.ds(at, half)],
        (((1,), (1,)), ((), ())),
        preferred_element_type=jnp.float32,
    )


def first_product_kernel(own_ref, rows_ref, half_ref):
    own, _, half = halves(rows_ref.shape[1])
    half_ref[...] = product(own_ref, rows_ref, own, half)


def first_product(scaled_own, dict_rows):
    count = scaled_own.shape[0]
    return kernel_call(
        first_product_kernel,
        shape(count, dict_rows.shape[0], dtype=jnp.float32),
        [VMEM] * 2,
        VMEM,
        count,
    )(scaled_own, dict_rows)


def code_half_kernel(own_ref, other_ref, first_ref, rows_ref, half_ref, scaled_ref):
    own, other, half = halves(rows_ref.shape[1])
    half_ref[...] = first_ref[...] + product(other_ref, rows_ref, other, half)
    scaled_ref[:, pl.ds(own, half)] = own_ref[...]
    scaled_ref[:, pl.ds(other, half)] = other_ref[...]


def code_half_of(scaled_own, scaled_other, first, dict_rows):
    count = scaled_own.shape[0]
    slots, width = dict_rows.shape
    return kernel_call(
        code_half_kernel,
        (shape(count, slots, dtype=jnp.float32), shape(count, width)),
        [VMEM] * 4,
        (VMEM, VMEM),
        count,
    )(scaled_own, scaled_other, first, dict_rows)


def final_kernel(
    rows, raw_ref, mine_ref, theirs_ref, turned_ref, enc_hbm, benc_ref, enc_ref, sems
):
    count, slots = raw_ref.shape
    width, depth = turned_ref.shape
    pieces = ROWS // rows
    code_grad = mine_ref[...] + theirs_ref[...]
    pre_grad = jnp.where(raw_ref[...] > 0.0, code_grad, 0.0).astype(jnp.bfloat16)
    place = lax.broadcasted_iota(jnp.int32, (depth, count), 0)
    token = lax.broadcasted_iota(jnp.int32, (depth, count), 1)
    core = lax.axis_index("tok")
    block = place // ROWS
    distance = jnp.zeros_like(place)
    for step in range(feat_bits()):
        distance |= (block >> step & 1) << sum_bit(step, core)
    source = (lax.axis_index("feat") ^ distance) * rows + place % ROWS // pieces
    order = jnp.where(token == source, 1.0, 0.0).astype(jnp.bfloat16)
    spread = jnp.dot(order, pre_grad, preferred_element_type=jnp.float32)
    piece = lax.broadcasted_iota(jnp.int32, (depth, slots), 0) % pieces
    copies = []
    for c in range(0, pieces, 2):
        pair = [jnp.where(piece == c + i, spread, 0.0).astype(jnp.bfloat16) for i in range(2)]
        out = jnp.dot(
            turned_ref[...],
            jnp.concatenate(pair, axis=1),
            preferred_element_type=jnp.float32,
        ).astype(jnp.bfloat16)
        for i in range(2):
            enc_ref[(c + i) * width : (c + i + 1) * width, :] = out[:, i * slots : (i + 1) * slots]
        part = pl.ds(c * width, 2 * width)
        copies.append(pltpu.make_async_copy(enc_ref.at[part], enc_hbm.at[part], sems.at[c // 2]))
        copies[-1].start()
    benc_ref[...] = jnp.sum(pre_grad.astype(jnp.float32), axis=0, keepdims=True)
    for copy in copies:
        copy.wait()


def final(raw, mine, theirs, turned_tokens, rows):
    count, slots = raw.shape
    pieces = ROWS // rows
    width = turned_tokens.shape[0] * pieces
    return kernel_call(
        functools.partial(final_kernel, rows),
        (shape(width, slots), shape(1, slots, dtype=jnp.float32)),
        [VMEM] * 4,
        (HBM, VMEM),
        count,
        [pltpu.VMEM((width, slots), jnp.bfloat16), pltpu.SemaphoreType.DMA((pieces // 2,))],
    )(raw, mine, theirs, turned_tokens)


def local(tokens, b_pre, pre_codes, top_idx, blocks, counts, dict_rows):
    rows, count = tokens.shape[0], top_idx.shape[0]
    half = dict_rows.shape[1] // 2
    steps = feat_bits()
    merged = min(MERGED, steps - 1) if count == ROWS else 0

    code, raw, sent, block, dict_rows, centered, bias = front(
        tokens, b_pre, pre_codes, top_idx, blocks, counts, dict_rows, merged > 0
    )
    for step in range(steps):
        arrived = swapped(sent, step)
        if step == 0:
            total = own_part(code, dict_rows, centered)
        if step >= merged:
            if step == merged > 0:
                block = joined(own, previous, half, sent)
            elif step > 0:
                block = joined(block, arrived_block, 0, sent)
            arrived_block = swapped(block, step)
        if step < steps - 1:
            own, previous = sent, arrived
            total, sent = added(total, own, arrived, step + 1 < merged)
    total = total + arrived.astype(jnp.float32)
    scaled_own = (0.25 * total).astype(jnp.bfloat16)
    scaled_other = swapped(scaled_own, 0)

    first = first_product(scaled_own, dict_rows)
    turned_tokens = turned(block, arrived_block, bias, scaled_own, count)

    code_half, scaled = code_half_of(scaled_own, scaled_other, first, dict_rows)
    theirs = lax.ppermute(code_half, "tok", [(i, 1 - i) for i in range(2)])
    grad_rows = lax.dot_general(
        code, scaled, (((0,), (0,)), ((), ())), preferred_element_type=jnp.float32
    ).astype(jnp.bfloat16)
    grad_enc, grad_benc = final(raw, code_half, theirs, turned_tokens, rows)
    return (grad_rows, grad_enc, grad_benc.reshape(-1))


def solution(mesh):
    return jax.shard_map(
        local,
        mesh=mesh,
        in_specs=(
            P(("grp", "feat"), "tok"),
            P(("grp", "tok")),
            P("grp", None),
            P("grp", None),
            P(("grp", "feat")),
            P(("grp", "feat")),
            P(("grp", "feat"), "tok"),
        ),
        out_specs=(P(("grp", "feat"), "tok"), P(("grp", "tok"), "feat"), P(("grp", "feat"))),
        check_vma=False,
    )
```

```python
import functools

import jax
import jax.numpy as jnp
from jax import lax
from jax.experimental import pallas as pl
from jax.experimental.pallas import tpu as pltpu
from jax.sharding import PartitionSpec as P

VMEM = pl.BlockSpec(memory_space=pltpu.VMEM)
SMEM = pl.BlockSpec(memory_space=pltpu.SMEM)
HBM = pl.BlockSpec(memory_space=pltpu.HBM)
ROWS = 16


def kernel_call(kernel, out_shape, in_specs, out_specs, tokens, scratch_shapes=()):
    limit = (16 if tokens <= ROWS else 40) * 2**20
    return pl.pallas_call(
        kernel,
        out_shape=out_shape,
        in_specs=in_specs,
        out_specs=out_specs,
        scratch_shapes=scratch_shapes,
        compiler_params=pltpu.CompilerParams(vmem_limit_bytes=limit),
        cost_estimate=pl.CostEstimate(flops=10**6, bytes_accessed=2**20, transcendentals=0),
    )


def shape(*sizes, dtype=jnp.bfloat16):
    return jax.ShapeDtypeStruct(sizes, dtype)


def feat_bits():
    return (lax.axis_size("feat") - 1).bit_length()


def sum_bit(step, core):
    return (step + core) % feat_bits()


def token_bit(step, core):
    last = feat_bits() - 1
    order = [sum_bit(at, core) for at in range(last + 1)]
    order.remove(last)
    return ([last] + order)[step]


def swapped(shard, bit_of, step):
    cores = lax.axis_size("tok")
    pairs = [
        (f * cores + c, (f ^ 1 << bit_of(step, c)) * cores + c)
        for f in range(lax.axis_size("feat"))
        for c in range(cores)
    ]
    return lax.ppermute(shard, ("feat", "tok"), pairs)


def halves(width):
    half = width // 2
    bit = lax.axis_index("feat") >> (lax.axis_index("tok") % feat_bits()) & 1
    return (
        pl.multiple_of(bit * half, half),
        pl.multiple_of((1 - bit) * half, half),
        half,
    )


def stacked(rows, pieces):
    width = rows.shape[1] // pieces
    return jnp.concatenate(
        [
            rows[i : i + 1, c * width : (c + 1) * width]
            for i in range(rows.shape[0])
            for c in range(pieces)
        ],
        axis=0,
    )


def share(code, rows_ref, centered_ref, at, half):
    total = jnp.dot(code, rows_ref[:, pl.ds(at, half)], preferred_element_type=jnp.float32)
    rows = centered_ref.shape[0]
    centered = centered_ref[:, pl.ds(at, half)]
    token = lax.broadcasted_iota(jnp.int32, (total.shape[0], 1), 0)
    first = lax.axis_index("feat") * rows
    for i in range(rows):
        total -= jnp.where(token == first + i, centered[i : i + 1, :], 0.0)
    return total


def front_kernel(
    tokens_hbm,
    bias_hbm,
    pre_hbm,
    top_hbm,
    rows_hbm,
    block_ref,
    count_ref,
    code_ref,
    raw_ref,
    sent_ref,
    rows_ref,
    centered_ref,
    tokens_ref,
    bias_ref,
    bias_flat,
    pre_ref,
    top_ref,
    sems,
):
    copies = [
        pltpu.make_async_copy(source, target, sems.at[i])
        for i, (source, target) in enumerate(
            (
                (top_hbm, top_ref),
                (pre_hbm, pre_ref),
                (tokens_hbm, tokens_ref),
                (bias_hbm, bias_flat),
                (rows_hbm, rows_ref),
            )
        )
    ]
    for copy in copies:
        copy.start()
    for copy in copies[:2]:
        copy.wait()
    count, latents = top_ref.shape
    slots, width = rows_ref.shape
    offsets = lax.broadcasted_iota(jnp.int32, (1, slots), 1)
    slot_ids = jnp.where(offsets < count_ref[0], block_ref[0] * slots + offsets, -1)
    top, pre = top_ref[...], pre_ref[...]
    raw = jnp.zeros((count, slots), jnp.float32)
    for k in range(latents):
        raw = jnp.where(top[:, k : k + 1] == slot_ids, pre[:, k : k + 1], raw)
    raw_ref[...] = raw
    code = jnp.maximum(raw, 0.0).astype(jnp.bfloat16)
    code_ref[...] = code

    for copy in copies[2:4]:
        copy.wait()
    tokens = tokens_ref[...].astype(jnp.float32)
    bias = bias_flat[...].astype(jnp.float32).reshape(1, width)
    bias_ref[...] = bias
    centered_ref[...] = (tokens - bias).astype(jnp.bfloat16).astype(jnp.float32)

    copies[4].wait()
    _, other, half = halves(width)
    sent_ref[...] = share(code, rows_ref, centered_ref, other, half).astype(jnp.bfloat16)


def front(tokens, b_pre, pre_codes, top_idx, blocks, counts, dict_rows):
    count = top_idx.shape[0]
    slots, width = dict_rows.shape
    return kernel_call(
        front_kernel,
        (
            shape(count, slots),
            shape(count, slots, dtype=jnp.float32),
            shape(count, width // 2),
            shape(slots, width),
            shape(*tokens.shape, dtype=jnp.float32),
            shape(*tokens.shape),
            shape(1, width, dtype=jnp.float32),
        ),
        [HBM] * 5 + [SMEM] * 2,
        (VMEM,) * 7,
        count,
        [
            pltpu.VMEM(b_pre.shape, b_pre.dtype),
            pltpu.VMEM(pre_codes.shape, pre_codes.dtype),
            pltpu.VMEM(top_idx.shape, top_idx.dtype),
            pltpu.SemaphoreType.DMA((5,)),
        ],
    )(
        *(
            pltpu.with_memory_space_constraint(array, pltpu.HBM)
            for array in (tokens, b_pre, pre_codes, top_idx, dict_rows)
        ),
        blocks,
        counts,
    )


def own_kernel(code_ref, rows_ref, centered_ref, total_ref):
    own, _, half = halves(rows_ref.shape[1])
    total_ref[...] = share(code_ref[...], rows_ref, centered_ref, own, half)


def own_part(code, dict_rows, centered):
    count, half = code.shape[0], dict_rows.shape[1] // 2
    return kernel_call(
        own_kernel, shape(count, half, dtype=jnp.float32), [VMEM] * 3, VMEM, count
    )(code, dict_rows, centered)


def pieces_kernel(own_ref, arrived_ref, bias_ref, block_ref, pieces_ref):
    pieces, width = pieces_ref.shape
    for i, ref in enumerate((own_ref, arrived_ref)):
        block_ref[:, i * width : (i + 1) * width] = stacked(
            ref[...].astype(jnp.float32), pieces
        ).astype(jnp.bfloat16)
    pieces_ref[...] = stacked(bias_ref[...], pieces)


def in_pieces(own, arrived, bias, count):
    pieces = ROWS // own.shape[0]
    width = own.shape[1] // pieces
    return kernel_call(
        pieces_kernel,
        (shape(ROWS, 2 * width), shape(pieces, width, dtype=jnp.float32)),
        [VMEM] * 3,
        (VMEM, VMEM),
        count,
    )(own, arrived, bias)


def turned_kernel(own_ref, arrived_ref, bias_ref, out_ref):
    pieces, width = bias_ref.shape
    bias = jnp.concatenate([bias_ref[...]] * (ROWS // pieces), axis=0)
    blocks = [
        (ref[:, at : at + width].astype(jnp.float32) - bias).astype(jnp.bfloat16)
        for ref in (own_ref, arrived_ref)
        for at in range(0, ref.shape[1], width)
    ]
    out_ref[...] = jnp.concatenate(blocks, axis=0).astype(jnp.float32).T.astype(jnp.bfloat16)


def turned(own, arrived, bias, count):
    blocks = 2 * own.shape[1] // bias.shape[1]
    return kernel_call(
        turned_kernel,
        shape(bias.shape[1], blocks * ROWS),
        [VMEM] * 3,
        VMEM,
        count,
    )(own, arrived, bias)


def product(part_ref, rows_ref, at, half):
    return lax.dot_general(
        part_ref[...],
        rows_ref[:, pl.ds(at, half)],
        (((1,), (1,)), ((), ())),
        preferred_element_type=jnp.float32,
    )


def first_product_kernel(own_ref, rows_ref, half_ref):
    own, _, half = halves(rows_ref.shape[1])
    half_ref[...] = product(own_ref, rows_ref, own, half)


def first_product(scaled_own, dict_rows):
    count = scaled_own.shape[0]
    return kernel_call(
        first_product_kernel,
        shape(count, dict_rows.shape[0], dtype=jnp.float32),
        [VMEM] * 2,
        VMEM,
        count,
    )(scaled_own, dict_rows)


def code_half_kernel(own_ref, other_ref, first_ref, rows_ref, half_ref, scaled_ref):
    own, other, half = halves(rows_ref.shape[1])
    half_ref[...] = first_ref[...] + product(other_ref, rows_ref, other, half)
    scaled_ref[:, pl.ds(own, half)] = own_ref[...]
    scaled_ref[:, pl.ds(other, half)] = other_ref[...]


def code_half_of(scaled_own, scaled_other, first, dict_rows):
    count = scaled_own.shape[0]
    slots, width = dict_rows.shape
    return kernel_call(
        code_half_kernel,
        (shape(count, slots, dtype=jnp.float32), shape(count, width)),
        [VMEM] * 4,
        (VMEM, VMEM),
        count,
    )(scaled_own, scaled_other, first, dict_rows)


def final_kernel(
    rows, raw_ref, mine_ref, theirs_ref, turned_ref, enc_hbm, benc_ref, enc_ref, sems
):
    count, slots = raw_ref.shape
    width, depth = turned_ref.shape
    pieces = ROWS // rows
    code_grad = mine_ref[...] + theirs_ref[...]
    pre_grad = jnp.where(raw_ref[...] > 0.0, code_grad, 0.0).astype(jnp.bfloat16)
    place = lax.broadcasted_iota(jnp.int32, (depth, count), 0)
    token = lax.broadcasted_iota(jnp.int32, (depth, count), 1)
    core = lax.axis_index("tok")
    block = place // ROWS
    distance = jnp.zeros_like(place)
    for step in range(feat_bits()):
        bit = sum(
            jnp.where(core == c, token_bit(step, c), 0) for c in range(lax.axis_size("tok"))
        )
        distance |= (block >> step & 1) << bit
    source = (lax.axis_index("feat") ^ distance) * rows + place % ROWS // pieces
    order = jnp.where(token == source, 1.0, 0.0).astype(jnp.bfloat16)
    spread = jnp.dot(order, pre_grad, preferred_element_type=jnp.float32)
    piece = lax.broadcasted_iota(jnp.int32, (depth, slots), 0) % pieces
    copies = []
    for c in range(0, pieces, 2):
        pair = [jnp.where(piece == c + i, spread, 0.0).astype(jnp.bfloat16) for i in range(2)]
        out = jnp.dot(
            turned_ref[...],
            jnp.concatenate(pair, axis=1),
            preferred_element_type=jnp.float32,
        ).astype(jnp.bfloat16)
        for i in range(2):
            enc_ref[(c + i) * width : (c + i + 1) * width, :] = out[:, i * slots : (i + 1) * slots]
        part = pl.ds(c * width, 2 * width)
        copies.append(pltpu.make_async_copy(enc_ref.at[part], enc_hbm.at[part], sems.at[c // 2]))
        copies[-1].start()
    benc_ref[...] = jnp.sum(pre_grad.astype(jnp.float32), axis=0, keepdims=True)
    for copy in copies:
        copy.wait()


def final(raw, mine, theirs, turned_tokens, rows):
    count, slots = raw.shape
    pieces = ROWS // rows
    width = turned_tokens.shape[0] * pieces
    return kernel_call(
        functools.partial(final_kernel, rows),
        (shape(width, slots), shape(1, slots, dtype=jnp.float32)),
        [VMEM] * 4,
        (HBM, VMEM),
        count,
        [pltpu.VMEM((width, slots), jnp.bfloat16), pltpu.SemaphoreType.DMA((pieces // 2,))],
    )(raw, mine, theirs, turned_tokens)


def local(tokens, b_pre, pre_codes, top_idx, blocks, counts, dict_rows):
    rows, count = tokens.shape[0], top_idx.shape[0]
    last = feat_bits() - 1
    arrived_tokens = swapped(tokens, token_bit, 0)
    code, raw, sent, dict_rows, centered, tokens, bias = front(
        tokens, b_pre, pre_codes, top_idx, blocks, counts, dict_rows
    )
    sent, arrived_tokens = lax.optimization_barrier((sent, arrived_tokens))
    for step in range(last + 1):
        arrived = swapped(sent, sum_bit, step)
        if step == 0:
            total = own_part(code, dict_rows, centered)
            block, bias = in_pieces(tokens, arrived_tokens, bias, count)
        elif step < last:
            block = jnp.concatenate([block, arrived_block], axis=1)
        if step < last:
            arrived_block = swapped(block, token_bit, step + 1)
        total = total + arrived.astype(jnp.float32)
        sent = total.astype(jnp.bfloat16)
    scaled_own = (0.25 * total).astype(jnp.bfloat16)
    scaled_other = swapped(scaled_own, sum_bit, 0)

    first = first_product(scaled_own, dict_rows)
    turned_tokens = turned(block, arrived_block, bias, count)

    code_half, scaled = code_half_of(scaled_own, scaled_other, first, dict_rows)
    theirs = lax.ppermute(code_half, "tok", [(i, 1 - i) for i in range(2)])
    grad_rows = lax.dot_general(
        code, scaled, (((0,), (0,)), ((), ())), preferred_element_type=jnp.float32
    ).astype(jnp.bfloat16)
    grad_enc, grad_benc = final(raw, code_half, theirs, turned_tokens, rows)
    return (grad_rows, grad_enc, grad_benc.reshape(-1))


def solution(mesh):
    return jax.shard_map(
        local,
        mesh=mesh,
        in_specs=(
            P(("grp", "feat"), "tok"),
            P(("grp", "tok")),
            P("grp", None),
            P("grp", None),
            P(("grp", "feat")),
            P(("grp", "feat")),
            P(("grp", "feat"), "tok"),
        ),
        out_specs=(P(("grp", "feat"), "tok"), P(("grp", "tok"), "feat"), P(("grp", "feat"))),
        check_vma=False,
    )
```

```python
import functools

import jax
import jax.numpy as jnp
from jax import lax
from jax.experimental import pallas as pl
from jax.experimental.pallas import tpu as pltpu
from jax.sharding import PartitionSpec as P

VMEM = pl.BlockSpec(memory_space=pltpu.VMEM)
SMEM = pl.BlockSpec(memory_space=pltpu.SMEM)
HBM = pl.BlockSpec(memory_space=pltpu.HBM)
ANY = pl.BlockSpec(memory_space=pl.ANY)
MERGED = 2
ROWS = 16


def kernel_call(kernel, out_shape, in_specs, out_specs, tokens, scratch_shapes=()):
    limit = (16 if tokens <= ROWS else 40) * 2**20
    return pl.pallas_call(
        kernel,
        out_shape=out_shape,
        in_specs=in_specs,
        out_specs=out_specs,
        scratch_shapes=scratch_shapes,
        compiler_params=pltpu.CompilerParams(vmem_limit_bytes=limit),
        cost_estimate=pl.CostEstimate(flops=10**6, bytes_accessed=2**20, transcendentals=0),
    )


def shape(*sizes, dtype=jnp.bfloat16):
    return jax.ShapeDtypeStruct(sizes, dtype)


def feat_bits():
    return (lax.axis_size("feat") - 1).bit_length()


def bit_of(step, core):
    last = feat_bits() - 1
    ends = [0, last] if core == 0 else [last, 0]
    return (ends + list(range(1, last)))[step] if last else 0


def swapped(shard, step):
    cores = lax.axis_size("tok")
    pairs = [
        (f * cores + c, (f ^ 1 << bit_of(step, c)) * cores + c)
        for f in range(lax.axis_size("feat"))
        for c in range(cores)
    ]
    return lax.ppermute(shard, ("feat", "tok"), pairs)


def stacked(rows, pieces):
    width = rows.shape[1] // pieces
    return jnp.concatenate(
        [
            rows[i : i + 1, c * width : (c + 1) * width]
            for i in range(rows.shape[0])
            for c in range(pieces)
        ],
        axis=0,
    )


def share(code, rows_ref, centered_ref, at, half):
    part = pl.ds(at, half)
    total = jnp.dot(code, rows_ref[:, part], preferred_element_type=jnp.float32)
    rows = centered_ref.shape[0]
    centered = centered_ref[:, part]
    token = lax.broadcasted_iota(jnp.int32, (total.shape[0], 1), 0)
    first = lax.axis_index("feat") * rows
    for i in range(rows):
        total -= jnp.where(token == first + i, centered[i : i + 1, :], 0.0)
    return total


def front_kernel(
    tokens_hbm,
    bias_hbm,
    pre_hbm,
    top_hbm,
    rows_hbm,
    block_ref,
    count_ref,
    code_ref,
    raw_ref,
    total_ref,
    sent_ref,
    rows_ref,
    centered_ref,
    tokens_ref,
    bias_ref,
    bias_flat,
    pre_ref,
    top_ref,
    sems,
):
    copies = [
        pltpu.make_async_copy(source, target, sems.at[i])
        for i, (source, target) in enumerate(
            (
                (top_hbm, top_ref),
                (pre_hbm, pre_ref),
                (tokens_hbm, tokens_ref),
                (bias_hbm, bias_flat),
                (rows_hbm, rows_ref),
            )
        )
    ]
    for copy in copies:
        copy.start()
    for copy in copies[:2]:
        copy.wait()
    count, latents = top_ref.shape
    slots, width = rows_ref.shape
    offsets = lax.broadcasted_iota(jnp.int32, (1, slots), 1)
    slot_ids = jnp.where(offsets < count_ref[0], block_ref[0] * slots + offsets, -1)
    top, pre = top_ref[...], pre_ref[...]
    raw = jnp.zeros((count, slots), jnp.float32)
    for k in range(latents):
        raw = jnp.where(top[:, k : k + 1] == slot_ids, pre[:, k : k + 1], raw)
    raw_ref[...] = raw
    code = jnp.maximum(raw, 0.0).astype(jnp.bfloat16)
    code_ref[...] = code

    for copy in copies[2:4]:
        copy.wait()
    tokens = tokens_ref[...].astype(jnp.float32)
    bias = bias_flat[...].astype(jnp.float32).reshape(1, width)
    bias_ref[...] = bias
    centered_ref[...] = (tokens - bias).astype(jnp.bfloat16).astype(jnp.float32)

    copies[4].wait()
    total = share(code, rows_ref, centered_ref, 0, width // 2)
    total_ref[...] = total
    sent_ref[...] = total.astype(jnp.bfloat16)


def front(tokens, b_pre, pre_codes, top_idx, blocks, counts, dict_rows):
    count = top_idx.shape[0]
    slots, width = dict_rows.shape
    return kernel_call(
        front_kernel,
        (
            shape(count, slots),
            shape(count, slots, dtype=jnp.float32),
            shape(count, width // 2, dtype=jnp.float32),
            shape(count, width // 2),
            shape(slots, width),
            shape(*tokens.shape, dtype=jnp.float32),
            shape(*tokens.shape),
            shape(1, width, dtype=jnp.float32),
        ),
        [HBM] * 5 + [SMEM] * 2,
        (VMEM,) * 8,
        count,
        [
            pltpu.VMEM(b_pre.shape, b_pre.dtype),
            pltpu.VMEM(pre_codes.shape, pre_codes.dtype),
            pltpu.VMEM(top_idx.shape, top_idx.dtype),
            pltpu.SemaphoreType.DMA((5,)),
        ],
    )(
        *(
            pltpu.with_memory_space_constraint(array, pltpu.HBM)
            for array in (tokens, b_pre, pre_codes, top_idx, dict_rows)
        ),
        blocks,
        counts,
    )


def second_kernel(
    code_ref, rows_ref, centered_ref, tokens_ref, bias_ref, total_ref, sent_ref, block_ref, pieces_ref
):
    half = total_ref.shape[1]
    total = share(code_ref[...], rows_ref, centered_ref, half, half)
    total_ref[...] = total
    sent_ref[:, :half] = total.astype(jnp.bfloat16)
    pieces = pieces_ref.shape[0]
    block = stacked(tokens_ref[...].astype(jnp.float32), pieces).astype(jnp.bfloat16)
    block_ref[...] = block
    if sent_ref.shape[1] > half:
        sent_ref[:, half:] = block
    pieces_ref[...] = stacked(bias_ref[...], pieces)


def second(code, dict_rows, centered, tokens, bias, merged):
    count, half = code.shape[0], dict_rows.shape[1] // 2
    pieces = ROWS // tokens.shape[0]
    width = tokens.shape[1] // pieces
    return kernel_call(
        second_kernel,
        (
            shape(count, half, dtype=jnp.float32),
            shape(count, half + (width if merged else 0)),
            shape(ROWS, width),
            shape(pieces, width, dtype=jnp.float32),
        ),
        [VMEM] * 5,
        (VMEM,) * 4,
        count,
    )(code, dict_rows, centered, tokens, bias)


def added_kernel(total_ref, own_ref, arrived_ref, after_ref, sum_ref, sent_ref):
    half = total_ref.shape[1]
    total = total_ref[...] + arrived_ref[:, :half].astype(jnp.float32)
    sum_ref[...] = total
    sent_ref[:, :half] = total.astype(jnp.bfloat16)
    if sent_ref.shape[1] > half:
        block = own_ref.shape[1] - half
        sent_ref[:, half : half + block] = own_ref[:, half:]
        sent_ref[:, half + block :] = arrived_ref[:, half:]


def added(total, own, arrived, after, merged):
    count, half = total.shape
    block = own.shape[1] - half
    return kernel_call(
        added_kernel,
        (
            shape(count, half, dtype=jnp.float32),
            shape(count, half + (2 * block if merged else 0)),
        ),
        [VMEM] * 3 + [ANY],
        (VMEM, VMEM),
        count,
    )(total, own, arrived, after)


def joined_kernel(skip, first_ref, second_ref, after_ref, out_ref):
    width = first_ref.shape[1] - skip
    out_ref[:, :width] = first_ref[:, skip:]
    out_ref[:, width:] = second_ref[:, skip:]


def joined(first, second, skip, after):
    return kernel_call(
        functools.partial(joined_kernel, skip),
        shape(first.shape[0], 2 * (first.shape[1] - skip)),
        [VMEM, VMEM, ANY],
        VMEM,
        first.shape[0],
    )(first, second, after)


def turned_kernel(own_ref, arrived_ref, bias_ref, after_ref, out_ref):
    pieces, width = bias_ref.shape
    bias = jnp.concatenate([bias_ref[...]] * (ROWS // pieces), axis=0)
    blocks = [
        (ref[:, at : at + width].astype(jnp.float32) - bias).astype(jnp.bfloat16)
        for ref in (own_ref, arrived_ref)
        for at in range(0, ref.shape[1], width)
    ]
    out_ref[...] = jnp.concatenate(blocks, axis=0).astype(jnp.float32).T.astype(jnp.bfloat16)


def turned(own, arrived, bias, after, count):
    blocks = 2 * own.shape[1] // bias.shape[1]
    return kernel_call(
        turned_kernel,
        shape(bias.shape[1], blocks * ROWS),
        [VMEM] * 3 + [ANY],
        VMEM,
        count,
    )(own, arrived, bias, after)


def product(part_ref, rows_ref, at, half):
    return lax.dot_general(
        part_ref[...],
        rows_ref[:, pl.ds(at, half)],
        (((1,), (1,)), ((), ())),
        preferred_element_type=jnp.float32,
    )


def first_product_kernel(first_ref, rows_ref, half_ref):
    half_ref[...] = product(first_ref, rows_ref, 0, first_ref.shape[1])


def first_product(scaled_first, dict_rows):
    count = scaled_first.shape[0]
    return kernel_call(
        first_product_kernel,
        shape(count, dict_rows.shape[0], dtype=jnp.float32),
        [VMEM] * 2,
        VMEM,
        count,
    )(scaled_first, dict_rows)


def code_half_kernel(first_ref, second_ref, product_ref, rows_ref, half_ref, scaled_ref):
    half = first_ref.shape[1]
    half_ref[...] = product_ref[...] + product(second_ref, rows_ref, half, half)
    scaled_ref[:, :half] = first_ref[...]
    scaled_ref[:, half:] = second_ref[...]


def code_half_of(scaled_first, scaled_second, first, dict_rows):
    count = scaled_first.shape[0]
    slots, width = dict_rows.shape
    return kernel_call(
        code_half_kernel,
        (shape(count, slots, dtype=jnp.float32), shape(count, width)),
        [VMEM] * 4,
        (VMEM, VMEM),
        count,
    )(scaled_first, scaled_second, first, dict_rows)


def final_kernel(
    rows, raw_ref, mine_ref, theirs_ref, turned_ref, enc_hbm, benc_ref, enc_ref, sems
):
    count, slots = raw_ref.shape
    width, depth = turned_ref.shape
    pieces = ROWS // rows
    code_grad = mine_ref[...] + theirs_ref[...]
    pre_grad = jnp.where(raw_ref[...] > 0.0, code_grad, 0.0).astype(jnp.bfloat16)
    place = lax.broadcasted_iota(jnp.int32, (depth, count), 0)
    token = lax.broadcasted_iota(jnp.int32, (depth, count), 1)
    core = lax.axis_index("tok")
    block = place // ROWS
    distance = jnp.zeros_like(place)
    for step in range(feat_bits()):
        bit = sum(
            jnp.where(core == c, bit_of(step, c), 0) for c in range(lax.axis_size("tok"))
        )
        distance |= (block >> step & 1) << bit
    source = (lax.axis_index("feat") ^ distance) * rows + place % ROWS // pieces
    order = jnp.where(token == source, 1.0, 0.0).astype(jnp.bfloat16)
    spread = jnp.dot(order, pre_grad, preferred_element_type=jnp.float32)
    piece = lax.broadcasted_iota(jnp.int32, (depth, slots), 0) % pieces
    copies = []
    for c in range(0, pieces, 2):
        pair = [jnp.where(piece == c + i, spread, 0.0).astype(jnp.bfloat16) for i in range(2)]
        out = jnp.dot(
            turned_ref[...],
            jnp.concatenate(pair, axis=1),
            preferred_element_type=jnp.float32,
        ).astype(jnp.bfloat16)
        for i in range(2):
            enc_ref[(c + i) * width : (c + i + 1) * width, :] = out[:, i * slots : (i + 1) * slots]
        part = pl.ds(c * width, 2 * width)
        copies.append(pltpu.make_async_copy(enc_ref.at[part], enc_hbm.at[part], sems.at[c // 2]))
        copies[-1].start()
    benc_ref[...] = jnp.sum(pre_grad.astype(jnp.float32), axis=0, keepdims=True)
    for copy in copies:
        copy.wait()


def final(raw, mine, theirs, turned_tokens, rows):
    count, slots = raw.shape
    pieces = ROWS // rows
    width = turned_tokens.shape[0] * pieces
    return kernel_call(
        functools.partial(final_kernel, rows),
        (shape(width, slots), shape(1, slots, dtype=jnp.float32)),
        [VMEM] * 4,
        (HBM, VMEM),
        count,
        [pltpu.VMEM((width, slots), jnp.bfloat16), pltpu.SemaphoreType.DMA((pieces // 2,))],
    )(raw, mine, theirs, turned_tokens)


def local(tokens, b_pre, pre_codes, top_idx, blocks, counts, dict_rows):
    rows, count = tokens.shape[0], top_idx.shape[0]
    steps = feat_bits()
    half = dict_rows.shape[1] // 2
    merged = min(MERGED, steps - 1) if count == ROWS else 0

    code, raw, total, sent, dict_rows, centered, tokens, bias = front(
        tokens, b_pre, pre_codes, top_idx, blocks, counts, dict_rows
    )
    for step in range(steps):
        arrived = swapped(sent, step)
        if step == 0:
            total_second, sent_second, block, bias = second(
                code, dict_rows, centered, tokens, bias, merged > 0
            )
        else:
            own, previous = sent_second, arrived_second
            total_second, sent_second = added(
                total_second, own, previous, sent, step < merged
            )
        arrived_second = swapped(sent_second, step)
        if step >= merged:
            if step == merged > 0:
                block = joined(own, previous, half, sent_second)
            elif step > 0:
                block = joined(block, arrived_block, 0, sent_second)
            arrived_block = swapped(block, step)
        total = total + arrived.astype(jnp.float32)
        sent = total.astype(jnp.bfloat16)
    scaled_first = (0.25 * total).astype(jnp.bfloat16)
    scaled_second = (0.25 * (total_second + arrived_second.astype(jnp.float32))).astype(
        jnp.bfloat16
    )
    first = first_product(scaled_first, dict_rows)
    code_half, scaled = code_half_of(scaled_first, scaled_second, first, dict_rows)
    turned_tokens = turned(block, arrived_block, bias, code_half, count)
    theirs = lax.ppermute(code_half, "tok", [(i, 1 - i) for i in range(2)])
    grad_rows = lax.dot_general(
        code, scaled, (((0,), (0,)), ((), ())), preferred_element_type=jnp.float32
    ).astype(jnp.bfloat16)
    grad_enc, grad_benc = final(raw, code_half, theirs, turned_tokens, rows)
    return (grad_rows, grad_enc, grad_benc.reshape(-1))


def solution(mesh):
    return jax.shard_map(
        local,
        mesh=mesh,
        in_specs=(
            P(("grp", "feat"), "tok"),
            P(("grp", "tok")),
            P("grp", None),
            P("grp", None),
            P(("grp", "feat")),
            P(("grp", "feat")),
            P(("grp", "feat"), "tok"),
        ),
        out_specs=(P(("grp", "feat"), "tok"), P(("grp", "tok"), "feat"), P(("grp", "feat"))),
        check_vma=False,
    )
```

```python
import functools

import jax
import jax.numpy as jnp
from jax import lax
from jax.experimental import pallas as pl
from jax.experimental.pallas import tpu as pltpu
from jax.sharding import PartitionSpec as P

VMEM = pl.BlockSpec(memory_space=pltpu.VMEM)
SMEM = pl.BlockSpec(memory_space=pltpu.SMEM)
HBM = pl.BlockSpec(memory_space=pltpu.HBM)
ANY = pl.BlockSpec(memory_space=pl.ANY)
MERGED = 2
ROWS = 16


def kernel_call(kernel, out_shape, in_specs, out_specs, tokens, scratch_shapes=()):
    limit = (16 if tokens <= ROWS else 40) * 2**20
    return pl.pallas_call(
        kernel,
        out_shape=out_shape,
        in_specs=in_specs,
        out_specs=out_specs,
        scratch_shapes=scratch_shapes,
        compiler_params=pltpu.CompilerParams(vmem_limit_bytes=limit),
        cost_estimate=pl.CostEstimate(flops=10**6, bytes_accessed=2**20, transcendentals=0),
    )


def shape(*sizes, dtype=jnp.bfloat16):
    return jax.ShapeDtypeStruct(sizes, dtype)


def first_width(width):
    return width // 2


def feat_bits():
    return (lax.axis_size("feat") - 1).bit_length()


def bit_of(step, core):
    last = feat_bits() - 1
    middle = list(range(1, last))
    return ([0, last] + middle if core == 0 else [last] + middle + [0])[step] if last else 0


def swapped(shard, step):
    cores = lax.axis_size("tok")
    pairs = [
        (f * cores + c, (f ^ 1 << bit_of(step, c)) * cores + c)
        for f in range(lax.axis_size("feat"))
        for c in range(cores)
    ]
    return lax.ppermute(shard, ("feat", "tok"), pairs)


def stacked(rows, pieces):
    width = rows.shape[1] // pieces
    return jnp.concatenate(
        [rows[:, c * width : (c + 1) * width] for c in range(pieces)], axis=0
    )


def share(code, rows_ref, centered_ref, at, width):
    part = pl.ds(at, width)
    total = jnp.dot(code, rows_ref[:, part], preferred_element_type=jnp.float32)
    rows = centered_ref.shape[0]
    centered = centered_ref[:, part]
    token = lax.broadcasted_iota(jnp.int32, (total.shape[0], 1), 0)
    first = lax.axis_index("feat") * rows
    for i in range(rows):
        total -= jnp.where(token == first + i, centered[i : i + 1, :], 0.0)
    return total


def front_kernel(
    tokens_hbm,
    bias_hbm,
    pre_hbm,
    top_hbm,
    rows_hbm,
    block_ref,
    count_ref,
    code_ref,
    raw_ref,
    total_ref,
    sent_ref,
    rows_ref,
    centered_ref,
    tokens_ref,
    bias_ref,
    bias_flat,
    pre_ref,
    top_ref,
    sems,
):
    copies = [
        pltpu.make_async_copy(source, target, sems.at[i])
        for i, (source, target) in enumerate(
            (
                (top_hbm, top_ref),
                (pre_hbm, pre_ref),
                (tokens_hbm, tokens_ref),
                (bias_hbm, bias_flat),
                (rows_hbm, rows_ref),
            )
        )
    ]
    for copy in copies:
        copy.start()
    for copy in copies[:2]:
        copy.wait()
    count, latents = top_ref.shape
    slots, width = rows_ref.shape
    offsets = lax.broadcasted_iota(jnp.int32, (1, slots), 1)
    slot_ids = jnp.where(offsets < count_ref[0], block_ref[0] * slots + offsets, -1)
    top, pre = top_ref[...], pre_ref[...]
    raw = jnp.zeros((count, slots), jnp.float32)
    for k in range(latents):
        raw = jnp.where(top[:, k : k + 1] == slot_ids, pre[:, k : k + 1], raw)
    raw_ref[...] = raw
    code = jnp.maximum(raw, 0.0).astype(jnp.bfloat16)
    code_ref[...] = code

    for copy in copies[2:4]:
        copy.wait()
    tokens = tokens_ref[...].astype(jnp.float32)
    bias = bias_flat[...].astype(jnp.float32).reshape(1, width)
    bias_ref[...] = bias
    centered_ref[...] = (tokens - bias).astype(jnp.bfloat16).astype(jnp.float32)

    copies[4].wait()
    total = share(code, rows_ref, centered_ref, 0, total_ref.shape[1])
    total_ref[...] = total
    sent_ref[...] = total.astype(jnp.bfloat16)


def front(tokens, b_pre, pre_codes, top_idx, blocks, counts, dict_rows):
    count = top_idx.shape[0]
    slots, width = dict_rows.shape
    return kernel_call(
        front_kernel,
        (
            shape(count, slots),
            shape(count, slots, dtype=jnp.float32),
            shape(count, first_width(width), dtype=jnp.float32),
            shape(count, first_width(width)),
            shape(slots, width),
            shape(*tokens.shape, dtype=jnp.float32),
            shape(*tokens.shape),
            shape(1, width, dtype=jnp.float32),
        ),
        [HBM] * 5 + [SMEM] * 2,
        (VMEM,) * 8,
        count,
        [
            pltpu.VMEM(b_pre.shape, b_pre.dtype),
            pltpu.VMEM(pre_codes.shape, pre_codes.dtype),
            pltpu.VMEM(top_idx.shape, top_idx.dtype),
            pltpu.SemaphoreType.DMA((5,)),
        ],
    )(
        *(
            pltpu.with_memory_space_constraint(array, pltpu.HBM)
            for array in (tokens, b_pre, pre_codes, top_idx, dict_rows)
        ),
        blocks,
        counts,
    )


def second_kernel(code_ref, rows_ref, centered_ref, tokens_ref, total_ref, sent_ref, block_ref):
    width = total_ref.shape[1]
    total = share(code_ref[...], rows_ref, centered_ref, rows_ref.shape[1] - width, width)
    total_ref[...] = total
    sent_ref[:, :width] = total.astype(jnp.bfloat16)
    pieces = ROWS // tokens_ref.shape[0]
    block = stacked(tokens_ref[...].astype(jnp.float32), pieces).astype(jnp.bfloat16)
    block_ref[...] = block
    if sent_ref.shape[1] > width:
        sent_ref[:, width:] = block


def second(code, dict_rows, centered, tokens, merged):
    count, width = code.shape[0], dict_rows.shape[1]
    chunk = width - first_width(width)
    block = tokens.shape[0] * width // ROWS
    return kernel_call(
        second_kernel,
        (
            shape(count, chunk, dtype=jnp.float32),
            shape(count, chunk + (block if merged else 0)),
            shape(ROWS, block),
        ),
        [VMEM] * 4,
        (VMEM,) * 3,
        count,
    )(code, dict_rows, centered, tokens)


def added_kernel(total_ref, own_ref, arrived_ref, after_ref, sum_ref, sent_ref):
    half = total_ref.shape[1]
    total = total_ref[...] + arrived_ref[:, :half].astype(jnp.float32)
    sum_ref[...] = total
    sent_ref[:, :half] = total.astype(jnp.bfloat16)
    if sent_ref.shape[1] > half:
        block = own_ref.shape[1] - half
        sent_ref[:, half : half + block] = own_ref[:, half:]
        sent_ref[:, half + block :] = arrived_ref[:, half:]


def added(total, own, arrived, after, merged):
    count, half = total.shape
    block = own.shape[1] - half
    return kernel_call(
        added_kernel,
        (
            shape(count, half, dtype=jnp.float32),
            shape(count, half + (2 * block if merged else 0)),
        ),
        [VMEM] * 3 + [ANY],
        (VMEM, VMEM),
        count,
    )(total, own, arrived, after)


def joined_kernel(skip, first_ref, second_ref, after_ref, out_ref):
    width = first_ref.shape[1] - skip
    out_ref[:, :width] = first_ref[:, skip:]
    out_ref[:, width:] = second_ref[:, skip:]


def joined(first, second, skip, after):
    return kernel_call(
        functools.partial(joined_kernel, skip),
        shape(first.shape[0], 2 * (first.shape[1] - skip)),
        [VMEM, VMEM, ANY],
        VMEM,
        first.shape[0],
    )(first, second, after)


def turned_kernel(rows, own_ref, arrived_ref, bias_ref, after_ref, out_ref):
    bias = jnp.concatenate([bias_ref[...]] * rows, axis=0)
    bias = stacked(bias, ROWS // rows)
    width = bias.shape[1]
    blocks = [
        (ref[:, at : at + width].astype(jnp.float32) - bias).astype(jnp.bfloat16)
        for ref in (own_ref, arrived_ref)
        for at in range(0, ref.shape[1], width)
    ]
    out_ref[...] = jnp.concatenate(blocks, axis=0).astype(jnp.float32).T.astype(jnp.bfloat16)


def turned(own, arrived, bias, after, rows, count):
    width = bias.shape[1] * rows // ROWS
    return kernel_call(
        functools.partial(turned_kernel, rows),
        shape(width, 2 * own.shape[1] // width * ROWS),
        [VMEM] * 3 + [ANY],
        VMEM,
        count,
    )(own, arrived, bias, after)


def scaled_of(total_ref, arrived_ref):
    total = total_ref[...] + arrived_ref[:, : total_ref.shape[1]].astype(jnp.float32)
    return (0.25 * total).astype(jnp.bfloat16)


def product(part, rows_ref, at):
    return lax.dot_general(
        part,
        rows_ref[:, at : at + part.shape[1]],
        (((1,), (1,)), ((), ())),
        preferred_element_type=jnp.float32,
    )


def first_product_kernel(total_ref, arrived_ref, rows_ref, scaled_ref, half_ref):
    scaled = scaled_of(total_ref, arrived_ref)
    scaled_ref[...] = scaled
    half_ref[...] = product(scaled, rows_ref, 0)


def second_product_kernel(
    total_ref, arrived_ref, rows_ref, first_ref, after_ref, scaled_ref, half_ref
):
    scaled = scaled_of(total_ref, arrived_ref)
    scaled_ref[...] = scaled
    half_ref[...] = first_ref[...] + product(scaled, rows_ref, rows_ref.shape[1] - scaled.shape[1])


def products(total, arrived, dict_rows, *first):
    count, width = total.shape
    return kernel_call(
        second_product_kernel if first else first_product_kernel,
        (shape(count, width), shape(count, dict_rows.shape[0], dtype=jnp.float32)),
        [VMEM] * 3 + ([VMEM, ANY] if first else []),
        (VMEM, VMEM),
        count,
    )(total, arrived, dict_rows, *first)


def grad_rows_kernel(at, code_ref, scaled_ref, *refs):
    out_hbm, mark_ref, out_ref, sems = refs[-4:]
    mark_ref[...] = jnp.zeros_like(mark_ref)
    slots, width = out_ref.shape
    code = code_ref[...].astype(jnp.float32).T.astype(jnp.bfloat16)
    step = width // sems.shape[0]
    copies = []
    for i in range(sems.shape[0]):
        part = pl.ds(i * step, step)
        out_ref[:, part] = jnp.dot(
            code, scaled_ref[:, part], preferred_element_type=jnp.float32
        ).astype(jnp.bfloat16)
        copies.append(
            pltpu.make_async_copy(
                out_ref.at[:, part], out_hbm.at[:, pl.ds(at + i * step, step)], sems.at[i]
            )
        )
        copies[-1].start()
    for copy in copies:
        copy.wait()


def grad_rows_part(code, scaled, width, written=None):
    count, slots = code.shape
    chunk = scaled.shape[1]
    at = 0 if written is None else width - chunk
    limit = (16 if count <= ROWS else 40) * 2**20
    return pl.pallas_call(
        functools.partial(grad_rows_kernel, at),
        out_shape=(shape(slots, width), shape(1, slots, dtype=jnp.float32)),
        in_specs=[VMEM] * 2 + ([] if written is None else [HBM]),
        out_specs=(HBM, VMEM),
        scratch_shapes=[
            pltpu.VMEM((slots, chunk), jnp.bfloat16),
            pltpu.SemaphoreType.DMA((2,)),
        ],
        input_output_aliases={} if written is None else {2: 0},
        compiler_params=pltpu.CompilerParams(vmem_limit_bytes=limit),
        cost_estimate=pl.CostEstimate(flops=10**6, bytes_accessed=2**20, transcendentals=0),
    )(code, scaled, *(() if written is None else (written,)))


def final_kernel(
    rows, raw_ref, mine_ref, theirs_ref, turned_ref, enc_hbm, benc_ref, enc_ref, sems
):
    count, slots = raw_ref.shape
    width, depth = turned_ref.shape
    pieces = ROWS // rows
    code_grad = mine_ref[...] + theirs_ref[...]
    pre_grad = jnp.where(raw_ref[...] > 0.0, code_grad, 0.0).astype(jnp.bfloat16)
    place = lax.broadcasted_iota(jnp.int32, (depth, count), 0)
    token = lax.broadcasted_iota(jnp.int32, (depth, count), 1)
    core = lax.axis_index("tok")
    block = place // ROWS
    distance = jnp.zeros_like(place)
    for step in range(feat_bits()):
        bit = sum(
            jnp.where(core == c, bit_of(step, c), 0) for c in range(lax.axis_size("tok"))
        )
        distance |= (block >> step & 1) << bit
    source = (lax.axis_index("feat") ^ distance) * rows + place % rows
    order = jnp.where(token == source, 1.0, 0.0).astype(jnp.bfloat16)
    spread = jnp.dot(order, pre_grad, preferred_element_type=jnp.float32)
    piece = lax.broadcasted_iota(jnp.int32, (depth, slots), 0) % ROWS // rows
    copies = []
    for c in range(0, pieces, 2):
        pair = [jnp.where(piece == c + i, spread, 0.0).astype(jnp.bfloat16) for i in range(2)]
        out = jnp.dot(
            turned_ref[...],
            jnp.concatenate(pair, axis=1),
            preferred_element_type=jnp.float32,
        ).astype(jnp.bfloat16)
        for i in range(2):
            enc_ref[(c + i) * width : (c + i + 1) * width, :] = out[:, i * slots : (i + 1) * slots]
        part = pl.ds(c * width, 2 * width)
        copies.append(pltpu.make_async_copy(enc_ref.at[part], enc_hbm.at[part], sems.at[c // 2]))
        copies[-1].start()
    benc_ref[...] = jnp.sum(pre_grad.astype(jnp.float32), axis=0, keepdims=True)
    for copy in copies:
        copy.wait()


def final(raw, mine, theirs, turned_tokens, rows):
    count, slots = raw.shape
    pieces = ROWS // rows
    width = turned_tokens.shape[0] * pieces
    return kernel_call(
        functools.partial(final_kernel, rows),
        (shape(width, slots), shape(1, slots, dtype=jnp.float32)),
        [VMEM] * 4,
        (HBM, VMEM),
        count,
        [pltpu.VMEM((width, slots), jnp.bfloat16), pltpu.SemaphoreType.DMA((pieces // 2,))],
    )(raw, mine, theirs, turned_tokens)


def local(tokens, b_pre, pre_codes, top_idx, blocks, counts, dict_rows):
    rows, count = tokens.shape[0], top_idx.shape[0]
    steps = feat_bits()
    width = dict_rows.shape[1]
    merged = min(MERGED, steps - 1) if count == ROWS else 0

    code, raw, total, sent, dict_rows, centered, tokens, bias = front(
        tokens, b_pre, pre_codes, top_idx, blocks, counts, dict_rows
    )
    for step in range(steps):
        arrived = swapped(sent, step)
        if step == 0:
            total_second, sent_second, block = second(
                code, dict_rows, centered, tokens, merged > 0
            )
        else:
            own, previous = sent_second, arrived_second
            total_second, sent_second = added(
                total_second, own, previous, sent, step < merged
            )
        arrived_second = swapped(sent_second, step)
        if step >= merged:
            if step == merged > 0:
                block = joined(own, previous, total_second.shape[1], sent_second)
            elif step > 0:
                block = joined(block, arrived_block, 0, sent_second)
            arrived_block = swapped(block, step)
        if step < steps - 1:
            total = total + arrived.astype(jnp.float32)
            sent = total.astype(jnp.bfloat16)
    scaled, product_first = products(total, arrived, dict_rows)
    grad_rows, mark = grad_rows_part(code, scaled, width)
    scaled, code_half = products(
        total_second, arrived_second, dict_rows, product_first, mark
    )
    theirs = lax.ppermute(code_half, "tok", [(i, 1 - i) for i in range(2)])
    grad_rows, _ = grad_rows_part(code, scaled, width, grad_rows)
    turned_tokens = turned(block, arrived_block, bias, code_half, rows, count)
    grad_enc, grad_benc = final(raw, code_half, theirs, turned_tokens, rows)
    return (grad_rows, grad_enc, grad_benc.reshape(-1))


def solution(mesh):
    return jax.shard_map(
        local,
        mesh=mesh,
        in_specs=(
            P(("grp", "feat"), "tok"),
            P(("grp", "tok")),
            P("grp", None),
            P("grp", None),
            P(("grp", "feat")),
            P(("grp", "feat")),
            P(("grp", "feat"), "tok"),
        ),
        out_specs=(P(("grp", "feat"), "tok"), P(("grp", "tok"), "feat"), P(("grp", "feat"))),
        check_vma=False,
    )
```

```python
import functools

import jax
import jax.numpy as jnp
from jax import lax
from jax.experimental import pallas as pl
from jax.experimental.pallas import tpu as pltpu
from jax.sharding import PartitionSpec as P

VMEM = pl.BlockSpec(memory_space=pltpu.VMEM)
SMEM = pl.BlockSpec(memory_space=pltpu.SMEM)
HBM = pl.BlockSpec(memory_space=pltpu.HBM)
ANY = pl.BlockSpec(memory_space=pl.ANY)
MERGED = 2
ROWS = 16


def kernel_call(kernel, out_shape, in_specs, out_specs, tokens, scratch_shapes=()):
    limit = (16 if tokens <= ROWS else 40) * 2**20
    return pl.pallas_call(
        kernel,
        out_shape=out_shape,
        in_specs=in_specs,
        out_specs=out_specs,
        scratch_shapes=scratch_shapes,
        compiler_params=pltpu.CompilerParams(vmem_limit_bytes=limit),
        cost_estimate=pl.CostEstimate(flops=10**6, bytes_accessed=2**20, transcendentals=0),
    )


def shape(*sizes, dtype=jnp.bfloat16):
    return jax.ShapeDtypeStruct(sizes, dtype)


def first_width(width):
    return width // 2


def feat_bits():
    return (lax.axis_size("feat") - 1).bit_length()


def bit_of(step, core):
    last = feat_bits() - 1
    middle = list(range(1, last))
    return ([0, last] + middle if core == 0 else [last] + middle + [0])[step] if last else 0


def swapped(shard, step):
    cores = lax.axis_size("tok")
    pairs = [
        (f * cores + c, (f ^ 1 << bit_of(step, c)) * cores + c)
        for f in range(lax.axis_size("feat"))
        for c in range(cores)
    ]
    return lax.ppermute(shard, ("feat", "tok"), pairs)


def stacked(rows, pieces):
    width = rows.shape[1] // pieces
    return jnp.concatenate(
        [rows[:, c * width : (c + 1) * width] for c in range(pieces)], axis=0
    )


def share(code, rows_ref, centered_ref, at, width):
    part = pl.ds(at, width)
    total = jnp.dot(code, rows_ref[:, part], preferred_element_type=jnp.float32)
    rows = centered_ref.shape[0]
    centered = centered_ref[:, part]
    token = lax.broadcasted_iota(jnp.int32, (total.shape[0], 1), 0)
    first = lax.axis_index("feat") * rows
    for i in range(rows):
        total -= jnp.where(token == first + i, centered[i : i + 1, :], 0.0)
    return total


def front_kernel(
    tokens_hbm,
    bias_hbm,
    pre_hbm,
    top_hbm,
    rows_hbm,
    block_ref,
    count_ref,
    code_ref,
    raw_ref,
    total_ref,
    sent_ref,
    rows_ref,
    centered_ref,
    tokens_ref,
    bias_ref,
    bias_flat,
    pre_ref,
    top_ref,
    sems,
):
    copies = [
        pltpu.make_async_copy(source, target, sems.at[i])
        for i, (source, target) in enumerate(
            (
                (top_hbm, top_ref),
                (pre_hbm, pre_ref),
                (tokens_hbm, tokens_ref),
                (bias_hbm, bias_flat),
                (rows_hbm, rows_ref),
            )
        )
    ]
    for copy in copies:
        copy.start()
    for copy in copies[:2]:
        copy.wait()
    count, latents = top_ref.shape
    slots, width = rows_ref.shape
    offsets = lax.broadcasted_iota(jnp.int32, (1, slots), 1)
    slot_ids = jnp.where(offsets < count_ref[0], block_ref[0] * slots + offsets, -1)
    top, pre = top_ref[...], pre_ref[...]
    raw = jnp.zeros((count, slots), jnp.float32)
    for k in range(latents):
        raw = jnp.where(top[:, k : k + 1] == slot_ids, pre[:, k : k + 1], raw)
    raw_ref[...] = raw
    code = jnp.maximum(raw, 0.0).astype(jnp.bfloat16)
    code_ref[...] = code

    for copy in copies[2:4]:
        copy.wait()
    tokens = tokens_ref[...].astype(jnp.float32)
    bias = bias_flat[...].astype(jnp.float32).reshape(1, width)
    bias_ref[...] = bias
    centered_ref[...] = (tokens - bias).astype(jnp.bfloat16).astype(jnp.float32)

    copies[4].wait()
    total = share(code, rows_ref, centered_ref, 0, total_ref.shape[1])
    total_ref[...] = total
    sent_ref[...] = total.astype(jnp.bfloat16)


def front(tokens, b_pre, pre_codes, top_idx, blocks, counts, dict_rows):
    count = top_idx.shape[0]
    slots, width = dict_rows.shape
    return kernel_call(
        front_kernel,
        (
            shape(count, slots),
            shape(count, slots, dtype=jnp.float32),
            shape(count, first_width(width), dtype=jnp.float32),
            shape(count, first_width(width)),
            shape(slots, width),
            shape(*tokens.shape, dtype=jnp.float32),
            shape(*tokens.shape),
            shape(1, width, dtype=jnp.float32),
        ),
        [HBM] * 5 + [SMEM] * 2,
        (VMEM,) * 8,
        count,
        [
            pltpu.VMEM(b_pre.shape, b_pre.dtype),
            pltpu.VMEM(pre_codes.shape, pre_codes.dtype),
            pltpu.VMEM(top_idx.shape, top_idx.dtype),
            pltpu.SemaphoreType.DMA((5,)),
        ],
    )(
        *(
            pltpu.with_memory_space_constraint(array, pltpu.HBM)
            for array in (tokens, b_pre, pre_codes, top_idx, dict_rows)
        ),
        blocks,
        counts,
    )


def second_kernel(
    code_ref, rows_ref, centered_ref, tokens_ref, total_ref, sent_ref, block_ref=None
):
    width = total_ref.shape[1]
    total = share(code_ref[...], rows_ref, centered_ref, rows_ref.shape[1] - width, width)
    total_ref[...] = total
    sent_ref[:, :width] = total.astype(jnp.bfloat16)
    pieces = ROWS // tokens_ref.shape[0]
    block = stacked(tokens_ref[...].astype(jnp.float32), pieces).astype(jnp.bfloat16)
    if block_ref is None:
        sent_ref[:, width:] = block
    else:
        block_ref[...] = block


def second(code, dict_rows, centered, tokens, merged):
    count, width = code.shape[0], dict_rows.shape[1]
    chunk = width - first_width(width)
    block = tokens.shape[0] * width // ROWS
    return kernel_call(
        second_kernel,
        (
            shape(count, chunk, dtype=jnp.float32),
            shape(count, chunk + (block if merged else 0)),
            *([] if merged else [shape(ROWS, block)]),
        ),
        [VMEM] * 4,
        (VMEM,) * (2 if merged else 3),
        count,
    )(code, dict_rows, centered, tokens)


def added_kernel(total_ref, own_ref, arrived_ref, after_ref, sum_ref, sent_ref):
    half = total_ref.shape[1]
    total = total_ref[...] + arrived_ref[:, :half].astype(jnp.float32)
    sum_ref[...] = total
    sent_ref[:, :half] = total.astype(jnp.bfloat16)
    if sent_ref.shape[1] > half:
        block = own_ref.shape[1] - half
        sent_ref[:, half : half + block] = own_ref[:, half:]
        sent_ref[:, half + block :] = arrived_ref[:, half:]


def added(total, own, arrived, after, merged):
    count, half = total.shape
    block = own.shape[1] - half
    return kernel_call(
        added_kernel,
        (
            shape(count, half, dtype=jnp.float32),
            shape(count, half + (2 * block if merged else 0)),
        ),
        [VMEM] * 3 + [ANY],
        (VMEM, VMEM),
        count,
    )(total, own, arrived, after)


def joined_kernel(skip, first_ref, second_ref, after_ref, out_ref):
    width = first_ref.shape[1] - skip
    out_ref[:, :width] = first_ref[:, skip:]
    out_ref[:, width:] = second_ref[:, skip:]


def joined(first, second, skip, after):
    return kernel_call(
        functools.partial(joined_kernel, skip),
        shape(first.shape[0], 2 * (first.shape[1] - skip)),
        [VMEM, VMEM, ANY],
        VMEM,
        first.shape[0],
    )(first, second, after)


def turned_kernel(rows, own_ref, arrived_ref, bias_ref, after_ref, out_ref):
    bias = jnp.concatenate([bias_ref[...]] * rows, axis=0)
    bias = stacked(bias, ROWS // rows)
    width = bias.shape[1]
    blocks = [
        (ref[:, at : at + width].astype(jnp.float32) - bias).astype(jnp.bfloat16)
        for ref in (own_ref, arrived_ref)
        for at in range(0, ref.shape[1], width)
    ]
    out_ref[...] = jnp.concatenate(blocks, axis=0).astype(jnp.float32).T.astype(jnp.bfloat16)


def turned(own, arrived, bias, after, rows, count):
    width = bias.shape[1] * rows // ROWS
    return kernel_call(
        functools.partial(turned_kernel, rows),
        shape(width, 2 * own.shape[1] // width * ROWS),
        [VMEM] * 3 + [ANY],
        VMEM,
        count,
    )(own, arrived, bias, after)


def scaled_of(total_ref, arrived_ref):
    total = total_ref[...] + arrived_ref[:, : total_ref.shape[1]].astype(jnp.float32)
    return (0.25 * total).astype(jnp.bfloat16)


def product(part, rows_ref, at):
    return lax.dot_general(
        part,
        rows_ref[:, at : at + part.shape[1]],
        (((1,), (1,)), ((), ())),
        preferred_element_type=jnp.float32,
    )


def first_product_kernel(total_ref, arrived_ref, rows_ref, scaled_ref, half_ref):
    scaled = scaled_of(total_ref, arrived_ref)
    scaled_ref[...] = scaled
    half_ref[...] = product(scaled, rows_ref, 0)


def second_product_kernel(
    total_ref, arrived_ref, rows_ref, first_ref, after_ref, scaled_ref, half_ref
):
    scaled = scaled_of(total_ref, arrived_ref)
    scaled_ref[...] = scaled
    half_ref[...] = first_ref[...] + product(scaled, rows_ref, rows_ref.shape[1] - scaled.shape[1])


def products(total, arrived, dict_rows, *first):
    count, width = total.shape
    return kernel_call(
        second_product_kernel if first else first_product_kernel,
        (shape(count, width), shape(count, dict_rows.shape[0], dtype=jnp.float32)),
        [VMEM] * 3 + ([VMEM, ANY] if first else []),
        (VMEM, VMEM),
        count,
    )(total, arrived, dict_rows, *first)


def grad_rows_kernel(at, code_ref, scaled_ref, other_ref, out_hbm, *refs):
    out_ref, sems = refs[-2:]
    slots, width = out_ref.shape
    code = code_ref[...].astype(jnp.float32).T.astype(jnp.bfloat16)
    step = width // sems.shape[0]
    copies = []
    for i in range(sems.shape[0]):
        part = pl.ds(i * step, step)
        out_ref[:, part] = jnp.dot(
            code, scaled_ref[:, part], preferred_element_type=jnp.float32
        ).astype(jnp.bfloat16)
        copies.append(
            pltpu.make_async_copy(
                out_ref.at[:, part], out_hbm.at[:, pl.ds(at + i * step, step)], sems.at[i]
            )
        )
        copies[-1].start()
    for copy in copies:
        copy.wait()


def first_rows_kernel(code_ref, scaled_ref, out_hbm, mark_ref, out_ref, sems):
    mark_ref[...] = jnp.zeros_like(mark_ref)
    grad_rows_kernel(0, code_ref, scaled_ref, None, out_hbm, out_ref, sems)


def grad_rows_part(code, scaled, width, written=None):
    count, slots = code.shape
    chunk = scaled.shape[1]
    limit = (16 if count <= ROWS else 40) * 2**20
    first = written is None
    mark = shape(1, slots, dtype=jnp.float32)
    return pl.pallas_call(
        first_rows_kernel if first else functools.partial(grad_rows_kernel, width - chunk),
        out_shape=(shape(slots, width), mark) if first else shape(slots, width),
        in_specs=[VMEM] * 2 + ([] if first else [HBM]),
        out_specs=(HBM, VMEM) if first else HBM,
        scratch_shapes=[
            pltpu.VMEM((slots, chunk), jnp.bfloat16),
            pltpu.SemaphoreType.DMA((2,)),
        ],
        input_output_aliases={} if first else {2: 0},
        compiler_params=pltpu.CompilerParams(vmem_limit_bytes=limit),
        cost_estimate=pl.CostEstimate(flops=10**6, bytes_accessed=2**20, transcendentals=0),
    )(code, scaled, *(() if first else (written,)))


def final_kernel(
    rows, raw_ref, mine_ref, theirs_ref, turned_ref, enc_hbm, benc_hbm, enc_ref, benc_ref, sems
):
    count, slots = raw_ref.shape
    width, depth = turned_ref.shape
    pieces = ROWS // rows
    code_grad = mine_ref[...] + theirs_ref[...]
    pre_grad = jnp.where(raw_ref[...] > 0.0, code_grad, 0.0).astype(jnp.bfloat16)
    benc_ref[...] = jnp.sum(pre_grad.astype(jnp.float32), axis=0, keepdims=True)
    copies = [pltpu.make_async_copy(benc_ref, benc_hbm, sems.at[pieces // 2])]
    copies[0].start()
    place = lax.broadcasted_iota(jnp.int32, (depth, count), 0)
    token = lax.broadcasted_iota(jnp.int32, (depth, count), 1)
    core = lax.axis_index("tok")
    block = place // ROWS
    distance = jnp.zeros_like(place)
    for step in range(feat_bits()):
        bit = sum(
            jnp.where(core == c, bit_of(step, c), 0) for c in range(lax.axis_size("tok"))
        )
        distance |= (block >> step & 1) << bit
    source = (lax.axis_index("feat") ^ distance) * rows + place % rows
    order = jnp.where(token == source, 1.0, 0.0).astype(jnp.bfloat16)
    spread = jnp.dot(order, pre_grad, preferred_element_type=jnp.float32)
    piece = lax.broadcasted_iota(jnp.int32, (depth, slots), 0) % ROWS // rows
    for c in range(0, pieces, 2):
        pair = [jnp.where(piece == c + i, spread, 0.0).astype(jnp.bfloat16) for i in range(2)]
        out = jnp.dot(
            turned_ref[...],
            jnp.concatenate(pair, axis=1),
            preferred_element_type=jnp.float32,
        ).astype(jnp.bfloat16)
        for i in range(2):
            enc_ref[(c + i) * width : (c + i + 1) * width, :] = out[:, i * slots : (i + 1) * slots]
        part = pl.ds(c * width, 2 * width)
        copies.append(pltpu.make_async_copy(enc_ref.at[part], enc_hbm.at[part], sems.at[c // 2]))
        copies[-1].start()
    for copy in copies:
        copy.wait()


def final(raw, mine, theirs, turned_tokens, rows):
    count, slots = raw.shape
    pieces = ROWS // rows
    width = turned_tokens.shape[0] * pieces
    return kernel_call(
        functools.partial(final_kernel, rows),
        (shape(width, slots), shape(1, slots, dtype=jnp.float32)),
        [VMEM] * 4,
        (HBM, HBM),
        count,
        [
            pltpu.VMEM((width, slots), jnp.bfloat16),
            pltpu.VMEM((1, slots), jnp.float32),
            pltpu.SemaphoreType.DMA((pieces // 2 + 1,)),
        ],
    )(raw, mine, theirs, turned_tokens)


def local(tokens, b_pre, pre_codes, top_idx, blocks, counts, dict_rows):
    rows, count = tokens.shape[0], top_idx.shape[0]
    steps = feat_bits()
    width = dict_rows.shape[1]
    merged = min(MERGED, steps - 1) if count == ROWS else 0

    code, raw, total, sent, dict_rows, centered, tokens, bias = front(
        tokens, b_pre, pre_codes, top_idx, blocks, counts, dict_rows
    )
    for step in range(steps):
        arrived = swapped(sent, step)
        if step == 0:
            total_second, sent_second, *block = second(
                code, dict_rows, centered, tokens, merged > 0
            )
        else:
            own, previous = sent_second, arrived_second
            total_second, sent_second = added(
                total_second, own, previous, sent, step < merged
            )
        arrived_second = swapped(sent_second, step)
        if step >= merged:
            if step == merged > 0:
                block = joined(own, previous, total_second.shape[1], sent_second)
            elif step == 0:
                (block,) = block
            else:
                block = joined(block, arrived_block, 0, sent_second)
            arrived_block = swapped(block, step)
        if step < steps - 1:
            total = total + arrived.astype(jnp.float32)
            sent = total.astype(jnp.bfloat16)
    scaled, product_first = products(total, arrived, dict_rows)
    grad_rows, mark = grad_rows_part(code, scaled, width)
    scaled, code_half = products(
        total_second, arrived_second, dict_rows, product_first, mark
    )
    theirs = lax.ppermute(code_half, "tok", [(i, 1 - i) for i in range(2)])
    grad_rows = grad_rows_part(code, scaled, width, grad_rows)
    turned_tokens = turned(block, arrived_block, bias, code_half, rows, count)
    grad_enc, grad_benc = final(raw, code_half, theirs, turned_tokens, rows)
    return (grad_rows, grad_enc, grad_benc.reshape(-1))


def solution(mesh):
    return jax.shard_map(
        local,
        mesh=mesh,
        in_specs=(
            P(("grp", "feat"), "tok"),
            P(("grp", "tok")),
            P("grp", None),
            P("grp", None),
            P(("grp", "feat")),
            P(("grp", "feat")),
            P(("grp", "feat"), "tok"),
        ),
        out_specs=(P(("grp", "feat"), "tok"), P(("grp", "tok"), "feat"), P(("grp", "feat"))),
        check_vma=False,
    )
```

```python
import functools

import jax
import jax.numpy as jnp
from jax import lax
from jax.experimental import pallas as pl
from jax.experimental.pallas import tpu as pltpu
from jax.sharding import PartitionSpec as P

VMEM = pl.BlockSpec(memory_space=pltpu.VMEM)
SMEM = pl.BlockSpec(memory_space=pltpu.SMEM)
HBM = pl.BlockSpec(memory_space=pltpu.HBM)
ANY = pl.BlockSpec(memory_space=pl.ANY)
MERGED = 2
ROWS = 16


def kernel_call(kernel, out_shape, in_specs, out_specs, tokens, scratch_shapes=()):
    limit = (16 if tokens <= ROWS else 40) * 2**20
    return pl.pallas_call(
        kernel,
        out_shape=out_shape,
        in_specs=in_specs,
        out_specs=out_specs,
        scratch_shapes=scratch_shapes,
        compiler_params=pltpu.CompilerParams(vmem_limit_bytes=limit),
        cost_estimate=pl.CostEstimate(flops=10**6, bytes_accessed=2**20, transcendentals=0),
    )


def shape(*sizes, dtype=jnp.bfloat16):
    return jax.ShapeDtypeStruct(sizes, dtype)


def first_width(width):
    return width // 2


def feat_bits():
    return (lax.axis_size("feat") - 1).bit_length()


def bit_of(step, core):
    last = feat_bits() - 1
    middle = list(range(1, last))
    return ([0, last] + middle if core == 0 else [last] + middle + [0])[step] if last else 0


def swapped(shard, step):
    cores = lax.axis_size("tok")
    pairs = [
        (f * cores + c, (f ^ 1 << bit_of(step, c)) * cores + c)
        for f in range(lax.axis_size("feat"))
        for c in range(cores)
    ]
    return lax.ppermute(shard, ("feat", "tok"), pairs)


def stacked(rows, pieces):
    width = rows.shape[1] // pieces
    return jnp.concatenate(
        [rows[:, c * width : (c + 1) * width] for c in range(pieces)], axis=0
    )


def share(code, rows_ref, centered_ref, at, width):
    part = pl.ds(at, width)
    total = jnp.dot(code, rows_ref[:, part], preferred_element_type=jnp.float32)
    rows = centered_ref.shape[0]
    centered = centered_ref[:, part]
    token = lax.broadcasted_iota(jnp.int32, (total.shape[0], 1), 0)
    first = lax.axis_index("feat") * rows
    for i in range(rows):
        total -= jnp.where(token == first + i, centered[i : i + 1, :], 0.0)
    return total


def front_kernel(
    tokens_hbm, bias_hbm, pre_hbm, top_hbm, rows_hbm, block_ref, count_ref, *refs
):
    code_ref, raw_ref, total_ref, sent_ref, rows_ref, centered_ref, bias_ref, *cut = refs[:-5]
    tokens_ref, bias_flat, pre_ref, top_ref, sems = refs[-5:]
    copies = [
        pltpu.make_async_copy(source, target, sems.at[i])
        for i, (source, target) in enumerate(
            (
                (top_hbm, top_ref),
                (pre_hbm, pre_ref),
                (tokens_hbm, tokens_ref),
                (bias_hbm, bias_flat),
                (rows_hbm, rows_ref),
            )
        )
    ]
    for copy in copies:
        copy.start()
    for copy in copies[:2]:
        copy.wait()
    count, latents = top_ref.shape
    slots, width = rows_ref.shape
    offsets = lax.broadcasted_iota(jnp.int32, (1, slots), 1)
    slot_ids = jnp.where(offsets < count_ref[0], block_ref[0] * slots + offsets, -1)
    top, pre = top_ref[...], pre_ref[...]
    raw = jnp.zeros((count, slots), jnp.float32)
    for k in range(latents):
        raw = jnp.where(top[:, k : k + 1] == slot_ids, pre[:, k : k + 1], raw)
    raw_ref[...] = raw
    code = jnp.maximum(raw, 0.0).astype(jnp.bfloat16)
    code_ref[...] = code

    for copy in copies[2:4]:
        copy.wait()
    tokens = tokens_ref[...].astype(jnp.float32)
    bias = bias_flat[...].astype(jnp.float32).reshape(1, width)
    bias_ref[...] = bias
    centered_ref[...] = (tokens - bias).astype(jnp.bfloat16).astype(jnp.float32)

    copies[4].wait()
    total = share(code, rows_ref, centered_ref, 0, total_ref.shape[1])
    total_ref[...] = total
    width = total.shape[1]
    sent_ref[:, :width] = total.astype(jnp.bfloat16)
    block = stacked(tokens, ROWS // tokens.shape[0]).astype(jnp.bfloat16)
    if cut:
        cut[0][...] = block
    else:
        sent_ref[:, width:] = block


def front(tokens, b_pre, pre_codes, top_idx, blocks, counts, dict_rows, merged):
    count = top_idx.shape[0]
    slots, width = dict_rows.shape
    chunk, block = first_width(width), tokens.shape[0] * width // ROWS
    return kernel_call(
        front_kernel,
        (
            shape(count, slots),
            shape(count, slots, dtype=jnp.float32),
            shape(count, chunk, dtype=jnp.float32),
            shape(count, chunk + (block if merged else 0)),
            shape(slots, width),
            shape(*tokens.shape, dtype=jnp.float32),
            shape(1, width, dtype=jnp.float32),
            *([] if merged else [shape(ROWS, block)]),
        ),
        [HBM] * 5 + [SMEM] * 2,
        (VMEM,) * (7 if merged else 8),
        count,
        [
            pltpu.VMEM(tokens.shape, tokens.dtype),
            pltpu.VMEM(b_pre.shape, b_pre.dtype),
            pltpu.VMEM(pre_codes.shape, pre_codes.dtype),
            pltpu.VMEM(top_idx.shape, top_idx.dtype),
            pltpu.SemaphoreType.DMA((5,)),
        ],
    )(
        *(
            pltpu.with_memory_space_constraint(array, pltpu.HBM)
            for array in (tokens, b_pre, pre_codes, top_idx, dict_rows)
        ),
        blocks,
        counts,
    )


def second_kernel(code_ref, rows_ref, centered_ref, total_ref, sent_ref):
    width = total_ref.shape[1]
    total = share(code_ref[...], rows_ref, centered_ref, rows_ref.shape[1] - width, width)
    total_ref[...] = total
    sent_ref[...] = total.astype(jnp.bfloat16)


def second(code, dict_rows, centered):
    count, width = code.shape[0], dict_rows.shape[1]
    chunk = width - first_width(width)
    return kernel_call(
        second_kernel,
        (shape(count, chunk, dtype=jnp.float32), shape(count, chunk)),
        [VMEM] * 3,
        (VMEM, VMEM),
        count,
    )(code, dict_rows, centered)


def added_kernel(total_ref, own_ref, arrived_ref, after_ref, sum_ref, sent_ref):
    half = total_ref.shape[1]
    total = total_ref[...] + arrived_ref[:, :half].astype(jnp.float32)
    sum_ref[...] = total
    sent_ref[:, :half] = total.astype(jnp.bfloat16)
    if sent_ref.shape[1] > half:
        block = own_ref.shape[1] - half
        sent_ref[:, half : half + block] = own_ref[:, half:]
        sent_ref[:, half + block :] = arrived_ref[:, half:]


def added(total, own, arrived, after, merged):
    count, half = total.shape
    block = own.shape[1] - half
    return kernel_call(
        added_kernel,
        (
            shape(count, half, dtype=jnp.float32),
            shape(count, half + (2 * block if merged else 0)),
        ),
        [VMEM] * 3 + [ANY],
        (VMEM, VMEM),
        count,
    )(total, own, arrived, after)


def joined_kernel(skip, first_ref, second_ref, after_ref, out_ref):
    width = first_ref.shape[1] - skip
    out_ref[:, :width] = first_ref[:, skip:]
    out_ref[:, width:] = second_ref[:, skip:]


def joined(first, second, skip, after):
    return kernel_call(
        functools.partial(joined_kernel, skip),
        shape(first.shape[0], 2 * (first.shape[1] - skip)),
        [VMEM, VMEM, ANY],
        VMEM,
        first.shape[0],
    )(first, second, after)


def turned_kernel(rows, own_ref, arrived_ref, bias_ref, after_ref, out_ref):
    bias = jnp.concatenate([bias_ref[...]] * rows, axis=0)
    bias = stacked(bias, ROWS // rows)
    width = bias.shape[1]
    blocks = [
        (ref[:, at : at + width].astype(jnp.float32) - bias).astype(jnp.bfloat16)
        for ref in (own_ref, arrived_ref)
        for at in range(0, ref.shape[1], width)
    ]
    out_ref[...] = jnp.concatenate(blocks, axis=0).astype(jnp.float32).T.astype(jnp.bfloat16)


def turned(own, arrived, bias, after, rows, count):
    width = bias.shape[1] * rows // ROWS
    return kernel_call(
        functools.partial(turned_kernel, rows),
        shape(width, 2 * own.shape[1] // width * ROWS),
        [VMEM] * 3 + [ANY],
        VMEM,
        count,
    )(own, arrived, bias, after)


def scaled_of(total_ref, arrived_ref):
    total = total_ref[...] + arrived_ref[:, : total_ref.shape[1]].astype(jnp.float32)
    return (0.25 * total).astype(jnp.bfloat16)


def product(part, rows_ref, at):
    return lax.dot_general(
        part,
        rows_ref[:, at : at + part.shape[1]],
        (((1,), (1,)), ((), ())),
        preferred_element_type=jnp.float32,
    )


def first_product_kernel(total_ref, arrived_ref, rows_ref, scaled_ref, half_ref):
    scaled = scaled_of(total_ref, arrived_ref)
    scaled_ref[...] = scaled
    half_ref[...] = product(scaled, rows_ref, 0)


def second_product_kernel(
    total_ref, arrived_ref, rows_ref, first_ref, after_ref, scaled_ref, half_ref
):
    scaled = scaled_of(total_ref, arrived_ref)
    scaled_ref[...] = scaled
    half_ref[...] = first_ref[...] + product(scaled, rows_ref, rows_ref.shape[1] - scaled.shape[1])


def products(total, arrived, dict_rows, *first):
    count, width = total.shape
    return kernel_call(
        second_product_kernel if first else first_product_kernel,
        (shape(count, width), shape(count, dict_rows.shape[0], dtype=jnp.float32)),
        [VMEM] * 3 + ([VMEM, ANY] if first else []),
        (VMEM, VMEM),
        count,
    )(total, arrived, dict_rows, *first)


def grad_rows_kernel(at, code_ref, scaled_ref, other_ref, out_hbm, *refs):
    out_ref, sems = refs[-2:]
    slots, width = out_ref.shape
    code = code_ref[...].astype(jnp.float32).T.astype(jnp.bfloat16)
    step = width // sems.shape[0]
    copies = []
    for i in range(sems.shape[0]):
        part = pl.ds(i * step, step)
        out_ref[:, part] = jnp.dot(
            code, scaled_ref[:, part], preferred_element_type=jnp.float32
        ).astype(jnp.bfloat16)
        copies.append(
            pltpu.make_async_copy(
                out_ref.at[:, part], out_hbm.at[:, pl.ds(at + i * step, step)], sems.at[i]
            )
        )
        copies[-1].start()
    for copy in copies:
        copy.wait()


def first_rows_kernel(code_ref, scaled_ref, out_hbm, mark_ref, out_ref, sems):
    mark_ref[...] = jnp.zeros_like(mark_ref)
    grad_rows_kernel(0, code_ref, scaled_ref, None, out_hbm, out_ref, sems)


def grad_rows_part(code, scaled, width, written=None):
    count, slots = code.shape
    chunk = scaled.shape[1]
    limit = (16 if count <= ROWS else 40) * 2**20
    first = written is None
    mark = shape(1, slots, dtype=jnp.float32)
    return pl.pallas_call(
        first_rows_kernel if first else functools.partial(grad_rows_kernel, width - chunk),
        out_shape=(shape(slots, width), mark) if first else shape(slots, width),
        in_specs=[VMEM] * 2 + ([] if first else [HBM]),
        out_specs=(HBM, VMEM) if first else HBM,
        scratch_shapes=[
            pltpu.VMEM((slots, chunk), jnp.bfloat16),
            pltpu.SemaphoreType.DMA((2,)),
        ],
        input_output_aliases={} if first else {2: 0},
        compiler_params=pltpu.CompilerParams(vmem_limit_bytes=limit),
        cost_estimate=pl.CostEstimate(flops=10**6, bytes_accessed=2**20, transcendentals=0),
    )(code, scaled, *(() if first else (written,)))


def final_kernel(
    rows, raw_ref, mine_ref, theirs_ref, turned_ref, enc_hbm, benc_hbm, enc_ref, benc_ref, sems
):
    count, slots = raw_ref.shape
    width, depth = turned_ref.shape
    pieces = ROWS // rows
    code_grad = mine_ref[...] + theirs_ref[...]
    pre_grad = jnp.where(raw_ref[...] > 0.0, code_grad, 0.0).astype(jnp.bfloat16)
    benc_ref[...] = jnp.sum(pre_grad.astype(jnp.float32), axis=0, keepdims=True)
    copies = [pltpu.make_async_copy(benc_ref, benc_hbm, sems.at[pieces // 2])]
    copies[0].start()
    place = lax.broadcasted_iota(jnp.int32, (depth, count), 0)
    token = lax.broadcasted_iota(jnp.int32, (depth, count), 1)
    core = lax.axis_index("tok")
    block = place // ROWS
    distance = jnp.zeros_like(place)
    for step in range(feat_bits()):
        bit = sum(
            jnp.where(core == c, bit_of(step, c), 0) for c in range(lax.axis_size("tok"))
        )
        distance |= (block >> step & 1) << bit
    source = (lax.axis_index("feat") ^ distance) * rows + place % rows
    order = jnp.where(token == source, 1.0, 0.0).astype(jnp.bfloat16)
    spread = jnp.dot(order, pre_grad, preferred_element_type=jnp.float32)
    piece = lax.broadcasted_iota(jnp.int32, (depth, slots), 0) % ROWS // rows
    for c in range(0, pieces, 2):
        pair = [jnp.where(piece == c + i, spread, 0.0).astype(jnp.bfloat16) for i in range(2)]
        out = jnp.dot(
            turned_ref[...],
            jnp.concatenate(pair, axis=1),
            preferred_element_type=jnp.float32,
        ).astype(jnp.bfloat16)
        for i in range(2):
            enc_ref[(c + i) * width : (c + i + 1) * width, :] = out[:, i * slots : (i + 1) * slots]
        part = pl.ds(c * width, 2 * width)
        copies.append(pltpu.make_async_copy(enc_ref.at[part], enc_hbm.at[part], sems.at[c // 2]))
        copies[-1].start()
    for copy in copies:
        copy.wait()


def final(raw, mine, theirs, turned_tokens, rows):
    count, slots = raw.shape
    pieces = ROWS // rows
    width = turned_tokens.shape[0] * pieces
    return kernel_call(
        functools.partial(final_kernel, rows),
        (shape(width, slots), shape(1, slots, dtype=jnp.float32)),
        [VMEM] * 4,
        (HBM, HBM),
        count,
        [
            pltpu.VMEM((width, slots), jnp.bfloat16),
            pltpu.VMEM((1, slots), jnp.float32),
            pltpu.SemaphoreType.DMA((pieces // 2 + 1,)),
        ],
    )(raw, mine, theirs, turned_tokens)


def local(tokens, b_pre, pre_codes, top_idx, blocks, counts, dict_rows):
    rows, count = tokens.shape[0], top_idx.shape[0]
    steps = feat_bits()
    width = dict_rows.shape[1]
    merged = min(MERGED, steps - 1) if count == ROWS else 0

    code, raw, total, sent, dict_rows, centered, bias, *block = front(
        tokens, b_pre, pre_codes, top_idx, blocks, counts, dict_rows, merged > 0
    )
    for step in range(steps):
        arrived = swapped(sent, step)
        if step == 0:
            total_second, sent_second = second(code, dict_rows, centered)
        else:
            total_second, sent_second = added(
                total_second, sent_second, arrived_second, sent, False
            )
        arrived_second = swapped(sent_second, step)
        if step >= merged:
            if step == merged > 0:
                block = joined(own, previous, total.shape[1], sent_second)
            elif step == 0:
                (block,) = block
            else:
                block = joined(block, arrived_block, 0, sent_second)
            arrived_block = swapped(block, step)
        if step < steps - 1:
            own, previous = sent, arrived
            total, sent = added(total, own, previous, sent_second, step + 1 < merged)
    scaled, product_first = products(total, arrived, dict_rows)
    grad_rows, mark = grad_rows_part(code, scaled, width)
    scaled, code_half = products(
        total_second, arrived_second, dict_rows, product_first, mark
    )
    theirs = lax.ppermute(code_half, "tok", [(i, 1 - i) for i in range(2)])
    grad_rows = grad_rows_part(code, scaled, width, grad_rows)
    turned_tokens = turned(block, arrived_block, bias, code_half, rows, count)
    grad_enc, grad_benc = final(raw, code_half, theirs, turned_tokens, rows)
    return (grad_rows, grad_enc, grad_benc.reshape(-1))


def solution(mesh):
    return jax.shard_map(
        local,
        mesh=mesh,
        in_specs=(
            P(("grp", "feat"), "tok"),
            P(("grp", "tok")),
            P("grp", None),
            P("grp", None),
            P(("grp", "feat")),
            P(("grp", "feat")),
            P(("grp", "feat"), "tok"),
        ),
        out_specs=(P(("grp", "feat"), "tok"), P(("grp", "tok"), "feat"), P(("grp", "feat"))),
        check_vma=False,
    )
```

```python
import functools

import jax
import jax.numpy as jnp
from jax import lax
from jax.experimental import pallas as pl
from jax.experimental.pallas import tpu as pltpu
from jax.sharding import PartitionSpec as P

VMEM = pl.BlockSpec(memory_space=pltpu.VMEM)
SMEM = pl.BlockSpec(memory_space=pltpu.SMEM)
HBM = pl.BlockSpec(memory_space=pltpu.HBM)
ANY = pl.BlockSpec(memory_space=pl.ANY)
MERGED = 2
ROWS = 16


def kernel_call(kernel, out_shape, in_specs, out_specs, tokens, scratch_shapes=(), aliases={}):
    limit = (16 if tokens <= ROWS else 40) * 2**20
    return pl.pallas_call(
        kernel,
        out_shape=out_shape,
        in_specs=in_specs,
        out_specs=out_specs,
        scratch_shapes=scratch_shapes,
        input_output_aliases=aliases,
        compiler_params=pltpu.CompilerParams(vmem_limit_bytes=limit),
        cost_estimate=pl.CostEstimate(flops=10**6, bytes_accessed=2**20, transcendentals=0),
    )


def shape(*sizes, dtype=jnp.bfloat16):
    return jax.ShapeDtypeStruct(sizes, dtype)


def first_width(width):
    return width // 2


def feat_bits():
    return (lax.axis_size("feat") - 1).bit_length()


def bit_of(step, core):
    bits = list(range(feat_bits()))
    return (bits[-1:] + bits[:-1] if core == 0 else bits)[step]


def swapped(shard, step):
    cores = lax.axis_size("tok")
    pairs = [
        (f * cores + c, (f ^ 1 << bit_of(step, c)) * cores + c)
        for f in range(lax.axis_size("feat"))
        for c in range(cores)
    ]
    return lax.ppermute(shard, ("feat", "tok"), pairs)


def stacked(rows, pieces):
    width = rows.shape[1] // pieces
    return jnp.concatenate(
        [rows[:, c * width : (c + 1) * width] for c in range(pieces)], axis=0
    )


def share(code, rows_ref, centered_ref, at, width):
    part = pl.ds(at, width)
    total = jnp.dot(code, rows_ref[:, part], preferred_element_type=jnp.float32)
    rows = centered_ref.shape[0]
    centered = centered_ref[:, part]
    token = lax.broadcasted_iota(jnp.int32, (total.shape[0], 1), 0)
    first = lax.axis_index("feat") * rows
    for i in range(rows):
        total -= jnp.where(token == first + i, centered[i : i + 1, :], 0.0)
    return total


def front_kernel(
    tokens_hbm, bias_hbm, pre_hbm, top_hbm, rows_hbm, block_ref, count_ref, *refs
):
    code_ref, raw_ref, total_ref, sent_ref, rows_ref, centered_ref, bias_ref, *cut = refs[:-5]
    tokens_ref, bias_flat, pre_ref, top_ref, sems = refs[-5:]
    copies = [
        pltpu.make_async_copy(source, target, sems.at[i])
        for i, (source, target) in enumerate(
            (
                (top_hbm, top_ref),
                (pre_hbm, pre_ref),
                (tokens_hbm, tokens_ref),
                (bias_hbm, bias_flat),
                (rows_hbm, rows_ref),
            )
        )
    ]
    for copy in copies:
        copy.start()
    for copy in copies[:2]:
        copy.wait()
    count, latents = top_ref.shape
    slots, width = rows_ref.shape
    offsets = lax.broadcasted_iota(jnp.int32, (1, slots), 1)
    slot_ids = jnp.where(offsets < count_ref[0], block_ref[0] * slots + offsets, -1)
    top, pre = top_ref[...], pre_ref[...]
    raw = jnp.zeros((count, slots), jnp.float32)
    for k in range(latents):
        raw = jnp.where(top[:, k : k + 1] == slot_ids, pre[:, k : k + 1], raw)
    raw_ref[...] = raw
    code = jnp.maximum(raw, 0.0).astype(jnp.bfloat16)
    code_ref[...] = code

    for copy in copies[2:4]:
        copy.wait()
    tokens = tokens_ref[...].astype(jnp.float32)
    bias = bias_flat[...].astype(jnp.float32).reshape(1, width)
    bias_ref[...] = bias
    centered_ref[...] = (tokens - bias).astype(jnp.bfloat16).astype(jnp.float32)

    copies[4].wait()
    total = share(code, rows_ref, centered_ref, 0, total_ref.shape[1])
    total_ref[...] = total
    width = total.shape[1]
    sent_ref[:, :width] = total.astype(jnp.bfloat16)
    block = stacked(tokens, ROWS // tokens.shape[0]).astype(jnp.bfloat16)
    if cut:
        cut[0][...] = block
    else:
        sent_ref[:, width:] = block


def front(tokens, b_pre, pre_codes, top_idx, blocks, counts, dict_rows, merged):
    count = top_idx.shape[0]
    slots, width = dict_rows.shape
    chunk, block = first_width(width), tokens.shape[0] * width // ROWS
    return kernel_call(
        front_kernel,
        (
            shape(count, slots),
            shape(count, slots, dtype=jnp.float32),
            shape(count, chunk, dtype=jnp.float32),
            shape(count, chunk + (block if merged else 0)),
            shape(slots, width),
            shape(*tokens.shape, dtype=jnp.float32),
            shape(1, width, dtype=jnp.float32),
            *([] if merged else [shape(ROWS, block)]),
        ),
        [HBM] * 5 + [SMEM] * 2,
        (VMEM,) * (7 if merged else 8),
        count,
        [
            pltpu.VMEM(tokens.shape, tokens.dtype),
            pltpu.VMEM(b_pre.shape, b_pre.dtype),
            pltpu.VMEM(pre_codes.shape, pre_codes.dtype),
            pltpu.VMEM(top_idx.shape, top_idx.dtype),
            pltpu.SemaphoreType.DMA((5,)),
        ],
    )(
        *(
            pltpu.with_memory_space_constraint(array, pltpu.HBM)
            for array in (tokens, b_pre, pre_codes, top_idx, dict_rows)
        ),
        blocks,
        counts,
    )


def second_kernel(code_ref, rows_ref, centered_ref, total_ref, sent_ref):
    width = total_ref.shape[1]
    total = share(code_ref[...], rows_ref, centered_ref, rows_ref.shape[1] - width, width)
    total_ref[...] = total
    sent_ref[...] = total.astype(jnp.bfloat16)


def second(code, dict_rows, centered):
    count, width = code.shape[0], dict_rows.shape[1]
    chunk = width - first_width(width)
    return kernel_call(
        second_kernel,
        (shape(count, chunk, dtype=jnp.float32), shape(count, chunk)),
        [VMEM] * 3,
        (VMEM, VMEM),
        count,
    )(code, dict_rows, centered)


def added_kernel(total_ref, own_ref, arrived_ref, after_ref, sum_ref, sent_ref):
    half = total_ref.shape[1]
    total = total_ref[...] + arrived_ref[:, :half].astype(jnp.float32)
    sum_ref[...] = total
    sent_ref[:, :half] = total.astype(jnp.bfloat16)
    if sent_ref.shape[1] > half:
        block = own_ref.shape[1] - half
        sent_ref[:, half : half + block] = own_ref[:, half:]
        sent_ref[:, half + block :] = arrived_ref[:, half:]


def added(total, own, arrived, after, merged):
    count, half = total.shape
    block = own.shape[1] - half
    return kernel_call(
        added_kernel,
        (
            shape(count, half, dtype=jnp.float32),
            shape(count, half + (2 * block if merged else 0)),
        ),
        [VMEM] * 3 + [ANY],
        (VMEM, VMEM),
        count,
    )(total, own, arrived, after)


def joined_kernel(skip, first_ref, second_ref, after_ref, out_ref):
    width = first_ref.shape[1] - skip
    out_ref[:, :width] = first_ref[:, skip:]
    out_ref[:, width:] = second_ref[:, skip:]


def joined(first, second, skip, after):
    return kernel_call(
        functools.partial(joined_kernel, skip),
        shape(first.shape[0], 2 * (first.shape[1] - skip)),
        [VMEM, VMEM, ANY],
        VMEM,
        first.shape[0],
    )(first, second, after)


def turned_kernel(rows, own_ref, arrived_ref, bias_ref, after_ref, out_ref):
    bias = jnp.concatenate([bias_ref[...]] * rows, axis=0)
    bias = stacked(bias, ROWS // rows)
    width = bias.shape[1]
    blocks = [
        (ref[:, at : at + width].astype(jnp.float32) - bias).astype(jnp.bfloat16)
        for ref in (own_ref, arrived_ref)
        for at in range(0, ref.shape[1], width)
    ]
    out_ref[...] = jnp.concatenate(blocks, axis=0).astype(jnp.float32).T.astype(jnp.bfloat16)


def turned(own, arrived, bias, after, rows, count):
    width = bias.shape[1] * rows // ROWS
    return kernel_call(
        functools.partial(turned_kernel, rows),
        shape(width, 2 * own.shape[1] // width * ROWS),
        [VMEM] * 3 + [ANY],
        VMEM,
        count,
    )(own, arrived, bias, after)


def scaled_of(total_ref, arrived_ref):
    total = total_ref[...] + arrived_ref[:, : total_ref.shape[1]].astype(jnp.float32)
    return (0.25 * total).astype(jnp.bfloat16)


def product(part, rows_ref, at):
    return lax.dot_general(
        part,
        rows_ref[:, at : at + part.shape[1]],
        (((1,), (1,)), ((), ())),
        preferred_element_type=jnp.float32,
    )


def first_product_kernel(total_ref, arrived_ref, rows_ref, scaled_ref, half_ref):
    scaled = scaled_of(total_ref, arrived_ref)
    scaled_ref[...] = scaled
    half_ref[...] = product(scaled, rows_ref, 0)


def second_product_kernel(
    total_ref, arrived_ref, rows_ref, first_ref, after_ref, scaled_ref, half_ref
):
    scaled = scaled_of(total_ref, arrived_ref)
    scaled_ref[...] = scaled
    half_ref[...] = first_ref[...] + product(scaled, rows_ref, rows_ref.shape[1] - scaled.shape[1])


def products(total, arrived, dict_rows, *first):
    count, width = total.shape
    return kernel_call(
        second_product_kernel if first else first_product_kernel,
        (shape(count, width), shape(count, dict_rows.shape[0], dtype=jnp.float32)),
        [VMEM] * 3 + ([VMEM, ANY] if first else []),
        (VMEM, VMEM),
        count,
    )(total, arrived, dict_rows, *first)


def outer(code_ref, scaled):
    code = code_ref[...].astype(jnp.float32).T.astype(jnp.bfloat16)
    return jnp.dot(code, scaled, preferred_element_type=jnp.float32).astype(jnp.bfloat16)


def first_rows_kernel(code_ref, scaled_ref, out_hbm, mark_ref, out_ref, sems):
    mark_ref[...] = jnp.zeros_like(mark_ref)
    step = out_ref.shape[1] // sems.shape[0]
    copies = []
    for i in range(sems.shape[0]):
        part = pl.ds(i * step, step)
        out_ref[:, part] = outer(code_ref, scaled_ref[:, part])
        copies.append(
            pltpu.make_async_copy(out_ref.at[:, part], out_hbm.at[:, part], sems.at[i])
        )
        copies[-1].start()
    for copy in copies:
        copy.wait()


def first_rows(code, scaled, width):
    count, slots = code.shape
    chunk = scaled.shape[1]
    return kernel_call(
        first_rows_kernel,
        (shape(slots, width), shape(1, slots, dtype=jnp.float32)),
        [VMEM] * 2,
        (HBM, VMEM),
        count,
        [pltpu.VMEM((slots, chunk), jnp.bfloat16), pltpu.SemaphoreType.DMA((2,))],
    )(code, scaled)


def second_rows_kernel(code_ref, scaled_ref, out_ref):
    out_ref[...] = outer(code_ref, scaled_ref[...])


def second_rows(code, scaled):
    count, slots = code.shape
    return kernel_call(
        second_rows_kernel, shape(slots, scaled.shape[1]), [VMEM] * 2, VMEM, count
    )(code, scaled)


def final_kernel(
    rows,
    raw_ref,
    mine_ref,
    theirs_ref,
    turned_ref,
    last_rows_ref,
    written_hbm,
    rows_hbm,
    enc_hbm,
    benc_hbm,
    enc_ref,
    benc_ref,
    sems,
):
    chunk = last_rows_ref.shape[1]
    last = rows_hbm.shape[1] - chunk
    copies = [
        pltpu.make_async_copy(last_rows_ref, rows_hbm.at[:, pl.ds(last, chunk)], sems.at[0])
    ]
    copies[0].start()
    count, slots = raw_ref.shape
    width, depth = turned_ref.shape
    pieces = ROWS // rows
    code_grad = mine_ref[...] + theirs_ref[...]
    pre_grad = jnp.where(raw_ref[...] > 0.0, code_grad, 0.0).astype(jnp.bfloat16)
    benc_ref[...] = jnp.sum(pre_grad.astype(jnp.float32), axis=0, keepdims=True)
    copies.append(pltpu.make_async_copy(benc_ref, benc_hbm, sems.at[1]))
    copies[1].start()
    place = lax.broadcasted_iota(jnp.int32, (depth, count), 0)
    token = lax.broadcasted_iota(jnp.int32, (depth, count), 1)
    core = lax.axis_index("tok")
    block = place // ROWS
    distance = jnp.zeros_like(place)
    for step in range(feat_bits()):
        bit = sum(
            jnp.where(core == c, bit_of(step, c), 0) for c in range(lax.axis_size("tok"))
        )
        distance |= (block >> step & 1) << bit
    source = (lax.axis_index("feat") ^ distance) * rows + place % rows
    order = jnp.where(token == source, 1.0, 0.0).astype(jnp.bfloat16)
    spread = jnp.dot(order, pre_grad, preferred_element_type=jnp.float32)
    piece = lax.broadcasted_iota(jnp.int32, (depth, slots), 0) % ROWS // rows
    for c in range(0, pieces, 2):
        pair = [jnp.where(piece == c + i, spread, 0.0).astype(jnp.bfloat16) for i in range(2)]
        out = jnp.dot(
            turned_ref[...],
            jnp.concatenate(pair, axis=1),
            preferred_element_type=jnp.float32,
        ).astype(jnp.bfloat16)
        for i in range(2):
            enc_ref[(c + i) * width : (c + i + 1) * width, :] = out[:, i * slots : (i + 1) * slots]
        part = pl.ds(c * width, 2 * width)
        copies.append(pltpu.make_async_copy(enc_ref.at[part], enc_hbm.at[part], sems.at[c // 2 + 2]))
        copies[-1].start()
    for copy in copies:
        copy.wait()


def final(raw, mine, theirs, turned_tokens, last_rows, written, rows):
    count, slots = raw.shape
    pieces = ROWS // rows
    width = turned_tokens.shape[0] * pieces
    return kernel_call(
        functools.partial(final_kernel, rows),
        (shape(slots, width), shape(width, slots), shape(1, slots, dtype=jnp.float32)),
        [VMEM] * 5 + [HBM],
        (HBM, HBM, HBM),
        count,
        [
            pltpu.VMEM((width, slots), jnp.bfloat16),
            pltpu.VMEM((1, slots), jnp.float32),
            pltpu.SemaphoreType.DMA((pieces // 2 + 2,)),
        ],
        {5: 0},
    )(raw, mine, theirs, turned_tokens, last_rows, written)


def local(tokens, b_pre, pre_codes, top_idx, blocks, counts, dict_rows):
    rows, count = tokens.shape[0], top_idx.shape[0]
    steps = feat_bits()
    width = dict_rows.shape[1]
    merged = min(MERGED, steps - 1) if count == ROWS else 0

    code, raw, total, sent, dict_rows, centered, bias, *block = front(
        tokens, b_pre, pre_codes, top_idx, blocks, counts, dict_rows, merged > 0
    )
    for step in range(steps):
        arrived = swapped(sent, step)
        if step == 0:
            total_second, sent_second = second(code, dict_rows, centered)
        else:
            total_second, sent_second = added(
                total_second, sent_second, arrived_second, sent, False
            )
        arrived_second = swapped(sent_second, step)
        if step >= merged:
            if step == merged > 0:
                block = joined(own, previous, total.shape[1], sent_second)
            elif step == 0:
                (block,) = block
            else:
                block = joined(block, arrived_block, 0, sent_second)
            arrived_block = swapped(block, step)
        if step < steps - 1:
            own, previous = sent, arrived
            total, sent = added(total, own, previous, sent_second, step + 1 < merged)
    scaled, product_first = products(total, arrived, dict_rows)
    written, mark = first_rows(code, scaled, width)
    scaled, code_half = products(
        total_second, arrived_second, dict_rows, product_first, mark
    )
    theirs = lax.ppermute(code_half, "tok", [(i, 1 - i) for i in range(2)])
    last_rows = second_rows(code, scaled)
    turned_tokens = turned(block, arrived_block, bias, code_half, rows, count)
    grad_rows, grad_enc, grad_benc = final(
        raw, code_half, theirs, turned_tokens, last_rows, written, rows
    )
    return (grad_rows, grad_enc, grad_benc.reshape(-1))


def solution(mesh):
    return jax.shard_map(
        local,
        mesh=mesh,
        in_specs=(
            P(("grp", "feat"), "tok"),
            P(("grp", "tok")),
            P("grp", None),
            P("grp", None),
            P(("grp", "feat")),
            P(("grp", "feat")),
            P(("grp", "feat"), "tok"),
        ),
        out_specs=(P(("grp", "feat"), "tok"), P(("grp", "tok"), "feat"), P(("grp", "feat"))),
        check_vma=False,
    )
```

```python
import functools

import jax
import jax.numpy as jnp
from jax import lax
from jax.experimental import pallas as pl
from jax.experimental.pallas import tpu as pltpu
from jax.sharding import PartitionSpec as P

VMEM = pl.BlockSpec(memory_space=pltpu.VMEM)
SMEM = pl.BlockSpec(memory_space=pltpu.SMEM)
HBM = pl.BlockSpec(memory_space=pltpu.HBM)
ANY = pl.BlockSpec(memory_space=pl.ANY)
EARLY = 10**9
ROWS = 16


def kernel_call(kernel, out_shape, in_specs, out_specs, tokens, scratch_shapes=(), flops=10**6):
    limit = (16 if tokens <= ROWS else 40) * 2**20
    return pl.pallas_call(
        kernel,
        out_shape=out_shape,
        in_specs=in_specs,
        out_specs=out_specs,
        scratch_shapes=scratch_shapes,
        compiler_params=pltpu.CompilerParams(vmem_limit_bytes=limit),
        cost_estimate=pl.CostEstimate(flops=flops, bytes_accessed=2**20, transcendentals=0),
    )


def shape(*sizes, dtype=jnp.bfloat16):
    return jax.ShapeDtypeStruct(sizes, dtype)


def first_width(width):
    return width // 2


def feat_bits():
    return (lax.axis_size("feat") - 1).bit_length()


def bit_of(step, core):
    bits = list(range(feat_bits()))
    return (bits[-1:] + bits[:-1] if core == 0 else bits)[step]


def swapped(shard, step):
    cores = lax.axis_size("tok")
    pairs = [
        (f * cores + c, (f ^ 1 << bit_of(step, c)) * cores + c)
        for f in range(lax.axis_size("feat"))
        for c in range(cores)
    ]
    return lax.ppermute(shard, ("feat", "tok"), pairs)


def stacked(rows, pieces):
    width = rows.shape[1] // pieces
    return jnp.concatenate(
        [rows[:, c * width : (c + 1) * width] for c in range(pieces)], axis=0
    )


def share(code, rows_ref, centered_ref, at, width):
    part = pl.ds(at, width)
    total = jnp.dot(code, rows_ref[:, part], preferred_element_type=jnp.float32)
    rows = centered_ref.shape[0]
    centered = centered_ref[:, part]
    token = lax.broadcasted_iota(jnp.int32, (total.shape[0], 1), 0)
    first = lax.axis_index("feat") * rows
    for i in range(rows):
        total -= jnp.where(token == first + i, centered[i : i + 1, :], 0.0)
    return total


def front_kernel(
    tokens_hbm, bias_hbm, pre_hbm, top_hbm, rows_hbm, block_ref, count_ref, *refs
):
    code_ref, raw_ref, total_ref, sent_ref, rows_ref, centered_ref, bias_ref, *cut = refs[:-5]
    tokens_ref, bias_flat, pre_ref, top_ref, sems = refs[-5:]
    copies = [
        pltpu.make_async_copy(source, target, sems.at[i])
        for i, (source, target) in enumerate(
            (
                (top_hbm, top_ref),
                (pre_hbm, pre_ref),
                (tokens_hbm, tokens_ref),
                (bias_hbm, bias_flat),
                (rows_hbm, rows_ref),
            )
        )
    ]
    for copy in copies:
        copy.start()
    for copy in copies[:2]:
        copy.wait()
    count, latents = top_ref.shape
    slots, width = rows_ref.shape
    offsets = lax.broadcasted_iota(jnp.int32, (1, slots), 1)
    slot_ids = jnp.where(offsets < count_ref[0], block_ref[0] * slots + offsets, -1)
    top, pre = top_ref[...], pre_ref[...]
    raw = jnp.zeros((count, slots), jnp.float32)
    for k in range(latents):
        raw = jnp.where(top[:, k : k + 1] == slot_ids, pre[:, k : k + 1], raw)
    raw_ref[...] = raw
    code = jnp.maximum(raw, 0.0).astype(jnp.bfloat16)
    code_ref[...] = code

    for copy in copies[2:4]:
        copy.wait()
    tokens = tokens_ref[...].astype(jnp.float32)
    bias = bias_flat[...].astype(jnp.float32).reshape(1, width)
    bias_ref[...] = bias
    centered_ref[...] = (tokens - bias).astype(jnp.bfloat16).astype(jnp.float32)

    copies[4].wait()
    total = share(code, rows_ref, centered_ref, 0, total_ref.shape[1])
    total_ref[...] = total
    width = total.shape[1]
    sent_ref[:, :width] = total.astype(jnp.bfloat16)
    block = stacked(tokens, ROWS // tokens.shape[0]).astype(jnp.bfloat16)
    if cut:
        cut[0][...] = block
    else:
        sent_ref[:, width:] = block


def front(tokens, b_pre, pre_codes, top_idx, blocks, counts, dict_rows, merged):
    count = top_idx.shape[0]
    slots, width = dict_rows.shape
    chunk, block = first_width(width), tokens.shape[0] * width // ROWS
    return kernel_call(
        front_kernel,
        (
            shape(count, slots),
            shape(count, slots, dtype=jnp.float32),
            shape(count, chunk, dtype=jnp.float32),
            shape(count, chunk + (block if merged else 0)),
            shape(slots, width),
            shape(*tokens.shape, dtype=jnp.float32),
            shape(1, width, dtype=jnp.float32),
            *([] if merged else [shape(ROWS, block)]),
        ),
        [HBM] * 5 + [SMEM] * 2,
        (VMEM,) * (7 if merged else 8),
        count,
        [
            pltpu.VMEM(tokens.shape, tokens.dtype),
            pltpu.VMEM(b_pre.shape, b_pre.dtype),
            pltpu.VMEM(pre_codes.shape, pre_codes.dtype),
            pltpu.VMEM(top_idx.shape, top_idx.dtype),
            pltpu.SemaphoreType.DMA((5,)),
        ],
    )(
        *(
            pltpu.with_memory_space_constraint(array, pltpu.HBM)
            for array in (tokens, b_pre, pre_codes, top_idx, dict_rows)
        ),
        blocks,
        counts,
    )


def second_kernel(code_ref, rows_ref, centered_ref, total_ref, sent_ref):
    width = total_ref.shape[1]
    total = share(code_ref[...], rows_ref, centered_ref, rows_ref.shape[1] - width, width)
    total_ref[...] = total
    sent_ref[...] = total.astype(jnp.bfloat16)


def second(code, dict_rows, centered):
    count, width = code.shape[0], dict_rows.shape[1]
    chunk = width - first_width(width)
    return kernel_call(
        second_kernel,
        (shape(count, chunk, dtype=jnp.float32), shape(count, chunk)),
        [VMEM] * 3,
        (VMEM, VMEM),
        count,
    )(code, dict_rows, centered)


def added_kernel(total_ref, own_ref, arrived_ref, after_ref, sum_ref, sent_ref):
    half = total_ref.shape[1]
    total = total_ref[...] + arrived_ref[:, :half].astype(jnp.float32)
    sum_ref[...] = total
    sent_ref[:, :half] = total.astype(jnp.bfloat16)
    if sent_ref.shape[1] > half:
        block = own_ref.shape[1] - half
        sent_ref[:, half : half + block] = own_ref[:, half:]
        sent_ref[:, half + block :] = arrived_ref[:, half:]


def added(total, own, arrived, after, merged, flops=10**6):
    count, half = total.shape
    block = own.shape[1] - half
    return kernel_call(
        added_kernel,
        (
            shape(count, half, dtype=jnp.float32),
            shape(count, half + (2 * block if merged else 0)),
        ),
        [VMEM] * 3 + [ANY],
        (VMEM, VMEM),
        count,
        flops=flops,
    )(total, own, arrived, after)


def joined_kernel(first_ref, second_ref, after_ref, out_ref):
    width = first_ref.shape[1]
    out_ref[:, :width] = first_ref[...]
    out_ref[:, width:] = second_ref[...]


def joined(first, second, after):
    return kernel_call(
        joined_kernel,
        shape(first.shape[0], 2 * first.shape[1]),
        [VMEM, VMEM, ANY],
        VMEM,
        first.shape[0],
    )(first, second, after)


def turned_kernel(skip, rows, own_ref, arrived_ref, bias_ref, out_ref):
    bias = jnp.concatenate([bias_ref[...]] * rows, axis=0)
    bias = stacked(bias, ROWS // rows)
    width = bias.shape[1]
    blocks = [
        (ref[:, at : at + width].astype(jnp.float32) - bias).astype(jnp.bfloat16)
        for ref in (own_ref, arrived_ref)
        for at in range(skip, ref.shape[1], width)
    ]
    out_ref[...] = jnp.concatenate(blocks, axis=0).astype(jnp.float32).T.astype(jnp.bfloat16)


def turned(own, arrived, skip, bias, rows, count):
    width = bias.shape[1] * rows // ROWS
    return kernel_call(
        functools.partial(turned_kernel, skip, rows),
        shape(width, 2 * (own.shape[1] - skip) // width * ROWS),
        [VMEM] * 3,
        VMEM,
        count,
    )(own, arrived, bias)


def scaled_of(total_ref, arrived_ref):
    total = total_ref[...] + arrived_ref[:, : total_ref.shape[1]].astype(jnp.float32)
    return (0.25 * total).astype(jnp.bfloat16)


def product(part, rows_ref, at):
    return lax.dot_general(
        part,
        rows_ref[:, at : at + part.shape[1]],
        (((1,), (1,)), ((), ())),
        preferred_element_type=jnp.float32,
    )


def first_product_kernel(total_ref, arrived_ref, rows_ref, scaled_ref, half_ref):
    scaled = scaled_of(total_ref, arrived_ref)
    scaled_ref[...] = scaled
    half_ref[...] = product(scaled, rows_ref, 0)


def second_product_kernel(total_ref, arrived_ref, rows_ref, first_ref, scaled_ref, half_ref):
    scaled = scaled_of(total_ref, arrived_ref)
    scaled_ref[...] = scaled
    half_ref[...] = first_ref[...] + product(scaled, rows_ref, rows_ref.shape[1] - scaled.shape[1])


def products(total, arrived, dict_rows, *first):
    count, width = total.shape
    return kernel_call(
        second_product_kernel if first else first_product_kernel,
        (shape(count, width), shape(count, dict_rows.shape[0], dtype=jnp.float32)),
        [VMEM] * (3 + len(first)),
        (VMEM, VMEM),
        count,
    )(total, arrived, dict_rows, *first)


def outer(code_ref, scaled):
    code = code_ref[...].astype(jnp.float32).T.astype(jnp.bfloat16)
    return jnp.dot(code, scaled, preferred_element_type=jnp.float32).astype(jnp.bfloat16)


def grad_rows_kernel(code_ref, first_ref, second_ref, out_ref):
    chunk = first_ref.shape[1]
    out_ref[:, :chunk] = outer(code_ref, first_ref[...])
    out_ref[:, chunk:] = outer(code_ref, second_ref[...])


def grad_rows_of(code, first, second):
    count, slots = code.shape
    return kernel_call(
        grad_rows_kernel,
        shape(slots, first.shape[1] + second.shape[1]),
        [VMEM] * 3,
        VMEM,
        count,
    )(code, first, second)


def final_kernel(
    rows,
    raw_ref,
    mine_ref,
    theirs_ref,
    turned_ref,
    rows_ref,
    rows_hbm,
    enc_hbm,
    benc_hbm,
    enc_ref,
    benc_ref,
    sems,
):
    copies = [pltpu.make_async_copy(rows_ref, rows_hbm, sems.at[0])]
    copies[0].start()
    count, slots = raw_ref.shape
    width, depth = turned_ref.shape
    pieces = ROWS // rows
    code_grad = mine_ref[...] + theirs_ref[...]
    pre_grad = jnp.where(raw_ref[...] > 0.0, code_grad, 0.0).astype(jnp.bfloat16)
    benc_ref[...] = jnp.sum(pre_grad.astype(jnp.float32), axis=0, keepdims=True)
    copies.append(pltpu.make_async_copy(benc_ref, benc_hbm, sems.at[1]))
    copies[1].start()
    place = lax.broadcasted_iota(jnp.int32, (depth, count), 0)
    token = lax.broadcasted_iota(jnp.int32, (depth, count), 1)
    core = lax.axis_index("tok")
    block = place // ROWS
    distance = jnp.zeros_like(place)
    for step in range(feat_bits()):
        bit = sum(
            jnp.where(core == c, bit_of(step, c), 0) for c in range(lax.axis_size("tok"))
        )
        distance |= (block >> step & 1) << bit
    source = (lax.axis_index("feat") ^ distance) * rows + place % rows
    order = jnp.where(token == source, 1.0, 0.0).astype(jnp.bfloat16)
    spread = jnp.dot(order, pre_grad, preferred_element_type=jnp.float32)
    piece = lax.broadcasted_iota(jnp.int32, (depth, slots), 0) % ROWS // rows
    for c in range(0, pieces, 2):
        pair = [jnp.where(piece == c + i, spread, 0.0).astype(jnp.bfloat16) for i in range(2)]
        out = jnp.dot(
            turned_ref[...],
            jnp.concatenate(pair, axis=1),
            preferred_element_type=jnp.float32,
        ).astype(jnp.bfloat16)
        for i in range(2):
            enc_ref[(c + i) * width : (c + i + 1) * width, :] = out[:, i * slots : (i + 1) * slots]
        part = pl.ds(c * width, 2 * width)
        copies.append(pltpu.make_async_copy(enc_ref.at[part], enc_hbm.at[part], sems.at[c // 2 + 2]))
        copies[-1].start()
    for copy in copies:
        copy.wait()


def final(raw, mine, theirs, turned_tokens, grad_rows, rows):
    count, slots = raw.shape
    pieces = ROWS // rows
    width = turned_tokens.shape[0] * pieces
    return kernel_call(
        functools.partial(final_kernel, rows),
        (shape(*grad_rows.shape), shape(width, slots), shape(1, slots, dtype=jnp.float32)),
        [VMEM] * 5,
        (HBM, HBM, HBM),
        count,
        [
            pltpu.VMEM((width, slots), jnp.bfloat16),
            pltpu.VMEM((1, slots), jnp.float32),
            pltpu.SemaphoreType.DMA((pieces // 2 + 2,)),
        ],
    )(raw, mine, theirs, turned_tokens, grad_rows)


def local(tokens, b_pre, pre_codes, top_idx, blocks, counts, dict_rows):
    rows, count = tokens.shape[0], top_idx.shape[0]
    steps = feat_bits()
    merged = count == ROWS

    code, raw, total, sent, dict_rows, centered, bias, *block = front(
        tokens, b_pre, pre_codes, top_idx, blocks, counts, dict_rows, merged
    )
    for step in range(steps):
        arrived = swapped(sent, step)
        if step == 0:
            total_second, sent_second = second(code, dict_rows, centered)
        else:
            total_second, sent_second = added(
                total_second, sent_second, arrived_second, sent, False, EARLY
            )
        arrived_second = swapped(sent_second, step)
        if not merged:
            own_block = joined(own_block, arrived_block, sent_second) if step else block[0]
            arrived_block = swapped(own_block, step)
        if step < steps - 1:
            total, sent = added(total, sent, arrived, sent_second, merged)
    skip = 0
    if merged:
        own_block, arrived_block, skip = sent, arrived, total.shape[1]

    scaled, product_first = products(total, arrived, dict_rows)
    turned_tokens = turned(own_block, arrived_block, skip, bias, rows, count)
    scaled_second, code_half = products(
        total_second, arrived_second, dict_rows, product_first
    )
    theirs = lax.ppermute(code_half, "tok", [(i, 1 - i) for i in range(2)])
    grad_rows = grad_rows_of(code, scaled, scaled_second)
    grad_rows, grad_enc, grad_benc = final(
        raw, code_half, theirs, turned_tokens, grad_rows, rows
    )
    return (grad_rows, grad_enc, grad_benc.reshape(-1))


def solution(mesh):
    return jax.shard_map(
        local,
        mesh=mesh,
        in_specs=(
            P(("grp", "feat"), "tok"),
            P(("grp", "tok")),
            P("grp", None),
            P("grp", None),
            P(("grp", "feat")),
            P(("grp", "feat")),
            P(("grp", "feat"), "tok"),
        ),
        out_specs=(P(("grp", "feat"), "tok"), P(("grp", "tok"), "feat"), P(("grp", "feat"))),
        check_vma=False,
    )
```

```python
import functools

import jax
import jax.numpy as jnp
from jax import lax
from jax.experimental import pallas as pl
from jax.experimental.pallas import tpu as pltpu
from jax.sharding import PartitionSpec as P

VMEM = pl.BlockSpec(memory_space=pltpu.VMEM)
SMEM = pl.BlockSpec(memory_space=pltpu.SMEM)
HBM = pl.BlockSpec(memory_space=pltpu.HBM)
ANY = pl.BlockSpec(memory_space=pl.ANY)
EARLY = 10**9
PARTS = 4
ROWS = 16


def kernel_call(kernel, out_shape, in_specs, out_specs, tokens, scratch_shapes=(), flops=10**6):
    limit = (16 if tokens <= ROWS else 40) * 2**20
    return pl.pallas_call(
        kernel,
        out_shape=out_shape,
        in_specs=in_specs,
        out_specs=out_specs,
        scratch_shapes=scratch_shapes,
        compiler_params=pltpu.CompilerParams(vmem_limit_bytes=limit),
        cost_estimate=pl.CostEstimate(flops=flops, bytes_accessed=2**20, transcendentals=0),
    )


def shape(*sizes, dtype=jnp.bfloat16):
    return jax.ShapeDtypeStruct(sizes, dtype)


def first_width(width):
    return width // 2


def feat_bits():
    return (lax.axis_size("feat") - 1).bit_length()


def bit_of(step, core, chunk):
    bits = list(range(feat_bits()))
    if core == 0:
        order = bits[-1:] + bits[:-1] if chunk == 0 else bits[:1] + bits[:0:-1]
    else:
        order = bits[1:] + bits[:1] if chunk == 0 else bits
    return order[step]


def swapped(shard, step, chunk):
    cores = lax.axis_size("tok")
    pairs = [
        (f * cores + c, (f ^ 1 << bit_of(step, c, chunk)) * cores + c)
        for f in range(lax.axis_size("feat"))
        for c in range(cores)
    ]
    return lax.ppermute(shard, ("feat", "tok"), pairs)


def stacked(rows, pieces):
    width = rows.shape[1] // pieces
    return jnp.concatenate(
        [rows[:, c * width : (c + 1) * width] for c in range(pieces)], axis=0
    )


def share(code, rows_ref, centered_ref, at, width):
    part = pl.ds(at, width)
    total = jnp.dot(code, rows_ref[:, part], preferred_element_type=jnp.float32)
    rows = centered_ref.shape[0]
    centered = centered_ref[:, part]
    token = lax.broadcasted_iota(jnp.int32, (total.shape[0], 1), 0)
    first = lax.axis_index("feat") * rows
    for i in range(rows):
        total -= jnp.where(token == first + i, centered[i : i + 1, :], 0.0)
    return total


def row_parts(rows_ref):
    slots, width = rows_ref.shape
    first, rows = first_width(width), slots // PARTS
    return [
        (pl.ds(i * rows, rows), columns)
        for columns in (pl.ds(0, first), pl.ds(first, width - first))
        for i in range(PARTS)
    ]


def front_kernel(
    tokens_hbm, bias_hbm, pre_hbm, top_hbm, rows_hbm, block_ref, count_ref, *refs
):
    code_ref, raw_ref, total_ref, sent_ref, rows_ref, centered_ref, bias_ref, *cut = refs[:-5]
    tokens_ref, bias_flat, pre_ref, top_ref, sems = refs[-5:]
    copies = [
        pltpu.make_async_copy(source, target, sems.at[i])
        for i, (source, target) in enumerate(
            (
                (top_hbm, top_ref),
                (pre_hbm, pre_ref),
                (tokens_hbm, tokens_ref),
                (bias_hbm, bias_flat),
                *((rows_hbm.at[part], rows_ref.at[part]) for part in row_parts(rows_ref)),
            )
        )
    ]
    for copy in copies:
        copy.start()
    for copy in copies[:2]:
        copy.wait()
    count, latents = top_ref.shape
    slots, width = rows_ref.shape
    offsets = lax.broadcasted_iota(jnp.int32, (1, slots), 1)
    slot_ids = jnp.where(offsets < count_ref[0], block_ref[0] * slots + offsets, -1)
    top, pre = top_ref[...], pre_ref[...]
    raw = jnp.zeros((count, slots), jnp.float32)
    for k in range(latents):
        raw = jnp.where(top[:, k : k + 1] == slot_ids, pre[:, k : k + 1], raw)
    raw_ref[...] = raw
    code = jnp.maximum(raw, 0.0).astype(jnp.bfloat16)
    code_ref[...] = code

    for copy in copies[2:4]:
        copy.wait()
    tokens = tokens_ref[...].astype(jnp.float32)
    bias = bias_flat[...].astype(jnp.float32).reshape(1, width)
    bias_ref[...] = bias
    centered_ref[...] = (tokens - bias).astype(jnp.bfloat16).astype(jnp.float32)

    for copy in copies[4 : 4 + PARTS]:
        copy.wait()
    total = share(code, rows_ref, centered_ref, 0, total_ref.shape[1])
    total_ref[...] = total
    width = total.shape[1]
    sent_ref[:, :width] = total.astype(jnp.bfloat16)
    block = stacked(tokens, ROWS // tokens.shape[0]).astype(jnp.bfloat16)
    if cut:
        cut[0][...] = block
    else:
        sent_ref[:, width:] = block
    for copy in copies[4 + PARTS :]:
        copy.wait()


def front(tokens, b_pre, pre_codes, top_idx, blocks, counts, dict_rows, merged):
    count = top_idx.shape[0]
    slots, width = dict_rows.shape
    chunk, block = first_width(width), tokens.shape[0] * width // ROWS
    return kernel_call(
        front_kernel,
        (
            shape(count, slots),
            shape(count, slots, dtype=jnp.float32),
            shape(count, chunk, dtype=jnp.float32),
            shape(count, chunk + (block if merged else 0)),
            shape(slots, width),
            shape(*tokens.shape, dtype=jnp.float32),
            shape(1, width, dtype=jnp.float32),
            *([] if merged else [shape(ROWS, block)]),
        ),
        [HBM] * 5 + [SMEM] * 2,
        (VMEM,) * (7 if merged else 8),
        count,
        [
            pltpu.VMEM(tokens.shape, tokens.dtype),
            pltpu.VMEM(b_pre.shape, b_pre.dtype),
            pltpu.VMEM(pre_codes.shape, pre_codes.dtype),
            pltpu.VMEM(top_idx.shape, top_idx.dtype),
            pltpu.SemaphoreType.DMA((4 + 2 * PARTS,)),
        ],
    )(
        *(
            pltpu.with_memory_space_constraint(array, pltpu.HBM)
            for array in (tokens, b_pre, pre_codes, top_idx, dict_rows)
        ),
        blocks,
        counts,
    )


def second_kernel(code_ref, rows_ref, centered_ref, total_ref, sent_ref):
    width = total_ref.shape[1]
    total = share(code_ref[...], rows_ref, centered_ref, rows_ref.shape[1] - width, width)
    total_ref[...] = total
    sent_ref[...] = total.astype(jnp.bfloat16)


def second(code, dict_rows, centered):
    count, width = code.shape[0], dict_rows.shape[1]
    chunk = width - first_width(width)
    return kernel_call(
        second_kernel,
        (shape(count, chunk, dtype=jnp.float32), shape(count, chunk)),
        [VMEM] * 3,
        (VMEM, VMEM),
        count,
    )(code, dict_rows, centered)


def added_kernel(total_ref, own_ref, arrived_ref, after_ref, sum_ref, sent_ref):
    half = total_ref.shape[1]
    total = total_ref[...] + arrived_ref[:, :half].astype(jnp.float32)
    sum_ref[...] = total
    sent_ref[:, :half] = total.astype(jnp.bfloat16)
    if sent_ref.shape[1] > half:
        block = own_ref.shape[1] - half
        sent_ref[:, half : half + block] = own_ref[:, half:]
        sent_ref[:, half + block :] = arrived_ref[:, half:]


def added(total, own, arrived, after, merged, flops=10**6):
    count, half = total.shape
    block = own.shape[1] - half
    return kernel_call(
        added_kernel,
        (
            shape(count, half, dtype=jnp.float32),
            shape(count, half + (2 * block if merged else 0)),
        ),
        [VMEM] * 3 + [ANY],
        (VMEM, VMEM),
        count,
        flops=flops,
    )(total, own, arrived, after)


def joined_kernel(first_ref, second_ref, after_ref, out_ref):
    width = first_ref.shape[1]
    out_ref[:, :width] = first_ref[...]
    out_ref[:, width:] = second_ref[...]


def joined(first, second, after):
    return kernel_call(
        joined_kernel,
        shape(first.shape[0], 2 * first.shape[1]),
        [VMEM, VMEM, ANY],
        VMEM,
        first.shape[0],
    )(first, second, after)


def turned_kernel(skip, rows, own_ref, arrived_ref, bias_ref, out_ref):
    bias = jnp.concatenate([bias_ref[...]] * rows, axis=0)
    bias = stacked(bias, ROWS // rows)
    width = bias.shape[1]
    blocks = [
        (ref[:, at : at + width].astype(jnp.float32) - bias).astype(jnp.bfloat16)
        for ref in (own_ref, arrived_ref)
        for at in range(skip, ref.shape[1], width)
    ]
    out_ref[...] = jnp.concatenate(blocks, axis=0).astype(jnp.float32).T.astype(jnp.bfloat16)


def turned(own, arrived, skip, bias, rows, count):
    width = bias.shape[1] * rows // ROWS
    return kernel_call(
        functools.partial(turned_kernel, skip, rows),
        shape(width, 2 * (own.shape[1] - skip) // width * ROWS),
        [VMEM] * 3,
        VMEM,
        count,
    )(own, arrived, bias)


def scaled_of(total_ref, arrived_ref):
    total = total_ref[...] + arrived_ref[:, : total_ref.shape[1]].astype(jnp.float32)
    return (0.25 * total).astype(jnp.bfloat16)


def product(part, rows_ref, at):
    return lax.dot_general(
        part,
        rows_ref[:, at : at + part.shape[1]],
        (((1,), (1,)), ((), ())),
        preferred_element_type=jnp.float32,
    )


def first_product_kernel(total_ref, arrived_ref, rows_ref, scaled_ref, half_ref):
    scaled = scaled_of(total_ref, arrived_ref)
    scaled_ref[...] = scaled
    half_ref[...] = product(scaled, rows_ref, 0)


def second_product_kernel(total_ref, arrived_ref, rows_ref, first_ref, scaled_ref, half_ref):
    scaled = scaled_of(total_ref, arrived_ref)
    scaled_ref[...] = scaled
    half_ref[...] = first_ref[...] + product(scaled, rows_ref, rows_ref.shape[1] - scaled.shape[1])


def products(total, arrived, dict_rows, *first):
    count, width = total.shape
    return kernel_call(
        second_product_kernel if first else first_product_kernel,
        (shape(count, width), shape(count, dict_rows.shape[0], dtype=jnp.float32)),
        [VMEM] * (3 + len(first)),
        (VMEM, VMEM),
        count,
    )(total, arrived, dict_rows, *first)


def outer(code_ref, scaled):
    code = code_ref[...].astype(jnp.float32).T.astype(jnp.bfloat16)
    return jnp.dot(code, scaled, preferred_element_type=jnp.float32).astype(jnp.bfloat16)


def grad_rows_kernel(code_ref, first_ref, second_ref, out_ref):
    chunk = first_ref.shape[1]
    out_ref[:, :chunk] = outer(code_ref, first_ref[...])
    out_ref[:, chunk:] = outer(code_ref, second_ref[...])


def grad_rows_of(code, first, second):
    count, slots = code.shape
    return kernel_call(
        grad_rows_kernel,
        shape(slots, first.shape[1] + second.shape[1]),
        [VMEM] * 3,
        VMEM,
        count,
    )(code, first, second)


def final_kernel(
    rows,
    raw_ref,
    mine_ref,
    theirs_ref,
    turned_ref,
    rows_ref,
    rows_hbm,
    enc_hbm,
    benc_hbm,
    enc_ref,
    benc_ref,
    sems,
):
    copies = [pltpu.make_async_copy(rows_ref, rows_hbm, sems.at[0])]
    copies[0].start()
    count, slots = raw_ref.shape
    width, depth = turned_ref.shape
    pieces = ROWS // rows
    code_grad = mine_ref[...] + theirs_ref[...]
    pre_grad = jnp.where(raw_ref[...] > 0.0, code_grad, 0.0).astype(jnp.bfloat16)
    benc_ref[...] = jnp.sum(pre_grad.astype(jnp.float32), axis=0, keepdims=True)
    copies.append(pltpu.make_async_copy(benc_ref, benc_hbm, sems.at[1]))
    copies[1].start()
    place = lax.broadcasted_iota(jnp.int32, (depth, count), 0)
    token = lax.broadcasted_iota(jnp.int32, (depth, count), 1)
    core = lax.axis_index("tok")
    block = place // ROWS
    distance = jnp.zeros_like(place)
    for step in range(feat_bits()):
        bit = sum(
            jnp.where(core == c, bit_of(step, c, 0), 0) for c in range(lax.axis_size("tok"))
        )
        distance |= (block >> step & 1) << bit
    source = (lax.axis_index("feat") ^ distance) * rows + place % rows
    order = jnp.where(token == source, 1.0, 0.0).astype(jnp.bfloat16)
    spread = jnp.dot(order, pre_grad, preferred_element_type=jnp.float32)
    piece = lax.broadcasted_iota(jnp.int32, (depth, slots), 0) % ROWS // rows
    for c in range(0, pieces, 2):
        pair = [jnp.where(piece == c + i, spread, 0.0).astype(jnp.bfloat16) for i in range(2)]
        out = jnp.dot(
            turned_ref[...],
            jnp.concatenate(pair, axis=1),
            preferred_element_type=jnp.float32,
        ).astype(jnp.bfloat16)
        for i in range(2):
            enc_ref[(c + i) * width : (c + i + 1) * width, :] = out[:, i * slots : (i + 1) * slots]
        part = pl.ds(c * width, 2 * width)
        copies.append(pltpu.make_async_copy(enc_ref.at[part], enc_hbm.at[part], sems.at[c // 2 + 2]))
        copies[-1].start()
    for copy in copies:
        copy.wait()


def final(raw, mine, theirs, turned_tokens, grad_rows, rows):
    count, slots = raw.shape
    pieces = ROWS // rows
    width = turned_tokens.shape[0] * pieces
    return kernel_call(
        functools.partial(final_kernel, rows),
        (shape(*grad_rows.shape), shape(width, slots), shape(1, slots, dtype=jnp.float32)),
        [VMEM] * 5,
        (HBM, HBM, HBM),
        count,
        [
            pltpu.VMEM((width, slots), jnp.bfloat16),
            pltpu.VMEM((1, slots), jnp.float32),
            pltpu.SemaphoreType.DMA((pieces // 2 + 2,)),
        ],
    )(raw, mine, theirs, turned_tokens, grad_rows)


def local(tokens, b_pre, pre_codes, top_idx, blocks, counts, dict_rows):
    rows, count = tokens.shape[0], top_idx.shape[0]
    steps = feat_bits()
    merged = count == ROWS

    code, raw, total, sent, dict_rows, centered, bias, *block = front(
        tokens, b_pre, pre_codes, top_idx, blocks, counts, dict_rows, merged
    )
    for step in range(steps):
        arrived = swapped(sent, step, 0)
        if step == 0:
            total_second, sent_second = second(code, dict_rows, centered)
        else:
            total_second, sent_second = added(
                total_second, sent_second, arrived_second, sent, False, EARLY
            )
        arrived_second = swapped(sent_second, step, 1)
        if not merged:
            own_block = joined(own_block, arrived_block, sent_second) if step else block[0]
            arrived_block = swapped(own_block, step, 0)
        if step < steps - 1:
            total, sent = added(total, sent, arrived, sent_second, merged)
    skip = 0
    if merged:
        own_block, arrived_block, skip = sent, arrived, total.shape[1]

    scaled, product_first = products(total, arrived, dict_rows)
    turned_tokens = turned(own_block, arrived_block, skip, bias, rows, count)
    scaled_second, code_half = products(
        total_second, arrived_second, dict_rows, product_first
    )
    theirs = lax.ppermute(code_half, "tok", [(i, 1 - i) for i in range(2)])
    grad_rows = grad_rows_of(code, scaled, scaled_second)
    grad_rows, grad_enc, grad_benc = final(
        raw, code_half, theirs, turned_tokens, grad_rows, rows
    )
    return (grad_rows, grad_enc, grad_benc.reshape(-1))


def solution(mesh):
    return jax.shard_map(
        local,
        mesh=mesh,
        in_specs=(
            P(("grp", "feat"), "tok"),
            P(("grp", "tok")),
            P("grp", None),
            P("grp", None),
            P(("grp", "feat")),
            P(("grp", "feat")),
            P(("grp", "feat"), "tok"),
        ),
        out_specs=(P(("grp", "feat"), "tok"), P(("grp", "tok"), "feat"), P(("grp", "feat"))),
        check_vma=False,
    )
```

```python
import functools

import jax
import jax.numpy as jnp
from jax import lax
from jax.experimental import pallas as pl
from jax.experimental.pallas import tpu as pltpu
from jax.sharding import PartitionSpec as P

VMEM = pl.BlockSpec(memory_space=pltpu.VMEM)
SMEM = pl.BlockSpec(memory_space=pltpu.SMEM)
HBM = pl.BlockSpec(memory_space=pltpu.HBM)
ANY = pl.BlockSpec(memory_space=pl.ANY)
EARLY = 10**9
ROWS = 16


def kernel_call(kernel, out_shape, in_specs, out_specs, tokens, scratch_shapes=(), flops=10**6):
    limit = (16 if tokens <= ROWS else 40) * 2**20
    return pl.pallas_call(
        kernel,
        out_shape=out_shape,
        in_specs=in_specs,
        out_specs=out_specs,
        scratch_shapes=scratch_shapes,
        compiler_params=pltpu.CompilerParams(vmem_limit_bytes=limit),
        cost_estimate=pl.CostEstimate(flops=flops, bytes_accessed=2**20, transcendentals=0),
    )


def shape(*sizes, dtype=jnp.bfloat16):
    return jax.ShapeDtypeStruct(sizes, dtype)


def first_width(width):
    return width // 2


def feat_bits():
    return (lax.axis_size("feat") - 1).bit_length()


def bit_of(step, core):
    bits = list(range(feat_bits()))
    return (bits[-1:] + bits[:-1] if core == 0 else bits)[step]


def swapped(shard, step):
    cores = lax.axis_size("tok")
    pairs = [
        (f * cores + c, (f ^ 1 << bit_of(step, c)) * cores + c)
        for f in range(lax.axis_size("feat"))
        for c in range(cores)
    ]
    return lax.ppermute(shard, ("feat", "tok"), pairs)


def stacked(rows, pieces):
    width = rows.shape[1] // pieces
    return jnp.concatenate(
        [rows[:, c * width : (c + 1) * width] for c in range(pieces)], axis=0
    )


def share(code, rows_ref, centered_ref, at, width):
    part = pl.ds(at, width)
    total = jnp.dot(code, rows_ref[:, part], preferred_element_type=jnp.float32)
    rows = centered_ref.shape[0]
    centered = centered_ref[:, part]
    token = lax.broadcasted_iota(jnp.int32, (total.shape[0], 1), 0)
    first = lax.axis_index("feat") * rows
    for i in range(rows):
        total -= jnp.where(token == first + i, centered[i : i + 1, :], 0.0)
    return total


def order_kernel(rows, order_ref):
    place = lax.broadcasted_iota(jnp.int32, order_ref.shape, 0)
    token = lax.broadcasted_iota(jnp.int32, order_ref.shape, 1)
    core = lax.axis_index("tok")
    block = place // ROWS
    distance = jnp.zeros_like(place)
    for step in range(feat_bits()):
        bit = sum(
            jnp.where(core == c, bit_of(step, c), 0) for c in range(lax.axis_size("tok"))
        )
        distance |= (block >> step & 1) << bit
    source = (lax.axis_index("feat") ^ distance) * rows + place % rows
    order_ref[...] = jnp.where(token == source, 1.0, 0.0).astype(jnp.bfloat16)


def order_of(rows, count):
    return kernel_call(
        functools.partial(order_kernel, rows),
        shape(ROWS * lax.axis_size("feat"), count),
        [],
        VMEM,
        count,
        flops=EARLY,
    )()


def front_kernel(
    tokens_ref, bias_flat, pre_ref, top_ref, rows_ref, block_ref, count_ref, after_ref, *refs
):
    code_ref, raw_ref, total_ref, sent_ref, centered_ref, bias_ref, *cut = refs
    count, latents = top_ref.shape
    slots, width = rows_ref.shape
    offsets = lax.broadcasted_iota(jnp.int32, (1, slots), 1)
    slot_ids = jnp.where(offsets < count_ref[0], block_ref[0] * slots + offsets, -1)
    top, pre = top_ref[...], pre_ref[...]
    raw = jnp.zeros((count, slots), jnp.float32)
    for k in range(latents):
        raw = jnp.where(top[:, k : k + 1] == slot_ids, pre[:, k : k + 1], raw)
    raw_ref[...] = raw
    code = jnp.maximum(raw, 0.0).astype(jnp.bfloat16)
    code_ref[...] = code

    tokens = tokens_ref[...].astype(jnp.float32)
    bias = bias_flat[...].astype(jnp.float32).reshape(1, width)
    bias_ref[...] = bias
    centered_ref[...] = (tokens - bias).astype(jnp.bfloat16).astype(jnp.float32)

    total = share(code, rows_ref, centered_ref, 0, total_ref.shape[1])
    total_ref[...] = total
    width = total.shape[1]
    sent_ref[:, :width] = total.astype(jnp.bfloat16)
    block = stacked(tokens, ROWS // tokens.shape[0]).astype(jnp.bfloat16)
    if cut:
        cut[0][...] = block
    else:
        sent_ref[:, width:] = block


def front(tokens, b_pre, pre_codes, top_idx, blocks, counts, dict_rows, after, merged):
    count = top_idx.shape[0]
    slots, width = dict_rows.shape
    chunk, block = first_width(width), tokens.shape[0] * width // ROWS
    return kernel_call(
        front_kernel,
        (
            shape(count, slots),
            shape(count, slots, dtype=jnp.float32),
            shape(count, chunk, dtype=jnp.float32),
            shape(count, chunk + (block if merged else 0)),
            shape(*tokens.shape, dtype=jnp.float32),
            shape(1, width, dtype=jnp.float32),
            *([] if merged else [shape(ROWS, block)]),
        ),
        [VMEM] * 5 + [SMEM] * 2 + [ANY],
        (VMEM,) * (6 if merged else 7),
        count,
    )(tokens, b_pre, pre_codes, top_idx, dict_rows, blocks, counts, after)


def second_kernel(code_ref, rows_ref, centered_ref, total_ref, sent_ref):
    width = total_ref.shape[1]
    total = share(code_ref[...], rows_ref, centered_ref, rows_ref.shape[1] - width, width)
    total_ref[...] = total
    sent_ref[...] = total.astype(jnp.bfloat16)


def second(code, dict_rows, centered):
    count, width = code.shape[0], dict_rows.shape[1]
    chunk = width - first_width(width)
    return kernel_call(
        second_kernel,
        (shape(count, chunk, dtype=jnp.float32), shape(count, chunk)),
        [VMEM] * 3,
        (VMEM, VMEM),
        count,
    )(code, dict_rows, centered)


def added_kernel(total_ref, own_ref, arrived_ref, after_ref, sum_ref, sent_ref):
    half = total_ref.shape[1]
    total = total_ref[...] + arrived_ref[:, :half].astype(jnp.float32)
    sum_ref[...] = total
    sent_ref[:, :half] = total.astype(jnp.bfloat16)
    if sent_ref.shape[1] > half:
        block = own_ref.shape[1] - half
        sent_ref[:, half : half + block] = own_ref[:, half:]
        sent_ref[:, half + block :] = arrived_ref[:, half:]


def added(total, own, arrived, after, merged, flops=10**6):
    count, half = total.shape
    block = own.shape[1] - half
    return kernel_call(
        added_kernel,
        (
            shape(count, half, dtype=jnp.float32),
            shape(count, half + (2 * block if merged else 0)),
        ),
        [VMEM] * 3 + [ANY],
        (VMEM, VMEM),
        count,
        flops=flops,
    )(total, own, arrived, after)


def joined_kernel(first_ref, second_ref, after_ref, out_ref):
    width = first_ref.shape[1]
    out_ref[:, :width] = first_ref[...]
    out_ref[:, width:] = second_ref[...]


def joined(first, second, after):
    return kernel_call(
        joined_kernel,
        shape(first.shape[0], 2 * first.shape[1]),
        [VMEM, VMEM, ANY],
        VMEM,
        first.shape[0],
    )(first, second, after)


def turned_kernel(skip, rows, own_ref, arrived_ref, bias_ref, out_ref):
    bias = jnp.concatenate([bias_ref[...]] * rows, axis=0)
    bias = stacked(bias, ROWS // rows)
    width = bias.shape[1]
    blocks = [
        (ref[:, at : at + width].astype(jnp.float32) - bias).astype(jnp.bfloat16)
        for ref in (own_ref, arrived_ref)
        for at in range(skip, ref.shape[1], width)
    ]
    out_ref[...] = jnp.concatenate(blocks, axis=0).astype(jnp.float32).T.astype(jnp.bfloat16)


def turned(own, arrived, skip, bias, rows, count):
    width = bias.shape[1] * rows // ROWS
    return kernel_call(
        functools.partial(turned_kernel, skip, rows),
        shape(width, 2 * (own.shape[1] - skip) // width * ROWS),
        [VMEM] * 3,
        VMEM,
        count,
    )(own, arrived, bias)


def scaled_of(total_ref, arrived_ref):
    total = total_ref[...] + arrived_ref[:, : total_ref.shape[1]].astype(jnp.float32)
    return (0.25 * total).astype(jnp.bfloat16)


def product(part, rows_ref, at):
    return lax.dot_general(
        part,
        rows_ref[:, at : at + part.shape[1]],
        (((1,), (1,)), ((), ())),
        preferred_element_type=jnp.float32,
    )


def first_product_kernel(total_ref, arrived_ref, rows_ref, scaled_ref, half_ref):
    scaled = scaled_of(total_ref, arrived_ref)
    scaled_ref[...] = scaled
    half_ref[...] = product(scaled, rows_ref, 0)


def second_product_kernel(total_ref, arrived_ref, rows_ref, first_ref, scaled_ref, half_ref):
    scaled = scaled_of(total_ref, arrived_ref)
    scaled_ref[...] = scaled
    half_ref[...] = first_ref[...] + product(scaled, rows_ref, rows_ref.shape[1] - scaled.shape[1])


def products(total, arrived, dict_rows, *first):
    count, width = total.shape
    return kernel_call(
        second_product_kernel if first else first_product_kernel,
        (shape(count, width), shape(count, dict_rows.shape[0], dtype=jnp.float32)),
        [VMEM] * (3 + len(first)),
        (VMEM, VMEM),
        count,
    )(total, arrived, dict_rows, *first)


def outer(code_ref, scaled):
    code = code_ref[...].astype(jnp.float32).T.astype(jnp.bfloat16)
    return jnp.dot(code, scaled, preferred_element_type=jnp.float32).astype(jnp.bfloat16)


def grad_rows_kernel(code_ref, first_ref, second_ref, out_ref):
    chunk = first_ref.shape[1]
    out_ref[:, :chunk] = outer(code_ref, first_ref[...])
    out_ref[:, chunk:] = outer(code_ref, second_ref[...])


def grad_rows_of(code, first, second):
    count, slots = code.shape
    return kernel_call(
        grad_rows_kernel,
        shape(slots, first.shape[1] + second.shape[1]),
        [VMEM] * 3,
        VMEM,
        count,
    )(code, first, second)


def final_kernel(
    rows,
    raw_ref,
    mine_ref,
    theirs_ref,
    turned_ref,
    order_ref,
    rows_ref,
    rows_hbm,
    enc_hbm,
    benc_hbm,
    enc_ref,
    benc_ref,
    sems,
):
    copies = [pltpu.make_async_copy(rows_ref, rows_hbm, sems.at[0])]
    copies[0].start()
    count, slots = raw_ref.shape
    width, depth = turned_ref.shape
    pieces = ROWS // rows
    code_grad = mine_ref[...] + theirs_ref[...]
    pre_grad = jnp.where(raw_ref[...] > 0.0, code_grad, 0.0).astype(jnp.bfloat16)
    benc_ref[...] = jnp.sum(pre_grad.astype(jnp.float32), axis=0, keepdims=True)
    copies.append(pltpu.make_async_copy(benc_ref, benc_hbm, sems.at[1]))
    copies[1].start()
    spread = jnp.dot(order_ref[...], pre_grad, preferred_element_type=jnp.float32)
    piece = lax.broadcasted_iota(jnp.int32, (depth, slots), 0) % ROWS // rows
    for c in range(0, pieces, 2):
        pair = [jnp.where(piece == c + i, spread, 0.0).astype(jnp.bfloat16) for i in range(2)]
        out = jnp.dot(
            turned_ref[...],
            jnp.concatenate(pair, axis=1),
            preferred_element_type=jnp.float32,
        ).astype(jnp.bfloat16)
        for i in range(2):
            enc_ref[(c + i) * width : (c + i + 1) * width, :] = out[:, i * slots : (i + 1) * slots]
        part = pl.ds(c * width, 2 * width)
        copies.append(pltpu.make_async_copy(enc_ref.at[part], enc_hbm.at[part], sems.at[c // 2 + 2]))
        copies[-1].start()
    for copy in copies:
        copy.wait()


def final(raw, mine, theirs, turned_tokens, order, grad_rows, rows):
    count, slots = raw.shape
    pieces = ROWS // rows
    width = turned_tokens.shape[0] * pieces
    return kernel_call(
        functools.partial(final_kernel, rows),
        (shape(*grad_rows.shape), shape(width, slots), shape(1, slots, dtype=jnp.float32)),
        [VMEM] * 6,
        (HBM, HBM, HBM),
        count,
        [
            pltpu.VMEM((width, slots), jnp.bfloat16),
            pltpu.VMEM((1, slots), jnp.float32),
            pltpu.SemaphoreType.DMA((pieces // 2 + 2,)),
        ],
    )(raw, mine, theirs, turned_tokens, order, grad_rows)


def local(tokens, b_pre, pre_codes, top_idx, blocks, counts, dict_rows):
    rows, count = tokens.shape[0], top_idx.shape[0]
    steps = feat_bits()
    merged = count == ROWS

    order = order_of(rows, count)
    code, raw, total, sent, centered, bias, *block = front(
        tokens, b_pre, pre_codes, top_idx, blocks, counts, dict_rows, order, merged
    )
    for step in range(steps):
        arrived = swapped(sent, step)
        if step == 0:
            total_second, sent_second = second(code, dict_rows, centered)
        else:
            total_second, sent_second = added(
                total_second, sent_second, arrived_second, sent, False, EARLY
            )
        arrived_second = swapped(sent_second, step)
        if not merged:
            own_block = joined(own_block, arrived_block, sent_second) if step else block[0]
            arrived_block = swapped(own_block, step)
        if step < steps - 1:
            total, sent = added(total, sent, arrived, sent_second, merged)
    skip = 0
    if merged:
        own_block, arrived_block, skip = sent, arrived, total.shape[1]

    scaled, product_first = products(total, arrived, dict_rows)
    turned_tokens = turned(own_block, arrived_block, skip, bias, rows, count)
    scaled_second, code_half = products(
        total_second, arrived_second, dict_rows, product_first
    )
    theirs = lax.ppermute(code_half, "tok", [(i, 1 - i) for i in range(2)])
    grad_rows = grad_rows_of(code, scaled, scaled_second)
    grad_rows, grad_enc, grad_benc = final(
        raw, code_half, theirs, turned_tokens, order, grad_rows, rows
    )
    return (grad_rows, grad_enc, grad_benc.reshape(-1))


def solution(mesh):
    return jax.shard_map(
        local,
        mesh=mesh,
        in_specs=(
            P(("grp", "feat"), "tok"),
            P(("grp", "tok")),
            P("grp", None),
            P("grp", None),
            P(("grp", "feat")),
            P(("grp", "feat")),
            P(("grp", "feat"), "tok"),
        ),
        out_specs=(P(("grp", "feat"), "tok"), P(("grp", "tok"), "feat"), P(("grp", "feat"))),
        check_vma=False,
    )
```

```python
import functools

import jax
import jax.numpy as jnp
from jax import lax
from jax.experimental import pallas as pl
from jax.experimental.pallas import tpu as pltpu
from jax.sharding import PartitionSpec as P

VMEM = pl.BlockSpec(memory_space=pltpu.VMEM)
SMEM = pl.BlockSpec(memory_space=pltpu.SMEM)
HBM = pl.BlockSpec(memory_space=pltpu.HBM)
ANY = pl.BlockSpec(memory_space=pl.ANY)
EARLY = 10**9
ROWS = 16


def kernel_call(kernel, out_shape, in_specs, out_specs, tokens, scratch_shapes=(), flops=10**6):
    limit = (16 if tokens <= ROWS else 40) * 2**20
    return pl.pallas_call(
        kernel,
        out_shape=out_shape,
        in_specs=in_specs,
        out_specs=out_specs,
        scratch_shapes=scratch_shapes,
        compiler_params=pltpu.CompilerParams(vmem_limit_bytes=limit),
        cost_estimate=pl.CostEstimate(flops=flops, bytes_accessed=2**20, transcendentals=0),
    )


def shape(*sizes, dtype=jnp.bfloat16):
    return jax.ShapeDtypeStruct(sizes, dtype)


def first_width(width):
    return width // 2


def feat_bits():
    return (lax.axis_size("feat") - 1).bit_length()


def bit_of(step, core, chunk):
    bits = list(range(feat_bits()))
    if core == 0:
        order = bits[-1:] + bits[:-1] if chunk == 0 else bits
    else:
        order = bits[1:] + bits[:1] if chunk == 0 else bits[:1] + bits[:0:-1]
    return order[step]


def swapped(shard, step, chunk):
    cores = lax.axis_size("tok")
    pairs = [
        (f * cores + c, (f ^ 1 << bit_of(step, c, chunk)) * cores + c)
        for f in range(lax.axis_size("feat"))
        for c in range(cores)
    ]
    return lax.ppermute(shard, ("feat", "tok"), pairs)


def stacked(rows, pieces):
    width = rows.shape[1] // pieces
    return jnp.concatenate(
        [rows[:, c * width : (c + 1) * width] for c in range(pieces)], axis=0
    )


def share(code, rows_ref, centered_ref, at, width):
    part = pl.ds(at, width)
    total = jnp.dot(code, rows_ref[:, part], preferred_element_type=jnp.float32)
    rows = centered_ref.shape[0]
    centered = centered_ref[:, part]
    token = lax.broadcasted_iota(jnp.int32, (total.shape[0], 1), 0)
    first = lax.axis_index("feat") * rows
    for i in range(rows):
        total -= jnp.where(token == first + i, centered[i : i + 1, :], 0.0)
    return total


def order_kernel(rows, order_ref):
    place = lax.broadcasted_iota(jnp.int32, order_ref.shape, 0)
    token = lax.broadcasted_iota(jnp.int32, order_ref.shape, 1)
    core = lax.axis_index("tok")
    block = place // ROWS
    distance = jnp.zeros_like(place)
    for step in range(feat_bits()):
        bit = sum(
            jnp.where(core == c, bit_of(step, c, 0), 0) for c in range(lax.axis_size("tok"))
        )
        distance |= (block >> step & 1) << bit
    source = (lax.axis_index("feat") ^ distance) * rows + place % rows
    order_ref[...] = jnp.where(token == source, 1.0, 0.0).astype(jnp.bfloat16)


def order_of(rows, count):
    return kernel_call(
        functools.partial(order_kernel, rows),
        shape(ROWS * lax.axis_size("feat"), count),
        [],
        VMEM,
        count,
        flops=EARLY,
    )()


def front_kernel(
    tokens_ref, bias_flat, pre_ref, top_ref, rows_ref, block_ref, count_ref, after_ref, *refs
):
    code_ref, raw_ref, total_ref, sent_ref, centered_ref, bias_ref, *cut = refs
    count, latents = top_ref.shape
    slots, width = rows_ref.shape
    offsets = lax.broadcasted_iota(jnp.int32, (1, slots), 1)
    slot_ids = jnp.where(offsets < count_ref[0], block_ref[0] * slots + offsets, -1)
    top, pre = top_ref[...], pre_ref[...]
    raw = jnp.zeros((count, slots), jnp.float32)
    for k in range(latents):
        raw = jnp.where(top[:, k : k + 1] == slot_ids, pre[:, k : k + 1], raw)
    raw_ref[...] = raw
    code = jnp.maximum(raw, 0.0).astype(jnp.bfloat16)
    code_ref[...] = code

    tokens = tokens_ref[...].astype(jnp.float32)
    bias = bias_flat[...].astype(jnp.float32).reshape(1, width)
    bias_ref[...] = bias
    centered_ref[...] = (tokens - bias).astype(jnp.bfloat16).astype(jnp.float32)

    total = share(code, rows_ref, centered_ref, 0, total_ref.shape[1])
    total_ref[...] = total
    width = total.shape[1]
    sent_ref[:, :width] = total.astype(jnp.bfloat16)
    block = stacked(tokens, ROWS // tokens.shape[0]).astype(jnp.bfloat16)
    if cut:
        cut[0][...] = block
    else:
        sent_ref[:, width:] = block


def front(tokens, b_pre, pre_codes, top_idx, blocks, counts, dict_rows, after, merged):
    count = top_idx.shape[0]
    slots, width = dict_rows.shape
    chunk, block = first_width(width), tokens.shape[0] * width // ROWS
    return kernel_call(
        front_kernel,
        (
            shape(count, slots),
            shape(count, slots, dtype=jnp.float32),
            shape(count, chunk, dtype=jnp.float32),
            shape(count, chunk + (block if merged else 0)),
            shape(*tokens.shape, dtype=jnp.float32),
            shape(1, width, dtype=jnp.float32),
            *([] if merged else [shape(ROWS, block)]),
        ),
        [VMEM] * 5 + [SMEM] * 2 + [ANY],
        (VMEM,) * (6 if merged else 7),
        count,
    )(tokens, b_pre, pre_codes, top_idx, dict_rows, blocks, counts, after)


def second_kernel(code_ref, rows_ref, centered_ref, total_ref, sent_ref):
    width = total_ref.shape[1]
    total = share(code_ref[...], rows_ref, centered_ref, rows_ref.shape[1] - width, width)
    total_ref[...] = total
    sent_ref[...] = total.astype(jnp.bfloat16)


def second(code, dict_rows, centered):
    count, width = code.shape[0], dict_rows.shape[1]
    chunk = width - first_width(width)
    return kernel_call(
        second_kernel,
        (shape(count, chunk, dtype=jnp.float32), shape(count, chunk)),
        [VMEM] * 3,
        (VMEM, VMEM),
        count,
    )(code, dict_rows, centered)


def added_kernel(total_ref, own_ref, arrived_ref, after_ref, sum_ref, sent_ref):
    half = total_ref.shape[1]
    total = total_ref[...] + arrived_ref[:, :half].astype(jnp.float32)
    sum_ref[...] = total
    sent_ref[:, :half] = total.astype(jnp.bfloat16)
    if sent_ref.shape[1] > half:
        block = own_ref.shape[1] - half
        sent_ref[:, half : half + block] = own_ref[:, half:]
        sent_ref[:, half + block :] = arrived_ref[:, half:]


def added(total, own, arrived, after, merged, flops=10**6):
    count, half = total.shape
    block = own.shape[1] - half
    return kernel_call(
        added_kernel,
        (
            shape(count, half, dtype=jnp.float32),
            shape(count, half + (2 * block if merged else 0)),
        ),
        [VMEM] * 3 + [ANY],
        (VMEM, VMEM),
        count,
        flops=flops,
    )(total, own, arrived, after)


def joined_kernel(first_ref, second_ref, after_ref, out_ref):
    width = first_ref.shape[1]
    out_ref[:, :width] = first_ref[...]
    out_ref[:, width:] = second_ref[...]


def joined(first, second, after):
    return kernel_call(
        joined_kernel,
        shape(first.shape[0], 2 * first.shape[1]),
        [VMEM, VMEM, ANY],
        VMEM,
        first.shape[0],
    )(first, second, after)


def turned_kernel(skip, rows, own_ref, arrived_ref, bias_ref, out_ref):
    bias = jnp.concatenate([bias_ref[...]] * rows, axis=0)
    bias = stacked(bias, ROWS // rows)
    width = bias.shape[1]
    blocks = [
        (ref[:, at : at + width].astype(jnp.float32) - bias).astype(jnp.bfloat16)
        for ref in (own_ref, arrived_ref)
        for at in range(skip, ref.shape[1], width)
    ]
    out_ref[...] = jnp.concatenate(blocks, axis=0).astype(jnp.float32).T.astype(jnp.bfloat16)


def turned(own, arrived, skip, bias, rows, count):
    width = bias.shape[1] * rows // ROWS
    return kernel_call(
        functools.partial(turned_kernel, skip, rows),
        shape(width, 2 * (own.shape[1] - skip) // width * ROWS),
        [VMEM] * 3,
        VMEM,
        count,
    )(own, arrived, bias)


def scaled_of(total_ref, arrived_ref):
    total = total_ref[...] + arrived_ref[:, : total_ref.shape[1]].astype(jnp.float32)
    return (0.25 * total).astype(jnp.bfloat16)


def product(part, rows_ref, at):
    return lax.dot_general(
        part,
        rows_ref[:, at : at + part.shape[1]],
        (((1,), (1,)), ((), ())),
        preferred_element_type=jnp.float32,
    )


def first_product_kernel(total_ref, arrived_ref, rows_ref, scaled_ref, half_ref):
    scaled = scaled_of(total_ref, arrived_ref)
    scaled_ref[...] = scaled
    half_ref[...] = product(scaled, rows_ref, 0)


def second_product_kernel(total_ref, arrived_ref, rows_ref, first_ref, scaled_ref, half_ref):
    scaled = scaled_of(total_ref, arrived_ref)
    scaled_ref[...] = scaled
    half_ref[...] = first_ref[...] + product(scaled, rows_ref, rows_ref.shape[1] - scaled.shape[1])


def products(total, arrived, dict_rows, *first):
    count, width = total.shape
    return kernel_call(
        second_product_kernel if first else first_product_kernel,
        (shape(count, width), shape(count, dict_rows.shape[0], dtype=jnp.float32)),
        [VMEM] * (3 + len(first)),
        (VMEM, VMEM),
        count,
    )(total, arrived, dict_rows, *first)


def outer(code_ref, scaled):
    code = code_ref[...].astype(jnp.float32).T.astype(jnp.bfloat16)
    return jnp.dot(code, scaled, preferred_element_type=jnp.float32).astype(jnp.bfloat16)


def grad_rows_kernel(code_ref, first_ref, second_ref, out_ref):
    chunk = first_ref.shape[1]
    out_ref[:, :chunk] = outer(code_ref, first_ref[...])
    out_ref[:, chunk:] = outer(code_ref, second_ref[...])


def grad_rows_of(code, first, second):
    count, slots = code.shape
    return kernel_call(
        grad_rows_kernel,
        shape(slots, first.shape[1] + second.shape[1]),
        [VMEM] * 3,
        VMEM,
        count,
    )(code, first, second)


def final_kernel(
    rows,
    raw_ref,
    mine_ref,
    theirs_ref,
    turned_ref,
    order_ref,
    rows_ref,
    rows_hbm,
    enc_hbm,
    benc_hbm,
    enc_ref,
    benc_ref,
    sems,
):
    copies = [pltpu.make_async_copy(rows_ref, rows_hbm, sems.at[0])]
    copies[0].start()
    count, slots = raw_ref.shape
    width, depth = turned_ref.shape
    pieces = ROWS // rows
    code_grad = mine_ref[...] + theirs_ref[...]
    pre_grad = jnp.where(raw_ref[...] > 0.0, code_grad, 0.0).astype(jnp.bfloat16)
    benc_ref[...] = jnp.sum(pre_grad.astype(jnp.float32), axis=0, keepdims=True)
    copies.append(pltpu.make_async_copy(benc_ref, benc_hbm, sems.at[1]))
    copies[1].start()
    spread = jnp.dot(order_ref[...], pre_grad, preferred_element_type=jnp.float32)
    piece = lax.broadcasted_iota(jnp.int32, (depth, slots), 0) % ROWS // rows
    for c in range(0, pieces, 2):
        pair = [jnp.where(piece == c + i, spread, 0.0).astype(jnp.bfloat16) for i in range(2)]
        out = jnp.dot(
            turned_ref[...],
            jnp.concatenate(pair, axis=1),
            preferred_element_type=jnp.float32,
        ).astype(jnp.bfloat16)
        for i in range(2):
            enc_ref[(c + i) * width : (c + i + 1) * width, :] = out[:, i * slots : (i + 1) * slots]
        part = pl.ds(c * width, 2 * width)
        copies.append(pltpu.make_async_copy(enc_ref.at[part], enc_hbm.at[part], sems.at[c // 2 + 2]))
        copies[-1].start()
    for copy in copies:
        copy.wait()


def final(raw, mine, theirs, turned_tokens, order, grad_rows, rows):
    count, slots = raw.shape
    pieces = ROWS // rows
    width = turned_tokens.shape[0] * pieces
    return kernel_call(
        functools.partial(final_kernel, rows),
        (shape(*grad_rows.shape), shape(width, slots), shape(1, slots, dtype=jnp.float32)),
        [VMEM] * 6,
        (HBM, HBM, HBM),
        count,
        [
            pltpu.VMEM((width, slots), jnp.bfloat16),
            pltpu.VMEM((1, slots), jnp.float32),
            pltpu.SemaphoreType.DMA((pieces // 2 + 2,)),
        ],
    )(raw, mine, theirs, turned_tokens, order, grad_rows)


def local(tokens, b_pre, pre_codes, top_idx, blocks, counts, dict_rows):
    rows, count = tokens.shape[0], top_idx.shape[0]
    steps = feat_bits()
    merged = count == ROWS

    order = order_of(rows, count)
    code, raw, total, sent, centered, bias, *block = front(
        tokens, b_pre, pre_codes, top_idx, blocks, counts, dict_rows, order, merged
    )
    for step in range(steps):
        arrived = swapped(sent, step, 0)
        if step == 0:
            total_second, sent_second = second(code, dict_rows, centered)
        else:
            total_second, sent_second = added(
                total_second, sent_second, arrived_second, sent, False, EARLY
            )
        arrived_second = swapped(sent_second, step, 1)
        if not merged:
            own_block = joined(own_block, arrived_block, sent_second) if step else block[0]
            arrived_block = swapped(own_block, step, 0)
        if step < steps - 1:
            total, sent = added(total, sent, arrived, sent_second, merged)
    skip = 0
    if merged:
        own_block, arrived_block, skip = sent, arrived, total.shape[1]

    scaled, product_first = products(total, arrived, dict_rows)
    turned_tokens = turned(own_block, arrived_block, skip, bias, rows, count)
    scaled_second, code_half = products(
        total_second, arrived_second, dict_rows, product_first
    )
    theirs = lax.ppermute(code_half, "tok", [(i, 1 - i) for i in range(2)])
    grad_rows = grad_rows_of(code, scaled, scaled_second)
    grad_rows, grad_enc, grad_benc = final(
        raw, code_half, theirs, turned_tokens, order, grad_rows, rows
    )
    return (grad_rows, grad_enc, grad_benc.reshape(-1))


def solution(mesh):
    return jax.shard_map(
        local,
        mesh=mesh,
        in_specs=(
            P(("grp", "feat"), "tok"),
            P(("grp", "tok")),
            P("grp", None),
            P("grp", None),
            P(("grp", "feat")),
            P(("grp", "feat")),
            P(("grp", "feat"), "tok"),
        ),
        out_specs=(P(("grp", "feat"), "tok"), P(("grp", "tok"), "feat"), P(("grp", "feat"))),
        check_vma=False,
    )
```

```python
import functools

import jax
import jax.numpy as jnp
from jax import lax
from jax.experimental import pallas as pl
from jax.experimental.pallas import tpu as pltpu
from jax.sharding import PartitionSpec as P

VMEM = pl.BlockSpec(memory_space=pltpu.VMEM)
SMEM = pl.BlockSpec(memory_space=pltpu.SMEM)
HBM = pl.BlockSpec(memory_space=pltpu.HBM)
ANY = pl.BlockSpec(memory_space=pl.ANY)
EARLY = 10**9
ROWS = 16


def kernel_call(kernel, out_shape, in_specs, out_specs, tokens, scratch_shapes=(), flops=10**6):
    limit = (16 if tokens <= ROWS else 40) * 2**20
    return pl.pallas_call(
        kernel,
        out_shape=out_shape,
        in_specs=in_specs,
        out_specs=out_specs,
        scratch_shapes=scratch_shapes,
        compiler_params=pltpu.CompilerParams(vmem_limit_bytes=limit),
        cost_estimate=pl.CostEstimate(flops=flops, bytes_accessed=2**20, transcendentals=0),
    )


def shape(*sizes, dtype=jnp.bfloat16):
    return jax.ShapeDtypeStruct(sizes, dtype)


def first_width(width):
    return width * 5 // 8 // 128 * 128


def feat_bits():
    return (lax.axis_size("feat") - 1).bit_length()


def bit_of(step, core, chunk):
    bits = list(range(feat_bits()))
    if core == 0:
        order = bits[-1:] + bits[:-1] if chunk == 0 else bits
    else:
        order = bits[1:] + bits[:1] if chunk == 0 else bits[:1] + bits[:0:-1]
    return order[step]


def swapped(shard, step, chunk):
    cores = lax.axis_size("tok")
    pairs = [
        (f * cores + c, (f ^ 1 << bit_of(step, c, chunk)) * cores + c)
        for f in range(lax.axis_size("feat"))
        for c in range(cores)
    ]
    return lax.ppermute(shard, ("feat", "tok"), pairs)


def stacked(rows, pieces):
    width = rows.shape[1] // pieces
    return jnp.concatenate(
        [rows[:, c * width : (c + 1) * width] for c in range(pieces)], axis=0
    )


def share(code, rows_ref, centered_ref, at, width):
    part = pl.ds(at, width)
    total = jnp.dot(code, rows_ref[:, part], preferred_element_type=jnp.float32)
    rows = centered_ref.shape[0]
    centered = centered_ref[:, part]
    token = lax.broadcasted_iota(jnp.int32, (total.shape[0], 1), 0)
    first = lax.axis_index("feat") * rows
    for i in range(rows):
        total -= jnp.where(token == first + i, centered[i : i + 1, :], 0.0)
    return total


def order_kernel(rows, order_ref):
    place = lax.broadcasted_iota(jnp.int32, order_ref.shape, 0)
    token = lax.broadcasted_iota(jnp.int32, order_ref.shape, 1)
    core = lax.axis_index("tok")
    block = place // ROWS
    distance = jnp.zeros_like(place)
    for step in range(feat_bits()):
        bit = sum(
            jnp.where(core == c, bit_of(step, c, 0), 0) for c in range(lax.axis_size("tok"))
        )
        distance |= (block >> step & 1) << bit
    source = (lax.axis_index("feat") ^ distance) * rows + place % rows
    order_ref[...] = jnp.where(token == source, 1.0, 0.0).astype(jnp.bfloat16)


def order_of(rows, count):
    return kernel_call(
        functools.partial(order_kernel, rows),
        shape(ROWS * lax.axis_size("feat"), count),
        [],
        VMEM,
        count,
        flops=EARLY,
    )()


def front_kernel(
    tokens_ref, bias_flat, pre_ref, top_ref, rows_ref, block_ref, count_ref, after_ref, *refs
):
    code_ref, raw_ref, total_ref, sent_ref, centered_ref, bias_ref, *cut = refs
    count, latents = top_ref.shape
    slots, width = rows_ref.shape
    offsets = lax.broadcasted_iota(jnp.int32, (1, slots), 1)
    slot_ids = jnp.where(offsets < count_ref[0], block_ref[0] * slots + offsets, -1)
    top, pre = top_ref[...], pre_ref[...]
    raw = jnp.zeros((count, slots), jnp.float32)
    for k in range(latents):
        raw = jnp.where(top[:, k : k + 1] == slot_ids, pre[:, k : k + 1], raw)
    raw_ref[...] = raw
    code = jnp.maximum(raw, 0.0).astype(jnp.bfloat16)
    code_ref[...] = code

    tokens = tokens_ref[...].astype(jnp.float32)
    bias = bias_flat[...].astype(jnp.float32).reshape(1, width)
    bias_ref[...] = bias
    centered_ref[...] = (tokens - bias).astype(jnp.bfloat16).astype(jnp.float32)

    total = share(code, rows_ref, centered_ref, 0, total_ref.shape[1])
    total_ref[...] = total
    width = total.shape[1]
    sent_ref[:, :width] = total.astype(jnp.bfloat16)
    block = stacked(tokens, ROWS // tokens.shape[0]).astype(jnp.bfloat16)
    if cut:
        cut[0][...] = block
    else:
        sent_ref[:, width:] = block


def front(tokens, b_pre, pre_codes, top_idx, blocks, counts, dict_rows, after, merged):
    count = top_idx.shape[0]
    slots, width = dict_rows.shape
    chunk, block = first_width(width), tokens.shape[0] * width // ROWS
    return kernel_call(
        front_kernel,
        (
            shape(count, slots),
            shape(count, slots, dtype=jnp.float32),
            shape(count, chunk, dtype=jnp.float32),
            shape(count, chunk + (block if merged else 0)),
            shape(*tokens.shape, dtype=jnp.float32),
            shape(1, width, dtype=jnp.float32),
            *([] if merged else [shape(ROWS, block)]),
        ),
        [VMEM] * 5 + [SMEM] * 2 + [ANY],
        (VMEM,) * (6 if merged else 7),
        count,
    )(tokens, b_pre, pre_codes, top_idx, dict_rows, blocks, counts, after)


def second_kernel(code_ref, rows_ref, centered_ref, total_ref, sent_ref):
    width = total_ref.shape[1]
    total = share(code_ref[...], rows_ref, centered_ref, rows_ref.shape[1] - width, width)
    total_ref[...] = total
    sent_ref[...] = total.astype(jnp.bfloat16)


def second(code, dict_rows, centered):
    count, width = code.shape[0], dict_rows.shape[1]
    chunk = width - first_width(width)
    return kernel_call(
        second_kernel,
        (shape(count, chunk, dtype=jnp.float32), shape(count, chunk)),
        [VMEM] * 3,
        (VMEM, VMEM),
        count,
    )(code, dict_rows, centered)


def added_kernel(total_ref, own_ref, arrived_ref, after_ref, sum_ref, sent_ref):
    half = total_ref.shape[1]
    total = total_ref[...] + arrived_ref[:, :half].astype(jnp.float32)
    sum_ref[...] = total
    sent_ref[:, :half] = total.astype(jnp.bfloat16)
    if sent_ref.shape[1] > half:
        block = own_ref.shape[1] - half
        sent_ref[:, half : half + block] = own_ref[:, half:]
        sent_ref[:, half + block :] = arrived_ref[:, half:]


def added(total, own, arrived, after, merged, flops=10**6):
    count, half = total.shape
    block = own.shape[1] - half
    return kernel_call(
        added_kernel,
        (
            shape(count, half, dtype=jnp.float32),
            shape(count, half + (2 * block if merged else 0)),
        ),
        [VMEM] * 3 + [ANY],
        (VMEM, VMEM),
        count,
        flops=flops,
    )(total, own, arrived, after)


def joined_kernel(first_ref, second_ref, after_ref, out_ref):
    width = first_ref.shape[1]
    out_ref[:, :width] = first_ref[...]
    out_ref[:, width:] = second_ref[...]


def joined(first, second, after):
    return kernel_call(
        joined_kernel,
        shape(first.shape[0], 2 * first.shape[1]),
        [VMEM, VMEM, ANY],
        VMEM,
        first.shape[0],
    )(first, second, after)


def turned_kernel(skip, rows, own_ref, arrived_ref, bias_ref, out_ref):
    bias = jnp.concatenate([bias_ref[...]] * rows, axis=0)
    bias = stacked(bias, ROWS // rows)
    width = bias.shape[1]
    blocks = [
        (ref[:, at : at + width].astype(jnp.float32) - bias).astype(jnp.bfloat16)
        for ref in (own_ref, arrived_ref)
        for at in range(skip, ref.shape[1], width)
    ]
    out_ref[...] = jnp.concatenate(blocks, axis=0).astype(jnp.float32).T.astype(jnp.bfloat16)


def turned(own, arrived, skip, bias, rows, count):
    width = bias.shape[1] * rows // ROWS
    return kernel_call(
        functools.partial(turned_kernel, skip, rows),
        shape(width, 2 * (own.shape[1] - skip) // width * ROWS),
        [VMEM] * 3,
        VMEM,
        count,
    )(own, arrived, bias)


def scaled_of(total_ref, arrived_ref):
    total = total_ref[...] + arrived_ref[:, : total_ref.shape[1]].astype(jnp.float32)
    return (0.25 * total).astype(jnp.bfloat16)


def product(part, rows_ref, at):
    return lax.dot_general(
        part,
        rows_ref[:, at : at + part.shape[1]],
        (((1,), (1,)), ((), ())),
        preferred_element_type=jnp.float32,
    )


def first_product_kernel(total_ref, arrived_ref, rows_ref, scaled_ref, half_ref):
    scaled = scaled_of(total_ref, arrived_ref)
    scaled_ref[...] = scaled
    half_ref[...] = product(scaled, rows_ref, 0)


def second_product_kernel(total_ref, arrived_ref, rows_ref, first_ref, scaled_ref, half_ref):
    scaled = scaled_of(total_ref, arrived_ref)
    scaled_ref[...] = scaled
    half_ref[...] = first_ref[...] + product(scaled, rows_ref, rows_ref.shape[1] - scaled.shape[1])


def products(total, arrived, dict_rows, *first):
    count, width = total.shape
    return kernel_call(
        second_product_kernel if first else first_product_kernel,
        (shape(count, width), shape(count, dict_rows.shape[0], dtype=jnp.float32)),
        [VMEM] * (3 + len(first)),
        (VMEM, VMEM),
        count,
    )(total, arrived, dict_rows, *first)


def outer(code_ref, scaled):
    code = code_ref[...].astype(jnp.float32).T.astype(jnp.bfloat16)
    return jnp.dot(code, scaled, preferred_element_type=jnp.float32).astype(jnp.bfloat16)


def grad_rows_kernel(code_ref, first_ref, second_ref, out_ref):
    chunk = first_ref.shape[1]
    out_ref[:, :chunk] = outer(code_ref, first_ref[...])
    out_ref[:, chunk:] = outer(code_ref, second_ref[...])


def grad_rows_of(code, first, second):
    count, slots = code.shape
    return kernel_call(
        grad_rows_kernel,
        shape(slots, first.shape[1] + second.shape[1]),
        [VMEM] * 3,
        VMEM,
        count,
    )(code, first, second)


def final_kernel(
    rows,
    raw_ref,
    mine_ref,
    theirs_ref,
    turned_ref,
    order_ref,
    rows_ref,
    rows_hbm,
    enc_hbm,
    benc_hbm,
    enc_ref,
    benc_ref,
    sems,
):
    copies = [pltpu.make_async_copy(rows_ref, rows_hbm, sems.at[0])]
    copies[0].start()
    count, slots = raw_ref.shape
    width, depth = turned_ref.shape
    pieces = ROWS // rows
    code_grad = mine_ref[...] + theirs_ref[...]
    pre_grad = jnp.where(raw_ref[...] > 0.0, code_grad, 0.0).astype(jnp.bfloat16)
    benc_ref[...] = jnp.sum(pre_grad.astype(jnp.float32), axis=0, keepdims=True)
    copies.append(pltpu.make_async_copy(benc_ref, benc_hbm, sems.at[1]))
    copies[1].start()
    spread = jnp.dot(order_ref[...], pre_grad, preferred_element_type=jnp.float32)
    piece = lax.broadcasted_iota(jnp.int32, (depth, slots), 0) % ROWS // rows
    for c in range(0, pieces, 2):
        pair = [jnp.where(piece == c + i, spread, 0.0).astype(jnp.bfloat16) for i in range(2)]
        out = jnp.dot(
            turned_ref[...],
            jnp.concatenate(pair, axis=1),
            preferred_element_type=jnp.float32,
        ).astype(jnp.bfloat16)
        for i in range(2):
            enc_ref[(c + i) * width : (c + i + 1) * width, :] = out[:, i * slots : (i + 1) * slots]
        part = pl.ds(c * width, 2 * width)
        copies.append(pltpu.make_async_copy(enc_ref.at[part], enc_hbm.at[part], sems.at[c // 2 + 2]))
        copies[-1].start()
    for copy in copies:
        copy.wait()


def final(raw, mine, theirs, turned_tokens, order, grad_rows, rows):
    count, slots = raw.shape
    pieces = ROWS // rows
    width = turned_tokens.shape[0] * pieces
    return kernel_call(
        functools.partial(final_kernel, rows),
        (shape(*grad_rows.shape), shape(width, slots), shape(1, slots, dtype=jnp.float32)),
        [VMEM] * 6,
        (HBM, HBM, HBM),
        count,
        [
            pltpu.VMEM((width, slots), jnp.bfloat16),
            pltpu.VMEM((1, slots), jnp.float32),
            pltpu.SemaphoreType.DMA((pieces // 2 + 2,)),
        ],
    )(raw, mine, theirs, turned_tokens, order, grad_rows)


def local(tokens, b_pre, pre_codes, top_idx, blocks, counts, dict_rows):
    rows, count = tokens.shape[0], top_idx.shape[0]
    steps = feat_bits()
    merged = count == ROWS

    order = order_of(rows, count)
    code, raw, total, sent, centered, bias, *block = front(
        tokens, b_pre, pre_codes, top_idx, blocks, counts, dict_rows, order, merged
    )
    for step in range(steps):
        arrived = swapped(sent, step, 0)
        if step == 0:
            total_second, sent_second = second(code, dict_rows, centered)
        else:
            total_second, sent_second = added(
                total_second, sent_second, arrived_second, sent, False, EARLY
            )
        arrived_second = swapped(sent_second, step, 1)
        if not merged:
            own_block = joined(own_block, arrived_block, sent_second) if step else block[0]
            arrived_block = swapped(own_block, step, 0)
        if step < steps - 1:
            total, sent = added(total, sent, arrived, sent_second, merged)
    skip = 0
    if merged:
        own_block, arrived_block, skip = sent, arrived, total.shape[1]

    scaled, product_first = products(total, arrived, dict_rows)
    turned_tokens = turned(own_block, arrived_block, skip, bias, rows, count)
    scaled_second, code_half = products(
        total_second, arrived_second, dict_rows, product_first
    )
    theirs = lax.ppermute(code_half, "tok", [(i, 1 - i) for i in range(2)])
    grad_rows = grad_rows_of(code, scaled, scaled_second)
    grad_rows, grad_enc, grad_benc = final(
        raw, code_half, theirs, turned_tokens, order, grad_rows, rows
    )
    return (grad_rows, grad_enc, grad_benc.reshape(-1))


def solution(mesh):
    return jax.shard_map(
        local,
        mesh=mesh,
        in_specs=(
            P(("grp", "feat"), "tok"),
            P(("grp", "tok")),
            P("grp", None),
            P("grp", None),
            P(("grp", "feat")),
            P(("grp", "feat")),
            P(("grp", "feat"), "tok"),
        ),
        out_specs=(P(("grp", "feat"), "tok"), P(("grp", "tok"), "feat"), P(("grp", "feat"))),
        check_vma=False,
    )
```

```python
import functools

import jax
import jax.numpy as jnp
from jax import lax
from jax.experimental import pallas as pl
from jax.experimental.pallas import tpu as pltpu
from jax.sharding import PartitionSpec as P

VMEM = pl.BlockSpec(memory_space=pltpu.VMEM)
SMEM = pl.BlockSpec(memory_space=pltpu.SMEM)
HBM = pl.BlockSpec(memory_space=pltpu.HBM)
ANY = pl.BlockSpec(memory_space=pl.ANY)
EARLY = 10**9
ROWS = 16


def kernel_call(kernel, out_shape, in_specs, out_specs, tokens, scratch_shapes=(), flops=10**6):
    limit = (16 if tokens <= ROWS else 40) * 2**20
    return pl.pallas_call(
        kernel,
        out_shape=out_shape,
        in_specs=in_specs,
        out_specs=out_specs,
        scratch_shapes=scratch_shapes,
        compiler_params=pltpu.CompilerParams(vmem_limit_bytes=limit),
        cost_estimate=pl.CostEstimate(flops=flops, bytes_accessed=2**20, transcendentals=0),
    )


def shape(*sizes, dtype=jnp.bfloat16):
    return jax.ShapeDtypeStruct(sizes, dtype)


def first_width(width):
    return width // 2


def feat_bits():
    return (lax.axis_size("feat") - 1).bit_length()


def bit_of(step, core):
    bits = list(range(feat_bits()))
    return (bits[-1:] + bits[:-1] if core == 0 else bits)[step]


def swapped(shard, step):
    cores = lax.axis_size("tok")
    pairs = [
        (f * cores + c, (f ^ 1 << bit_of(step, c)) * cores + c)
        for f in range(lax.axis_size("feat"))
        for c in range(cores)
    ]
    return lax.ppermute(shard, ("feat", "tok"), pairs)


def stacked(rows, pieces):
    width = rows.shape[1] // pieces
    return jnp.concatenate(
        [rows[:, c * width : (c + 1) * width] for c in range(pieces)], axis=0
    )


def share(code, rows_ref, centered_ref, at, width):
    part = pl.ds(at, width)
    total = jnp.dot(code, rows_ref[:, part], preferred_element_type=jnp.float32)
    rows = centered_ref.shape[0]
    centered = centered_ref[:, part]
    token = lax.broadcasted_iota(jnp.int32, (total.shape[0], 1), 0)
    first = lax.axis_index("feat") * rows
    for i in range(rows):
        total -= jnp.where(token == first + i, centered[i : i + 1, :], 0.0)
    return total


def order_kernel(rows, order_ref):
    target = lax.broadcasted_iota(jnp.int32, order_ref.shape, 0)
    place = lax.broadcasted_iota(jnp.int32, order_ref.shape, 1)
    core = lax.axis_index("tok")
    block = place // ROWS
    distance = jnp.zeros_like(place)
    for step in range(feat_bits()):
        bit = sum(
            jnp.where(core == c, bit_of(step, c), 0) for c in range(lax.axis_size("tok"))
        )
        distance |= (block >> step & 1) << bit
    token = (lax.axis_index("feat") ^ distance) * rows + place % rows
    piece = place % ROWS // rows
    count = rows * lax.axis_size("feat")
    order_ref[...] = jnp.where(target == piece * count + token, 1.0, 0.0).astype(jnp.bfloat16)


def order_of(rows, count):
    depth = ROWS * lax.axis_size("feat")
    return kernel_call(
        functools.partial(order_kernel, rows),
        shape(depth, depth),
        [],
        VMEM,
        count,
        flops=EARLY,
    )()


def front_kernel(
    tokens_ref, bias_flat, pre_ref, top_ref, rows_ref, block_ref, count_ref, after_ref, *refs
):
    code_ref, raw_ref, total_ref, sent_ref, centered_ref, bias_ref, *cut = refs
    count, latents = top_ref.shape
    slots, width = rows_ref.shape
    offsets = lax.broadcasted_iota(jnp.int32, (1, slots), 1)
    slot_ids = jnp.where(offsets < count_ref[0], block_ref[0] * slots + offsets, -1)
    top, pre = top_ref[...], pre_ref[...]
    raw = jnp.zeros((count, slots), jnp.float32)
    for k in range(latents):
        raw = jnp.where(top[:, k : k + 1] == slot_ids, pre[:, k : k + 1], raw)
    raw_ref[...] = raw
    code = jnp.maximum(raw, 0.0).astype(jnp.bfloat16)
    code_ref[...] = code

    tokens = tokens_ref[...].astype(jnp.float32)
    bias = bias_flat[...].astype(jnp.float32).reshape(1, width)
    bias_ref[...] = bias
    centered_ref[...] = (tokens - bias).astype(jnp.bfloat16).astype(jnp.float32)

    total = share(code, rows_ref, centered_ref, 0, total_ref.shape[1])
    total_ref[...] = total
    width = total.shape[1]
    sent_ref[:, :width] = total.astype(jnp.bfloat16)
    block = stacked(tokens, ROWS // tokens.shape[0]).astype(jnp.bfloat16)
    if cut:
        cut[0][...] = block
    else:
        sent_ref[:, width:] = block


def front(tokens, b_pre, pre_codes, top_idx, blocks, counts, dict_rows, after, merged):
    count = top_idx.shape[0]
    slots, width = dict_rows.shape
    chunk, block = first_width(width), tokens.shape[0] * width // ROWS
    return kernel_call(
        front_kernel,
        (
            shape(count, slots),
            shape(count, slots, dtype=jnp.float32),
            shape(count, chunk, dtype=jnp.float32),
            shape(count, chunk + (block if merged else 0)),
            shape(*tokens.shape, dtype=jnp.float32),
            shape(1, width, dtype=jnp.float32),
            *([] if merged else [shape(ROWS, block)]),
        ),
        [VMEM] * 5 + [SMEM] * 2 + [ANY],
        (VMEM,) * (6 if merged else 7),
        count,
    )(tokens, b_pre, pre_codes, top_idx, dict_rows, blocks, counts, after)


def second_kernel(code_ref, rows_ref, centered_ref, total_ref, sent_ref):
    width = total_ref.shape[1]
    total = share(code_ref[...], rows_ref, centered_ref, rows_ref.shape[1] - width, width)
    total_ref[...] = total
    sent_ref[...] = total.astype(jnp.bfloat16)


def second(code, dict_rows, centered):
    count, width = code.shape[0], dict_rows.shape[1]
    chunk = width - first_width(width)
    return kernel_call(
        second_kernel,
        (shape(count, chunk, dtype=jnp.float32), shape(count, chunk)),
        [VMEM] * 3,
        (VMEM, VMEM),
        count,
    )(code, dict_rows, centered)


def added_kernel(total_ref, own_ref, arrived_ref, after_ref, sum_ref, sent_ref):
    half = total_ref.shape[1]
    total = total_ref[...] + arrived_ref[:, :half].astype(jnp.float32)
    sum_ref[...] = total
    sent_ref[:, :half] = total.astype(jnp.bfloat16)
    if sent_ref.shape[1] > half:
        block = own_ref.shape[1] - half
        sent_ref[:, half : half + block] = own_ref[:, half:]
        sent_ref[:, half + block :] = arrived_ref[:, half:]


def added(total, own, arrived, after, merged, flops=10**6):
    count, half = total.shape
    block = own.shape[1] - half
    return kernel_call(
        added_kernel,
        (
            shape(count, half, dtype=jnp.float32),
            shape(count, half + (2 * block if merged else 0)),
        ),
        [VMEM] * 3 + [ANY],
        (VMEM, VMEM),
        count,
        flops=flops,
    )(total, own, arrived, after)


def joined_kernel(first_ref, second_ref, after_ref, out_ref):
    width = first_ref.shape[1]
    out_ref[:, :width] = first_ref[...]
    out_ref[:, width:] = second_ref[...]


def joined(first, second, after):
    return kernel_call(
        joined_kernel,
        shape(first.shape[0], 2 * first.shape[1]),
        [VMEM, VMEM, ANY],
        VMEM,
        first.shape[0],
    )(first, second, after)


def turned_kernel(skip, rows, own_ref, arrived_ref, bias_ref, order_ref, out_ref):
    bias = jnp.concatenate([bias_ref[...]] * rows, axis=0)
    bias = stacked(bias, ROWS // rows)
    width = bias.shape[1]
    blocks = [
        (ref[:, at : at + width].astype(jnp.float32) - bias).astype(jnp.bfloat16)
        for ref in (own_ref, arrived_ref)
        for at in range(skip, ref.shape[1], width)
    ]
    ordered = jnp.dot(
        order_ref[...], jnp.concatenate(blocks, axis=0), preferred_element_type=jnp.float32
    )
    out_ref[...] = ordered.T.astype(jnp.bfloat16)


def turned(own, arrived, skip, bias, order, rows, count):
    width = bias.shape[1] * rows // ROWS
    return kernel_call(
        functools.partial(turned_kernel, skip, rows),
        shape(width, 2 * (own.shape[1] - skip) // width * ROWS),
        [VMEM] * 4,
        VMEM,
        count,
    )(own, arrived, bias, order)


def scaled_of(total_ref, arrived_ref):
    total = total_ref[...] + arrived_ref[:, : total_ref.shape[1]].astype(jnp.float32)
    return (0.25 * total).astype(jnp.bfloat16)


def product(part, rows_ref, at):
    return lax.dot_general(
        part,
        rows_ref[:, at : at + part.shape[1]],
        (((1,), (1,)), ((), ())),
        preferred_element_type=jnp.float32,
    )


def first_product_kernel(total_ref, arrived_ref, rows_ref, scaled_ref, half_ref):
    scaled = scaled_of(total_ref, arrived_ref)
    scaled_ref[...] = scaled
    half_ref[...] = product(scaled, rows_ref, 0)


def second_product_kernel(total_ref, arrived_ref, rows_ref, first_ref, scaled_ref, half_ref):
    scaled = scaled_of(total_ref, arrived_ref)
    scaled_ref[...] = scaled
    half_ref[...] = first_ref[...] + product(scaled, rows_ref, rows_ref.shape[1] - scaled.shape[1])


def products(total, arrived, dict_rows, *first):
    count, width = total.shape
    return kernel_call(
        second_product_kernel if first else first_product_kernel,
        (shape(count, width), shape(count, dict_rows.shape[0], dtype=jnp.float32)),
        [VMEM] * (3 + len(first)),
        (VMEM, VMEM),
        count,
    )(total, arrived, dict_rows, *first)


def outer(code_ref, scaled):
    code = code_ref[...].astype(jnp.float32).T.astype(jnp.bfloat16)
    return jnp.dot(code, scaled, preferred_element_type=jnp.float32).astype(jnp.bfloat16)


def grad_rows_kernel(code_ref, first_ref, second_ref, out_ref):
    chunk = first_ref.shape[1]
    out_ref[:, :chunk] = outer(code_ref, first_ref[...])
    out_ref[:, chunk:] = outer(code_ref, second_ref[...])


def grad_rows_of(code, first, second):
    count, slots = code.shape
    return kernel_call(
        grad_rows_kernel,
        shape(slots, first.shape[1] + second.shape[1]),
        [VMEM] * 3,
        VMEM,
        count,
    )(code, first, second)


def final_kernel(
    rows,
    raw_ref,
    mine_ref,
    theirs_ref,
    turned_ref,
    rows_ref,
    rows_hbm,
    enc_hbm,
    benc_hbm,
    enc_ref,
    benc_ref,
    sems,
):
    copies = [pltpu.make_async_copy(rows_ref, rows_hbm, sems.at[0])]
    copies[0].start()
    count, slots = raw_ref.shape
    width = turned_ref.shape[0]
    pieces = ROWS // rows
    code_grad = mine_ref[...] + theirs_ref[...]
    pre_grad = jnp.where(raw_ref[...] > 0.0, code_grad, 0.0).astype(jnp.bfloat16)
    benc_ref[...] = jnp.sum(pre_grad.astype(jnp.float32), axis=0, keepdims=True)
    copies.append(pltpu.make_async_copy(benc_ref, benc_hbm, sems.at[1]))
    copies[1].start()
    zeros = jnp.zeros_like(pre_grad)
    for c in range(0, pieces, 2):
        pair = [
            jnp.concatenate([zeros] * at + [pre_grad] + [zeros] * (pieces - 1 - at), axis=0)
            for at in (c, c + 1)
        ]
        out = jnp.dot(
            turned_ref[...],
            jnp.concatenate(pair, axis=1),
            preferred_element_type=jnp.float32,
        ).astype(jnp.bfloat16)
        for i in range(2):
            enc_ref[(c + i) * width : (c + i + 1) * width, :] = out[:, i * slots : (i + 1) * slots]
        part = pl.ds(c * width, 2 * width)
        copies.append(pltpu.make_async_copy(enc_ref.at[part], enc_hbm.at[part], sems.at[c // 2 + 2]))
        copies[-1].start()
    for copy in copies:
        copy.wait()


def final(raw, mine, theirs, turned_tokens, grad_rows, rows):
    count, slots = raw.shape
    pieces = ROWS // rows
    width = turned_tokens.shape[0] * pieces
    return kernel_call(
        functools.partial(final_kernel, rows),
        (shape(*grad_rows.shape), shape(width, slots), shape(1, slots, dtype=jnp.float32)),
        [VMEM] * 5,
        (HBM, HBM, HBM),
        count,
        [
            pltpu.VMEM((width, slots), jnp.bfloat16),
            pltpu.VMEM((1, slots), jnp.float32),
            pltpu.SemaphoreType.DMA((pieces // 2 + 2,)),
        ],
    )(raw, mine, theirs, turned_tokens, grad_rows)


def local(tokens, b_pre, pre_codes, top_idx, blocks, counts, dict_rows):
    rows, count = tokens.shape[0], top_idx.shape[0]
    steps = feat_bits()
    merged = count == ROWS

    order = order_of(rows, count)
    code, raw, total, sent, centered, bias, *block = front(
        tokens, b_pre, pre_codes, top_idx, blocks, counts, dict_rows, order, merged
    )
    for step in range(steps):
        arrived = swapped(sent, step)
        if step == 0:
            total_second, sent_second = second(code, dict_rows, centered)
        else:
            total_second, sent_second = added(
                total_second, sent_second, arrived_second, sent, False, EARLY
            )
        arrived_second = swapped(sent_second, step)
        if not merged:
            own_block = joined(own_block, arrived_block, sent_second) if step else block[0]
            arrived_block = swapped(own_block, step)
        if step < steps - 1:
            total, sent = added(total, sent, arrived, sent_second, merged)
    skip = 0
    if merged:
        own_block, arrived_block, skip = sent, arrived, total.shape[1]

    scaled, product_first = products(total, arrived, dict_rows)
    turned_tokens = turned(own_block, arrived_block, skip, bias, order, rows, count)
    scaled_second, code_half = products(
        total_second, arrived_second, dict_rows, product_first
    )
    theirs = lax.ppermute(code_half, "tok", [(i, 1 - i) for i in range(2)])
    grad_rows = grad_rows_of(code, scaled, scaled_second)
    grad_rows, grad_enc, grad_benc = final(
        raw, code_half, theirs, turned_tokens, grad_rows, rows
    )
    return (grad_rows, grad_enc, grad_benc.reshape(-1))


def solution(mesh):
    return jax.shard_map(
        local,
        mesh=mesh,
        in_specs=(
            P(("grp", "feat"), "tok"),
            P(("grp", "tok")),
            P("grp", None),
            P("grp", None),
            P(("grp", "feat")),
            P(("grp", "feat")),
            P(("grp", "feat"), "tok"),
        ),
        out_specs=(P(("grp", "feat"), "tok"), P(("grp", "tok"), "feat"), P(("grp", "feat"))),
        check_vma=False,
    )
```

```python
import functools

import jax
import jax.numpy as jnp
from jax import lax
from jax.experimental import pallas as pl
from jax.experimental.pallas import tpu as pltpu
from jax.sharding import PartitionSpec as P

VMEM = pl.BlockSpec(memory_space=pltpu.VMEM)
SMEM = pl.BlockSpec(memory_space=pltpu.SMEM)
HBM = pl.BlockSpec(memory_space=pltpu.HBM)
ANY = pl.BlockSpec(memory_space=pl.ANY)
EARLY = 10**9
ROWS = 16


def kernel_call(kernel, out_shape, in_specs, out_specs, tokens, scratch_shapes=(), flops=10**6):
    limit = (16 if tokens <= ROWS else 40) * 2**20
    return pl.pallas_call(
        kernel,
        out_shape=out_shape,
        in_specs=in_specs,
        out_specs=out_specs,
        scratch_shapes=scratch_shapes,
        compiler_params=pltpu.CompilerParams(vmem_limit_bytes=limit),
        cost_estimate=pl.CostEstimate(flops=flops, bytes_accessed=2**20, transcendentals=0),
    )


def shape(*sizes, dtype=jnp.bfloat16):
    return jax.ShapeDtypeStruct(sizes, dtype)


def first_width(width):
    return width // 2


def feat_bits():
    return (lax.axis_size("feat") - 1).bit_length()


def bit_of(step, core):
    bits = list(range(feat_bits()))
    return (bits[-1:] + bits[:-1] if core == 0 else bits)[step]


def swapped(shard, step):
    cores = lax.axis_size("tok")
    pairs = [
        (f * cores + c, (f ^ 1 << bit_of(step, c)) * cores + c)
        for f in range(lax.axis_size("feat"))
        for c in range(cores)
    ]
    return lax.ppermute(shard, ("feat", "tok"), pairs)


def stacked(rows, pieces):
    width = rows.shape[1] // pieces
    return jnp.concatenate(
        [rows[:, c * width : (c + 1) * width] for c in range(pieces)], axis=0
    )


def share(code, rows_ref, centered_ref, at, width):
    part = pl.ds(at, width)
    total = jnp.dot(code, rows_ref[:, part], preferred_element_type=jnp.float32)
    rows = centered_ref.shape[0]
    centered = centered_ref[:, part]
    token = lax.broadcasted_iota(jnp.int32, (total.shape[0], 1), 0)
    first = lax.axis_index("feat") * rows
    for i in range(rows):
        total -= jnp.where(token == first + i, centered[i : i + 1, :], 0.0)
    return total


def order_kernel(rows, order_ref):
    target = lax.broadcasted_iota(jnp.int32, order_ref.shape, 0)
    place = lax.broadcasted_iota(jnp.int32, order_ref.shape, 1)
    core = lax.axis_index("tok")
    block = place // ROWS
    distance = jnp.zeros_like(place)
    for step in range(feat_bits()):
        bit = sum(
            jnp.where(core == c, bit_of(step, c), 0) for c in range(lax.axis_size("tok"))
        )
        distance |= (block >> step & 1) << bit
    token = (lax.axis_index("feat") ^ distance) * rows + place % rows
    piece = place % ROWS // rows
    count = rows * lax.axis_size("feat")
    order_ref[...] = jnp.where(target == piece * count + token, 1.0, 0.0).astype(jnp.bfloat16)


def order_of(rows, count):
    depth = ROWS * lax.axis_size("feat")
    return kernel_call(
        functools.partial(order_kernel, rows),
        shape(depth, depth),
        [],
        VMEM,
        count,
        flops=EARLY,
    )()


def front_kernel(
    tokens_ref, bias_flat, pre_ref, top_ref, rows_ref, block_ref, count_ref, after_ref, *refs
):
    code_ref, raw_ref, total_ref, sent_ref, centered_ref, bias_ref, *cut = refs
    count, latents = top_ref.shape
    slots, width = rows_ref.shape
    offsets = lax.broadcasted_iota(jnp.int32, (1, slots), 1)
    slot_ids = jnp.where(offsets < count_ref[0], block_ref[0] * slots + offsets, -1)
    top, pre = top_ref[...], pre_ref[...]
    raw = jnp.zeros((count, slots), jnp.float32)
    for k in range(latents):
        raw = jnp.where(top[:, k : k + 1] == slot_ids, pre[:, k : k + 1], raw)
    raw_ref[...] = raw
    code = jnp.maximum(raw, 0.0).astype(jnp.bfloat16)
    code_ref[...] = code

    tokens = tokens_ref[...].astype(jnp.float32)
    bias = bias_flat[...].astype(jnp.float32).reshape(1, width)
    bias_ref[...] = bias
    centered_ref[...] = (tokens - bias).astype(jnp.bfloat16).astype(jnp.float32)

    total = share(code, rows_ref, centered_ref, 0, total_ref.shape[1])
    total_ref[...] = total
    width = total.shape[1]
    sent_ref[:, :width] = total.astype(jnp.bfloat16)
    block = stacked(tokens, ROWS // tokens.shape[0]).astype(jnp.bfloat16)
    if cut:
        cut[0][...] = block
    else:
        sent_ref[:, width:] = block


def front(tokens, b_pre, pre_codes, top_idx, blocks, counts, dict_rows, after, merged):
    count = top_idx.shape[0]
    slots, width = dict_rows.shape
    chunk, block = first_width(width), tokens.shape[0] * width // ROWS
    return kernel_call(
        front_kernel,
        (
            shape(count, slots),
            shape(count, slots, dtype=jnp.float32),
            shape(count, chunk, dtype=jnp.float32),
            shape(count, chunk + (block if merged else 0)),
            shape(*tokens.shape, dtype=jnp.float32),
            shape(1, width, dtype=jnp.float32),
            *([] if merged else [shape(ROWS, block)]),
        ),
        [VMEM] * 5 + [SMEM] * 2 + [ANY],
        (VMEM,) * (6 if merged else 7),
        count,
    )(tokens, b_pre, pre_codes, top_idx, dict_rows, blocks, counts, after)


def second_kernel(code_ref, rows_ref, centered_ref, total_ref, sent_ref):
    width = total_ref.shape[1]
    total = share(code_ref[...], rows_ref, centered_ref, rows_ref.shape[1] - width, width)
    total_ref[...] = total
    sent_ref[...] = total.astype(jnp.bfloat16)


def second(code, dict_rows, centered):
    count, width = code.shape[0], dict_rows.shape[1]
    chunk = width - first_width(width)
    return kernel_call(
        second_kernel,
        (shape(count, chunk, dtype=jnp.float32), shape(count, chunk)),
        [VMEM] * 3,
        (VMEM, VMEM),
        count,
    )(code, dict_rows, centered)


def added_kernel(total_ref, own_ref, arrived_ref, after_ref, sum_ref, sent_ref):
    half = total_ref.shape[1]
    total = total_ref[...] + arrived_ref[:, :half].astype(jnp.float32)
    sum_ref[...] = total
    sent_ref[:, :half] = total.astype(jnp.bfloat16)
    if sent_ref.shape[1] > half:
        block = own_ref.shape[1] - half
        sent_ref[:, half : half + block] = own_ref[:, half:]
        sent_ref[:, half + block :] = arrived_ref[:, half:]


def added(total, own, arrived, after, merged, flops=10**6):
    count, half = total.shape
    block = own.shape[1] - half
    return kernel_call(
        added_kernel,
        (
            shape(count, half, dtype=jnp.float32),
            shape(count, half + (2 * block if merged else 0)),
        ),
        [VMEM] * 3 + [ANY],
        (VMEM, VMEM),
        count,
        flops=flops,
    )(total, own, arrived, after)


def joined_kernel(first_ref, second_ref, after_ref, out_ref):
    width = first_ref.shape[1]
    out_ref[:, :width] = first_ref[...]
    out_ref[:, width:] = second_ref[...]


def joined(first, second, after):
    return kernel_call(
        joined_kernel,
        shape(first.shape[0], 2 * first.shape[1]),
        [VMEM, VMEM, ANY],
        VMEM,
        first.shape[0],
    )(first, second, after)


def turned_kernel(skip, rows, own_ref, arrived_ref, bias_ref, order_ref, out_ref):
    bias = jnp.concatenate([bias_ref[...]] * rows, axis=0)
    bias = stacked(bias, ROWS // rows)
    width = bias.shape[1]
    blocks = [
        (ref[:, at : at + width].astype(jnp.float32) - bias).astype(jnp.bfloat16)
        for ref in (own_ref, arrived_ref)
        for at in range(skip, ref.shape[1], width)
    ]
    ordered = jnp.dot(
        order_ref[...], jnp.concatenate(blocks, axis=0), preferred_element_type=jnp.float32
    )
    out_ref[...] = ordered.T.astype(jnp.bfloat16)


def turned(own, arrived, skip, bias, order, rows, count):
    width = bias.shape[1] * rows // ROWS
    return kernel_call(
        functools.partial(turned_kernel, skip, rows),
        shape(width, 2 * (own.shape[1] - skip) // width * ROWS),
        [VMEM] * 4,
        VMEM,
        count,
    )(own, arrived, bias, order)


def scaled_of(total_ref, arrived_ref):
    total = total_ref[...] + arrived_ref[:, : total_ref.shape[1]].astype(jnp.float32)
    return (0.25 * total).astype(jnp.bfloat16)


def product(part, rows_ref, at):
    return lax.dot_general(
        part,
        rows_ref[:, at : at + part.shape[1]],
        (((1,), (1,)), ((), ())),
        preferred_element_type=jnp.float32,
    )


def first_product_kernel(total_ref, arrived_ref, rows_ref, scaled_ref, half_ref):
    scaled = scaled_of(total_ref, arrived_ref)
    scaled_ref[...] = scaled
    half_ref[...] = product(scaled, rows_ref, 0)


def second_product_kernel(
    total_ref, arrived_ref, rows_ref, first_ref, after_ref, scaled_ref, half_ref
):
    scaled = scaled_of(total_ref, arrived_ref)
    scaled_ref[...] = scaled
    half_ref[...] = first_ref[...] + product(scaled, rows_ref, rows_ref.shape[1] - scaled.shape[1])


def products(total, arrived, dict_rows, *first):
    count, width = total.shape
    return kernel_call(
        second_product_kernel if first else first_product_kernel,
        (shape(count, width), shape(count, dict_rows.shape[0], dtype=jnp.float32)),
        [VMEM] * 3 + ([VMEM, ANY] if first else []),
        (VMEM, VMEM),
        count,
    )(total, arrived, dict_rows, *first)


def outer(code_ref, scaled):
    code = code_ref[...].astype(jnp.float32).T.astype(jnp.bfloat16)
    return jnp.dot(code, scaled, preferred_element_type=jnp.float32).astype(jnp.bfloat16)


def grad_rows_kernel(code_ref, first_ref, second_ref, out_hbm, out_ref, sems):
    at = 0
    copies = []
    for i, ref in enumerate((first_ref, second_ref)):
        part = pl.ds(at, ref.shape[1])
        out_ref[:, part] = outer(code_ref, ref[...])
        copies.append(
            pltpu.make_async_copy(out_ref.at[:, part], out_hbm.at[:, part], sems.at[i])
        )
        copies[-1].start()
        at += ref.shape[1]
    for copy in copies:
        copy.wait()


def grad_rows_of(code, first, second):
    count, slots = code.shape
    width = first.shape[1] + second.shape[1]
    return kernel_call(
        grad_rows_kernel,
        shape(slots, width),
        [VMEM] * 3,
        HBM,
        count,
        [pltpu.VMEM((slots, width), jnp.bfloat16), pltpu.SemaphoreType.DMA((2,))],
    )(code, first, second)


def final_kernel(
    rows,
    raw_ref,
    mine_ref,
    theirs_ref,
    turned_ref,
    enc_hbm,
    benc_hbm,
    enc_ref,
    benc_ref,
    sems,
):
    count, slots = raw_ref.shape
    width = turned_ref.shape[0]
    pieces = ROWS // rows
    code_grad = mine_ref[...] + theirs_ref[...]
    pre_grad = jnp.where(raw_ref[...] > 0.0, code_grad, 0.0).astype(jnp.bfloat16)
    benc_ref[...] = jnp.sum(pre_grad.astype(jnp.float32), axis=0, keepdims=True)
    copies = [pltpu.make_async_copy(benc_ref, benc_hbm, sems.at[0])]
    copies[0].start()
    zeros = jnp.zeros_like(pre_grad)
    group = pieces // 2
    for c in range(0, pieces, group):
        placed = [
            jnp.concatenate([zeros] * at + [pre_grad] + [zeros] * (pieces - 1 - at), axis=0)
            for at in range(c, c + group)
        ]
        out = jnp.dot(
            turned_ref[...],
            jnp.concatenate(placed, axis=1),
            preferred_element_type=jnp.float32,
        ).astype(jnp.bfloat16)
        for i in range(group):
            enc_ref[(c + i) * width : (c + i + 1) * width, :] = out[:, i * slots : (i + 1) * slots]
        for i in range(0, group, 2):
            part = pl.ds((c + i) * width, 2 * width)
            copies.append(
                pltpu.make_async_copy(enc_ref.at[part], enc_hbm.at[part], sems.at[(c + i) // 2 + 1])
            )
            copies[-1].start()
    for copy in copies:
        copy.wait()


def final(raw, mine, theirs, turned_tokens, rows):
    count, slots = raw.shape
    pieces = ROWS // rows
    width = turned_tokens.shape[0] * pieces
    return kernel_call(
        functools.partial(final_kernel, rows),
        (shape(width, slots), shape(1, slots, dtype=jnp.float32)),
        [VMEM] * 4,
        (HBM, HBM),
        count,
        [
            pltpu.VMEM((width, slots), jnp.bfloat16),
            pltpu.VMEM((1, slots), jnp.float32),
            pltpu.SemaphoreType.DMA((pieces // 2 + 1,)),
        ],
    )(raw, mine, theirs, turned_tokens)


def local(tokens, b_pre, pre_codes, top_idx, blocks, counts, dict_rows):
    rows, count = tokens.shape[0], top_idx.shape[0]
    steps = feat_bits()
    merged = count == ROWS

    order = order_of(rows, count)
    code, raw, total, sent, centered, bias, *block = front(
        tokens, b_pre, pre_codes, top_idx, blocks, counts, dict_rows, order, merged
    )
    for step in range(steps):
        arrived = swapped(sent, step)
        if step == 0:
            total_second, sent_second = second(code, dict_rows, centered)
        else:
            total_second, sent_second = added(
                total_second, sent_second, arrived_second, sent, False, EARLY
            )
        arrived_second = swapped(sent_second, step)
        if not merged:
            own_block = joined(own_block, arrived_block, sent_second) if step else block[0]
            arrived_block = swapped(own_block, step)
        if step < steps - 1:
            total, sent = added(total, sent, arrived, sent_second, merged)
    skip = 0
    if merged:
        own_block, arrived_block, skip = sent, arrived, total.shape[1]

    scaled, product_first = products(total, arrived, dict_rows)
    turned_tokens = turned(own_block, arrived_block, skip, bias, order, rows, count)
    scaled_second, code_half = products(
        total_second, arrived_second, dict_rows, product_first, turned_tokens
    )
    theirs = lax.ppermute(code_half, "tok", [(i, 1 - i) for i in range(2)])
    grad_rows = grad_rows_of(code, scaled, scaled_second)
    grad_enc, grad_benc = final(raw, code_half, theirs, turned_tokens, rows)
    return (grad_rows, grad_enc, grad_benc.reshape(-1))


def solution(mesh):
    return jax.shard_map(
        local,
        mesh=mesh,
        in_specs=(
            P(("grp", "feat"), "tok"),
            P(("grp", "tok")),
            P("grp", None),
            P("grp", None),
            P(("grp", "feat")),
            P(("grp", "feat")),
            P(("grp", "feat"), "tok"),
        ),
        out_specs=(P(("grp", "feat"), "tok"), P(("grp", "tok"), "feat"), P(("grp", "feat"))),
        check_vma=False,
    )
```

```python
import functools

import jax
import jax.numpy as jnp
from jax import lax
from jax.experimental import pallas as pl
from jax.experimental.pallas import tpu as pltpu
from jax.sharding import PartitionSpec as P

VMEM = pl.BlockSpec(memory_space=pltpu.VMEM)
SMEM = pl.BlockSpec(memory_space=pltpu.SMEM)
HBM = pl.BlockSpec(memory_space=pltpu.HBM)
ANY = pl.BlockSpec(memory_space=pl.ANY)
EARLY = 10**9
ROWS = 16


def kernel_call(kernel, out_shape, in_specs, out_specs, tokens, scratch_shapes=(), flops=10**6):
    limit = (16 if tokens <= ROWS else 40) * 2**20
    return pl.pallas_call(
        kernel,
        out_shape=out_shape,
        in_specs=in_specs,
        out_specs=out_specs,
        scratch_shapes=scratch_shapes,
        compiler_params=pltpu.CompilerParams(vmem_limit_bytes=limit),
        cost_estimate=pl.CostEstimate(flops=flops, bytes_accessed=2**20, transcendentals=0),
    )


def shape(*sizes, dtype=jnp.bfloat16):
    return jax.ShapeDtypeStruct(sizes, dtype)


def first_width(width):
    return width // 2


def feat_bits():
    return (lax.axis_size("feat") - 1).bit_length()


def bit_of(step, core):
    bits = list(range(feat_bits()))
    return (bits[-1:] + bits[:-1] if core == 0 else bits[:1] + bits[:0:-1])[step]


def swapped(shard, step):
    cores = lax.axis_size("tok")
    pairs = [
        (f * cores + c, (f ^ 1 << bit_of(step, c)) * cores + c)
        for f in range(lax.axis_size("feat"))
        for c in range(cores)
    ]
    return lax.ppermute(shard, ("feat", "tok"), pairs)


def stacked(rows, pieces):
    width = rows.shape[1] // pieces
    return jnp.concatenate(
        [rows[:, c * width : (c + 1) * width] for c in range(pieces)], axis=0
    )


def share(code, rows_ref, centered_ref, at, width):
    part = pl.ds(at, width)
    total = jnp.dot(code, rows_ref[:, part], preferred_element_type=jnp.float32)
    rows = centered_ref.shape[0]
    centered = centered_ref[:, part]
    token = lax.broadcasted_iota(jnp.int32, (total.shape[0], 1), 0)
    first = lax.axis_index("feat") * rows
    for i in range(rows):
        total -= jnp.where(token == first + i, centered[i : i + 1, :], 0.0)
    return total


def order_kernel(rows, order_ref):
    target = lax.broadcasted_iota(jnp.int32, order_ref.shape, 0)
    place = lax.broadcasted_iota(jnp.int32, order_ref.shape, 1)
    core = lax.axis_index("tok")
    block = place // ROWS
    distance = jnp.zeros_like(place)
    for step in range(feat_bits()):
        bit = sum(
            jnp.where(core == c, bit_of(step, c), 0) for c in range(lax.axis_size("tok"))
        )
        distance |= (block >> step & 1) << bit
    token = (lax.axis_index("feat") ^ distance) * rows + place % rows
    piece = place % ROWS // rows
    count = rows * lax.axis_size("feat")
    order_ref[...] = jnp.where(target == piece * count + token, 1.0, 0.0).astype(jnp.bfloat16)


def order_of(rows, count):
    depth = ROWS * lax.axis_size("feat")
    return kernel_call(
        functools.partial(order_kernel, rows),
        shape(depth, depth),
        [],
        VMEM,
        count,
        flops=EARLY,
    )()


def front_kernel(
    tokens_ref, bias_flat, pre_ref, top_ref, rows_ref, block_ref, count_ref, after_ref, *refs
):
    code_ref, raw_ref, total_ref, sent_ref, centered_ref, bias_ref, *cut = refs
    count, latents = top_ref.shape
    slots, width = rows_ref.shape
    offsets = lax.broadcasted_iota(jnp.int32, (1, slots), 1)
    slot_ids = jnp.where(offsets < count_ref[0], block_ref[0] * slots + offsets, -1)
    top, pre = top_ref[...], pre_ref[...]
    raw = jnp.zeros((count, slots), jnp.float32)
    for k in range(latents):
        raw = jnp.where(top[:, k : k + 1] == slot_ids, pre[:, k : k + 1], raw)
    raw_ref[...] = raw
    code = jnp.maximum(raw, 0.0).astype(jnp.bfloat16)
    code_ref[...] = code

    tokens = tokens_ref[...].astype(jnp.float32)
    bias = bias_flat[...].astype(jnp.float32).reshape(1, width)
    bias_ref[...] = bias
    centered_ref[...] = (tokens - bias).astype(jnp.bfloat16).astype(jnp.float32)

    total = share(code, rows_ref, centered_ref, 0, total_ref.shape[1])
    total_ref[...] = total
    width = total.shape[1]
    sent_ref[:, :width] = total.astype(jnp.bfloat16)
    block = stacked(tokens, ROWS // tokens.shape[0]).astype(jnp.bfloat16)
    if cut:
        cut[0][...] = block
    else:
        sent_ref[:, width:] = block


def front(tokens, b_pre, pre_codes, top_idx, blocks, counts, dict_rows, after, merged):
    count = top_idx.shape[0]
    slots, width = dict_rows.shape
    chunk, block = first_width(width), tokens.shape[0] * width // ROWS
    return kernel_call(
        front_kernel,
        (
            shape(count, slots),
            shape(count, slots, dtype=jnp.float32),
            shape(count, chunk, dtype=jnp.float32),
            shape(count, chunk + (block if merged else 0)),
            shape(*tokens.shape, dtype=jnp.float32),
            shape(1, width, dtype=jnp.float32),
            *([] if merged else [shape(ROWS, block)]),
        ),
        [VMEM] * 5 + [SMEM] * 2 + [ANY],
        (VMEM,) * (6 if merged else 7),
        count,
    )(tokens, b_pre, pre_codes, top_idx, dict_rows, blocks, counts, after)


def second_kernel(code_ref, rows_ref, centered_ref, total_ref, sent_ref):
    width = total_ref.shape[1]
    total = share(code_ref[...], rows_ref, centered_ref, rows_ref.shape[1] - width, width)
    total_ref[...] = total
    sent_ref[...] = total.astype(jnp.bfloat16)


def second(code, dict_rows, centered):
    count, width = code.shape[0], dict_rows.shape[1]
    chunk = width - first_width(width)
    return kernel_call(
        second_kernel,
        (shape(count, chunk, dtype=jnp.float32), shape(count, chunk)),
        [VMEM] * 3,
        (VMEM, VMEM),
        count,
    )(code, dict_rows, centered)


def added_kernel(total_ref, own_ref, arrived_ref, after_ref, sum_ref, sent_ref):
    half = total_ref.shape[1]
    total = total_ref[...] + arrived_ref[:, :half].astype(jnp.float32)
    sum_ref[...] = total
    sent_ref[:, :half] = total.astype(jnp.bfloat16)
    if sent_ref.shape[1] > half:
        block = own_ref.shape[1] - half
        sent_ref[:, half : half + block] = own_ref[:, half:]
        sent_ref[:, half + block :] = arrived_ref[:, half:]


def added(total, own, arrived, after, merged, flops=10**6):
    count, half = total.shape
    block = own.shape[1] - half
    return kernel_call(
        added_kernel,
        (
            shape(count, half, dtype=jnp.float32),
            shape(count, half + (2 * block if merged else 0)),
        ),
        [VMEM] * 3 + [ANY],
        (VMEM, VMEM),
        count,
        flops=flops,
    )(total, own, arrived, after)


def joined_kernel(first_ref, second_ref, after_ref, out_ref):
    width = first_ref.shape[1]
    out_ref[:, :width] = first_ref[...]
    out_ref[:, width:] = second_ref[...]


def joined(first, second, after):
    return kernel_call(
        joined_kernel,
        shape(first.shape[0], 2 * first.shape[1]),
        [VMEM, VMEM, ANY],
        VMEM,
        first.shape[0],
    )(first, second, after)


def turned_kernel(skip, rows, own_ref, arrived_ref, bias_ref, order_ref, out_ref):
    bias = jnp.concatenate([bias_ref[...]] * rows, axis=0)
    bias = stacked(bias, ROWS // rows)
    width = bias.shape[1]
    blocks = [
        (ref[:, at : at + width].astype(jnp.float32) - bias).astype(jnp.bfloat16)
        for ref in (own_ref, arrived_ref)
        for at in range(skip, ref.shape[1], width)
    ]
    ordered = jnp.dot(
        order_ref[...], jnp.concatenate(blocks, axis=0), preferred_element_type=jnp.float32
    )
    out_ref[...] = ordered.T.astype(jnp.bfloat16)


def turned(own, arrived, skip, bias, order, rows, count):
    width = bias.shape[1] * rows // ROWS
    return kernel_call(
        functools.partial(turned_kernel, skip, rows),
        shape(width, 2 * (own.shape[1] - skip) // width * ROWS),
        [VMEM] * 4,
        VMEM,
        count,
    )(own, arrived, bias, order)


def scaled_of(total_ref, arrived_ref):
    total = total_ref[...] + arrived_ref[:, : total_ref.shape[1]].astype(jnp.float32)
    return (0.25 * total).astype(jnp.bfloat16)


def product(part, rows_ref, at):
    return lax.dot_general(
        part,
        rows_ref[:, at : at + part.shape[1]],
        (((1,), (1,)), ((), ())),
        preferred_element_type=jnp.float32,
    )


def first_product_kernel(total_ref, arrived_ref, rows_ref, scaled_ref, half_ref):
    scaled = scaled_of(total_ref, arrived_ref)
    scaled_ref[...] = scaled
    half_ref[...] = product(scaled, rows_ref, 0)


def second_product_kernel(
    total_ref, arrived_ref, rows_ref, first_ref, after_ref, scaled_ref, half_ref
):
    scaled = scaled_of(total_ref, arrived_ref)
    scaled_ref[...] = scaled
    half_ref[...] = first_ref[...] + product(scaled, rows_ref, rows_ref.shape[1] - scaled.shape[1])


def products(total, arrived, dict_rows, *first):
    count, width = total.shape
    return kernel_call(
        second_product_kernel if first else first_product_kernel,
        (shape(count, width), shape(count, dict_rows.shape[0], dtype=jnp.float32)),
        [VMEM] * 3 + ([VMEM, ANY] if first else []),
        (VMEM, VMEM),
        count,
    )(total, arrived, dict_rows, *first)


def outer(code_ref, scaled):
    code = code_ref[...].astype(jnp.float32).T.astype(jnp.bfloat16)
    return jnp.dot(code, scaled, preferred_element_type=jnp.float32).astype(jnp.bfloat16)


def grad_rows_kernel(code_ref, first_ref, second_ref, out_ref):
    chunk = first_ref.shape[1]
    out_ref[:, :chunk] = outer(code_ref, first_ref[...])
    out_ref[:, chunk:] = outer(code_ref, second_ref[...])


def grad_rows_of(code, first, second):
    count, slots = code.shape
    return kernel_call(
        grad_rows_kernel,
        shape(slots, first.shape[1] + second.shape[1]),
        [VMEM] * 3,
        VMEM,
        count,
    )(code, first, second)


def final_kernel(
    rows,
    raw_ref,
    mine_ref,
    theirs_ref,
    turned_ref,
    rows_ref,
    rows_hbm,
    enc_hbm,
    benc_hbm,
    enc_ref,
    benc_ref,
    sems,
):
    copies = [pltpu.make_async_copy(rows_ref, rows_hbm, sems.at[0])]
    copies[0].start()
    count, slots = raw_ref.shape
    width = turned_ref.shape[0]
    pieces = ROWS // rows
    code_grad = mine_ref[...] + theirs_ref[...]
    pre_grad = jnp.where(raw_ref[...] > 0.0, code_grad, 0.0).astype(jnp.bfloat16)
    benc_ref[...] = jnp.sum(pre_grad.astype(jnp.float32), axis=0, keepdims=True)
    copies.append(pltpu.make_async_copy(benc_ref, benc_hbm, sems.at[1]))
    copies[1].start()
    zeros = jnp.zeros_like(pre_grad)
    group = pieces // 2
    for c in range(0, pieces, group):
        placed = [
            jnp.concatenate([zeros] * at + [pre_grad] + [zeros] * (pieces - 1 - at), axis=0)
            for at in range(c, c + group)
        ]
        out = jnp.dot(
            turned_ref[...],
            jnp.concatenate(placed, axis=1),
            preferred_element_type=jnp.float32,
        ).astype(jnp.bfloat16)
        for i in range(group):
            enc_ref[(c + i) * width : (c + i + 1) * width, :] = out[:, i * slots : (i + 1) * slots]
        for i in range(0, group, 2):
            part = pl.ds((c + i) * width, 2 * width)
            copies.append(
                pltpu.make_async_copy(enc_ref.at[part], enc_hbm.at[part], sems.at[(c + i) // 2 + 2])
            )
            copies[-1].start()
    for copy in copies:
        copy.wait()


def final(raw, mine, theirs, turned_tokens, grad_rows, rows):
    count, slots = raw.shape
    pieces = ROWS // rows
    width = turned_tokens.shape[0] * pieces
    return kernel_call(
        functools.partial(final_kernel, rows),
        (shape(*grad_rows.shape), shape(width, slots), shape(1, slots, dtype=jnp.float32)),
        [VMEM] * 5,
        (HBM, HBM, HBM),
        count,
        [
            pltpu.VMEM((width, slots), jnp.bfloat16),
            pltpu.VMEM((1, slots), jnp.float32),
            pltpu.SemaphoreType.DMA((pieces // 2 + 2,)),
        ],
    )(raw, mine, theirs, turned_tokens, grad_rows)


def local(tokens, b_pre, pre_codes, top_idx, blocks, counts, dict_rows):
    rows, count = tokens.shape[0], top_idx.shape[0]
    steps = feat_bits()
    merged = count == ROWS

    order = order_of(rows, count)
    code, raw, total, sent, centered, bias, *block = front(
        tokens, b_pre, pre_codes, top_idx, blocks, counts, dict_rows, order, merged
    )
    for step in range(steps):
        arrived = swapped(sent, step)
        if step == 0:
            total_second, sent_second = second(code, dict_rows, centered)
        else:
            total_second, sent_second = added(
                total_second, sent_second, arrived_second, sent, False, EARLY
            )
        arrived_second = swapped(sent_second, step)
        if not merged:
            own_block = joined(own_block, arrived_block, sent_second) if step else block[0]
            arrived_block = swapped(own_block, step)
        if step < steps - 1:
            total, sent = added(total, sent, arrived, sent_second, merged)
    skip = 0
    if merged:
        own_block, arrived_block, skip = sent, arrived, total.shape[1]

    scaled, product_first = products(total, arrived, dict_rows)
    turned_tokens = turned(own_block, arrived_block, skip, bias, order, rows, count)
    scaled_second, code_half = products(
        total_second, arrived_second, dict_rows, product_first, turned_tokens
    )
    theirs = lax.ppermute(code_half, "tok", [(i, 1 - i) for i in range(2)])
    grad_rows = grad_rows_of(code, scaled, scaled_second)
    grad_rows, grad_enc, grad_benc = final(
        raw, code_half, theirs, turned_tokens, grad_rows, rows
    )
    return (grad_rows, grad_enc, grad_benc.reshape(-1))


def solution(mesh):
    return jax.shard_map(
        local,
        mesh=mesh,
        in_specs=(
            P(("grp", "feat"), "tok"),
            P(("grp", "tok")),
            P("grp", None),
            P("grp", None),
            P(("grp", "feat")),
            P(("grp", "feat")),
            P(("grp", "feat"), "tok"),
        ),
        out_specs=(P(("grp", "feat"), "tok"), P(("grp", "tok"), "feat"), P(("grp", "feat"))),
        check_vma=False,
    )
```

```python
import functools

import jax
import jax.numpy as jnp
from jax import lax
from jax.experimental import pallas as pl
from jax.experimental.pallas import tpu as pltpu
from jax.sharding import PartitionSpec as P

VMEM = pl.BlockSpec(memory_space=pltpu.VMEM)
SMEM = pl.BlockSpec(memory_space=pltpu.SMEM)
HBM = pl.BlockSpec(memory_space=pltpu.HBM)
ANY = pl.BlockSpec(memory_space=pl.ANY)
EARLY = 10**9
ROWS = 16


def kernel_call(kernel, out_shape, in_specs, out_specs, tokens, scratch_shapes=(), aliases={}, flops=10**6):
    limit = (16 if tokens <= ROWS else 40) * 2**20
    return pl.pallas_call(
        kernel,
        out_shape=out_shape,
        in_specs=in_specs,
        out_specs=out_specs,
        scratch_shapes=scratch_shapes,
        input_output_aliases=aliases,
        compiler_params=pltpu.CompilerParams(vmem_limit_bytes=limit),
        cost_estimate=pl.CostEstimate(flops=flops, bytes_accessed=2**20, transcendentals=0),
    )


def shape(*sizes, dtype=jnp.bfloat16):
    return jax.ShapeDtypeStruct(sizes, dtype)


def first_width(width):
    return width * 9 // 16 // 128 * 128


def feat_bits():
    return (lax.axis_size("feat") - 1).bit_length()


def bit_of(step, core):
    bits = list(range(feat_bits()))
    return (bits[-1:] + bits[:-1] if core == 0 else bits)[step]


def swapped(shard, step):
    cores = lax.axis_size("tok")
    pairs = [
        (f * cores + c, (f ^ 1 << bit_of(step, c)) * cores + c)
        for f in range(lax.axis_size("feat"))
        for c in range(cores)
    ]
    return lax.ppermute(shard, ("feat", "tok"), pairs)


def stacked(rows, pieces):
    width = rows.shape[1] // pieces
    return jnp.concatenate(
        [rows[:, c * width : (c + 1) * width] for c in range(pieces)], axis=0
    )


def share(code, rows_ref, centered_ref, at, width):
    part = pl.ds(at, width)
    total = jnp.dot(code, rows_ref[:, part], preferred_element_type=jnp.float32)
    rows = centered_ref.shape[0]
    centered = centered_ref[:, part]
    token = lax.broadcasted_iota(jnp.int32, (total.shape[0], 1), 0)
    first = lax.axis_index("feat") * rows
    for i in range(rows):
        total -= jnp.where(token == first + i, centered[i : i + 1, :], 0.0)
    return total


def order_kernel(rows, order_ref):
    target = lax.broadcasted_iota(jnp.int32, order_ref.shape, 0)
    place = lax.broadcasted_iota(jnp.int32, order_ref.shape, 1)
    core = lax.axis_index("tok")
    block = place // ROWS
    distance = jnp.zeros_like(place)
    for step in range(feat_bits()):
        bit = sum(
            jnp.where(core == c, bit_of(step, c), 0) for c in range(lax.axis_size("tok"))
        )
        distance |= (block >> step & 1) << bit
    token = (lax.axis_index("feat") ^ distance) * rows + place % rows
    piece = place % ROWS // rows
    count = rows * lax.axis_size("feat")
    order_ref[...] = jnp.where(target == piece * count + token, 1.0, 0.0).astype(jnp.bfloat16)


def order_of(rows, count):
    depth = ROWS * lax.axis_size("feat")
    return kernel_call(
        functools.partial(order_kernel, rows),
        shape(depth, depth),
        [],
        VMEM,
        count,
        flops=EARLY,
    )()


def front_kernel(
    tokens_ref, bias_flat, pre_ref, top_ref, rows_ref, block_ref, count_ref, after_ref, *refs
):
    code_ref, raw_ref, total_ref, sent_ref, centered_ref, bias_ref, *cut = refs
    count, latents = top_ref.shape
    slots, width = rows_ref.shape
    offsets = lax.broadcasted_iota(jnp.int32, (1, slots), 1)
    slot_ids = jnp.where(offsets < count_ref[0], block_ref[0] * slots + offsets, -1)
    top, pre = top_ref[...], pre_ref[...]
    raw = jnp.zeros((count, slots), jnp.float32)
    for k in range(latents):
        raw = jnp.where(top[:, k : k + 1] == slot_ids, pre[:, k : k + 1], raw)
    raw_ref[...] = raw
    code = jnp.maximum(raw, 0.0).astype(jnp.bfloat16)
    code_ref[...] = code

    tokens = tokens_ref[...].astype(jnp.float32)
    bias = bias_flat[...].astype(jnp.float32).reshape(1, width)
    bias_ref[...] = bias
    centered_ref[...] = (tokens - bias).astype(jnp.bfloat16).astype(jnp.float32)

    total = share(code, rows_ref, centered_ref, 0, total_ref.shape[1])
    total_ref[...] = total
    width = total.shape[1]
    sent_ref[:, :width] = total.astype(jnp.bfloat16)
    block = stacked(tokens, ROWS // tokens.shape[0]).astype(jnp.bfloat16)
    if cut:
        cut[0][...] = block
    else:
        sent_ref[:, width:] = block


def front(tokens, b_pre, pre_codes, top_idx, blocks, counts, dict_rows, after, merged):
    count = top_idx.shape[0]
    slots, width = dict_rows.shape
    chunk, block = first_width(width), tokens.shape[0] * width // ROWS
    return kernel_call(
        front_kernel,
        (
            shape(count, slots),
            shape(count, slots, dtype=jnp.float32),
            shape(count, chunk, dtype=jnp.float32),
            shape(count, chunk + (block if merged else 0)),
            shape(*tokens.shape, dtype=jnp.float32),
            shape(1, width, dtype=jnp.float32),
            *([] if merged else [shape(ROWS, block)]),
        ),
        [VMEM] * 5 + [SMEM] * 2 + [ANY],
        (VMEM,) * (6 if merged else 7),
        count,
    )(tokens, b_pre, pre_codes, top_idx, dict_rows, blocks, counts, after)


def second_kernel(code_ref, rows_ref, centered_ref, total_ref, sent_ref):
    width = total_ref.shape[1]
    total = share(code_ref[...], rows_ref, centered_ref, rows_ref.shape[1] - width, width)
    total_ref[...] = total
    sent_ref[...] = total.astype(jnp.bfloat16)


def second(code, dict_rows, centered):
    count, width = code.shape[0], dict_rows.shape[1]
    chunk = width - first_width(width)
    return kernel_call(
        second_kernel,
        (shape(count, chunk, dtype=jnp.float32), shape(count, chunk)),
        [VMEM] * 3,
        (VMEM, VMEM),
        count,
    )(code, dict_rows, centered)


def added_kernel(total_ref, own_ref, arrived_ref, after_ref, sum_ref, sent_ref):
    half = total_ref.shape[1]
    total = total_ref[...] + arrived_ref[:, :half].astype(jnp.float32)
    sum_ref[...] = total
    sent_ref[:, :half] = total.astype(jnp.bfloat16)
    if sent_ref.shape[1] > half:
        block = own_ref.shape[1] - half
        sent_ref[:, half : half + block] = own_ref[:, half:]
        sent_ref[:, half + block :] = arrived_ref[:, half:]


def added(total, own, arrived, after, merged, flops=10**6):
    count, half = total.shape
    block = own.shape[1] - half
    return kernel_call(
        added_kernel,
        (
            shape(count, half, dtype=jnp.float32),
            shape(count, half + (2 * block if merged else 0)),
        ),
        [VMEM] * 3 + [ANY],
        (VMEM, VMEM),
        count,
        flops=flops,
    )(total, own, arrived, after)


def joined_kernel(first_ref, second_ref, after_ref, out_ref):
    width = first_ref.shape[1]
    out_ref[:, :width] = first_ref[...]
    out_ref[:, width:] = second_ref[...]


def joined(first, second, after):
    return kernel_call(
        joined_kernel,
        shape(first.shape[0], 2 * first.shape[1]),
        [VMEM, VMEM, ANY],
        VMEM,
        first.shape[0],
    )(first, second, after)


def turned_kernel(skip, rows, own_ref, arrived_ref, bias_ref, order_ref, out_ref):
    bias = jnp.concatenate([bias_ref[...]] * rows, axis=0)
    bias = stacked(bias, ROWS // rows)
    width = bias.shape[1]
    blocks = [
        (ref[:, at : at + width].astype(jnp.float32) - bias).astype(jnp.bfloat16)
        for ref in (own_ref, arrived_ref)
        for at in range(skip, ref.shape[1], width)
    ]
    ordered = jnp.dot(
        order_ref[...], jnp.concatenate(blocks, axis=0), preferred_element_type=jnp.float32
    )
    out_ref[...] = ordered.T.astype(jnp.bfloat16)


def turned(own, arrived, skip, bias, order, rows, count):
    width = bias.shape[1] * rows // ROWS
    return kernel_call(
        functools.partial(turned_kernel, skip, rows),
        shape(width, 2 * (own.shape[1] - skip) // width * ROWS),
        [VMEM] * 4,
        VMEM,
        count,
    )(own, arrived, bias, order)


def scaled_of(total_ref, arrived_ref):
    total = total_ref[...] + arrived_ref[:, : total_ref.shape[1]].astype(jnp.float32)
    return (0.25 * total).astype(jnp.bfloat16)


def product(part, rows_ref, at):
    return lax.dot_general(
        part,
        rows_ref[:, at : at + part.shape[1]],
        (((1,), (1,)), ((), ())),
        preferred_element_type=jnp.float32,
    )


def first_product_kernel(total_ref, arrived_ref, rows_ref, scaled_ref, half_ref):
    scaled = scaled_of(total_ref, arrived_ref)
    scaled_ref[...] = scaled
    half_ref[...] = product(scaled, rows_ref, 0)


def second_product_kernel(
    total_ref, arrived_ref, rows_ref, first_ref, after_ref, scaled_ref, half_ref
):
    scaled = scaled_of(total_ref, arrived_ref)
    scaled_ref[...] = scaled
    half_ref[...] = first_ref[...] + product(scaled, rows_ref, rows_ref.shape[1] - scaled.shape[1])


def products(total, arrived, dict_rows, *first):
    count, width = total.shape
    return kernel_call(
        second_product_kernel if first else first_product_kernel,
        (shape(count, width), shape(count, dict_rows.shape[0], dtype=jnp.float32)),
        [VMEM] * 3 + ([VMEM, ANY] if first else []),
        (VMEM, VMEM),
        count,
    )(total, arrived, dict_rows, *first)


def outer(code_ref, scaled):
    code = code_ref[...].astype(jnp.float32).T.astype(jnp.bfloat16)
    return jnp.dot(code, scaled, preferred_element_type=jnp.float32).astype(jnp.bfloat16)


def grad_rows_kernel(code_ref, first_ref, second_ref, out_hbm, last_ref, out_ref, sem):
    chunk = first_ref.shape[1]
    out_ref[...] = outer(code_ref, first_ref[...])
    copy = pltpu.make_async_copy(out_ref, out_hbm.at[:, pl.ds(0, chunk)], sem)
    copy.start()
    last_ref[...] = outer(code_ref, second_ref[...])
    copy.wait()


def grad_rows_of(code, first, second):
    count, slots = code.shape
    chunk, rest = first.shape[1], second.shape[1]
    return kernel_call(
        grad_rows_kernel,
        (shape(slots, chunk + rest), shape(slots, rest)),
        [VMEM] * 3,
        (HBM, VMEM),
        count,
        [pltpu.VMEM((slots, chunk), jnp.bfloat16), pltpu.SemaphoreType.DMA],
    )(code, first, second)


def final_kernel(
    rows,
    raw_ref,
    mine_ref,
    theirs_ref,
    turned_ref,
    last_ref,
    written_hbm,
    rows_hbm,
    enc_hbm,
    benc_hbm,
    enc_ref,
    benc_ref,
    sems,
):
    rest = last_ref.shape[1]
    features = pl.ds(rows_hbm.shape[1] - rest, rest)
    copies = [pltpu.make_async_copy(last_ref, rows_hbm.at[:, features], sems.at[0])]
    copies[0].start()
    count, slots = raw_ref.shape
    width = turned_ref.shape[0]
    pieces = ROWS // rows
    code_grad = mine_ref[...] + theirs_ref[...]
    pre_grad = jnp.where(raw_ref[...] > 0.0, code_grad, 0.0).astype(jnp.bfloat16)
    benc_ref[...] = jnp.sum(pre_grad.astype(jnp.float32), axis=0, keepdims=True)
    copies.append(pltpu.make_async_copy(benc_ref, benc_hbm, sems.at[1]))
    copies[1].start()
    zeros = jnp.zeros_like(pre_grad)
    group = pieces // 2
    for c in range(0, pieces, group):
        placed = [
            jnp.concatenate([zeros] * at + [pre_grad] + [zeros] * (pieces - 1 - at), axis=0)
            for at in range(c, c + group)
        ]
        out = jnp.dot(
            turned_ref[...],
            jnp.concatenate(placed, axis=1),
            preferred_element_type=jnp.float32,
        ).astype(jnp.bfloat16)
        for i in range(group):
            enc_ref[(c + i) * width : (c + i + 1) * width, :] = out[:, i * slots : (i + 1) * slots]
        for i in range(0, group, 2):
            part = pl.ds((c + i) * width, 2 * width)
            copies.append(
                pltpu.make_async_copy(enc_ref.at[part], enc_hbm.at[part], sems.at[(c + i) // 2 + 2])
            )
            copies[-1].start()
    for copy in copies:
        copy.wait()


def final(raw, mine, theirs, turned_tokens, last, written, rows):
    count, slots = raw.shape
    pieces = ROWS // rows
    width = turned_tokens.shape[0] * pieces
    return kernel_call(
        functools.partial(final_kernel, rows),
        (shape(*written.shape), shape(width, slots), shape(1, slots, dtype=jnp.float32)),
        [VMEM] * 5 + [HBM],
        (HBM, HBM, HBM),
        count,
        [
            pltpu.VMEM((width, slots), jnp.bfloat16),
            pltpu.VMEM((1, slots), jnp.float32),
            pltpu.SemaphoreType.DMA((pieces // 2 + 2,)),
        ],
        aliases={5: 0},
    )(raw, mine, theirs, turned_tokens, last, written)


def local(tokens, b_pre, pre_codes, top_idx, blocks, counts, dict_rows):
    rows, count = tokens.shape[0], top_idx.shape[0]
    steps = feat_bits()
    merged = count == ROWS

    order = order_of(rows, count)
    code, raw, total, sent, centered, bias, *block = front(
        tokens, b_pre, pre_codes, top_idx, blocks, counts, dict_rows, order, merged
    )
    for step in range(steps):
        arrived = swapped(sent, step)
        if step == 0:
            total_second, sent_second = second(code, dict_rows, centered)
        else:
            total_second, sent_second = added(
                total_second, sent_second, arrived_second, sent, False, EARLY
            )
        arrived_second = swapped(sent_second, step)
        if not merged:
            own_block = joined(own_block, arrived_block, sent_second) if step else block[0]
            arrived_block = swapped(own_block, step)
        if step < steps - 1:
            total, sent = added(total, sent, arrived, sent_second, merged)
    skip = 0
    if merged:
        own_block, arrived_block, skip = sent, arrived, total.shape[1]

    scaled, product_first = products(total, arrived, dict_rows)
    turned_tokens = turned(own_block, arrived_block, skip, bias, order, rows, count)
    scaled_second, code_half = products(
        total_second, arrived_second, dict_rows, product_first, turned_tokens
    )
    theirs = lax.ppermute(code_half, "tok", [(i, 1 - i) for i in range(2)])
    written, last = grad_rows_of(code, scaled, scaled_second)
    grad_rows, grad_enc, grad_benc = final(
        raw, code_half, theirs, turned_tokens, last, written, rows
    )
    return (grad_rows, grad_enc, grad_benc.reshape(-1))


def solution(mesh):
    return jax.shard_map(
        local,
        mesh=mesh,
        in_specs=(
            P(("grp", "feat"), "tok"),
            P(("grp", "tok")),
            P("grp", None),
            P("grp", None),
            P(("grp", "feat")),
            P(("grp", "feat")),
            P(("grp", "feat"), "tok"),
        ),
        out_specs=(P(("grp", "feat"), "tok"), P(("grp", "tok"), "feat"), P(("grp", "feat"))),
        check_vma=False,
    )
```

```python
import functools

import jax
import jax.numpy as jnp
from jax import lax
from jax.experimental import pallas as pl
from jax.experimental.pallas import tpu as pltpu
from jax.sharding import PartitionSpec as P

VMEM = pl.BlockSpec(memory_space=pltpu.VMEM)
SMEM = pl.BlockSpec(memory_space=pltpu.SMEM)
HBM = pl.BlockSpec(memory_space=pltpu.HBM)
ANY = pl.BlockSpec(memory_space=pl.ANY)
EARLY = 10**9
ROWS = 16


def kernel_call(kernel, out_shape, in_specs, out_specs, tokens, scratch_shapes=(), flops=10**6):
    limit = (16 if tokens <= ROWS else 40) * 2**20
    return pl.pallas_call(
        kernel,
        out_shape=out_shape,
        in_specs=in_specs,
        out_specs=out_specs,
        scratch_shapes=scratch_shapes,
        compiler_params=pltpu.CompilerParams(vmem_limit_bytes=limit),
        cost_estimate=pl.CostEstimate(flops=flops, bytes_accessed=2**20, transcendentals=0),
    )


def shape(*sizes, dtype=jnp.bfloat16):
    return jax.ShapeDtypeStruct(sizes, dtype)


def first_width(width):
    return width // 2


def feat_bits():
    return (lax.axis_size("feat") - 1).bit_length()


def bit_of(step, core, chunk):
    bits = list(range(feat_bits()))
    if core == 0:
        return (bits[-1:] + bits[:-1] if chunk == 0 else bits[::-1])[step]
    return bits[step]


def swapped(shard, step, chunk):
    cores = lax.axis_size("tok")
    pairs = [
        (f * cores + c, (f ^ 1 << bit_of(step, c, chunk)) * cores + c)
        for f in range(lax.axis_size("feat"))
        for c in range(cores)
    ]
    return lax.ppermute(shard, ("feat", "tok"), pairs)


def stacked(rows, pieces):
    width = rows.shape[1] // pieces
    return jnp.concatenate(
        [rows[:, c * width : (c + 1) * width] for c in range(pieces)], axis=0
    )


def share(code, rows_ref, centered_ref, at, width):
    part = pl.ds(at, width)
    total = jnp.dot(code, rows_ref[:, part], preferred_element_type=jnp.float32)
    rows = centered_ref.shape[0]
    centered = centered_ref[:, part]
    token = lax.broadcasted_iota(jnp.int32, (total.shape[0], 1), 0)
    first = lax.axis_index("feat") * rows
    for i in range(rows):
        total -= jnp.where(token == first + i, centered[i : i + 1, :], 0.0)
    return total


def order_kernel(rows, order_ref):
    target = lax.broadcasted_iota(jnp.int32, order_ref.shape, 0)
    place = lax.broadcasted_iota(jnp.int32, order_ref.shape, 1)
    core = lax.axis_index("tok")
    block = place // ROWS
    distance = jnp.zeros_like(place)
    for step in range(feat_bits()):
        bit = sum(
            jnp.where(core == c, bit_of(step, c, 0), 0) for c in range(lax.axis_size("tok"))
        )
        distance |= (block >> step & 1) << bit
    token = (lax.axis_index("feat") ^ distance) * rows + place % rows
    piece = place % ROWS // rows
    count = rows * lax.axis_size("feat")
    order_ref[...] = jnp.where(target == piece * count + token, 1.0, 0.0).astype(jnp.bfloat16)


def order_of(rows, count):
    depth = ROWS * lax.axis_size("feat")
    return kernel_call(
        functools.partial(order_kernel, rows),
        shape(depth, depth),
        [],
        VMEM,
        count,
        flops=EARLY,
    )()


def front_kernel(
    tokens_ref, bias_flat, pre_ref, top_ref, rows_ref, block_ref, count_ref, after_ref, *refs
):
    code_ref, raw_ref, total_ref, sent_ref, centered_ref, bias_ref, *cut = refs
    count, latents = top_ref.shape
    slots, width = rows_ref.shape
    offsets = lax.broadcasted_iota(jnp.int32, (1, slots), 1)
    slot_ids = jnp.where(offsets < count_ref[0], block_ref[0] * slots + offsets, -1)
    top, pre = top_ref[...], pre_ref[...]
    raw = jnp.zeros((count, slots), jnp.float32)
    for k in range(latents):
        raw = jnp.where(top[:, k : k + 1] == slot_ids, pre[:, k : k + 1], raw)
    raw_ref[...] = raw
    code = jnp.maximum(raw, 0.0).astype(jnp.bfloat16)
    code_ref[...] = code

    tokens = tokens_ref[...].astype(jnp.float32)
    bias = bias_flat[...].astype(jnp.float32).reshape(1, width)
    bias_ref[...] = bias
    centered_ref[...] = (tokens - bias).astype(jnp.bfloat16).astype(jnp.float32)

    total = share(code, rows_ref, centered_ref, 0, total_ref.shape[1])
    total_ref[...] = total
    width = total.shape[1]
    sent_ref[:, :width] = total.astype(jnp.bfloat16)
    block = stacked(tokens, ROWS // tokens.shape[0]).astype(jnp.bfloat16)
    if cut:
        cut[0][...] = block
    else:
        sent_ref[:, width:] = block


def front(tokens, b_pre, pre_codes, top_idx, blocks, counts, dict_rows, after, merged):
    count = top_idx.shape[0]
    slots, width = dict_rows.shape
    chunk, block = first_width(width), tokens.shape[0] * width // ROWS
    return kernel_call(
        front_kernel,
        (
            shape(count, slots),
            shape(count, slots, dtype=jnp.float32),
            shape(count, chunk, dtype=jnp.float32),
            shape(count, chunk + (block if merged else 0)),
            shape(*tokens.shape, dtype=jnp.float32),
            shape(1, width, dtype=jnp.float32),
            *([] if merged else [shape(ROWS, block)]),
        ),
        [VMEM] * 5 + [SMEM] * 2 + [ANY],
        (VMEM,) * (6 if merged else 7),
        count,
    )(tokens, b_pre, pre_codes, top_idx, dict_rows, blocks, counts, after)


def second_kernel(code_ref, rows_ref, centered_ref, total_ref, sent_ref):
    width = total_ref.shape[1]
    total = share(code_ref[...], rows_ref, centered_ref, rows_ref.shape[1] - width, width)
    total_ref[...] = total
    sent_ref[...] = total.astype(jnp.bfloat16)


def second(code, dict_rows, centered):
    count, width = code.shape[0], dict_rows.shape[1]
    chunk = width - first_width(width)
    return kernel_call(
        second_kernel,
        (shape(count, chunk, dtype=jnp.float32), shape(count, chunk)),
        [VMEM] * 3,
        (VMEM, VMEM),
        count,
    )(code, dict_rows, centered)


def added_kernel(total_ref, own_ref, arrived_ref, after_ref, sum_ref, sent_ref):
    half = total_ref.shape[1]
    total = total_ref[...] + arrived_ref[:, :half].astype(jnp.float32)
    sum_ref[...] = total
    sent_ref[:, :half] = total.astype(jnp.bfloat16)
    if sent_ref.shape[1] > half:
        block = own_ref.shape[1] - half
        sent_ref[:, half : half + block] = own_ref[:, half:]
        sent_ref[:, half + block :] = arrived_ref[:, half:]


def added(total, own, arrived, after, merged, flops=10**6):
    count, half = total.shape
    block = own.shape[1] - half
    return kernel_call(
        added_kernel,
        (
            shape(count, half, dtype=jnp.float32),
            shape(count, half + (2 * block if merged else 0)),
        ),
        [VMEM] * 3 + [ANY],
        (VMEM, VMEM),
        count,
        flops=flops,
    )(total, own, arrived, after)


def joined_kernel(first_ref, second_ref, after_ref, out_ref):
    width = first_ref.shape[1]
    out_ref[:, :width] = first_ref[...]
    out_ref[:, width:] = second_ref[...]


def joined(first, second, after):
    return kernel_call(
        joined_kernel,
        shape(first.shape[0], 2 * first.shape[1]),
        [VMEM, VMEM, ANY],
        VMEM,
        first.shape[0],
    )(first, second, after)


def turned_kernel(skip, rows, own_ref, arrived_ref, bias_ref, order_ref, out_ref):
    bias = jnp.concatenate([bias_ref[...]] * rows, axis=0)
    bias = stacked(bias, ROWS // rows)
    width = bias.shape[1]
    blocks = [
        (ref[:, at : at + width].astype(jnp.float32) - bias).astype(jnp.bfloat16)
        for ref in (own_ref, arrived_ref)
        for at in range(skip, ref.shape[1], width)
    ]
    ordered = jnp.dot(
        order_ref[...], jnp.concatenate(blocks, axis=0), preferred_element_type=jnp.float32
    )
    out_ref[...] = ordered.T.astype(jnp.bfloat16)


def turned(own, arrived, skip, bias, order, rows, count):
    width = bias.shape[1] * rows // ROWS
    return kernel_call(
        functools.partial(turned_kernel, skip, rows),
        shape(width, 2 * (own.shape[1] - skip) // width * ROWS),
        [VMEM] * 4,
        VMEM,
        count,
    )(own, arrived, bias, order)


def scaled_of(total_ref, arrived_ref):
    total = total_ref[...] + arrived_ref[:, : total_ref.shape[1]].astype(jnp.float32)
    return (0.25 * total).astype(jnp.bfloat16)


def product(part, rows_ref, at):
    return lax.dot_general(
        part,
        rows_ref[:, at : at + part.shape[1]],
        (((1,), (1,)), ((), ())),
        preferred_element_type=jnp.float32,
    )


def first_product_kernel(total_ref, arrived_ref, rows_ref, scaled_ref, half_ref):
    scaled = scaled_of(total_ref, arrived_ref)
    scaled_ref[...] = scaled
    half_ref[...] = product(scaled, rows_ref, 0)


def second_product_kernel(total_ref, arrived_ref, rows_ref, first_ref, scaled_ref, half_ref):
    scaled = scaled_of(total_ref, arrived_ref)
    scaled_ref[...] = scaled
    half_ref[...] = first_ref[...] + product(scaled, rows_ref, rows_ref.shape[1] - scaled.shape[1])


def products(total, arrived, dict_rows, *first):
    count, width = total.shape
    return kernel_call(
        second_product_kernel if first else first_product_kernel,
        (shape(count, width), shape(count, dict_rows.shape[0], dtype=jnp.float32)),
        [VMEM] * (3 + len(first)),
        (VMEM, VMEM),
        count,
    )(total, arrived, dict_rows, *first)


def outer(code_ref, scaled):
    code = code_ref[...].astype(jnp.float32).T.astype(jnp.bfloat16)
    return jnp.dot(code, scaled, preferred_element_type=jnp.float32).astype(jnp.bfloat16)


def grad_rows_kernel(code_ref, first_ref, second_ref, out_ref):
    chunk = first_ref.shape[1]
    out_ref[:, :chunk] = outer(code_ref, first_ref[...])
    out_ref[:, chunk:] = outer(code_ref, second_ref[...])


def grad_rows_of(code, first, second):
    count, slots = code.shape
    return kernel_call(
        grad_rows_kernel,
        shape(slots, first.shape[1] + second.shape[1]),
        [VMEM] * 3,
        VMEM,
        count,
    )(code, first, second)


def final_kernel(
    rows,
    raw_ref,
    mine_ref,
    theirs_ref,
    turned_ref,
    rows_ref,
    rows_hbm,
    enc_hbm,
    benc_hbm,
    enc_ref,
    benc_ref,
    sems,
):
    copies = [pltpu.make_async_copy(rows_ref, rows_hbm, sems.at[0])]
    copies[0].start()
    count, slots = raw_ref.shape
    width = turned_ref.shape[0]
    pieces = ROWS // rows
    code_grad = mine_ref[...] + theirs_ref[...]
    pre_grad = jnp.where(raw_ref[...] > 0.0, code_grad, 0.0).astype(jnp.bfloat16)
    benc_ref[...] = jnp.sum(pre_grad.astype(jnp.float32), axis=0, keepdims=True)
    copies.append(pltpu.make_async_copy(benc_ref, benc_hbm, sems.at[1]))
    copies[1].start()
    zeros = jnp.zeros_like(pre_grad)
    for c in range(0, pieces, 2):
        pair = [
            jnp.concatenate([zeros] * at + [pre_grad] + [zeros] * (pieces - 1 - at), axis=0)
            for at in (c, c + 1)
        ]
        out = jnp.dot(
            turned_ref[...],
            jnp.concatenate(pair, axis=1),
            preferred_element_type=jnp.float32,
        ).astype(jnp.bfloat16)
        for i in range(2):
            enc_ref[(c + i) * width : (c + i + 1) * width, :] = out[:, i * slots : (i + 1) * slots]
        part = pl.ds(c * width, 2 * width)
        copies.append(pltpu.make_async_copy(enc_ref.at[part], enc_hbm.at[part], sems.at[c // 2 + 2]))
        copies[-1].start()
    for copy in copies:
        copy.wait()


def final(raw, mine, theirs, turned_tokens, grad_rows, rows):
    count, slots = raw.shape
    pieces = ROWS // rows
    width = turned_tokens.shape[0] * pieces
    return kernel_call(
        functools.partial(final_kernel, rows),
        (shape(*grad_rows.shape), shape(width, slots), shape(1, slots, dtype=jnp.float32)),
        [VMEM] * 5,
        (HBM, HBM, HBM),
        count,
        [
            pltpu.VMEM((width, slots), jnp.bfloat16),
            pltpu.VMEM((1, slots), jnp.float32),
            pltpu.SemaphoreType.DMA((pieces // 2 + 2,)),
        ],
    )(raw, mine, theirs, turned_tokens, grad_rows)


def local(tokens, b_pre, pre_codes, top_idx, blocks, counts, dict_rows):
    rows, count = tokens.shape[0], top_idx.shape[0]
    steps = feat_bits()
    merged = count == ROWS

    order = order_of(rows, count)
    code, raw, total, sent, centered, bias, *block = front(
        tokens, b_pre, pre_codes, top_idx, blocks, counts, dict_rows, order, merged
    )
    for step in range(steps):
        arrived = swapped(sent, step, 0)
        if step == 0:
            total_second, sent_second = second(code, dict_rows, centered)
        else:
            total_second, sent_second = added(
                total_second, sent_second, arrived_second, sent, False, EARLY
            )
        arrived_second = swapped(sent_second, step, 1)
        if not merged:
            own_block = joined(own_block, arrived_block, sent_second) if step else block[0]
            arrived_block = swapped(own_block, step, 0)
        if step < steps - 1:
            total, sent = added(total, sent, arrived, sent_second, merged)
    skip = 0
    if merged:
        own_block, arrived_block, skip = sent, arrived, total.shape[1]

    scaled, product_first = products(total, arrived, dict_rows)
    turned_tokens = turned(own_block, arrived_block, skip, bias, order, rows, count)
    scaled_second, code_half = products(
        total_second, arrived_second, dict_rows, product_first
    )
    theirs = lax.ppermute(code_half, "tok", [(i, 1 - i) for i in range(2)])
    grad_rows = grad_rows_of(code, scaled, scaled_second)
    grad_rows, grad_enc, grad_benc = final(
        raw, code_half, theirs, turned_tokens, grad_rows, rows
    )
    return (grad_rows, grad_enc, grad_benc.reshape(-1))


def solution(mesh):
    return jax.shard_map(
        local,
        mesh=mesh,
        in_specs=(
            P(("grp", "feat"), "tok"),
            P(("grp", "tok")),
            P("grp", None),
            P("grp", None),
            P(("grp", "feat")),
            P(("grp", "feat")),
            P(("grp", "feat"), "tok"),
        ),
        out_specs=(P(("grp", "feat"), "tok"), P(("grp", "tok"), "feat"), P(("grp", "feat"))),
        check_vma=False,
    )
```

```python
import functools

import jax
import jax.numpy as jnp
from jax import lax
from jax.experimental import pallas as pl
from jax.experimental.pallas import tpu as pltpu
from jax.sharding import PartitionSpec as P

VMEM = pl.BlockSpec(memory_space=pltpu.VMEM)
SMEM = pl.BlockSpec(memory_space=pltpu.SMEM)
HBM = pl.BlockSpec(memory_space=pltpu.HBM)
ANY = pl.BlockSpec(memory_space=pl.ANY)
EARLY = 10**9
ROWS = 16


def kernel_call(kernel, out_shape, in_specs, out_specs, tokens, scratch_shapes=(), flops=10**6):
    limit = (16 if tokens <= ROWS else 40) * 2**20
    return pl.pallas_call(
        kernel,
        out_shape=out_shape,
        in_specs=in_specs,
        out_specs=out_specs,
        scratch_shapes=scratch_shapes,
        compiler_params=pltpu.CompilerParams(vmem_limit_bytes=limit),
        cost_estimate=pl.CostEstimate(flops=flops, bytes_accessed=2**20, transcendentals=0),
    )


def shape(*sizes, dtype=jnp.bfloat16):
    return jax.ShapeDtypeStruct(sizes, dtype)


def first_width(width):
    return width // 2


def feat_bits():
    return (lax.axis_size("feat") - 1).bit_length()


def bit_of(step, core):
    bits = list(range(feat_bits()))
    return (bits[::-1] if core == 0 else bits)[step]


def swapped(shard, step):
    cores = lax.axis_size("tok")
    pairs = [
        (f * cores + c, (f ^ 1 << bit_of(step, c)) * cores + c)
        for f in range(lax.axis_size("feat"))
        for c in range(cores)
    ]
    return lax.ppermute(shard, ("feat", "tok"), pairs)


def stacked(rows, pieces):
    width = rows.shape[1] // pieces
    return jnp.concatenate(
        [rows[:, c * width : (c + 1) * width] for c in range(pieces)], axis=0
    )


def share(code, rows_ref, centered_ref, at, width):
    part = pl.ds(at, width)
    total = jnp.dot(code, rows_ref[:, part], preferred_element_type=jnp.float32)
    rows = centered_ref.shape[0]
    centered = centered_ref[:, part]
    token = lax.broadcasted_iota(jnp.int32, (total.shape[0], 1), 0)
    first = lax.axis_index("feat") * rows
    for i in range(rows):
        total -= jnp.where(token == first + i, centered[i : i + 1, :], 0.0)
    return total


def order_kernel(rows, order_ref):
    target = lax.broadcasted_iota(jnp.int32, order_ref.shape, 0)
    place = lax.broadcasted_iota(jnp.int32, order_ref.shape, 1)
    core = lax.axis_index("tok")
    block = place // ROWS
    distance = jnp.zeros_like(place)
    for step in range(feat_bits()):
        bit = sum(
            jnp.where(core == c, bit_of(step, c), 0) for c in range(lax.axis_size("tok"))
        )
        distance |= (block >> step & 1) << bit
    token = (lax.axis_index("feat") ^ distance) * rows + place % rows
    piece = place % ROWS // rows
    count = rows * lax.axis_size("feat")
    order_ref[...] = jnp.where(target == piece * count + token, 1.0, 0.0).astype(jnp.bfloat16)


def order_of(rows, count):
    depth = ROWS * lax.axis_size("feat")
    return kernel_call(
        functools.partial(order_kernel, rows),
        shape(depth, depth),
        [],
        VMEM,
        count,
        flops=EARLY,
    )()


def front_kernel(
    tokens_ref, bias_flat, pre_ref, top_ref, rows_ref, block_ref, count_ref, after_ref, *refs
):
    code_ref, raw_ref, total_ref, sent_ref, centered_ref, bias_ref, *cut = refs
    count, latents = top_ref.shape
    slots, width = rows_ref.shape
    offsets = lax.broadcasted_iota(jnp.int32, (1, slots), 1)
    slot_ids = jnp.where(offsets < count_ref[0], block_ref[0] * slots + offsets, -1)
    top, pre = top_ref[...], pre_ref[...]
    raw = jnp.zeros((count, slots), jnp.float32)
    for k in range(latents):
        raw = jnp.where(top[:, k : k + 1] == slot_ids, pre[:, k : k + 1], raw)
    raw_ref[...] = raw
    code = jnp.maximum(raw, 0.0).astype(jnp.bfloat16)
    code_ref[...] = code

    tokens = tokens_ref[...].astype(jnp.float32)
    bias = bias_flat[...].astype(jnp.float32).reshape(1, width)
    bias_ref[...] = bias
    centered_ref[...] = (tokens - bias).astype(jnp.bfloat16).astype(jnp.float32)

    total = share(code, rows_ref, centered_ref, 0, total_ref.shape[1])
    total_ref[...] = total
    width = total.shape[1]
    sent_ref[:, :width] = total.astype(jnp.bfloat16)
    block = stacked(tokens, ROWS // tokens.shape[0]).astype(jnp.bfloat16)
    if cut:
        cut[0][...] = block
    else:
        sent_ref[:, width:] = block


def front(tokens, b_pre, pre_codes, top_idx, blocks, counts, dict_rows, after, merged):
    count = top_idx.shape[0]
    slots, width = dict_rows.shape
    chunk, block = first_width(width), tokens.shape[0] * width // ROWS
    return kernel_call(
        front_kernel,
        (
            shape(count, slots),
            shape(count, slots, dtype=jnp.float32),
            shape(count, chunk, dtype=jnp.float32),
            shape(count, chunk + (block if merged else 0)),
            shape(*tokens.shape, dtype=jnp.float32),
            shape(1, width, dtype=jnp.float32),
            *([] if merged else [shape(ROWS, block)]),
        ),
        [VMEM] * 5 + [SMEM] * 2 + [ANY],
        (VMEM,) * (6 if merged else 7),
        count,
    )(tokens, b_pre, pre_codes, top_idx, dict_rows, blocks, counts, after)


def second_kernel(code_ref, rows_ref, centered_ref, total_ref, sent_ref):
    width = total_ref.shape[1]
    total = share(code_ref[...], rows_ref, centered_ref, rows_ref.shape[1] - width, width)
    total_ref[...] = total
    sent_ref[...] = total.astype(jnp.bfloat16)


def second(code, dict_rows, centered):
    count, width = code.shape[0], dict_rows.shape[1]
    chunk = width - first_width(width)
    return kernel_call(
        second_kernel,
        (shape(count, chunk, dtype=jnp.float32), shape(count, chunk)),
        [VMEM] * 3,
        (VMEM, VMEM),
        count,
    )(code, dict_rows, centered)


def added_kernel(total_ref, own_ref, arrived_ref, after_ref, sum_ref, sent_ref):
    half = total_ref.shape[1]
    total = total_ref[...] + arrived_ref[:, :half].astype(jnp.float32)
    sum_ref[...] = total
    sent_ref[:, :half] = total.astype(jnp.bfloat16)
    if sent_ref.shape[1] > half:
        block = own_ref.shape[1] - half
        sent_ref[:, half : half + block] = own_ref[:, half:]
        sent_ref[:, half + block :] = arrived_ref[:, half:]


def added(total, own, arrived, after, merged, flops=10**6):
    count, half = total.shape
    block = own.shape[1] - half
    return kernel_call(
        added_kernel,
        (
            shape(count, half, dtype=jnp.float32),
            shape(count, half + (2 * block if merged else 0)),
        ),
        [VMEM] * 3 + [ANY],
        (VMEM, VMEM),
        count,
        flops=flops,
    )(total, own, arrived, after)


def joined_kernel(first_ref, second_ref, after_ref, out_ref):
    width = first_ref.shape[1]
    out_ref[:, :width] = first_ref[...]
    out_ref[:, width:] = second_ref[...]


def joined(first, second, after):
    return kernel_call(
        joined_kernel,
        shape(first.shape[0], 2 * first.shape[1]),
        [VMEM, VMEM, ANY],
        VMEM,
        first.shape[0],
    )(first, second, after)


def turned_kernel(skip, rows, own_ref, arrived_ref, bias_ref, order_ref, out_ref):
    bias = jnp.concatenate([bias_ref[...]] * rows, axis=0)
    bias = stacked(bias, ROWS // rows)
    width = bias.shape[1]
    blocks = [
        (ref[:, at : at + width].astype(jnp.float32) - bias).astype(jnp.bfloat16)
        for ref in (own_ref, arrived_ref)
        for at in range(skip, ref.shape[1], width)
    ]
    ordered = jnp.dot(
        order_ref[...], jnp.concatenate(blocks, axis=0), preferred_element_type=jnp.float32
    )
    out_ref[...] = ordered.T.astype(jnp.bfloat16)


def turned(own, arrived, skip, bias, order, rows, count):
    width = bias.shape[1] * rows // ROWS
    return kernel_call(
        functools.partial(turned_kernel, skip, rows),
        shape(width, 2 * (own.shape[1] - skip) // width * ROWS),
        [VMEM] * 4,
        VMEM,
        count,
    )(own, arrived, bias, order)


def scaled_of(total_ref, arrived_ref):
    total = total_ref[...] + arrived_ref[:, : total_ref.shape[1]].astype(jnp.float32)
    return (0.25 * total).astype(jnp.bfloat16)


def product(part, rows_ref, at):
    return lax.dot_general(
        part,
        rows_ref[:, at : at + part.shape[1]],
        (((1,), (1,)), ((), ())),
        preferred_element_type=jnp.float32,
    )


def first_product_kernel(total_ref, arrived_ref, rows_ref, scaled_ref, half_ref):
    scaled = scaled_of(total_ref, arrived_ref)
    scaled_ref[...] = scaled
    half_ref[...] = product(scaled, rows_ref, 0)


def second_product_kernel(total_ref, arrived_ref, rows_ref, first_ref, scaled_ref, half_ref):
    scaled = scaled_of(total_ref, arrived_ref)
    scaled_ref[...] = scaled
    half_ref[...] = first_ref[...] + product(scaled, rows_ref, rows_ref.shape[1] - scaled.shape[1])


def products(total, arrived, dict_rows, *first):
    count, width = total.shape
    return kernel_call(
        second_product_kernel if first else first_product_kernel,
        (shape(count, width), shape(count, dict_rows.shape[0], dtype=jnp.float32)),
        [VMEM] * (3 + len(first)),
        (VMEM, VMEM),
        count,
    )(total, arrived, dict_rows, *first)


def outer(code_ref, scaled):
    code = code_ref[...].astype(jnp.float32).T.astype(jnp.bfloat16)
    return jnp.dot(code, scaled, preferred_element_type=jnp.float32).astype(jnp.bfloat16)


def grad_rows_kernel(code_ref, first_ref, second_ref, out_ref):
    chunk = first_ref.shape[1]
    out_ref[:, :chunk] = outer(code_ref, first_ref[...])
    out_ref[:, chunk:] = outer(code_ref, second_ref[...])


def grad_rows_of(code, first, second):
    count, slots = code.shape
    return kernel_call(
        grad_rows_kernel,
        shape(slots, first.shape[1] + second.shape[1]),
        [VMEM] * 3,
        VMEM,
        count,
    )(code, first, second)


def final_kernel(
    rows,
    raw_ref,
    mine_ref,
    theirs_ref,
    turned_ref,
    rows_ref,
    rows_hbm,
    enc_hbm,
    benc_hbm,
    enc_ref,
    benc_ref,
    sems,
):
    copies = [pltpu.make_async_copy(rows_ref, rows_hbm, sems.at[0])]
    copies[0].start()
    count, slots = raw_ref.shape
    width = turned_ref.shape[0]
    pieces = ROWS // rows
    code_grad = mine_ref[...] + theirs_ref[...]
    pre_grad = jnp.where(raw_ref[...] > 0.0, code_grad, 0.0).astype(jnp.bfloat16)
    benc_ref[...] = jnp.sum(pre_grad.astype(jnp.float32), axis=0, keepdims=True)
    copies.append(pltpu.make_async_copy(benc_ref, benc_hbm, sems.at[1]))
    copies[1].start()
    zeros = jnp.zeros_like(pre_grad)
    for c in range(0, pieces, 2):
        pair = [
            jnp.concatenate([zeros] * at + [pre_grad] + [zeros] * (pieces - 1 - at), axis=0)
            for at in (c, c + 1)
        ]
        out = jnp.dot(
            turned_ref[...],
            jnp.concatenate(pair, axis=1),
            preferred_element_type=jnp.float32,
        ).astype(jnp.bfloat16)
        for i in range(2):
            enc_ref[(c + i) * width : (c + i + 1) * width, :] = out[:, i * slots : (i + 1) * slots]
        part = pl.ds(c * width, 2 * width)
        copies.append(pltpu.make_async_copy(enc_ref.at[part], enc_hbm.at[part], sems.at[c // 2 + 2]))
        copies[-1].start()
    for copy in copies:
        copy.wait()


def final(raw, mine, theirs, turned_tokens, grad_rows, rows):
    count, slots = raw.shape
    pieces = ROWS // rows
    width = turned_tokens.shape[0] * pieces
    return kernel_call(
        functools.partial(final_kernel, rows),
        (shape(*grad_rows.shape), shape(width, slots), shape(1, slots, dtype=jnp.float32)),
        [VMEM] * 5,
        (HBM, HBM, HBM),
        count,
        [
            pltpu.VMEM((width, slots), jnp.bfloat16),
            pltpu.VMEM((1, slots), jnp.float32),
            pltpu.SemaphoreType.DMA((pieces // 2 + 2,)),
        ],
    )(raw, mine, theirs, turned_tokens, grad_rows)


def local(tokens, b_pre, pre_codes, top_idx, blocks, counts, dict_rows):
    rows, count = tokens.shape[0], top_idx.shape[0]
    steps = feat_bits()
    merged = count == ROWS

    order = order_of(rows, count)
    code, raw, total, sent, centered, bias, *block = front(
        tokens, b_pre, pre_codes, top_idx, blocks, counts, dict_rows, order, merged
    )
    for step in range(steps):
        arrived = swapped(sent, step)
        if step == 0:
            total_second, sent_second = second(code, dict_rows, centered)
        else:
            total_second, sent_second = added(
                total_second, sent_second, arrived_second, sent, False, EARLY
            )
        arrived_second = swapped(sent_second, step)
        if not merged:
            own_block = joined(own_block, arrived_block, sent_second) if step else block[0]
            arrived_block = swapped(own_block, step)
        if step < steps - 1:
            total, sent = added(total, sent, arrived, sent_second, merged)
    skip = 0
    if merged:
        own_block, arrived_block, skip = sent, arrived, total.shape[1]

    scaled, product_first = products(total, arrived, dict_rows)
    turned_tokens = turned(own_block, arrived_block, skip, bias, order, rows, count)
    scaled_second, code_half = products(
        total_second, arrived_second, dict_rows, product_first
    )
    theirs = lax.ppermute(code_half, "tok", [(i, 1 - i) for i in range(2)])
    grad_rows = grad_rows_of(code, scaled, scaled_second)
    grad_rows, grad_enc, grad_benc = final(
        raw, code_half, theirs, turned_tokens, grad_rows, rows
    )
    return (grad_rows, grad_enc, grad_benc.reshape(-1))


def solution(mesh):
    return jax.shard_map(
        local,
        mesh=mesh,
        in_specs=(
            P(("grp", "feat"), "tok"),
            P(("grp", "tok")),
            P("grp", None),
            P("grp", None),
            P(("grp", "feat")),
            P(("grp", "feat")),
            P(("grp", "feat"), "tok"),
        ),
        out_specs=(P(("grp", "feat"), "tok"), P(("grp", "tok"), "feat"), P(("grp", "feat"))),
        check_vma=False,
    )
```

```python
import functools

import jax
import jax.numpy as jnp
from jax import lax
from jax.experimental import pallas as pl
from jax.experimental.pallas import tpu as pltpu
from jax.sharding import PartitionSpec as P

VMEM = pl.BlockSpec(memory_space=pltpu.VMEM)
SMEM = pl.BlockSpec(memory_space=pltpu.SMEM)
HBM = pl.BlockSpec(memory_space=pltpu.HBM)
ANY = pl.BlockSpec(memory_space=pl.ANY)
EARLY = 10**9
ROWS = 16


def kernel_call(kernel, out_shape, in_specs, out_specs, tokens, scratch_shapes=(), flops=10**6):
    limit = (16 if tokens <= ROWS else 40) * 2**20
    return pl.pallas_call(
        kernel,
        out_shape=out_shape,
        in_specs=in_specs,
        out_specs=out_specs,
        scratch_shapes=scratch_shapes,
        compiler_params=pltpu.CompilerParams(vmem_limit_bytes=limit),
        cost_estimate=pl.CostEstimate(flops=flops, bytes_accessed=2**20, transcendentals=0),
    )


def shape(*sizes, dtype=jnp.bfloat16):
    return jax.ShapeDtypeStruct(sizes, dtype)


def first_width(width):
    return width // 2


def feat_bits():
    return (lax.axis_size("feat") - 1).bit_length()


def bit_of(step, core):
    bits = list(range(feat_bits()))
    first = bits[-1:] + bits[:-1]
    return (first if core == 0 else bits[1:2] + bits[:1] + bits[2:])[step]


def swapped(shard, step):
    cores = lax.axis_size("tok")
    pairs = [
        (f * cores + c, (f ^ 1 << bit_of(step, c)) * cores + c)
        for f in range(lax.axis_size("feat"))
        for c in range(cores)
    ]
    return lax.ppermute(shard, ("feat", "tok"), pairs)


def stacked(rows, pieces):
    width = rows.shape[1] // pieces
    return jnp.concatenate(
        [rows[:, c * width : (c + 1) * width] for c in range(pieces)], axis=0
    )


def share(code, rows_ref, centered_ref, at, width):
    part = pl.ds(at, width)
    total = jnp.dot(code, rows_ref[:, part], preferred_element_type=jnp.float32)
    rows = centered_ref.shape[0]
    centered = centered_ref[:, part]
    token = lax.broadcasted_iota(jnp.int32, (total.shape[0], 1), 0)
    first = lax.axis_index("feat") * rows
    for i in range(rows):
        total -= jnp.where(token == first + i, centered[i : i + 1, :], 0.0)
    return total


def order_kernel(rows, order_ref):
    target = lax.broadcasted_iota(jnp.int32, order_ref.shape, 0)
    place = lax.broadcasted_iota(jnp.int32, order_ref.shape, 1)
    core = lax.axis_index("tok")
    block = place // ROWS
    distance = jnp.zeros_like(place)
    for step in range(feat_bits()):
        bit = sum(
            jnp.where(core == c, bit_of(step, c), 0) for c in range(lax.axis_size("tok"))
        )
        distance |= (block >> step & 1) << bit
    token = (lax.axis_index("feat") ^ distance) * rows + place % rows
    piece = place % ROWS // rows
    count = rows * lax.axis_size("feat")
    order_ref[...] = jnp.where(target == piece * count + token, 1.0, 0.0).astype(jnp.bfloat16)


def order_of(rows, count):
    depth = ROWS * lax.axis_size("feat")
    return kernel_call(
        functools.partial(order_kernel, rows),
        shape(depth, depth),
        [],
        VMEM,
        count,
        flops=EARLY,
    )()


def front_kernel(
    tokens_ref, bias_flat, pre_ref, top_ref, rows_ref, block_ref, count_ref, after_ref, *refs
):
    code_ref, raw_ref, total_ref, sent_ref, centered_ref, bias_ref, *cut = refs
    count, latents = top_ref.shape
    slots, width = rows_ref.shape
    offsets = lax.broadcasted_iota(jnp.int32, (1, slots), 1)
    slot_ids = jnp.where(offsets < count_ref[0], block_ref[0] * slots + offsets, -1)
    top, pre = top_ref[...], pre_ref[...]
    raw = jnp.zeros((count, slots), jnp.float32)
    for k in range(latents):
        raw = jnp.where(top[:, k : k + 1] == slot_ids, pre[:, k : k + 1], raw)
    raw_ref[...] = raw
    code = jnp.maximum(raw, 0.0).astype(jnp.bfloat16)
    code_ref[...] = code

    tokens = tokens_ref[...].astype(jnp.float32)
    bias = bias_flat[...].astype(jnp.float32).reshape(1, width)
    bias_ref[...] = bias
    centered_ref[...] = (tokens - bias).astype(jnp.bfloat16).astype(jnp.float32)

    total = share(code, rows_ref, centered_ref, 0, total_ref.shape[1])
    total_ref[...] = total
    width = total.shape[1]
    sent_ref[:, :width] = total.astype(jnp.bfloat16)
    block = stacked(tokens, ROWS // tokens.shape[0]).astype(jnp.bfloat16)
    if cut:
        cut[0][...] = block
    else:
        sent_ref[:, width:] = block


def front(tokens, b_pre, pre_codes, top_idx, blocks, counts, dict_rows, after, merged):
    count = top_idx.shape[0]
    slots, width = dict_rows.shape
    chunk, block = first_width(width), tokens.shape[0] * width // ROWS
    return kernel_call(
        front_kernel,
        (
            shape(count, slots),
            shape(count, slots, dtype=jnp.float32),
            shape(count, chunk, dtype=jnp.float32),
            shape(count, chunk + (block if merged else 0)),
            shape(*tokens.shape, dtype=jnp.float32),
            shape(1, width, dtype=jnp.float32),
            *([] if merged else [shape(ROWS, block)]),
        ),
        [VMEM] * 5 + [SMEM] * 2 + [ANY],
        (VMEM,) * (6 if merged else 7),
        count,
    )(tokens, b_pre, pre_codes, top_idx, dict_rows, blocks, counts, after)


def second_kernel(code_ref, rows_ref, centered_ref, total_ref, sent_ref):
    width = total_ref.shape[1]
    total = share(code_ref[...], rows_ref, centered_ref, rows_ref.shape[1] - width, width)
    total_ref[...] = total
    sent_ref[...] = total.astype(jnp.bfloat16)


def second(code, dict_rows, centered):
    count, width = code.shape[0], dict_rows.shape[1]
    chunk = width - first_width(width)
    return kernel_call(
        second_kernel,
        (shape(count, chunk, dtype=jnp.float32), shape(count, chunk)),
        [VMEM] * 3,
        (VMEM, VMEM),
        count,
    )(code, dict_rows, centered)


def added_kernel(total_ref, own_ref, arrived_ref, after_ref, sum_ref, sent_ref):
    half = total_ref.shape[1]
    total = total_ref[...] + arrived_ref[:, :half].astype(jnp.float32)
    sum_ref[...] = total
    sent_ref[:, :half] = total.astype(jnp.bfloat16)
    if sent_ref.shape[1] > half:
        block = own_ref.shape[1] - half
        sent_ref[:, half : half + block] = own_ref[:, half:]
        sent_ref[:, half + block :] = arrived_ref[:, half:]


def added(total, own, arrived, after, merged, flops=10**6):
    count, half = total.shape
    block = own.shape[1] - half
    return kernel_call(
        added_kernel,
        (
            shape(count, half, dtype=jnp.float32),
            shape(count, half + (2 * block if merged else 0)),
        ),
        [VMEM] * 3 + [ANY],
        (VMEM, VMEM),
        count,
        flops=flops,
    )(total, own, arrived, after)


def joined_kernel(first_ref, second_ref, after_ref, out_ref):
    width = first_ref.shape[1]
    out_ref[:, :width] = first_ref[...]
    out_ref[:, width:] = second_ref[...]


def joined(first, second, after):
    return kernel_call(
        joined_kernel,
        shape(first.shape[0], 2 * first.shape[1]),
        [VMEM, VMEM, ANY],
        VMEM,
        first.shape[0],
    )(first, second, after)


def turned_kernel(skip, rows, own_ref, arrived_ref, bias_ref, order_ref, out_ref):
    bias = jnp.concatenate([bias_ref[...]] * rows, axis=0)
    bias = stacked(bias, ROWS // rows)
    width = bias.shape[1]
    blocks = [
        (ref[:, at : at + width].astype(jnp.float32) - bias).astype(jnp.bfloat16)
        for ref in (own_ref, arrived_ref)
        for at in range(skip, ref.shape[1], width)
    ]
    ordered = jnp.dot(
        order_ref[...], jnp.concatenate(blocks, axis=0), preferred_element_type=jnp.float32
    )
    out_ref[...] = ordered.T.astype(jnp.bfloat16)


def turned(own, arrived, skip, bias, order, rows, count):
    width = bias.shape[1] * rows // ROWS
    return kernel_call(
        functools.partial(turned_kernel, skip, rows),
        shape(width, 2 * (own.shape[1] - skip) // width * ROWS),
        [VMEM] * 4,
        VMEM,
        count,
    )(own, arrived, bias, order)


def scaled_of(total_ref, arrived_ref):
    total = total_ref[...] + arrived_ref[:, : total_ref.shape[1]].astype(jnp.float32)
    return (0.25 * total).astype(jnp.bfloat16)


def product(part, rows_ref, at):
    return lax.dot_general(
        part,
        rows_ref[:, at : at + part.shape[1]],
        (((1,), (1,)), ((), ())),
        preferred_element_type=jnp.float32,
    )


def first_product_kernel(total_ref, arrived_ref, rows_ref, scaled_ref, half_ref):
    scaled = scaled_of(total_ref, arrived_ref)
    scaled_ref[...] = scaled
    half_ref[...] = product(scaled, rows_ref, 0)


def second_product_kernel(total_ref, arrived_ref, rows_ref, first_ref, scaled_ref, half_ref):
    scaled = scaled_of(total_ref, arrived_ref)
    scaled_ref[...] = scaled
    half_ref[...] = first_ref[...] + product(scaled, rows_ref, rows_ref.shape[1] - scaled.shape[1])


def products(total, arrived, dict_rows, *first):
    count, width = total.shape
    return kernel_call(
        second_product_kernel if first else first_product_kernel,
        (shape(count, width), shape(count, dict_rows.shape[0], dtype=jnp.float32)),
        [VMEM] * (3 + len(first)),
        (VMEM, VMEM),
        count,
    )(total, arrived, dict_rows, *first)


def outer(code_ref, scaled):
    code = code_ref[...].astype(jnp.float32).T.astype(jnp.bfloat16)
    return jnp.dot(code, scaled, preferred_element_type=jnp.float32).astype(jnp.bfloat16)


def grad_rows_kernel(code_ref, first_ref, second_ref, out_ref):
    chunk = first_ref.shape[1]
    out_ref[:, :chunk] = outer(code_ref, first_ref[...])
    out_ref[:, chunk:] = outer(code_ref, second_ref[...])


def grad_rows_of(code, first, second):
    count, slots = code.shape
    return kernel_call(
        grad_rows_kernel,
        shape(slots, first.shape[1] + second.shape[1]),
        [VMEM] * 3,
        VMEM,
        count,
    )(code, first, second)


def final_kernel(
    rows,
    raw_ref,
    mine_ref,
    theirs_ref,
    turned_ref,
    rows_ref,
    rows_hbm,
    enc_hbm,
    benc_hbm,
    enc_ref,
    benc_ref,
    sems,
):
    copies = [pltpu.make_async_copy(rows_ref, rows_hbm, sems.at[0])]
    copies[0].start()
    count, slots = raw_ref.shape
    width = turned_ref.shape[0]
    pieces = ROWS // rows
    code_grad = mine_ref[...] + theirs_ref[...]
    pre_grad = jnp.where(raw_ref[...] > 0.0, code_grad, 0.0).astype(jnp.bfloat16)
    benc_ref[...] = jnp.sum(pre_grad.astype(jnp.float32), axis=0, keepdims=True)
    copies.append(pltpu.make_async_copy(benc_ref, benc_hbm, sems.at[1]))
    copies[1].start()
    zeros = jnp.zeros_like(pre_grad)
    for c in range(0, pieces, 2):
        pair = [
            jnp.concatenate([zeros] * at + [pre_grad] + [zeros] * (pieces - 1 - at), axis=0)
            for at in (c, c + 1)
        ]
        out = jnp.dot(
            turned_ref[...],
            jnp.concatenate(pair, axis=1),
            preferred_element_type=jnp.float32,
        ).astype(jnp.bfloat16)
        for i in range(2):
            enc_ref[(c + i) * width : (c + i + 1) * width, :] = out[:, i * slots : (i + 1) * slots]
        part = pl.ds(c * width, 2 * width)
        copies.append(pltpu.make_async_copy(enc_ref.at[part], enc_hbm.at[part], sems.at[c // 2 + 2]))
        copies[-1].start()
    for copy in copies:
        copy.wait()


def final(raw, mine, theirs, turned_tokens, grad_rows, rows):
    count, slots = raw.shape
    pieces = ROWS // rows
    width = turned_tokens.shape[0] * pieces
    return kernel_call(
        functools.partial(final_kernel, rows),
        (shape(*grad_rows.shape), shape(width, slots), shape(1, slots, dtype=jnp.float32)),
        [VMEM] * 5,
        (HBM, HBM, HBM),
        count,
        [
            pltpu.VMEM((width, slots), jnp.bfloat16),
            pltpu.VMEM((1, slots), jnp.float32),
            pltpu.SemaphoreType.DMA((pieces // 2 + 2,)),
        ],
    )(raw, mine, theirs, turned_tokens, grad_rows)


def local(tokens, b_pre, pre_codes, top_idx, blocks, counts, dict_rows):
    rows, count = tokens.shape[0], top_idx.shape[0]
    steps = feat_bits()
    merged = count == ROWS

    order = order_of(rows, count)
    code, raw, total, sent, centered, bias, *block = front(
        tokens, b_pre, pre_codes, top_idx, blocks, counts, dict_rows, order, merged
    )
    for step in range(steps):
        arrived = swapped(sent, step)
        if step == 0:
            total_second, sent_second = second(code, dict_rows, centered)
        else:
            total_second, sent_second = added(
                total_second, sent_second, arrived_second, sent, False, EARLY
            )
        arrived_second = swapped(sent_second, step)
        if not merged:
            own_block = joined(own_block, arrived_block, sent_second) if step else block[0]
            arrived_block = swapped(own_block, step)
        if step < steps - 1:
            total, sent = added(total, sent, arrived, sent_second, merged)
    skip = 0
    if merged:
        own_block, arrived_block, skip = sent, arrived, total.shape[1]

    scaled, product_first = products(total, arrived, dict_rows)
    turned_tokens = turned(own_block, arrived_block, skip, bias, order, rows, count)
    scaled_second, code_half = products(
        total_second, arrived_second, dict_rows, product_first
    )
    theirs = lax.ppermute(code_half, "tok", [(i, 1 - i) for i in range(2)])
    grad_rows = grad_rows_of(code, scaled, scaled_second)
    grad_rows, grad_enc, grad_benc = final(
        raw, code_half, theirs, turned_tokens, grad_rows, rows
    )
    return (grad_rows, grad_enc, grad_benc.reshape(-1))


def solution(mesh):
    return jax.shard_map(
        local,
        mesh=mesh,
        in_specs=(
            P(("grp", "feat"), "tok"),
            P(("grp", "tok")),
            P("grp", None),
            P("grp", None),
            P(("grp", "feat")),
            P(("grp", "feat")),
            P(("grp", "feat"), "tok"),
        ),
        out_specs=(P(("grp", "feat"), "tok"), P(("grp", "tok"), "feat"), P(("grp", "feat"))),
        check_vma=False,
    )
```

```python
import functools

import jax
import jax.numpy as jnp
from jax import lax
from jax.experimental import pallas as pl
from jax.experimental.pallas import tpu as pltpu
from jax.sharding import PartitionSpec as P

VMEM = pl.BlockSpec(memory_space=pltpu.VMEM)
SMEM = pl.BlockSpec(memory_space=pltpu.SMEM)
HBM = pl.BlockSpec(memory_space=pltpu.HBM)
ANY = pl.BlockSpec(memory_space=pl.ANY)
EARLY = 10**9
ROWS = 16


def kernel_call(kernel, out_shape, in_specs, out_specs, tokens, scratch_shapes=(), flops=10**6):
    limit = (16 if tokens <= ROWS else 40) * 2**20
    return pl.pallas_call(
        kernel,
        out_shape=out_shape,
        in_specs=in_specs,
        out_specs=out_specs,
        scratch_shapes=scratch_shapes,
        compiler_params=pltpu.CompilerParams(vmem_limit_bytes=limit),
        cost_estimate=pl.CostEstimate(flops=flops, bytes_accessed=2**20, transcendentals=0),
    )


def shape(*sizes, dtype=jnp.bfloat16):
    return jax.ShapeDtypeStruct(sizes, dtype)


def first_width(width):
    return width * 7 // 16 // 128 * 128


def feat_bits():
    return (lax.axis_size("feat") - 1).bit_length()


def bit_of(step, core):
    bits = list(range(feat_bits()))
    first = bits[-1:] + bits[:-1]
    return (first if core == 0 else bits[1:2] + bits[:1] + bits[2:])[step]


def swapped(shard, step):
    cores = lax.axis_size("tok")
    pairs = [
        (f * cores + c, (f ^ 1 << bit_of(step, c)) * cores + c)
        for f in range(lax.axis_size("feat"))
        for c in range(cores)
    ]
    return lax.ppermute(shard, ("feat", "tok"), pairs)


def stacked(rows, pieces):
    width = rows.shape[1] // pieces
    return jnp.concatenate(
        [rows[:, c * width : (c + 1) * width] for c in range(pieces)], axis=0
    )


def share(code, rows_ref, centered_ref, at, width):
    part = pl.ds(at, width)
    total = jnp.dot(code, rows_ref[:, part], preferred_element_type=jnp.float32)
    rows = centered_ref.shape[0]
    centered = centered_ref[:, part]
    token = lax.broadcasted_iota(jnp.int32, (total.shape[0], 1), 0)
    first = lax.axis_index("feat") * rows
    for i in range(rows):
        total -= jnp.where(token == first + i, centered[i : i + 1, :], 0.0)
    return total


def order_kernel(rows, order_ref):
    target = lax.broadcasted_iota(jnp.int32, order_ref.shape, 0)
    place = lax.broadcasted_iota(jnp.int32, order_ref.shape, 1)
    core = lax.axis_index("tok")
    block = place // ROWS
    distance = jnp.zeros_like(place)
    for step in range(feat_bits()):
        bit = sum(
            jnp.where(core == c, bit_of(step, c), 0) for c in range(lax.axis_size("tok"))
        )
        distance |= (block >> step & 1) << bit
    token = (lax.axis_index("feat") ^ distance) * rows + place % rows
    piece = place % ROWS // rows
    count = rows * lax.axis_size("feat")
    order_ref[...] = jnp.where(target == piece * count + token, 1.0, 0.0).astype(jnp.bfloat16)


def order_of(rows, count):
    depth = ROWS * lax.axis_size("feat")
    return kernel_call(
        functools.partial(order_kernel, rows),
        shape(depth, depth),
        [],
        VMEM,
        count,
        flops=EARLY,
    )()


def front_kernel(
    tokens_ref, bias_flat, pre_ref, top_ref, rows_ref, block_ref, count_ref, after_ref, *refs
):
    code_ref, raw_ref, total_ref, sent_ref, centered_ref, bias_ref, *cut = refs
    count, latents = top_ref.shape
    slots, width = rows_ref.shape
    offsets = lax.broadcasted_iota(jnp.int32, (1, slots), 1)
    slot_ids = jnp.where(offsets < count_ref[0], block_ref[0] * slots + offsets, -1)
    top, pre = top_ref[...], pre_ref[...]
    raw = jnp.zeros((count, slots), jnp.float32)
    for k in range(latents):
        raw = jnp.where(top[:, k : k + 1] == slot_ids, pre[:, k : k + 1], raw)
    raw_ref[...] = raw
    code = jnp.maximum(raw, 0.0).astype(jnp.bfloat16)
    code_ref[...] = code

    tokens = tokens_ref[...].astype(jnp.float32)
    bias = bias_flat[...].astype(jnp.float32).reshape(1, width)
    bias_ref[...] = bias
    centered_ref[...] = (tokens - bias).astype(jnp.bfloat16).astype(jnp.float32)

    total = share(code, rows_ref, centered_ref, 0, total_ref.shape[1])
    total_ref[...] = total
    width = total.shape[1]
    sent_ref[:, :width] = total.astype(jnp.bfloat16)
    block = stacked(tokens, ROWS // tokens.shape[0]).astype(jnp.bfloat16)
    if cut:
        cut[0][...] = block
    else:
        sent_ref[:, width:] = block


def front(tokens, b_pre, pre_codes, top_idx, blocks, counts, dict_rows, after, merged):
    count = top_idx.shape[0]
    slots, width = dict_rows.shape
    chunk, block = first_width(width), tokens.shape[0] * width // ROWS
    return kernel_call(
        front_kernel,
        (
            shape(count, slots),
            shape(count, slots, dtype=jnp.float32),
            shape(count, chunk, dtype=jnp.float32),
            shape(count, chunk + (block if merged else 0)),
            shape(*tokens.shape, dtype=jnp.float32),
            shape(1, width, dtype=jnp.float32),
            *([] if merged else [shape(ROWS, block)]),
        ),
        [VMEM] * 5 + [SMEM] * 2 + [ANY],
        (VMEM,) * (6 if merged else 7),
        count,
    )(tokens, b_pre, pre_codes, top_idx, dict_rows, blocks, counts, after)


def second_kernel(code_ref, rows_ref, centered_ref, total_ref, sent_ref):
    width = total_ref.shape[1]
    total = share(code_ref[...], rows_ref, centered_ref, rows_ref.shape[1] - width, width)
    total_ref[...] = total
    sent_ref[...] = total.astype(jnp.bfloat16)


def second(code, dict_rows, centered):
    count, width = code.shape[0], dict_rows.shape[1]
    chunk = width - first_width(width)
    return kernel_call(
        second_kernel,
        (shape(count, chunk, dtype=jnp.float32), shape(count, chunk)),
        [VMEM] * 3,
        (VMEM, VMEM),
        count,
    )(code, dict_rows, centered)


def added_kernel(total_ref, own_ref, arrived_ref, after_ref, sum_ref, sent_ref):
    half = total_ref.shape[1]
    total = total_ref[...] + arrived_ref[:, :half].astype(jnp.float32)
    sum_ref[...] = total
    sent_ref[:, :half] = total.astype(jnp.bfloat16)
    if sent_ref.shape[1] > half:
        block = own_ref.shape[1] - half
        sent_ref[:, half : half + block] = own_ref[:, half:]
        sent_ref[:, half + block :] = arrived_ref[:, half:]


def added(total, own, arrived, after, merged, flops=10**6):
    count, half = total.shape
    block = own.shape[1] - half
    return kernel_call(
        added_kernel,
        (
            shape(count, half, dtype=jnp.float32),
            shape(count, half + (2 * block if merged else 0)),
        ),
        [VMEM] * 3 + [ANY],
        (VMEM, VMEM),
        count,
        flops=flops,
    )(total, own, arrived, after)


def joined_kernel(first_ref, second_ref, after_ref, out_ref):
    width = first_ref.shape[1]
    out_ref[:, :width] = first_ref[...]
    out_ref[:, width:] = second_ref[...]


def joined(first, second, after):
    return kernel_call(
        joined_kernel,
        shape(first.shape[0], 2 * first.shape[1]),
        [VMEM, VMEM, ANY],
        VMEM,
        first.shape[0],
    )(first, second, after)


def turned_kernel(skip, rows, own_ref, arrived_ref, bias_ref, order_ref, out_ref):
    bias = jnp.concatenate([bias_ref[...]] * rows, axis=0)
    bias = stacked(bias, ROWS // rows)
    width = bias.shape[1]
    blocks = [
        (ref[:, at : at + width].astype(jnp.float32) - bias).astype(jnp.bfloat16)
        for ref in (own_ref, arrived_ref)
        for at in range(skip, ref.shape[1], width)
    ]
    ordered = jnp.dot(
        order_ref[...], jnp.concatenate(blocks, axis=0), preferred_element_type=jnp.float32
    )
    out_ref[...] = ordered.T.astype(jnp.bfloat16)


def turned(own, arrived, skip, bias, order, rows, count):
    width = bias.shape[1] * rows // ROWS
    return kernel_call(
        functools.partial(turned_kernel, skip, rows),
        shape(width, 2 * (own.shape[1] - skip) // width * ROWS),
        [VMEM] * 4,
        VMEM,
        count,
    )(own, arrived, bias, order)


def scaled_of(total_ref, arrived_ref):
    total = total_ref[...] + arrived_ref[:, : total_ref.shape[1]].astype(jnp.float32)
    return (0.25 * total).astype(jnp.bfloat16)


def product(part, rows_ref, at):
    return lax.dot_general(
        part,
        rows_ref[:, at : at + part.shape[1]],
        (((1,), (1,)), ((), ())),
        preferred_element_type=jnp.float32,
    )


def first_product_kernel(total_ref, arrived_ref, rows_ref, scaled_ref, half_ref):
    scaled = scaled_of(total_ref, arrived_ref)
    scaled_ref[...] = scaled
    half_ref[...] = product(scaled, rows_ref, 0)


def second_product_kernel(total_ref, arrived_ref, rows_ref, first_ref, scaled_ref, half_ref):
    scaled = scaled_of(total_ref, arrived_ref)
    scaled_ref[...] = scaled
    half_ref[...] = first_ref[...] + product(scaled, rows_ref, rows_ref.shape[1] - scaled.shape[1])


def products(total, arrived, dict_rows, *first):
    count, width = total.shape
    return kernel_call(
        second_product_kernel if first else first_product_kernel,
        (shape(count, width), shape(count, dict_rows.shape[0], dtype=jnp.float32)),
        [VMEM] * (3 + len(first)),
        (VMEM, VMEM),
        count,
    )(total, arrived, dict_rows, *first)


def outer(code_ref, scaled):
    code = code_ref[...].astype(jnp.float32).T.astype(jnp.bfloat16)
    return jnp.dot(code, scaled, preferred_element_type=jnp.float32).astype(jnp.bfloat16)


def grad_rows_kernel(code_ref, first_ref, second_ref, out_ref):
    chunk = first_ref.shape[1]
    out_ref[:, :chunk] = outer(code_ref, first_ref[...])
    out_ref[:, chunk:] = outer(code_ref, second_ref[...])


def grad_rows_of(code, first, second):
    count, slots = code.shape
    return kernel_call(
        grad_rows_kernel,
        shape(slots, first.shape[1] + second.shape[1]),
        [VMEM] * 3,
        VMEM,
        count,
    )(code, first, second)


def final_kernel(
    rows,
    raw_ref,
    mine_ref,
    theirs_ref,
    turned_ref,
    rows_ref,
    rows_hbm,
    enc_hbm,
    benc_hbm,
    enc_ref,
    benc_ref,
    sems,
):
    copies = [pltpu.make_async_copy(rows_ref, rows_hbm, sems.at[0])]
    copies[0].start()
    count, slots = raw_ref.shape
    width = turned_ref.shape[0]
    pieces = ROWS // rows
    code_grad = mine_ref[...] + theirs_ref[...]
    pre_grad = jnp.where(raw_ref[...] > 0.0, code_grad, 0.0).astype(jnp.bfloat16)
    benc_ref[...] = jnp.sum(pre_grad.astype(jnp.float32), axis=0, keepdims=True)
    copies.append(pltpu.make_async_copy(benc_ref, benc_hbm, sems.at[1]))
    copies[1].start()
    zeros = jnp.zeros_like(pre_grad)
    for c in range(0, pieces, 2):
        pair = [
            jnp.concatenate([zeros] * at + [pre_grad] + [zeros] * (pieces - 1 - at), axis=0)
            for at in (c, c + 1)
        ]
        out = jnp.dot(
            turned_ref[...],
            jnp.concatenate(pair, axis=1),
            preferred_element_type=jnp.float32,
        ).astype(jnp.bfloat16)
        for i in range(2):
            enc_ref[(c + i) * width : (c + i + 1) * width, :] = out[:, i * slots : (i + 1) * slots]
        part = pl.ds(c * width, 2 * width)
        copies.append(pltpu.make_async_copy(enc_ref.at[part], enc_hbm.at[part], sems.at[c // 2 + 2]))
        copies[-1].start()
    for copy in copies:
        copy.wait()


def final(raw, mine, theirs, turned_tokens, grad_rows, rows):
    count, slots = raw.shape
    pieces = ROWS // rows
    width = turned_tokens.shape[0] * pieces
    return kernel_call(
        functools.partial(final_kernel, rows),
        (shape(*grad_rows.shape), shape(width, slots), shape(1, slots, dtype=jnp.float32)),
        [VMEM] * 5,
        (HBM, HBM, HBM),
        count,
        [
            pltpu.VMEM((width, slots), jnp.bfloat16),
            pltpu.VMEM((1, slots), jnp.float32),
            pltpu.SemaphoreType.DMA((pieces // 2 + 2,)),
        ],
    )(raw, mine, theirs, turned_tokens, grad_rows)


def local(tokens, b_pre, pre_codes, top_idx, blocks, counts, dict_rows):
    rows, count = tokens.shape[0], top_idx.shape[0]
    steps = feat_bits()
    merged = count == ROWS

    order = order_of(rows, count)
    code, raw, total, sent, centered, bias, *block = front(
        tokens, b_pre, pre_codes, top_idx, blocks, counts, dict_rows, order, merged
    )
    for step in range(steps):
        arrived = swapped(sent, step)
        if step == 0:
            total_second, sent_second = second(code, dict_rows, centered)
        else:
            total_second, sent_second = added(
                total_second, sent_second, arrived_second, sent, False, EARLY
            )
        arrived_second = swapped(sent_second, step)
        if not merged:
            own_block = joined(own_block, arrived_block, sent_second) if step else block[0]
            arrived_block = swapped(own_block, step)
        if step < steps - 1:
            total, sent = added(total, sent, arrived, sent_second, merged)
    skip = 0
    if merged:
        own_block, arrived_block, skip = sent, arrived, total.shape[1]

    scaled, product_first = products(total, arrived, dict_rows)
    turned_tokens = turned(own_block, arrived_block, skip, bias, order, rows, count)
    scaled_second, code_half = products(
        total_second, arrived_second, dict_rows, product_first
    )
    theirs = lax.ppermute(code_half, "tok", [(i, 1 - i) for i in range(2)])
    grad_rows = grad_rows_of(code, scaled, scaled_second)
    grad_rows, grad_enc, grad_benc = final(
        raw, code_half, theirs, turned_tokens, grad_rows, rows
    )
    return (grad_rows, grad_enc, grad_benc.reshape(-1))


def solution(mesh):
    return jax.shard_map(
        local,
        mesh=mesh,
        in_specs=(
            P(("grp", "feat"), "tok"),
            P(("grp", "tok")),
            P("grp", None),
            P("grp", None),
            P(("grp", "feat")),
            P(("grp", "feat")),
            P(("grp", "feat"), "tok"),
        ),
        out_specs=(P(("grp", "feat"), "tok"), P(("grp", "tok"), "feat"), P(("grp", "feat"))),
        check_vma=False,
    )
```

```python
import functools

import jax
import jax.numpy as jnp
from jax import lax
from jax.experimental import pallas as pl
from jax.experimental.pallas import tpu as pltpu
from jax.sharding import PartitionSpec as P

VMEM = pl.BlockSpec(memory_space=pltpu.VMEM)
SMEM = pl.BlockSpec(memory_space=pltpu.SMEM)
HBM = pl.BlockSpec(memory_space=pltpu.HBM)
ANY = pl.BlockSpec(memory_space=pl.ANY)
EARLY = 10**9
ROWS = 16


def kernel_call(kernel, out_shape, in_specs, out_specs, tokens, scratch_shapes=(), flops=10**6):
    limit = (16 if tokens <= ROWS else 40) * 2**20
    return pl.pallas_call(
        kernel,
        out_shape=out_shape,
        in_specs=in_specs,
        out_specs=out_specs,
        scratch_shapes=scratch_shapes,
        compiler_params=pltpu.CompilerParams(vmem_limit_bytes=limit),
        cost_estimate=pl.CostEstimate(flops=flops, bytes_accessed=2**20, transcendentals=0),
    )


def shape(*sizes, dtype=jnp.bfloat16):
    return jax.ShapeDtypeStruct(sizes, dtype)


def first_width(width):
    return width * 9 // 16 // 128 * 128


def feat_bits():
    return (lax.axis_size("feat") - 1).bit_length()


def bit_of(step, core):
    bits = list(range(feat_bits()))
    first = bits[-1:] + bits[:-1]
    return (first if core == 0 else bits[1:2] + bits[:1] + bits[2:])[step]


def swapped(shard, step):
    cores = lax.axis_size("tok")
    pairs = [
        (f * cores + c, (f ^ 1 << bit_of(step, c)) * cores + c)
        for f in range(lax.axis_size("feat"))
        for c in range(cores)
    ]
    return lax.ppermute(shard, ("feat", "tok"), pairs)


def stacked(rows, pieces):
    width = rows.shape[1] // pieces
    return jnp.concatenate(
        [rows[:, c * width : (c + 1) * width] for c in range(pieces)], axis=0
    )


def share(code, rows_ref, centered_ref, at, width):
    part = pl.ds(at, width)
    total = jnp.dot(code, rows_ref[:, part], preferred_element_type=jnp.float32)
    rows = centered_ref.shape[0]
    centered = centered_ref[:, part]
    token = lax.broadcasted_iota(jnp.int32, (total.shape[0], 1), 0)
    first = lax.axis_index("feat") * rows
    for i in range(rows):
        total -= jnp.where(token == first + i, centered[i : i + 1, :], 0.0)
    return total


def order_kernel(rows, order_ref):
    target = lax.broadcasted_iota(jnp.int32, order_ref.shape, 0)
    place = lax.broadcasted_iota(jnp.int32, order_ref.shape, 1)
    core = lax.axis_index("tok")
    block = place // ROWS
    distance = jnp.zeros_like(place)
    for step in range(feat_bits()):
        bit = sum(
            jnp.where(core == c, bit_of(step, c), 0) for c in range(lax.axis_size("tok"))
        )
        distance |= (block >> step & 1) << bit
    token = (lax.axis_index("feat") ^ distance) * rows + place % rows
    piece = place % ROWS // rows
    count = rows * lax.axis_size("feat")
    order_ref[...] = jnp.where(target == piece * count + token, 1.0, 0.0).astype(jnp.bfloat16)


def order_of(rows, count):
    depth = ROWS * lax.axis_size("feat")
    return kernel_call(
        functools.partial(order_kernel, rows),
        shape(depth, depth),
        [],
        VMEM,
        count,
        flops=EARLY,
    )()


def front_kernel(
    tokens_ref, bias_flat, pre_ref, top_ref, rows_ref, block_ref, count_ref, after_ref, *refs
):
    code_ref, raw_ref, total_ref, sent_ref, centered_ref, bias_ref, *cut = refs
    count, latents = top_ref.shape
    slots, width = rows_ref.shape
    offsets = lax.broadcasted_iota(jnp.int32, (1, slots), 1)
    slot_ids = jnp.where(offsets < count_ref[0], block_ref[0] * slots + offsets, -1)
    top, pre = top_ref[...], pre_ref[...]
    raw = jnp.zeros((count, slots), jnp.float32)
    for k in range(latents):
        raw = jnp.where(top[:, k : k + 1] == slot_ids, pre[:, k : k + 1], raw)
    raw_ref[...] = raw
    code = jnp.maximum(raw, 0.0).astype(jnp.bfloat16)
    code_ref[...] = code

    tokens = tokens_ref[...].astype(jnp.float32)
    bias = bias_flat[...].astype(jnp.float32).reshape(1, width)
    bias_ref[...] = bias
    centered_ref[...] = (tokens - bias).astype(jnp.bfloat16).astype(jnp.float32)

    total = share(code, rows_ref, centered_ref, 0, total_ref.shape[1])
    total_ref[...] = total
    width = total.shape[1]
    sent_ref[:, :width] = total.astype(jnp.bfloat16)
    block = stacked(tokens, ROWS // tokens.shape[0]).astype(jnp.bfloat16)
    if cut:
        cut[0][...] = block
    else:
        sent_ref[:, width:] = block


def front(tokens, b_pre, pre_codes, top_idx, blocks, counts, dict_rows, after, merged):
    count = top_idx.shape[0]
    slots, width = dict_rows.shape
    chunk, block = first_width(width), tokens.shape[0] * width // ROWS
    return kernel_call(
        front_kernel,
        (
            shape(count, slots),
            shape(count, slots, dtype=jnp.float32),
            shape(count, chunk, dtype=jnp.float32),
            shape(count, chunk + (block if merged else 0)),
            shape(*tokens.shape, dtype=jnp.float32),
            shape(1, width, dtype=jnp.float32),
            *([] if merged else [shape(ROWS, block)]),
        ),
        [VMEM] * 5 + [SMEM] * 2 + [ANY],
        (VMEM,) * (6 if merged else 7),
        count,
    )(tokens, b_pre, pre_codes, top_idx, dict_rows, blocks, counts, after)


def second_kernel(code_ref, rows_ref, centered_ref, total_ref, sent_ref):
    width = total_ref.shape[1]
    total = share(code_ref[...], rows_ref, centered_ref, rows_ref.shape[1] - width, width)
    total_ref[...] = total
    sent_ref[...] = total.astype(jnp.bfloat16)


def second(code, dict_rows, centered):
    count, width = code.shape[0], dict_rows.shape[1]
    chunk = width - first_width(width)
    return kernel_call(
        second_kernel,
        (shape(count, chunk, dtype=jnp.float32), shape(count, chunk)),
        [VMEM] * 3,
        (VMEM, VMEM),
        count,
    )(code, dict_rows, centered)


def added_kernel(total_ref, own_ref, arrived_ref, after_ref, sum_ref, sent_ref):
    half = total_ref.shape[1]
    total = total_ref[...] + arrived_ref[:, :half].astype(jnp.float32)
    sum_ref[...] = total
    sent_ref[:, :half] = total.astype(jnp.bfloat16)
    if sent_ref.shape[1] > half:
        block = own_ref.shape[1] - half
        sent_ref[:, half : half + block] = own_ref[:, half:]
        sent_ref[:, half + block :] = arrived_ref[:, half:]


def added(total, own, arrived, after, merged, flops=10**6):
    count, half = total.shape
    block = own.shape[1] - half
    return kernel_call(
        added_kernel,
        (
            shape(count, half, dtype=jnp.float32),
            shape(count, half + (2 * block if merged else 0)),
        ),
        [VMEM] * 3 + [ANY],
        (VMEM, VMEM),
        count,
        flops=flops,
    )(total, own, arrived, after)


def joined_kernel(first_ref, second_ref, after_ref, out_ref):
    width = first_ref.shape[1]
    out_ref[:, :width] = first_ref[...]
    out_ref[:, width:] = second_ref[...]


def joined(first, second, after):
    return kernel_call(
        joined_kernel,
        shape(first.shape[0], 2 * first.shape[1]),
        [VMEM, VMEM, ANY],
        VMEM,
        first.shape[0],
    )(first, second, after)


def turned_kernel(skip, rows, own_ref, arrived_ref, bias_ref, order_ref, out_ref):
    bias = jnp.concatenate([bias_ref[...]] * rows, axis=0)
    bias = stacked(bias, ROWS // rows)
    width = bias.shape[1]
    blocks = [
        (ref[:, at : at + width].astype(jnp.float32) - bias).astype(jnp.bfloat16)
        for ref in (own_ref, arrived_ref)
        for at in range(skip, ref.shape[1], width)
    ]
    ordered = jnp.dot(
        order_ref[...], jnp.concatenate(blocks, axis=0), preferred_element_type=jnp.float32
    )
    out_ref[...] = ordered.T.astype(jnp.bfloat16)


def turned(own, arrived, skip, bias, order, rows, count):
    width = bias.shape[1] * rows // ROWS
    return kernel_call(
        functools.partial(turned_kernel, skip, rows),
        shape(width, 2 * (own.shape[1] - skip) // width * ROWS),
        [VMEM] * 4,
        VMEM,
        count,
    )(own, arrived, bias, order)


def scaled_of(total_ref, arrived_ref):
    total = total_ref[...] + arrived_ref[:, : total_ref.shape[1]].astype(jnp.float32)
    return (0.25 * total).astype(jnp.bfloat16)


def product(part, rows_ref, at):
    return lax.dot_general(
        part,
        rows_ref[:, at : at + part.shape[1]],
        (((1,), (1,)), ((), ())),
        preferred_element_type=jnp.float32,
    )


def first_product_kernel(total_ref, arrived_ref, rows_ref, scaled_ref, half_ref):
    scaled = scaled_of(total_ref, arrived_ref)
    scaled_ref[...] = scaled
    half_ref[...] = product(scaled, rows_ref, 0)


def second_product_kernel(total_ref, arrived_ref, rows_ref, first_ref, scaled_ref, half_ref):
    scaled = scaled_of(total_ref, arrived_ref)
    scaled_ref[...] = scaled
    half_ref[...] = first_ref[...] + product(scaled, rows_ref, rows_ref.shape[1] - scaled.shape[1])


def products(total, arrived, dict_rows, *first):
    count, width = total.shape
    return kernel_call(
        second_product_kernel if first else first_product_kernel,
        (shape(count, width), shape(count, dict_rows.shape[0], dtype=jnp.float32)),
        [VMEM] * (3 + len(first)),
        (VMEM, VMEM),
        count,
    )(total, arrived, dict_rows, *first)


def outer(code_ref, scaled):
    code = code_ref[...].astype(jnp.float32).T.astype(jnp.bfloat16)
    return jnp.dot(code, scaled, preferred_element_type=jnp.float32).astype(jnp.bfloat16)


def grad_rows_kernel(code_ref, first_ref, second_ref, out_ref):
    chunk = first_ref.shape[1]
    out_ref[:, :chunk] = outer(code_ref, first_ref[...])
    out_ref[:, chunk:] = outer(code_ref, second_ref[...])


def grad_rows_of(code, first, second):
    count, slots = code.shape
    return kernel_call(
        grad_rows_kernel,
        shape(slots, first.shape[1] + second.shape[1]),
        [VMEM] * 3,
        VMEM,
        count,
    )(code, first, second)


def final_kernel(
    rows,
    raw_ref,
    mine_ref,
    theirs_ref,
    turned_ref,
    rows_ref,
    rows_hbm,
    enc_hbm,
    benc_hbm,
    enc_ref,
    benc_ref,
    sems,
):
    copies = [pltpu.make_async_copy(rows_ref, rows_hbm, sems.at[0])]
    copies[0].start()
    count, slots = raw_ref.shape
    width = turned_ref.shape[0]
    pieces = ROWS // rows
    code_grad = mine_ref[...] + theirs_ref[...]
    pre_grad = jnp.where(raw_ref[...] > 0.0, code_grad, 0.0).astype(jnp.bfloat16)
    benc_ref[...] = jnp.sum(pre_grad.astype(jnp.float32), axis=0, keepdims=True)
    copies.append(pltpu.make_async_copy(benc_ref, benc_hbm, sems.at[1]))
    copies[1].start()
    zeros = jnp.zeros_like(pre_grad)
    for c in range(0, pieces, 2):
        pair = [
            jnp.concatenate([zeros] * at + [pre_grad] + [zeros] * (pieces - 1 - at), axis=0)
            for at in (c, c + 1)
        ]
        out = jnp.dot(
            turned_ref[...],
            jnp.concatenate(pair, axis=1),
            preferred_element_type=jnp.float32,
        ).astype(jnp.bfloat16)
        for i in range(2):
            enc_ref[(c + i) * width : (c + i + 1) * width, :] = out[:, i * slots : (i + 1) * slots]
        part = pl.ds(c * width, 2 * width)
        copies.append(pltpu.make_async_copy(enc_ref.at[part], enc_hbm.at[part], sems.at[c // 2 + 2]))
        copies[-1].start()
    for copy in copies:
        copy.wait()


def final(raw, mine, theirs, turned_tokens, grad_rows, rows):
    count, slots = raw.shape
    pieces = ROWS // rows
    width = turned_tokens.shape[0] * pieces
    return kernel_call(
        functools.partial(final_kernel, rows),
        (shape(*grad_rows.shape), shape(width, slots), shape(1, slots, dtype=jnp.float32)),
        [VMEM] * 5,
        (HBM, HBM, HBM),
        count,
        [
            pltpu.VMEM((width, slots), jnp.bfloat16),
            pltpu.VMEM((1, slots), jnp.float32),
            pltpu.SemaphoreType.DMA((pieces // 2 + 2,)),
        ],
    )(raw, mine, theirs, turned_tokens, grad_rows)


def local(tokens, b_pre, pre_codes, top_idx, blocks, counts, dict_rows):
    rows, count = tokens.shape[0], top_idx.shape[0]
    steps = feat_bits()
    merged = count == ROWS

    order = order_of(rows, count)
    code, raw, total, sent, centered, bias, *block = front(
        tokens, b_pre, pre_codes, top_idx, blocks, counts, dict_rows, order, merged
    )
    for step in range(steps):
        arrived = swapped(sent, step)
        if step == 0:
            total_second, sent_second = second(code, dict_rows, centered)
        else:
            total_second, sent_second = added(
                total_second, sent_second, arrived_second, sent, False, EARLY
            )
        arrived_second = swapped(sent_second, step)
        if not merged:
            own_block = joined(own_block, arrived_block, sent_second) if step else block[0]
            arrived_block = swapped(own_block, step)
        if step < steps - 1:
            total, sent = added(total, sent, arrived, sent_second, merged)
    skip = 0
    if merged:
        own_block, arrived_block, skip = sent, arrived, total.shape[1]

    scaled, product_first = products(total, arrived, dict_rows)
    turned_tokens = turned(own_block, arrived_block, skip, bias, order, rows, count)
    scaled_second, code_half = products(
        total_second, arrived_second, dict_rows, product_first
    )
    theirs = lax.ppermute(code_half, "tok", [(i, 1 - i) for i in range(2)])
    grad_rows = grad_rows_of(code, scaled, scaled_second)
    grad_rows, grad_enc, grad_benc = final(
        raw, code_half, theirs, turned_tokens, grad_rows, rows
    )
    return (grad_rows, grad_enc, grad_benc.reshape(-1))


def solution(mesh):
    return jax.shard_map(
        local,
        mesh=mesh,
        in_specs=(
            P(("grp", "feat"), "tok"),
            P(("grp", "tok")),
            P("grp", None),
            P("grp", None),
            P(("grp", "feat")),
            P(("grp", "feat")),
            P(("grp", "feat"), "tok"),
        ),
        out_specs=(P(("grp", "feat"), "tok"), P(("grp", "tok"), "feat"), P(("grp", "feat"))),
        check_vma=False,
    )
```

```python
import functools

import jax
import jax.numpy as jnp
from jax import lax
from jax.experimental import pallas as pl
from jax.experimental.pallas import tpu as pltpu
from jax.sharding import PartitionSpec as P

VMEM = pl.BlockSpec(memory_space=pltpu.VMEM)
SMEM = pl.BlockSpec(memory_space=pltpu.SMEM)
HBM = pl.BlockSpec(memory_space=pltpu.HBM)
ANY = pl.BlockSpec(memory_space=pl.ANY)
EARLY = 10**9
ROWS = 16


def kernel_call(kernel, out_shape, in_specs, out_specs, tokens, scratch_shapes=(), flops=10**6):
    limit = (16 if tokens <= ROWS else 40) * 2**20
    return pl.pallas_call(
        kernel,
        out_shape=out_shape,
        in_specs=in_specs,
        out_specs=out_specs,
        scratch_shapes=scratch_shapes,
        compiler_params=pltpu.CompilerParams(vmem_limit_bytes=limit),
        cost_estimate=pl.CostEstimate(flops=flops, bytes_accessed=2**20, transcendentals=0),
    )


def shape(*sizes, dtype=jnp.bfloat16):
    return jax.ShapeDtypeStruct(sizes, dtype)


def first_width(width):
    return width // 2


def feat_bits():
    return (lax.axis_size("feat") - 1).bit_length()


def bit_of(step, core):
    bits = list(range(feat_bits()))
    first = bits[-1:] + bits[:-1]
    return (first if core == 0 else bits[1:2] + bits[:1] + bits[2:])[step]


def swapped(shard, step):
    cores = lax.axis_size("tok")
    pairs = [
        (f * cores + c, (f ^ 1 << bit_of(step, c)) * cores + c)
        for f in range(lax.axis_size("feat"))
        for c in range(cores)
    ]
    return lax.ppermute(shard, ("feat", "tok"), pairs)


def stacked(rows, pieces):
    width = rows.shape[1] // pieces
    return jnp.concatenate(
        [rows[:, c * width : (c + 1) * width] for c in range(pieces)], axis=0
    )


def share(code, rows_ref, centered_ref, at, width):
    part = pl.ds(at, width)
    total = jnp.dot(code, rows_ref[:, part], preferred_element_type=jnp.float32)
    rows = centered_ref.shape[0]
    centered = centered_ref[:, part]
    token = lax.broadcasted_iota(jnp.int32, (total.shape[0], 1), 0)
    first = lax.axis_index("feat") * rows
    for i in range(rows):
        total -= jnp.where(token == first + i, centered[i : i + 1, :], 0.0)
    return total


def order_kernel(rows, order_ref):
    target = lax.broadcasted_iota(jnp.int32, order_ref.shape, 0)
    place = lax.broadcasted_iota(jnp.int32, order_ref.shape, 1)
    core = lax.axis_index("tok")
    block = place // ROWS
    distance = jnp.zeros_like(place)
    for step in range(feat_bits()):
        bit = sum(
            jnp.where(core == c, bit_of(step, c), 0) for c in range(lax.axis_size("tok"))
        )
        distance |= (block >> step & 1) << bit
    token = (lax.axis_index("feat") ^ distance) * rows + place % rows
    piece = place % ROWS // rows
    count = rows * lax.axis_size("feat")
    order_ref[...] = jnp.where(target == piece * count + token, 1.0, 0.0).astype(jnp.bfloat16)


def order_of(rows, count):
    depth = ROWS * lax.axis_size("feat")
    return kernel_call(
        functools.partial(order_kernel, rows),
        shape(depth, depth),
        [],
        VMEM,
        count,
        flops=EARLY,
    )()


def front_kernel(
    tokens_ref, bias_flat, pre_ref, top_ref, rows_ref, block_ref, count_ref, after_ref, *refs
):
    code_ref, raw_ref, total_ref, sent_ref, centered_ref, bias_ref, *cut = refs
    count, latents = top_ref.shape
    slots, width = rows_ref.shape
    offsets = lax.broadcasted_iota(jnp.int32, (1, slots), 1)
    slot_ids = jnp.where(offsets < count_ref[0], block_ref[0] * slots + offsets, -1)
    top, pre = top_ref[...], pre_ref[...]
    raw = jnp.zeros((count, slots), jnp.float32)
    for k in range(latents):
        raw = jnp.where(top[:, k : k + 1] == slot_ids, pre[:, k : k + 1], raw)
    raw_ref[...] = raw
    code = jnp.maximum(raw, 0.0).astype(jnp.bfloat16)
    code_ref[...] = code

    tokens = tokens_ref[...].astype(jnp.float32)
    bias = bias_flat[...].astype(jnp.float32).reshape(1, width)
    bias_ref[...] = bias
    centered_ref[...] = (tokens - bias).astype(jnp.bfloat16).astype(jnp.float32)

    total = share(code, rows_ref, centered_ref, 0, total_ref.shape[1])
    total_ref[...] = total
    width = total.shape[1]
    sent_ref[:, :width] = total.astype(jnp.bfloat16)
    block = stacked(tokens, ROWS // tokens.shape[0]).astype(jnp.bfloat16)
    if cut:
        cut[0][...] = block
    else:
        sent_ref[:, width:] = block


def front(tokens, b_pre, pre_codes, top_idx, blocks, counts, dict_rows, after, merged):
    count = top_idx.shape[0]
    slots, width = dict_rows.shape
    chunk, block = first_width(width), tokens.shape[0] * width // ROWS
    return kernel_call(
        front_kernel,
        (
            shape(count, slots),
            shape(count, slots, dtype=jnp.float32),
            shape(count, chunk, dtype=jnp.float32),
            shape(count, chunk + (block if merged else 0)),
            shape(*tokens.shape, dtype=jnp.float32),
            shape(1, width, dtype=jnp.float32),
            *([] if merged else [shape(ROWS, block)]),
        ),
        [VMEM] * 5 + [SMEM] * 2 + [ANY],
        (VMEM,) * (6 if merged else 7),
        count,
    )(tokens, b_pre, pre_codes, top_idx, dict_rows, blocks, counts, after)


def second_kernel(code_ref, rows_ref, centered_ref, total_ref, sent_ref):
    width = total_ref.shape[1]
    total = share(code_ref[...], rows_ref, centered_ref, rows_ref.shape[1] - width, width)
    total_ref[...] = total
    sent_ref[...] = total.astype(jnp.bfloat16)


def second(code, dict_rows, centered):
    count, width = code.shape[0], dict_rows.shape[1]
    chunk = width - first_width(width)
    return kernel_call(
        second_kernel,
        (shape(count, chunk, dtype=jnp.float32), shape(count, chunk)),
        [VMEM] * 3,
        (VMEM, VMEM),
        count,
    )(code, dict_rows, centered)


def added_kernel(total_ref, own_ref, arrived_ref, after_ref, sum_ref, sent_ref):
    half = total_ref.shape[1]
    total = total_ref[...] + arrived_ref[:, :half].astype(jnp.float32)
    sum_ref[...] = total
    sent_ref[:, :half] = total.astype(jnp.bfloat16)
    if sent_ref.shape[1] > half:
        block = own_ref.shape[1] - half
        sent_ref[:, half : half + block] = own_ref[:, half:]
        sent_ref[:, half + block :] = arrived_ref[:, half:]


def added(total, own, arrived, after, merged, flops=10**6):
    count, half = total.shape
    block = own.shape[1] - half
    return kernel_call(
        added_kernel,
        (
            shape(count, half, dtype=jnp.float32),
            shape(count, half + (2 * block if merged else 0)),
        ),
        [VMEM] * 3 + [ANY],
        (VMEM, VMEM),
        count,
        flops=flops,
    )(total, own, arrived, after)


def joined_kernel(first_ref, second_ref, after_ref, out_ref):
    width = first_ref.shape[1]
    out_ref[:, :width] = first_ref[...]
    out_ref[:, width:] = second_ref[...]


def joined(first, second, after):
    return kernel_call(
        joined_kernel,
        shape(first.shape[0], 2 * first.shape[1]),
        [VMEM, VMEM, ANY],
        VMEM,
        first.shape[0],
    )(first, second, after)


def turned_kernel(skip, rows, own_ref, arrived_ref, bias_ref, order_ref, out_ref):
    bias = jnp.concatenate([bias_ref[...]] * rows, axis=0)
    bias = stacked(bias, ROWS // rows)
    width = bias.shape[1]
    blocks = [
        (ref[:, at : at + width].astype(jnp.float32) - bias).astype(jnp.bfloat16)
        for ref in (own_ref, arrived_ref)
        for at in range(skip, ref.shape[1], width)
    ]
    ordered = jnp.dot(
        order_ref[...], jnp.concatenate(blocks, axis=0), preferred_element_type=jnp.float32
    )
    out_ref[...] = ordered.T.astype(jnp.bfloat16)


def turned(own, arrived, skip, bias, order, rows, count):
    width = bias.shape[1] * rows // ROWS
    return kernel_call(
        functools.partial(turned_kernel, skip, rows),
        shape(width, 2 * (own.shape[1] - skip) // width * ROWS),
        [VMEM] * 4,
        VMEM,
        count,
    )(own, arrived, bias, order)


def scaled_of(total_ref, arrived_ref):
    total = total_ref[...] + arrived_ref[:, : total_ref.shape[1]].astype(jnp.float32)
    return (0.25 * total).astype(jnp.bfloat16)


def product(part, rows_ref, at):
    return lax.dot_general(
        part,
        rows_ref[:, at : at + part.shape[1]],
        (((1,), (1,)), ((), ())),
        preferred_element_type=jnp.float32,
    )


def first_product_kernel(total_ref, arrived_ref, rows_ref, scaled_ref, half_ref):
    scaled = scaled_of(total_ref, arrived_ref)
    scaled_ref[...] = scaled
    half_ref[...] = product(scaled, rows_ref, 0)


def second_product_kernel(
    total_ref, arrived_ref, rows_ref, first_ref, after_ref, scaled_ref, half_ref
):
    scaled = scaled_of(total_ref, arrived_ref)
    scaled_ref[...] = scaled
    half_ref[...] = first_ref[...] + product(scaled, rows_ref, rows_ref.shape[1] - scaled.shape[1])


def products(total, arrived, dict_rows, *first):
    count, width = total.shape
    return kernel_call(
        second_product_kernel if first else first_product_kernel,
        (shape(count, width), shape(count, dict_rows.shape[0], dtype=jnp.float32)),
        [VMEM] * 3 + ([VMEM, ANY] if first else []),
        (VMEM, VMEM),
        count,
    )(total, arrived, dict_rows, *first)


def outer(code_ref, scaled):
    code = code_ref[...].astype(jnp.float32).T.astype(jnp.bfloat16)
    return jnp.dot(code, scaled, preferred_element_type=jnp.float32).astype(jnp.bfloat16)


def grad_rows_kernel(code_ref, first_ref, second_ref, out_ref):
    chunk = first_ref.shape[1]
    out_ref[:, :chunk] = outer(code_ref, first_ref[...])
    out_ref[:, chunk:] = outer(code_ref, second_ref[...])


def grad_rows_of(code, first, second):
    count, slots = code.shape
    return kernel_call(
        grad_rows_kernel,
        shape(slots, first.shape[1] + second.shape[1]),
        [VMEM] * 3,
        VMEM,
        count,
    )(code, first, second)


def final_kernel(
    rows,
    raw_ref,
    mine_ref,
    theirs_ref,
    turned_ref,
    rows_ref,
    rows_hbm,
    enc_hbm,
    benc_hbm,
    enc_ref,
    benc_ref,
    sems,
):
    copies = [pltpu.make_async_copy(rows_ref, rows_hbm, sems.at[0])]
    copies[0].start()
    count, slots = raw_ref.shape
    width = turned_ref.shape[0]
    pieces = ROWS // rows
    code_grad = mine_ref[...] + theirs_ref[...]
    pre_grad = jnp.where(raw_ref[...] > 0.0, code_grad, 0.0).astype(jnp.bfloat16)
    benc_ref[...] = jnp.sum(pre_grad.astype(jnp.float32), axis=0, keepdims=True)
    copies.append(pltpu.make_async_copy(benc_ref, benc_hbm, sems.at[1]))
    copies[1].start()
    zeros = jnp.zeros_like(pre_grad)
    group = pieces // 2
    for c in range(0, pieces, group):
        placed = [
            jnp.concatenate([zeros] * at + [pre_grad] + [zeros] * (pieces - 1 - at), axis=0)
            for at in range(c, c + group)
        ]
        out = jnp.dot(
            turned_ref[...],
            jnp.concatenate(placed, axis=1),
            preferred_element_type=jnp.float32,
        ).astype(jnp.bfloat16)
        for i in range(group):
            enc_ref[(c + i) * width : (c + i + 1) * width, :] = out[:, i * slots : (i + 1) * slots]
        for i in range(0, group, 2):
            part = pl.ds((c + i) * width, 2 * width)
            copies.append(
                pltpu.make_async_copy(enc_ref.at[part], enc_hbm.at[part], sems.at[(c + i) // 2 + 2])
            )
            copies[-1].start()
    for copy in copies:
        copy.wait()


def final(raw, mine, theirs, turned_tokens, grad_rows, rows):
    count, slots = raw.shape
    pieces = ROWS // rows
    width = turned_tokens.shape[0] * pieces
    return kernel_call(
        functools.partial(final_kernel, rows),
        (shape(*grad_rows.shape), shape(width, slots), shape(1, slots, dtype=jnp.float32)),
        [VMEM] * 5,
        (HBM, HBM, HBM),
        count,
        [
            pltpu.VMEM((width, slots), jnp.bfloat16),
            pltpu.VMEM((1, slots), jnp.float32),
            pltpu.SemaphoreType.DMA((pieces // 2 + 2,)),
        ],
    )(raw, mine, theirs, turned_tokens, grad_rows)


def local(tokens, b_pre, pre_codes, top_idx, blocks, counts, dict_rows):
    rows, count = tokens.shape[0], top_idx.shape[0]
    steps = feat_bits()
    merged = count == ROWS

    order = order_of(rows, count)
    code, raw, total, sent, centered, bias, *block = front(
        tokens, b_pre, pre_codes, top_idx, blocks, counts, dict_rows, order, merged
    )
    for step in range(steps):
        arrived = swapped(sent, step)
        if step == 0:
            total_second, sent_second = second(code, dict_rows, centered)
        else:
            total_second, sent_second = added(
                total_second, sent_second, arrived_second, sent, False, EARLY
            )
        arrived_second = swapped(sent_second, step)
        if not merged:
            own_block = joined(own_block, arrived_block, sent_second) if step else block[0]
            arrived_block = swapped(own_block, step)
        if step < steps - 1:
            total, sent = added(total, sent, arrived, sent_second, merged)
    skip = 0
    if merged:
        own_block, arrived_block, skip = sent, arrived, total.shape[1]

    scaled, product_first = products(total, arrived, dict_rows)
    turned_tokens = turned(own_block, arrived_block, skip, bias, order, rows, count)
    scaled_second, code_half = products(
        total_second, arrived_second, dict_rows, product_first, turned_tokens
    )
    theirs = lax.ppermute(code_half, "tok", [(i, 1 - i) for i in range(2)])
    grad_rows = grad_rows_of(code, scaled, scaled_second)
    grad_rows, grad_enc, grad_benc = final(
        raw, code_half, theirs, turned_tokens, grad_rows, rows
    )
    return (grad_rows, grad_enc, grad_benc.reshape(-1))


def solution(mesh):
    return jax.shard_map(
        local,
        mesh=mesh,
        in_specs=(
            P(("grp", "feat"), "tok"),
            P(("grp", "tok")),
            P("grp", None),
            P("grp", None),
            P(("grp", "feat")),
            P(("grp", "feat")),
            P(("grp", "feat"), "tok"),
        ),
        out_specs=(P(("grp", "feat"), "tok"), P(("grp", "tok"), "feat"), P(("grp", "feat"))),
        check_vma=False,
    )
```
